32 devices in a mesh: ctx: 8 (over z, y), head: 4 (over x, core).
Axes of the slice: x: 2, y: 2, z: 4, core: 2. Of those that a mesh axis runs over, the one named last changes fastest.
Arguments:
- q_lin: bfloat16 [1024, 8192], P('ctx', 'head'), may hold values from -6 to 6
- k_lin: bfloat16 [1024, 8192], P('ctx', 'head'), may hold values from -6 to 6
- v_lin: bfloat16 [1024, 8192], P('ctx', 'head'), may hold values from -70 to 70
- log_decay: float32 [64, 1024], P('head', 'ctx'), may hold values from -1 to 0
- gate: bfloat16 [1024, 8192], P('ctx', 'head'), may hold values from -6 to 6
- norm_gain: float32 [8192], P('head'), may hold values from 0.1 to 1.9
- queries: bfloat16 [1024, 8192], P('ctx', 'head'), may hold values from -8 to 8
- keys: bfloat16 [1024, 1024], P('ctx', 'head'), may hold values from -4 to 4
- values: bfloat16 [1024, 1024], P('ctx', 'head'), may hold values from -6 to 6
- order: int32 [8], P('ctx'), may hold values from 0 to 7, each once
Outputs:
- mixed: bfloat16 [1024, 8192], P('ctx', 'head')
- attended: bfloat16 [1024, 8192], P('ctx', 'head')
The draws below stay inside these ranges and needn't reach their ends.
Inputs may be any that keep to these rules, and one draw needn't show every extreme that they name: order is a permutation of the 8 sequence shards.
All inputs are finite; a program needn't handle non-finite values.
Results may differ from the reference program's by a relative error of at most 0.0045.
Values may be sent and summed in bfloat16 or wider, within the bound.
No kernel may reach another device: no remote copies, remote signals or barrier semaphores. Data moves between devices by JAX's collectives and lax.ppermute only.
A program may use at most 128 MiB of HBM per device.

```python
import math
import jax
import jax.numpy as jnp
from jax import lax

H = 64
HD = 128
KVH = 8
TOK_DEV = 128
BLOCK = 128
SEQ = 1024
N_CTX = 8


def draw_log_decay(key, part):
    parts = jax.random.split(key, 7)
    rank = jax.random.permutation(parts[0], H)
    kind = rank % 4
    fast = kind == 0
    medium = kind == 1
    fast_rate = jnp.exp(jax.random.uniform(parts[1], (H,), jnp.float32, math.log(1.0 / 50.0), math.log(1.0 / 30.0)))
    medium_rate = jnp.exp(jax.random.uniform(parts[6], (H,), jnp.float32, math.log(1.0 / TOK_DEV), math.log(3.0 / TOK_DEV)))
    slow_rate = jnp.exp(jax.random.uniform(parts[2], (H,), jnp.float32, math.log(0.05 * math.log(10.0) / SEQ), math.log(0.35 * math.log(10.0) / SEQ)))
    rate = jnp.where(fast, fast_rate, jnp.where(medium, medium_rate, slow_rate))
    factor = jnp.exp(jax.random.uniform(parts[3], (H, SEQ), jnp.float32, math.log(0.5), math.log(2.0)))
    values = -rate[:, None] * factor
    spots = jax.random.randint(parts[4], (H, 2), 0, SEQ)
    keep = jax.random.uniform(parts[5], (H, 2), jnp.float32, 0.5, 0.8)
    hit = lax.iota(jnp.int32, SEQ)[None, None, :] == spots[:, :, None]
    values = values + jnp.sum(jnp.where(hit, jnp.log(keep)[:, :, None], 0.0), axis=1)
    values = jnp.maximum(values, -1.0)
    return values.astype(jnp.float32)


def draw_v_lin(key, part):
    parts = jax.random.split(key, 3)
    width = H * HD
    base = jnp.clip(jax.random.normal(parts[0], (SEQ, width), jnp.float32), -4.0, 4.0)
    column = jnp.exp(jax.random.uniform(parts[1], (width,), jnp.float32, 0.0, math.log(10.0))) / math.sqrt(10.0)
    rising = jnp.exp(math.log(3.0) * lax.iota(jnp.float32, width) / (width - 1)) / math.sqrt(3.0)
    row = jnp.exp(jax.random.uniform(parts[2], (SEQ,), jnp.float32, 0.0, math.log(10.0))) / math.sqrt(10.0)
    return (base * (column * rising)[None, :] * row[:, None]).astype(jnp.bfloat16)


def draw_queries(key, part):
    base_key = jax.random.fold_in(key, 11)
    base = jnp.clip(jax.random.normal(base_key, (SEQ, H, HD), jnp.float32), -4.0, 4.0)
    return base.reshape(SEQ, H * HD).astype(jnp.bfloat16)


def draw_keys(key, part):
    base_key = jax.random.fold_in(key, 13)
    base = jnp.clip(jax.random.normal(base_key, (SEQ, KVH, HD), jnp.float32), -4.0, 4.0)
    return base.reshape(SEQ, KVH * HD).astype(jnp.bfloat16)


def block_levels(rng, dims, shards, least, top_value):
    factor_of = 1.0
    for axis_at, blocks in shards:
        steps = jax.random.uniform(jax.random.fold_in(jax.random.fold_in(rng, 6), axis_at), (blocks,), jnp.float32, least / len(shards), top_value / len(shards))
        factor_of = factor_of * jnp.repeat(jnp.exp(steps), dims[axis_at] // blocks).reshape((-1,) + (1,) * (len(dims) - 1 - axis_at))
    return factor_of


def bell_draw(stream_key, shape, deviation, bound, shards=(), kind=jnp.bfloat16):
    gain = block_levels(stream_key, shape, shards, -0.22, 0.18) if shards else 1.0
    drawn = jax.random.normal(stream_key, shape, jnp.float32) * deviation * gain
    return jnp.minimum(jnp.maximum(drawn, -bound), bound).astype(kind)


def setup_inputs(seed: int = 0) -> dict:
    arg_keys = jax.random.split(jax.random.key(seed), 11)
    q_lin = bell_draw(arg_keys[0], (SEQ, H * HD), 1.0, 6.0, ((0, 8), (1, 4)))
    k_lin = bell_draw(arg_keys[1], (SEQ, H * HD), 1.0, 6.0, ((0, 8), (1, 4)))
    v_lin = draw_v_lin(jax.random.fold_in(arg_keys[10], 71), 0)
    log_decay = draw_log_decay(jax.random.fold_in(arg_keys[10], 71), 0)
    gate = bell_draw(arg_keys[4], (SEQ, H * HD), 1.5, 6.0, ((0, 8), (1, 4)))
    norm_gain = jnp.clip(1.0 + 0.18 * jax.random.normal(arg_keys[5], (H * HD,), jnp.float32), 0.1, 1.9)
    queries = draw_queries(jax.random.fold_in(arg_keys[10], 71), 0)
    keys = draw_keys(jax.random.fold_in(arg_keys[10], 71), 0)
    values = bell_draw(arg_keys[8], (SEQ, KVH * HD), 1.0, 6.0, ((0, 8), (1, 4)))
    order = jax.random.permutation(arg_keys[9], N_CTX).astype(jnp.int32)
    return {"q_lin": q_lin, "k_lin": k_lin, "v_lin": v_lin, "log_decay": log_decay, "gate": gate, "norm_gain": norm_gain, "queries": queries, "keys": keys, "values": values, "order": order}


EPS = 1e-06
HIGH = lax.Precision.HIGHEST

def lightning_blocks(qa, ka, va, decay_log, state0):
    total = qa.shape[0]
    heads = qa.shape[1]
    count = total // BLOCK
    qb_all = qa.reshape(count, BLOCK, heads, HD)
    kb_all = ka.reshape(count, BLOCK, heads, HD)
    vb_all = va.reshape(count, BLOCK, heads, HD)
    gb_all = decay_log.reshape(heads, count, BLOCK).transpose(1, 0, 2)

    def step(state, pieces):
        qb, kb, vb, gb = pieces
        cum = jnp.cumsum(gb, axis=1)
        scores = jnp.einsum('thd,shd->hts', qb.astype(jnp.float32), kb.astype(jnp.float32), precision=HIGH)
        lower = lax.iota(jnp.int32, BLOCK)[:, None] >= lax.iota(jnp.int32, BLOCK)[None, :]
        diff = cum[:, :, None] - cum[:, None, :]
        decay = jnp.where(lower[None], jnp.exp(jnp.where(lower[None], diff, 0.0)), 0.0)
        weights = (scores * decay).astype(jnp.bfloat16)
        intra = jnp.einsum('hts,shd->thd', weights.astype(jnp.float32), vb.astype(jnp.float32), precision=HIGH)
        qdec = qb.astype(jnp.float32) * jnp.exp(cum).T[:, :, None]
        inter = jnp.einsum('thd,hde->the', qdec, state, precision=HIGH)
        kdec = kb.astype(jnp.float32) * jnp.exp(cum[:, -1:] - cum).T[:, :, None]
        update = jnp.einsum('thd,the->hde', kdec, vb.astype(jnp.float32), precision=HIGH)
        state_new = jnp.exp(cum[:, -1])[:, None, None] * state + update
        return (state_new, intra + inter)
    state, outs = lax.scan(step, state0, (qb_all, kb_all, vb_all, gb_all))
    return (outs.reshape(total, heads, HD), state)

def reference(q_lin, k_lin, v_lin, log_decay, gate, norm_gain, queries, keys, values, order):
    qa = jax.nn.silu(q_lin.astype(jnp.float32)).astype(jnp.bfloat16).reshape(SEQ, H, HD)
    ka = jax.nn.silu(k_lin.astype(jnp.float32)).astype(jnp.bfloat16).reshape(SEQ, H, HD)
    va = jax.nn.silu(v_lin.astype(jnp.float32)).astype(jnp.bfloat16).reshape(SEQ, H, HD)
    state0 = jnp.zeros((H, HD, HD), jnp.float32)
    lin, state_end = lightning_blocks(qa, ka, va, log_decay, state0)
    squares = lax.optimization_barrier(jnp.sum(lin * lin, axis=(1, 2)))
    inv = lax.rsqrt(squares / (H * HD) + EPS)
    gated = jax.nn.sigmoid(gate.astype(jnp.float32).reshape(SEQ, H, HD))
    mixed = (lin * inv[:, None, None] * norm_gain.reshape(H, HD) * gated).astype(jnp.bfloat16).reshape(SEQ, H * HD)
    group = H // KVH
    keys_f = keys.astype(jnp.float32).reshape(SEQ, KVH, HD)
    values_f = values.astype(jnp.float32).reshape(SEQ, KVH, HD)
    kpos = lax.iota(jnp.int32, SEQ)
    scale = 1.0 / math.sqrt(HD)

    def shard(index):
        rows = lax.dynamic_slice_in_dim(queries, (index * TOK_DEV).astype(jnp.int32), TOK_DEV, 0)
        qg = rows.astype(jnp.float32).reshape(TOK_DEV, KVH, group, HD)
        qpos = order[index] * TOK_DEV + lax.iota(jnp.int32, TOK_DEV)
        scores = jnp.einsum('tkgd,skd->kgts', qg, keys_f, precision=HIGH) * scale
        mask = kpos[None, :] <= qpos[:, None]
        masked = jnp.where(mask, scores, -1e+30)
        top = lax.optimization_barrier(jnp.max(masked, axis=-1))
        probs = jnp.where(mask, jnp.exp(masked - top[..., None]), 0.0)
        den = lax.optimization_barrier(jnp.sum(probs, axis=-1))
        acc = jnp.einsum('kgts,skd->kgtd', probs.astype(jnp.bfloat16).astype(jnp.float32), values_f, precision=HIGH)
        out = acc / den[..., None]
        return out.transpose(2, 0, 1, 3).reshape(TOK_DEV, H * HD).astype(jnp.bfloat16)
    attended = lax.map(shard, jnp.arange(N_CTX, dtype=jnp.int32)).reshape(SEQ, H * HD)
    return (mixed, attended)
```

```python
import functools
import math

import jax
import jax.numpy as jnp
from jax import lax
from jax.experimental import pallas as pl
from jax.experimental.pallas import tpu as pltpu
from jax.sharding import PartitionSpec as P

HD = 128
EPS = 1e-06
HIGH = lax.Precision.HIGHEST
F32 = jnp.float32
BF16 = jnp.bfloat16
NT = (((1,), (1,)), ((), ()))
TN = (((0,), (0,)), ((), ()))
MIB = 1 << 20


def silu16(x):
    x = x.astype(F32)
    return (x / (1.0 + jnp.exp(-x))).astype(BF16)


def lower_ones(size):
    rows = lax.broadcasted_iota(jnp.int32, (size, size), 0)
    cols = lax.broadcasted_iota(jnp.int32, (size, size), 1)
    return rows >= cols


def head_cols(h):
    return slice(h * HD, (h + 1) * HD)


def my_rank(group):
    return lax.rem(lax.axis_index("ctx"), group)


def dyn(index, size):
    return pl.ds(pl.multiple_of(index * size, size), size)


def state_kernel(group, heads, ld_ref, k_ref, v_ref, *rest):
    outs, (states, totals) = rest[:group], rest[group:]
    tokens = k_ref.shape[0]
    per = heads // group
    rank = my_rank(group)
    ld = ld_ref[...]
    tri = lower_ones(tokens).astype(F32)
    cum = lax.dot_general(tri, ld, NT, precision=HIGH, preferred_element_type=F32)
    weight = jnp.exp(cum[tokens - 1 : tokens, :] - cum)
    total = jnp.broadcast_to(jnp.exp(jnp.sum(ld, axis=1, keepdims=True)), (heads, HD))
    high = total.astype(BF16).astype(F32)
    low = total - high
    totals[...] = jnp.zeros_like(totals)
    for k in range(group):
        totals[k * 16 : k * 16 + per, :] = high[k * per : (k + 1) * per]
        totals[k * 16 + 8 : k * 16 + 8 + per, :] = low[k * per : (k + 1) * per]
    for h in range(heads):
        ka = silu16(k_ref[:, head_cols(h)])
        va = silu16(v_ref[:, head_cols(h)])
        kdec = ka.astype(F32) * weight[:, h : h + 1]
        khigh = kdec.astype(BF16)
        klow = (kdec - khigh.astype(F32)).astype(BF16)
        state = lax.dot_general(khigh, va, TN, preferred_element_type=F32)
        state += lax.dot_general(klow, va, TN, preferred_element_type=F32)
        states[h * HD : (h + 1) * HD, :] = state.astype(BF16)
    for s in range(group):
        dest = rank ^ s
        outs[s][: per * HD, :] = states[dyn(dest, per * HD), :]
        outs[s][per * HD :, :] = totals[dyn(dest, 16), :].astype(BF16)


def decay_row(slots, k, base, j):
    tail = slots[k, base : base + 16, :].astype(F32)
    return tail[j : j + 1] + tail[8 + j : 9 + j]


def fill_slots(group, rank, pays, slots):
    for s in range(group):
        slots[rank ^ s] = pays[s][...]


def total_kernel(group, per, *refs):
    pays, out, slots = refs[:group], refs[group], refs[group + 1]
    fill_slots(group, my_rank(group), pays, slots)
    base = per * HD
    tails = []
    for j in range(per):
        state = slots[0, j * HD : (j + 1) * HD, :].astype(F32)
        whole = decay_row(slots, 0, base, j)
        for k in range(1, group):
            decay = decay_row(slots, k, base, j)
            state = decay * state + slots[k, j * HD : (j + 1) * HD, :].astype(F32)
            whole = whole * decay
        out[j * HD : (j + 1) * HD, :] = state.astype(BF16)
        tails.append(whole)
    pad = [jnp.zeros((8 - per, HD), F32)] if per < 8 else []
    total = jnp.concatenate(tails + pad, axis=0)
    high = total.astype(BF16).astype(F32)
    out[base:, :] = jnp.concatenate([high, total - high], axis=0).astype(BF16)


def prefix_kernel(group, per, carried, *refs):
    pays, refs = refs[:group], refs[group:]
    carry = None
    if carried:
        carry, refs = refs[0], refs[1:]
    outs, slots, prefixes = refs[:group], refs[group], refs[group + 1]
    rank = my_rank(group)
    fill_slots(group, rank, pays, slots)
    base = per * HD
    for j in range(per):
        rows = slice(j * HD, (j + 1) * HD)
        state = carry[rows, :].astype(F32) if carried else jnp.zeros((HD, HD), F32)
        prefixes[0, rows, :] = state.astype(BF16)
        for k in range(group - 1):
            state = decay_row(slots, k, base, j) * state + slots[k, rows, :].astype(F32)
            prefixes[k + 1, rows, :] = state.astype(BF16)
    for s in range(group):
        outs[s][...] = prefixes[rank ^ s]


def intra_kernel(heads, ld_ref, q_ref, k_ref, v_ref, out_ref):
    tokens = q_ref.shape[0]
    ld = ld_ref[...]
    lower = lower_ones(tokens)
    tri = lower.astype(F32)
    cum = lax.dot_general(tri, ld, NT, precision=HIGH, preferred_element_type=F32)
    cum_t = lax.dot_general(ld, tri, NT, precision=HIGH, preferred_element_type=F32)
    bias = jnp.where(lower, 0.0, -1e30)
    for h in range(heads):
        qa = silu16(q_ref[:, head_cols(h)])
        ka = silu16(k_ref[:, head_cols(h)])
        va = silu16(v_ref[:, head_cols(h)])
        scores = lax.dot_general(qa, ka, NT, preferred_element_type=F32)
        decay = jnp.exp((cum[:, h : h + 1] - cum_t[h : h + 1, :]) + bias)
        weights = (scores * decay).astype(BF16)
        out_ref[:, head_cols(h)] = jnp.dot(weights, va, preferred_element_type=F32)


def inter_kernel(group, heads, ld_ref, q_ref, intra_ref, *rest):
    parts, (lin_ref, squares_ref, states) = rest[:group], rest[group:]
    tokens = q_ref.shape[0]
    per = heads // group
    rank = my_rank(group)
    for s in range(group):
        states[dyn(rank ^ s, per * HD), :] = parts[s][...]
    tri = lower_ones(tokens).astype(F32)
    cum = lax.dot_general(tri, ld_ref[...], NT, precision=HIGH, preferred_element_type=F32)
    decay = jnp.exp(cum)
    acc = jnp.zeros((tokens, HD), F32)
    for h in range(heads):
        qa = silu16(q_ref[:, head_cols(h)])
        inter = jnp.dot(qa, states[h * HD : (h + 1) * HD, :], preferred_element_type=F32)
        lin = intra_ref[:, head_cols(h)] + inter * decay[:, h : h + 1]
        lin_ref[:, head_cols(h)] = lin
        acc += lin * lin
    ones = jnp.ones((8, HD), F32)
    squares_ref[...] = lax.dot_general(ones, acc, NT, precision=HIGH, preferred_element_type=F32)


def mixed_kernel(heads, columns, lin_ref, gate_ref, gain_ref, *rest):
    squares, out_ref = rest[:-1], rest[-1]
    total = squares[0][...]
    for part in squares[1:]:
        total = total + part[...]
    inv = jnp.transpose(lax.rsqrt(total / columns + EPS))[:, 0:1]
    for h in range(heads):
        cols = head_cols(h)
        gate = 1.0 / (1.0 + jnp.exp(-gate_ref[:, cols].astype(F32)))
        out_ref[:, cols] = (lin_ref[:, cols] * inv * gain_ref[:, cols] * gate).astype(BF16)


def softmax_kernel(count, group, block, heads, order_ref, q_ref, *rest):
    chunks, (out_ref, kv, bias_ref) = rest[:count], rest[count:]
    tokens = q_ref.shape[0]
    width = chunks[0].shape[1] // 2
    kv_heads = width // HD
    share = heads // kv_heads
    me = lax.axis_index("ctx")
    rank, mine = lax.rem(me, group), lax.div(me, group)
    groups = count // group
    for i in range(count):
        s, d = divmod(i, groups)
        place = lax.rem(mine + groups - d, groups) * group + (rank ^ s)
        kv[dyn(place, tokens), :] = chunks[i][...]
    first = order_ref[0] * tokens
    scale = math.log2(math.e) / math.sqrt(HD)
    blocks = count * tokens // block
    pack = 2 if share % 2 == 0 else 1

    def allowed(start):
        qpos = first + lax.broadcasted_iota(jnp.int32, (tokens, block), 0)
        kpos = start + lax.broadcasted_iota(jnp.int32, (tokens, block), 1)
        return jnp.where(kpos <= qpos, 0.0, -1e30)

    def query(h):
        return jnp.concatenate([q_ref[:, head_cols(h + i)] for i in range(pack)], axis=0)

    def store(h, value):
        for i in range(pack):
            out_ref[:, head_cols(h + i)] = value[i * tokens : (i + 1) * tokens]

    def scores(h, start):
        g = h // share
        keys = kv[pl.ds(start, block), head_cols(g)]
        raw = lax.dot_general(query(h), keys, NT, preferred_element_type=F32)
        return raw.reshape(pack, tokens, block) + bias_ref[...][None]

    def weigh(h, start, probs):
        values = kv[pl.ds(start, block), width + (h // share) * HD : width + (h // share + 1) * HD]
        flat = probs.astype(BF16).reshape(pack * tokens, block)
        return jnp.dot(flat, values, preferred_element_type=F32)

    if blocks == 1:
        bias_ref[...] = allowed(0)
        for h in range(0, heads, pack):
            raw = scores(h, 0)
            top = jnp.max(raw, axis=-1, keepdims=True)
            probs = jnp.exp2((raw - top) * scale)
            den = jnp.sum(probs, axis=-1, keepdims=True).reshape(pack * tokens, 1)
            store(h, (weigh(h, 0, probs) / den).astype(BF16))
        return

    reach = lax.div(first + tokens - 1, block) + 1
    for h in range(0, heads, pack):

        def step(i, carry):
            top, den, acc = carry
            start = pl.multiple_of(i * block, block)
            bias_ref[...] = allowed(start)
            raw = scores(h, start)
            new = jnp.maximum(top, jnp.max(raw, axis=-1, keepdims=True))
            alpha = jnp.exp2((top - new) * scale)
            probs = jnp.exp2((raw - new) * scale)
            den = den * alpha + jnp.sum(probs, axis=-1, keepdims=True)
            acc = acc * alpha.reshape(pack * tokens, 1) + weigh(h, start, probs)
            return new, den, acc

        top, den, acc = lax.fori_loop(
            0,
            reach,
            step,
            (
                jnp.full((pack, tokens, 1), -1e30, F32),
                jnp.zeros((pack, tokens, 1), F32),
                jnp.zeros((pack * tokens, HD), F32),
            ),
        )
        store(h, (acc / den.reshape(pack * tokens, 1)).astype(BF16))


def call(kernel, name, outs, args, scratch=(), flops=0, exps=0, limit=16, smem=()):
    size = sum(math.prod(x.shape) * x.dtype.itemsize for x in list(args) + list(outs))
    spaces = [pltpu.SMEM if i in smem else pltpu.VMEM for i in range(len(args))]
    return pl.pallas_call(
        kernel,
        name=name,
        out_shape=list(outs),
        in_specs=[pl.BlockSpec(memory_space=space) for space in spaces],
        out_specs=[pl.BlockSpec(memory_space=pltpu.VMEM) for _ in outs],
        scratch_shapes=list(scratch),
        cost_estimate=pl.CostEstimate(flops=flops, bytes_accessed=size, transcendentals=exps),
        compiler_params=pltpu.CompilerParams(vmem_limit_bytes=limit * MIB),
    )(*args)


def body(q_lin, k_lin, v_lin, log_decay, gate, norm_gain, queries, keys, values, order):
    tokens, width = q_lin.shape
    heads = log_decay.shape[0]
    n, nh = lax.axis_size("ctx"), lax.axis_size("head")
    group = 4 if n % 4 == 0 else 2 if n % 2 == 0 else 1
    groups = n // group
    per = heads // group
    rows = per * HD + 16
    cube = tokens * width * HD
    shape = jax.ShapeDtypeStruct

    def swap(x, s):
        return lax.ppermute(x, "ctx", [(c, c ^ s) for c in range(n)])

    def ahead(x, d, wrap):
        pairs = [(c, (c + d * group) % n) for c in range(n) if wrap or c + d * group < n]
        return lax.ppermute(x, "ctx", pairs)

    pays = call(
        functools.partial(state_kernel, group, heads),
        "block_states",
        [shape((rows, HD), BF16)] * group,
        (log_decay, k_lin, v_lin),
        [pltpu.VMEM((heads * HD, HD), BF16), pltpu.VMEM((group * 16, HD), F32)],
        flops=4 * cube,
        exps=2 * tokens * width,
    )
    pays = [pays[0]] + [swap(pays[s], s) for s in range(1, group)]

    kv = jnp.concatenate([keys, values], axis=1)
    own = [kv] + [ahead(kv, d, True) for d in range(1, groups)]
    chunks = own + [swap(x, s) for s in range(1, group) for x in own]

    (intra,) = call(
        functools.partial(intra_kernel, heads),
        "intra_block",
        [shape((tokens, width), F32)],
        (log_decay, q_lin, k_lin, v_lin),
        flops=4 * cube,
        exps=4 * tokens * width,
    )

    slots = pltpu.VMEM((group, rows, HD), BF16)
    carry = ()
    if groups > 1:
        (total,) = call(
            functools.partial(total_kernel, group, per),
            "group_state",
            [shape((rows, HD), BF16)],
            pays,
            [slots],
            flops=2 * per * HD * HD * group,
        )
        before = ahead(total, 1, False)
        shift = 1
        while shift < groups - 1:
            earlier = ahead(before, shift, False).astype(F32)
            later = before.astype(F32)
            decay = later[per * HD :][:per] + later[per * HD + 8 :][:per]
            prior = earlier[per * HD :][:per] + earlier[per * HD + 8 :][:per]
            state = later[: per * HD] + jnp.repeat(decay, HD, axis=0) * earlier[: per * HD]
            both = decay * prior
            high = both.astype(BF16).astype(F32)
            pad = jnp.zeros((8 - per, HD), F32)
            before = jnp.concatenate([state, high, pad, both - high, pad], axis=0).astype(BF16)
            shift *= 2
        carry = (before,)
    prefixes = call(
        functools.partial(prefix_kernel, group, per, bool(carry)),
        "prefix_states",
        [shape((per * HD, HD), BF16)] * group,
        (*pays, *carry),
        [slots, pltpu.VMEM((group, per * HD, HD), BF16)],
        flops=2 * per * HD * HD * group,
    )
    prefixes = [prefixes[0]] + [swap(prefixes[s], s) for s in range(1, group)]

    lin, squares = call(
        functools.partial(inter_kernel, group, heads),
        "inter_block",
        [shape((tokens, width), F32), shape((8, tokens), F32)],
        (log_decay, q_lin, intra, *prefixes),
        [pltpu.VMEM((heads * HD, HD), BF16)],
        flops=2 * cube,
        exps=tokens * width,
    )
    parts = [squares] + [
        lax.ppermute(squares, "head", [(i, (i + d) % nh) for i in range(nh)]) for d in range(1, nh)
    ]
    (mixed,) = call(
        functools.partial(mixed_kernel, heads, float(width * nh)),
        "gated_norm",
        [shape((tokens, width), BF16)],
        (lin, gate, norm_gain.reshape(1, width), *parts),
        flops=4 * tokens * width,
        exps=tokens * width,
    )

    span = n * tokens
    block = min(span, 1024)
    (attended,) = call(
        functools.partial(softmax_kernel, n, group, block, heads),
        "softmax_attention",
        [shape((tokens, width), BF16)],
        (order, queries, *chunks),
        [pltpu.VMEM((span, kv.shape[1]), BF16), pltpu.VMEM((tokens, block), F32)],
        flops=4 * tokens * width * span,
        exps=tokens * span * heads,
        limit=16 + 5 * span * kv.shape[1] // MIB,
        smem=(0,),
    )
    return (mixed, attended)


def solution(mesh):
    return jax.shard_map(
        body,
        mesh=mesh,
        in_specs=(
            P("ctx", "head"),
            P("ctx", "head"),
            P("ctx", "head"),
            P("head", "ctx"),
            P("ctx", "head"),
            P("head"),
            P("ctx", "head"),
            P("ctx", "head"),
            P("ctx", "head"),
            P("ctx"),
        ),
        out_specs=(P("ctx", "head"), P("ctx", "head")),
        check_vma=False,
    )
```

```python
import functools
import math

import jax
import jax.numpy as jnp
from jax import lax
from jax.experimental import pallas as pl
from jax.experimental.pallas import tpu as pltpu
from jax.sharding import PartitionSpec as P

HD = 128
EPS = 1e-06
HIGH = lax.Precision.HIGHEST
F32 = jnp.float32
BF16 = jnp.bfloat16
NT = (((1,), (1,)), ((), ()))
TN = (((0,), (0,)), ((), ()))
MIB = 1 << 20


def silu16(x):
    x = x.astype(F32)
    return (x / (1.0 + jnp.exp(-x))).astype(BF16)


def lower_ones(size):
    rows = lax.broadcasted_iota(jnp.int32, (size, size), 0)
    cols = lax.broadcasted_iota(jnp.int32, (size, size), 1)
    return rows >= cols


def head_cols(h):
    return slice(h * HD, (h + 1) * HD)


def dyn(index, size):
    return pl.ds(pl.multiple_of(index * size, size), size)


def state_kernel(group, heads, ld_ref, k_ref, v_ref, out_ref):
    tokens = k_ref.shape[0]
    per = heads // group
    ld = ld_ref[...]
    tri = lower_ones(tokens).astype(F32)
    cum = lax.dot_general(tri, ld, NT, precision=HIGH, preferred_element_type=F32)
    weight = jnp.exp(cum[tokens - 1 : tokens, :] - cum)
    total = jnp.broadcast_to(jnp.exp(jnp.sum(ld, axis=1, keepdims=True)), (heads, HD))
    high = total.astype(BF16).astype(F32)
    low = total - high
    pad = [jnp.zeros((8 - per, HD), F32)] if per < 8 else []
    for h in range(heads):
        ka = silu16(k_ref[:, head_cols(h)])
        va = silu16(v_ref[:, head_cols(h)])
        kdec = ka.astype(F32) * weight[:, h : h + 1]
        khigh = kdec.astype(BF16)
        klow = (kdec - khigh.astype(F32)).astype(BF16)
        state = lax.dot_general(khigh, va, TN, preferred_element_type=F32)
        state += lax.dot_general(klow, va, TN, preferred_element_type=F32)
        k, j = divmod(h, per)
        out_ref[k, j * HD : (j + 1) * HD, :] = state.astype(BF16)
    for k in range(group):
        mine = slice(k * per, (k + 1) * per)
        tail = jnp.concatenate([high[mine], *pad, low[mine], *pad], axis=0)
        out_ref[k, per * HD :, :] = tail.astype(BF16)


def decay_row(slots, k, base, j):
    tail = slots[k, base : base + 16, :].astype(F32)
    return tail[j : j + 1] + tail[8 + j : 9 + j]


def total_kernel(group, per, slots, out):
    base = per * HD
    tails = []
    for j in range(per):
        state = slots[0, j * HD : (j + 1) * HD, :].astype(F32)
        whole = decay_row(slots, 0, base, j)
        for k in range(1, group):
            decay = decay_row(slots, k, base, j)
            state = decay * state + slots[k, j * HD : (j + 1) * HD, :].astype(F32)
            whole = whole * decay
        out[j * HD : (j + 1) * HD, :] = state.astype(BF16)
        tails.append(whole)
    pad = [jnp.zeros((8 - per, HD), F32)] if per < 8 else []
    total = jnp.concatenate(tails + pad, axis=0)
    high = total.astype(BF16).astype(F32)
    out[base:, :] = jnp.concatenate([high, total - high], axis=0).astype(BF16)


def prefix_kernel(group, per, carried, slots, *refs):
    out = refs[-1]
    base = per * HD
    for j in range(per):
        rows = slice(j * HD, (j + 1) * HD)
        state = refs[0][rows, :].astype(F32) if carried else jnp.zeros((HD, HD), F32)
        out[0, rows, :] = state.astype(BF16)
        for k in range(group - 1):
            state = decay_row(slots, k, base, j) * state + slots[k, rows, :].astype(F32)
            out[k + 1, rows, :] = state.astype(BF16)


def intra_kernel(heads, ld_ref, q_ref, k_ref, v_ref, out_ref):
    tokens = q_ref.shape[0]
    ld = ld_ref[...]
    lower = lower_ones(tokens)
    tri = lower.astype(F32)
    cum = lax.dot_general(tri, ld, NT, precision=HIGH, preferred_element_type=F32)
    cum_t = lax.dot_general(ld, tri, NT, precision=HIGH, preferred_element_type=F32)
    bias = jnp.where(lower, 0.0, -1e30)
    for h in range(heads):
        qa = silu16(q_ref[:, head_cols(h)])
        ka = silu16(k_ref[:, head_cols(h)])
        va = silu16(v_ref[:, head_cols(h)])
        scores = lax.dot_general(qa, ka, NT, preferred_element_type=F32)
        decay = jnp.exp((cum[:, h : h + 1] - cum_t[h : h + 1, :]) + bias)
        weights = (scores * decay).astype(BF16)
        out_ref[:, head_cols(h)] = jnp.dot(weights, va, preferred_element_type=F32)


def inter_kernel(group, heads, ld_ref, q_ref, intra_ref, states, lin_ref, squares_ref):
    tokens = q_ref.shape[0]
    per = heads // group
    tri = lower_ones(tokens).astype(F32)
    cum = lax.dot_general(tri, ld_ref[...], NT, precision=HIGH, preferred_element_type=F32)
    decay = jnp.exp(cum)
    acc = jnp.zeros((tokens, HD), F32)
    for h in range(heads):
        qa = silu16(q_ref[:, head_cols(h)])
        k, j = divmod(h, per)
        state = states[k, j * HD : (j + 1) * HD, :]
        inter = jnp.dot(qa, state, preferred_element_type=F32)
        lin = intra_ref[:, head_cols(h)] + inter * decay[:, h : h + 1]
        lin_ref[:, head_cols(h)] = lin
        acc += lin * lin
    ones = jnp.ones((8, HD), F32)
    squares_ref[...] = lax.dot_general(ones, acc, NT, precision=HIGH, preferred_element_type=F32)


def mixed_kernel(heads, columns, lin_ref, gate_ref, gain_ref, *rest):
    squares, out_ref = rest[:-1], rest[-1]
    total = squares[0][...]
    for part in squares[1:]:
        total = total + part[...]
    inv = jnp.transpose(lax.rsqrt(total / columns + EPS))[:, 0:1]
    for h in range(heads):
        cols = head_cols(h)
        gate = 1.0 / (1.0 + jnp.exp(-gate_ref[:, cols].astype(F32)))
        out_ref[:, cols] = (lin_ref[:, cols] * inv * gain_ref[:, cols] * gate).astype(BF16)


def softmax_kernel(count, group, block, heads, order_ref, q_ref, *rest):
    chunks, (out_ref, kv, bias_ref) = rest[:group], rest[group:]
    tokens = q_ref.shape[0]
    width = chunks[0].shape[1] // 2
    kv_heads = width // HD
    share = heads // kv_heads
    me = lax.axis_index("ctx")
    rank, mine = lax.rem(me, group), lax.div(me, group)
    groups = count // group
    for i in range(count):
        s, d = divmod(i, groups)
        place = lax.rem(mine + groups - d, groups) * group + (rank ^ s)
        kv[dyn(place, tokens), :] = chunks[s][d * tokens : (d + 1) * tokens, :]
    first = order_ref[0] * tokens
    scale = math.log2(math.e) / math.sqrt(HD)
    blocks = count * tokens // block
    pack = 2 if share % 2 == 0 else 1

    def allowed(start):
        qpos = first + lax.broadcasted_iota(jnp.int32, (tokens, block), 0)
        kpos = start + lax.broadcasted_iota(jnp.int32, (tokens, block), 1)
        return jnp.where(kpos <= qpos, 0.0, -1e30)

    def query(h):
        return jnp.concatenate([q_ref[:, head_cols(h + i)] for i in range(pack)], axis=0)

    def store(h, value):
        for i in range(pack):
            out_ref[:, head_cols(h + i)] = value[i * tokens : (i + 1) * tokens]

    def scores(h, start):
        g = h // share
        keys = kv[pl.ds(start, block), head_cols(g)]
        raw = lax.dot_general(query(h), keys, NT, preferred_element_type=F32)
        return raw.reshape(pack, tokens, block) + bias_ref[...][None]

    def weigh(h, start, probs):
        values = kv[pl.ds(start, block), width + (h // share) * HD : width + (h // share + 1) * HD]
        flat = probs.astype(BF16).reshape(pack * tokens, block)
        return jnp.dot(flat, values, preferred_element_type=F32)

    if blocks == 1:
        bias_ref[...] = allowed(0)
        for h in range(0, heads, pack):
            raw = scores(h, 0)
            top = jnp.max(raw, axis=-1, keepdims=True)
            probs = jnp.exp2((raw - top) * scale)
            den = jnp.sum(probs, axis=-1, keepdims=True).reshape(pack * tokens, 1)
            store(h, (weigh(h, 0, probs) / den).astype(BF16))
        return

    reach = lax.div(first + tokens - 1, block) + 1
    for h in range(0, heads, pack):

        def step(i, carry):
            top, den, acc = carry
            start = pl.multiple_of(i * block, block)
            bias_ref[...] = allowed(start)
            raw = scores(h, start)
            new = jnp.maximum(top, jnp.max(raw, axis=-1, keepdims=True))
            alpha = jnp.exp2((top - new) * scale)
            probs = jnp.exp2((raw - new) * scale)
            den = den * alpha + jnp.sum(probs, axis=-1, keepdims=True)
            acc = acc * alpha.reshape(pack * tokens, 1) + weigh(h, start, probs)
            return new, den, acc

        top, den, acc = lax.fori_loop(
            0,
            reach,
            step,
            (
                jnp.full((pack, tokens, 1), -1e30, F32),
                jnp.zeros((pack, tokens, 1), F32),
                jnp.zeros((pack * tokens, HD), F32),
            ),
        )
        store(h, (acc / den.reshape(pack * tokens, 1)).astype(BF16))


def call(kernel, name, outs, args, scratch=(), flops=0, exps=0, limit=16, smem=()):
    size = sum(math.prod(x.shape) * x.dtype.itemsize for x in list(args) + list(outs))
    spaces = [pltpu.SMEM if i in smem else pltpu.VMEM for i in range(len(args))]
    return pl.pallas_call(
        kernel,
        name=name,
        out_shape=list(outs),
        in_specs=[pl.BlockSpec(memory_space=space) for space in spaces],
        out_specs=[pl.BlockSpec(memory_space=pltpu.VMEM) for _ in outs],
        scratch_shapes=list(scratch),
        cost_estimate=pl.CostEstimate(flops=flops, bytes_accessed=size, transcendentals=exps),
        compiler_params=pltpu.CompilerParams(vmem_limit_bytes=limit * MIB),
    )(*args)


def body(q_lin, k_lin, v_lin, log_decay, gate, norm_gain, queries, keys, values, order):
    tokens, width = q_lin.shape
    heads = log_decay.shape[0]
    n, nh = lax.axis_size("ctx"), lax.axis_size("head")
    group = 4 if n % 4 == 0 else 2 if n % 2 == 0 else 1
    groups = n // group
    per = heads // group
    rows = per * HD + 16
    cube = tokens * width * HD
    shape = jax.ShapeDtypeStruct

    ranks = [[a * group + r for r in range(group)] for a in range(groups)]

    def exchange(x):
        return lax.all_to_all(x, "ctx", 0, 0, axis_index_groups=ranks)

    def ahead(x, d, wrap):
        pairs = [(c, (c + d * group) % n) for c in range(n) if wrap or c + d * group < n]
        return lax.ppermute(x, "ctx", pairs)

    kv = jnp.concatenate([keys, values], axis=1)
    own = jnp.concatenate([kv] + [ahead(kv, d, True) for d in range(1, groups)], axis=0)

    (pays,) = call(
        functools.partial(state_kernel, group, heads),
        "block_states",
        [shape((group, rows, HD), BF16)],
        (log_decay, k_lin, v_lin),
        flops=4 * cube,
        exps=2 * tokens * width,
    )
    pays = exchange(pays)
    chunks = [own] + [
        lax.ppermute(own, "ctx", [(c, c ^ s) for c in range(n)]) for s in range(1, group)
    ]

    (intra,) = call(
        functools.partial(intra_kernel, heads),
        "intra_block",
        [shape((tokens, width), F32)],
        (log_decay, q_lin, k_lin, v_lin),
        flops=4 * cube,
        exps=4 * tokens * width,
    )

    carry = ()
    if groups > 1:
        (total,) = call(
            functools.partial(total_kernel, group, per),
            "group_state",
            [shape((rows, HD), BF16)],
            (pays,),
            flops=2 * per * HD * HD * group,
        )
        before = ahead(total, 1, False)
        shift = 1
        while shift < groups - 1:
            earlier = ahead(before, shift, False).astype(F32)
            later = before.astype(F32)
            decay = later[per * HD :][:per] + later[per * HD + 8 :][:per]
            prior = earlier[per * HD :][:per] + earlier[per * HD + 8 :][:per]
            state = later[: per * HD] + jnp.repeat(decay, HD, axis=0) * earlier[: per * HD]
            both = decay * prior
            high = both.astype(BF16).astype(F32)
            pad = jnp.zeros((8 - per, HD), F32)
            before = jnp.concatenate([state, high, pad, both - high, pad], axis=0).astype(BF16)
            shift *= 2
        carry = (before,)
    (prefixes,) = call(
        functools.partial(prefix_kernel, group, per, bool(carry)),
        "prefix_states",
        [shape((group, per * HD, HD), BF16)],
        (pays, *carry),
        flops=2 * per * HD * HD * group,
    )
    prefixes = exchange(prefixes)

    lin, squares = call(
        functools.partial(inter_kernel, group, heads),
        "inter_block",
        [shape((tokens, width), F32), shape((8, tokens), F32)],
        (log_decay, q_lin, intra, prefixes),
        flops=2 * cube,
        exps=tokens * width,
    )
    parts = [squares] + [
        lax.ppermute(squares, "head", [(i, (i + d) % nh) for i in range(nh)]) for d in range(1, nh)
    ]
    (mixed,) = call(
        functools.partial(mixed_kernel, heads, float(width * nh)),
        "gated_norm",
        [shape((tokens, width), BF16)],
        (lin, gate, norm_gain.reshape(1, width), *parts),
        flops=4 * tokens * width,
        exps=tokens * width,
    )

    span = n * tokens
    block = min(span, 1024)
    (attended,) = call(
        functools.partial(softmax_kernel, n, group, block, heads),
        "softmax_attention",
        [shape((tokens, width), BF16)],
        (order, queries, *chunks),
        [pltpu.VMEM((span, kv.shape[1]), BF16), pltpu.VMEM((tokens, block), F32)],
        flops=4 * tokens * width * span,
        exps=tokens * span * heads,
        limit=16 + 5 * span * kv.shape[1] // MIB,
        smem=(0,),
    )
    return (mixed, attended)


def solution(mesh):
    return jax.shard_map(
        body,
        mesh=mesh,
        in_specs=(
            P("ctx", "head"),
            P("ctx", "head"),
            P("ctx", "head"),
            P("head", "ctx"),
            P("ctx", "head"),
            P("head"),
            P("ctx", "head"),
            P("ctx", "head"),
            P("ctx", "head"),
            P("ctx"),
        ),
        out_specs=(P("ctx", "head"), P("ctx", "head")),
        check_vma=False,
    )
```

```python
import functools
import math

import jax
import jax.numpy as jnp
from jax import lax
from jax.experimental import pallas as pl
from jax.experimental.pallas import tpu as pltpu
from jax.sharding import PartitionSpec as P

HD = 128
EPS = 1e-06
HIGH = lax.Precision.HIGHEST
F32 = jnp.float32
BF16 = jnp.bfloat16
NT = (((1,), (1,)), ((), ()))
TN = (((0,), (0,)), ((), ()))
MIB = 1 << 20
VMEM = pl.BlockSpec(memory_space=pltpu.VMEM)
HBM = pl.BlockSpec(memory_space=pltpu.HBM)


def silu16(x):
    x = x.astype(F32)
    return (x / (1.0 + jnp.exp(-x))).astype(BF16)


def lower_ones(size):
    rows = lax.broadcasted_iota(jnp.int32, (size, size), 0)
    cols = lax.broadcasted_iota(jnp.int32, (size, size), 1)
    return rows >= cols


def head_cols(h):
    return slice(h * HD, (h + 1) * HD)


def my_rank(group):
    return lax.rem(lax.axis_index("ctx"), group)


def dyn(index, size):
    return pl.ds(pl.multiple_of(index * size, size), size)


def triangle_kernel(ones_ref, bias_ref):
    lower = lower_ones(ones_ref.shape[0])
    ones_ref[...] = lower.astype(F32)
    bias_ref[...] = jnp.where(lower, 0.0, -1e30)


def state_kernel(group, heads, tri_ref, ld_ref, k_ref, v_ref, *rest):
    outs, (ka_ref, va_ref, states, totals) = rest[:group], rest[group:]
    tokens = k_ref.shape[0]
    per = heads // group
    rank = my_rank(group)
    ld = ld_ref[...]
    cum = lax.dot_general(tri_ref[...], ld, NT, precision=HIGH, preferred_element_type=F32)
    weight = jnp.exp(cum[tokens - 1 : tokens, :] - cum)
    total = jnp.broadcast_to(jnp.exp(jnp.sum(ld, axis=1, keepdims=True)), (heads, HD))
    high = total.astype(BF16).astype(F32)
    low = total - high
    totals[...] = jnp.zeros_like(totals)
    for k in range(group):
        totals[k * 16 : k * 16 + per, :] = high[k * per : (k + 1) * per]
        totals[k * 16 + 8 : k * 16 + 8 + per, :] = low[k * per : (k + 1) * per]
    for h in range(heads):
        ka = silu16(k_ref[:, head_cols(h)])
        va = silu16(v_ref[:, head_cols(h)])
        ka_ref[:, head_cols(h)] = ka
        va_ref[:, head_cols(h)] = va
        kdec = ka.astype(F32) * weight[:, h : h + 1]
        khigh = kdec.astype(BF16)
        klow = (kdec - khigh.astype(F32)).astype(BF16)
        state = lax.dot_general(khigh, va, TN, preferred_element_type=F32)
        state += lax.dot_general(klow, va, TN, preferred_element_type=F32)
        states[h * HD : (h + 1) * HD, :] = state.astype(BF16)
    for s in range(group):
        dest = rank ^ s
        outs[s][: per * HD, :] = states[dyn(dest, per * HD), :]
        outs[s][per * HD :, :] = totals[dyn(dest, 16), :].astype(BF16)


def decay_row(slots, k, base, j):
    tail = slots[k, base : base + 16, :].astype(F32)
    return tail[j : j + 1] + tail[8 + j : 9 + j]


def fill_slots(group, rank, pays, slots):
    for s in range(group):
        slots[rank ^ s] = pays[s][...]


def total_kernel(group, per, *refs):
    pays, out, slots = refs[:group], refs[group], refs[group + 1]
    fill_slots(group, my_rank(group), pays, slots)
    base = per * HD
    tails = []
    for j in range(per):
        state = slots[0, j * HD : (j + 1) * HD, :].astype(F32)
        whole = decay_row(slots, 0, base, j)
        for k in range(1, group):
            decay = decay_row(slots, k, base, j)
            state = decay * state + slots[k, j * HD : (j + 1) * HD, :].astype(F32)
            whole = whole * decay
        out[j * HD : (j + 1) * HD, :] = state.astype(BF16)
        tails.append(whole)
    pad = [jnp.zeros((8 - per, HD), F32)] if per < 8 else []
    total = jnp.concatenate(tails + pad, axis=0)
    high = total.astype(BF16).astype(F32)
    out[base:, :] = jnp.concatenate([high, total - high], axis=0).astype(BF16)


def prefix_kernel(group, per, carried, *refs):
    pays, refs = refs[:group], refs[group:]
    carry = None
    if carried:
        carry, refs = refs[0], refs[1:]
    outs, slots, prefixes = refs[:group], refs[group], refs[group + 1]
    rank = my_rank(group)
    later = lax.axis_index("ctx") >= group
    fill_slots(group, rank, pays, slots)
    base = per * HD
    for j in range(per):
        rows = slice(j * HD, (j + 1) * HD)
        state = jnp.zeros((HD, HD), F32)
        if carried:
            state = jnp.where(later, carry[rows, :].astype(F32), state)
        prefixes[0, rows, :] = state.astype(BF16)
        for k in range(group - 1):
            state = decay_row(slots, k, base, j) * state + slots[k, rows, :].astype(F32)
            prefixes[k + 1, rows, :] = state.astype(BF16)
    for s in range(group):
        outs[s][...] = prefixes[rank ^ s]


def intra_kernel(heads, tri_ref, bias_ref, ld_ref, q_ref, ka_ref, va_ref, gate_ref, gain_ref, *outs):
    intra_ref, qa_ref, gain_out, decay_out = outs
    ld = ld_ref[...]
    tri = tri_ref[...]
    bias = bias_ref[...]
    cum = lax.dot_general(tri, ld, NT, precision=HIGH, preferred_element_type=F32)
    cum_t = lax.dot_general(ld, tri, NT, precision=HIGH, preferred_element_type=F32)
    decay_out[...] = jnp.exp(cum)
    for h in range(heads):
        cols = head_cols(h)
        qa = silu16(q_ref[:, cols])
        qa_ref[:, cols] = qa
        scores = lax.dot_general(qa, ka_ref[:, cols], NT, preferred_element_type=F32)
        decay = jnp.exp((cum[:, h : h + 1] - cum_t[h : h + 1, :]) + bias)
        weights = (scores * decay).astype(BF16)
        intra_ref[:, cols] = jnp.dot(weights, va_ref[:, cols], preferred_element_type=F32)
        gate = 1.0 / (1.0 + jnp.exp(-gate_ref[:, cols].astype(F32)))
        gain_out[:, cols] = gate * gain_ref[:, cols]


def inter_kernel(group, heads, decay_ref, qa_ref, intra_ref, *rest):
    parts, (lin_ref, squares_ref, states) = rest[:group], rest[group:]
    tokens = qa_ref.shape[0]
    per = heads // group
    rank = my_rank(group)
    for s in range(group):
        states[dyn(rank ^ s, per * HD), :] = parts[s][...]
    decay = decay_ref[...]
    acc = jnp.zeros((tokens, HD), F32)
    for h in range(heads):
        cols = head_cols(h)
        state = states[h * HD : (h + 1) * HD, :]
        inter = jnp.dot(qa_ref[:, cols], state, preferred_element_type=F32)
        lin = intra_ref[:, cols] + inter * decay[:, h : h + 1]
        lin_ref[:, cols] = lin
        acc += lin * lin
    ones = jnp.ones((8, HD), F32)
    squares_ref[...] = lax.dot_general(ones, acc, NT, precision=HIGH, preferred_element_type=F32)


def mixed_kernel(heads, columns, lin_ref, gain_ref, *rest):
    squares, out_ref = rest[:-1], rest[-1]
    total = squares[0][...]
    for part in squares[1:]:
        total = total + part[...]
    inv = jnp.transpose(lax.rsqrt(total / columns + EPS))[:, 0:1]
    for h in range(heads):
        cols = head_cols(h)
        out_ref[:, cols] = (lin_ref[:, cols] * inv * gain_ref[:, cols]).astype(BF16)


def softmax_kernel(count, group, block, g, kv_heads, order_ref, q_ref, *rest):
    chunks, (out_ref, kv, bias_ref) = rest[:group], rest[-3:]
    tokens = q_ref.shape[0]
    heads = q_ref.shape[1] // HD
    me = lax.axis_index("ctx")
    rank, mine = lax.rem(me, group), lax.div(me, group)
    groups = count // group
    for i in range(count):
        s, d = divmod(i, groups)
        place = lax.rem(mine + groups - d, groups) * group + (rank ^ s)
        rows = slice(d * tokens, (d + 1) * tokens)
        kv[dyn(place, tokens), :HD] = chunks[s][rows, head_cols(g)]
        kv[dyn(place, tokens), HD:] = chunks[s][rows, head_cols(kv_heads + g)]
    first = order_ref[0] * tokens
    scale = math.log2(math.e) / math.sqrt(HD)
    blocks = count * tokens // block
    pack = 2 if heads % 2 == 0 else 1

    def allowed(start):
        qpos = first + lax.broadcasted_iota(jnp.int32, (tokens, block), 0)
        kpos = start + lax.broadcasted_iota(jnp.int32, (tokens, block), 1)
        return jnp.where(kpos <= qpos, 0.0, -1e30)

    def query(h):
        return jnp.concatenate([q_ref[:, head_cols(h + i)] for i in range(pack)], axis=0)

    def store(h, value):
        for i in range(pack):
            out_ref[:, head_cols(h + i)] = value[i * tokens : (i + 1) * tokens]

    def scores(h, start):
        keys = kv[pl.ds(start, block), :HD]
        raw = lax.dot_general(query(h), keys, NT, preferred_element_type=F32)
        return raw.reshape(pack, tokens, block) + bias_ref[...][None]

    def weigh(start, probs):
        values = kv[pl.ds(start, block), HD:]
        flat = probs.astype(BF16).reshape(pack * tokens, block)
        return jnp.dot(flat, values, preferred_element_type=F32)

    if blocks == 1:
        bias_ref[...] = allowed(0)
        for h in range(0, heads, pack):
            raw = scores(h, 0)
            top = jnp.max(raw, axis=-1, keepdims=True)
            probs = jnp.exp2((raw - top) * scale)
            den = jnp.sum(probs, axis=-1, keepdims=True).reshape(pack * tokens, 1)
            store(h, (weigh(0, probs) / den).astype(BF16))
        return

    reach = lax.div(first + tokens - 1, block) + 1
    for h in range(0, heads, pack):

        def step(i, carry):
            top, den, acc = carry
            start = pl.multiple_of(i * block, block)
            bias_ref[...] = allowed(start)
            raw = scores(h, start)
            new = jnp.maximum(top, jnp.max(raw, axis=-1, keepdims=True))
            alpha = jnp.exp2((top - new) * scale)
            probs = jnp.exp2((raw - new) * scale)
            den = den * alpha + jnp.sum(probs, axis=-1, keepdims=True)
            acc = acc * alpha.reshape(pack * tokens, 1) + weigh(start, probs)
            return new, den, acc

        top, den, acc = lax.fori_loop(
            0,
            reach,
            step,
            (
                jnp.full((pack, tokens, 1), -1e30, F32),
                jnp.zeros((pack, tokens, 1), F32),
                jnp.zeros((pack * tokens, HD), F32),
            ),
        )
        store(h, (acc / den.reshape(pack * tokens, 1)).astype(BF16))


def call(
    kernel, name, outs, args, scratch=(), flops=0, exps=0, limit=16, specs=None, after=(), **more
):
    size = sum(math.prod(x.shape) * x.dtype.itemsize for x in list(args) + list(outs))
    more.setdefault("out_specs", [VMEM for _ in outs])
    specs = list(specs or [VMEM for _ in args]) + [HBM for _ in after]
    count = len(args)

    def run(*refs):
        kernel(*refs[:count], *refs[count + len(after) :])

    return pl.pallas_call(
        run,
        name=name,
        out_shape=list(outs),
        in_specs=specs,
        scratch_shapes=list(scratch),
        cost_estimate=pl.CostEstimate(flops=flops, bytes_accessed=size, transcendentals=exps),
        compiler_params=pltpu.CompilerParams(vmem_limit_bytes=limit * MIB),
        **more,
    )(*args, *after)


def body(q_lin, k_lin, v_lin, log_decay, gate, norm_gain, queries, keys, values, order):
    tokens, width = q_lin.shape
    heads = log_decay.shape[0]
    kv_width = keys.shape[1]
    kv_heads = kv_width // HD
    n, nh = lax.axis_size("ctx"), lax.axis_size("head")
    group = 4 if n % 4 == 0 else 2 if n % 2 == 0 else 1
    groups = n // group
    per = heads // group
    rows = per * HD + 16
    cube = tokens * width * HD
    shape = jax.ShapeDtypeStruct

    def swap(x, s):
        return lax.ppermute(x, "ctx", [(c, c ^ s) for c in range(n)])

    def swap_all(xs):
        return [xs[0]] + [swap(xs[s], s) for s in range(1, group)]

    def ahead(x, d):
        return lax.ppermute(x, "ctx", [(c, (c + d * group) % n) for c in range(n)])

    tri, bias = call(
        triangle_kernel, "triangle", [shape((tokens, tokens), F32)] * 2, (), flops=1 << 31
    )
    kv = jnp.concatenate([keys, values], axis=1)
    far = [ahead(kv, d) for d in range(1, groups)]
    own = jnp.concatenate([kv] + far, axis=0)

    *pays, ka, va = call(
        functools.partial(state_kernel, group, heads),
        "block_states",
        [shape((rows, HD), BF16)] * group + [shape((tokens, width), BF16)] * 2,
        (tri, log_decay, k_lin, v_lin),
        [pltpu.VMEM((heads * HD, HD), BF16), pltpu.VMEM((group * 16, HD), F32)],
        flops=4 * cube,
        exps=2 * tokens * width,
    )
    pays = swap_all(pays)
    chunks = [own] + [swap(own, s) for s in range(1, group)]

    intra, qa, gain, decay = call(
        functools.partial(intra_kernel, heads),
        "intra_block",
        [
            shape((tokens, width), F32),
            shape((tokens, width), BF16),
            shape((tokens, width), F32),
            shape((tokens, heads), F32),
        ],
        (tri, bias, log_decay, q_lin, ka, va, gate, norm_gain.reshape(1, width)),
        flops=4 * cube,
        exps=4 * tokens * width,
    )

    slots = pltpu.VMEM((group, rows, HD), BF16)
    carry = ()
    if groups > 1:
        (total,) = call(
            functools.partial(total_kernel, group, per),
            "group_state",
            [shape((rows, HD), BF16)],
            pays,
            [slots],
            flops=2 * per * HD * HD * group,
            after=far,
        )
        before = ahead(total, 1)
        shift = 1
        while shift < groups - 1:
            mine = lax.div(lax.axis_index("ctx"), group)
            later = jnp.where(mine >= 1, before, 0).astype(F32)
            earlier = ahead(later.astype(BF16), shift)
            earlier = jnp.where(mine >= shift + 1, earlier, 0).astype(F32)
            step = later[per * HD :][:per] + later[per * HD + 8 :][:per]
            prior = earlier[per * HD :][:per] + earlier[per * HD + 8 :][:per]
            state = later[: per * HD] + jnp.repeat(step, HD, axis=0) * earlier[: per * HD]
            both = jnp.where(mine >= shift + 1, step * prior, step)
            high = both.astype(BF16).astype(F32)
            pad = jnp.zeros((8 - per, HD), F32)
            before = jnp.concatenate([state, high, pad, both - high, pad], axis=0).astype(BF16)
            shift *= 2
        carry = (before,)
    prefixes = call(
        functools.partial(prefix_kernel, group, per, bool(carry)),
        "prefix_states",
        [shape((per * HD, HD), BF16)] * group,
        (*pays, *carry),
        [slots, pltpu.VMEM((group, per * HD, HD), BF16)],
        flops=2 * per * HD * HD * group,
        after=(intra,),
    )
    prefixes = swap_all(prefixes)

    span = n * tokens
    block = min(span, 1024)
    share = width // kv_heads

    def attend(g, *done):
        columns = pl.BlockSpec((tokens, share), functools.partial(lambda g, i: (0, g), g))
        held = [pl.BlockSpec(x.shape, lambda i: (0, 0)) for x in chunks]
        return call(
            functools.partial(softmax_kernel, n, group, block, g, kv_heads),
            "softmax_attention",
            [shape((tokens, width), BF16)],
            (order, queries, *chunks, *done),
            [pltpu.VMEM((span, 2 * HD), BF16), pltpu.VMEM((tokens, block), F32)],
            flops=4 * tokens * share * span,
            exps=tokens * span * share // HD,
            limit=16 + 6 * span * 2 * kv_width // MIB,
            specs=[pl.BlockSpec(memory_space=pltpu.SMEM), columns, *held, *[HBM for _ in done]],
            out_specs=[columns],
            grid=(1,),
            input_output_aliases={2 + group: 0} if done else {},
        )

    attended = attend(0)
    lin, squares = call(
        functools.partial(inter_kernel, group, heads),
        "inter_block",
        [shape((tokens, width), F32), shape((8, tokens), F32)],
        (decay, qa, intra, *prefixes),
        [pltpu.VMEM((heads * HD, HD), BF16)],
        flops=2 * cube,
        after=attended,
    )
    if nh & (nh - 1) == 0:
        parts, shift = [squares], 1
        while shift < nh:
            held = parts[0] if len(parts) == 1 else parts[0] + parts[1]
            parts = [held, lax.ppermute(held, "head", [(i, i ^ shift) for i in range(nh)])]
            shift *= 2
    else:
        turns = [[(i, (i + d) % nh) for i in range(nh)] for d in range(1, nh)]
        parts = [squares] + [lax.ppermute(squares, "head", turn) for turn in turns]
    (mixed,) = call(
        functools.partial(mixed_kernel, heads, float(width * nh)),
        "gated_norm",
        [shape((tokens, width), BF16)],
        (lin, gain, *parts),
        flops=4 * tokens * width,
    )

    for g in range(1, kv_heads):
        attended = attend(g, *attended)
    return (mixed, attended[0])


def solution(mesh):
    return jax.shard_map(
        body,
        mesh=mesh,
        in_specs=(
            P("ctx", "head"),
            P("ctx", "head"),
            P("ctx", "head"),
            P("head", "ctx"),
            P("ctx", "head"),
            P("head"),
            P("ctx", "head"),
            P("ctx", "head"),
            P("ctx", "head"),
            P("ctx"),
        ),
        out_specs=(P("ctx", "head"), P("ctx", "head")),
        check_vma=False,
    )
```

```python
import functools
import math

import jax
import jax.numpy as jnp
from jax import lax
from jax.experimental import pallas as pl
from jax.experimental.pallas import tpu as pltpu
from jax.sharding import PartitionSpec as P

HD = 128
EPS = 1e-06
HIGH = lax.Precision.HIGHEST
F32 = jnp.float32
BF16 = jnp.bfloat16
NT = (((1,), (1,)), ((), ()))
TN = (((0,), (0,)), ((), ()))
MIB = 1 << 20
VMEM = pl.BlockSpec(memory_space=pltpu.VMEM)
HBM = pl.BlockSpec(memory_space=pltpu.HBM)


def silu16(x):
    x = x.astype(F32)
    return (x / (1.0 + jnp.exp(-x))).astype(BF16)


def lower_ones(size):
    rows = lax.broadcasted_iota(jnp.int32, (size, size), 0)
    cols = lax.broadcasted_iota(jnp.int32, (size, size), 1)
    return rows >= cols


def head_cols(h):
    return slice(h * HD, (h + 1) * HD)


def my_rank(group):
    return lax.rem(lax.axis_index("ctx"), group)


def dyn(index, size):
    return pl.ds(pl.multiple_of(index * size, size), size)


def triangle_kernel(ones_ref, bias_ref):
    lower = lower_ones(ones_ref.shape[0])
    ones_ref[...] = lower.astype(F32)
    bias_ref[...] = jnp.where(lower, 0.0, -1e30)


def state_kernel(group, heads, tri_ref, ld_ref, k_ref, v_ref, *rest):
    outs, (ka_ref, va_ref, states, totals) = rest[:group], rest[group:]
    tokens = k_ref.shape[0]
    per = heads // group
    rank = my_rank(group)
    ld = ld_ref[...]
    cum = lax.dot_general(tri_ref[...], ld, NT, precision=HIGH, preferred_element_type=F32)
    weight = jnp.exp(cum[tokens - 1 : tokens, :] - cum)
    total = jnp.broadcast_to(jnp.exp(jnp.sum(ld, axis=1, keepdims=True)), (heads, HD))
    high = total.astype(BF16).astype(F32)
    low = total - high
    totals[...] = jnp.zeros_like(totals)
    for k in range(group):
        totals[k * 16 : k * 16 + per, :] = high[k * per : (k + 1) * per]
        totals[k * 16 + 8 : k * 16 + 8 + per, :] = low[k * per : (k + 1) * per]
    for h in range(heads):
        ka = silu16(k_ref[:, head_cols(h)])
        va = silu16(v_ref[:, head_cols(h)])
        ka_ref[:, head_cols(h)] = ka
        va_ref[:, head_cols(h)] = va
        kdec = ka.astype(F32) * weight[:, h : h + 1]
        khigh = kdec.astype(BF16)
        klow = (kdec - khigh.astype(F32)).astype(BF16)
        state = lax.dot_general(khigh, va, TN, preferred_element_type=F32)
        state += lax.dot_general(klow, va, TN, preferred_element_type=F32)
        states[h * HD : (h + 1) * HD, :] = state.astype(BF16)
    for s in range(group):
        dest = rank ^ s
        outs[s][: per * HD, :] = states[dyn(dest, per * HD), :]
        outs[s][per * HD :, :] = totals[dyn(dest, 16), :].astype(BF16)


def stack_kernel(*refs):
    tokens = refs[0].shape[0]
    for i, part in enumerate(refs[:-1]):
        refs[-1][i * tokens : (i + 1) * tokens, :] = part[...]


def decay_row(slots, k, base, j):
    tail = slots[k, base : base + 16, :].astype(F32)
    return tail[j : j + 1] + tail[8 + j : 9 + j]


def fill_slots(group, rank, pays, slots):
    for s in range(group):
        slots[rank ^ s] = pays[s][...]


def total_kernel(group, per, *refs):
    pays, out, slots = refs[:group], refs[group], refs[group + 1]
    fill_slots(group, my_rank(group), pays, slots)
    base = per * HD
    tails = []
    for j in range(per):
        state = slots[0, j * HD : (j + 1) * HD, :].astype(F32)
        whole = decay_row(slots, 0, base, j)
        for k in range(1, group):
            decay = decay_row(slots, k, base, j)
            state = decay * state + slots[k, j * HD : (j + 1) * HD, :].astype(F32)
            whole = whole * decay
        out[j * HD : (j + 1) * HD, :] = state.astype(BF16)
        tails.append(whole)
    pad = [jnp.zeros((8 - per, HD), F32)] if per < 8 else []
    total = jnp.concatenate(tails + pad, axis=0)
    high = total.astype(BF16).astype(F32)
    out[base:, :] = jnp.concatenate([high, total - high], axis=0).astype(BF16)


def prefix_kernel(group, per, carried, *refs):
    pays, refs = refs[:group], refs[group:]
    carry = None
    if carried:
        carry, refs = refs[0], refs[1:]
    outs, slots, prefixes = refs[:group], refs[group], refs[group + 1]
    rank = my_rank(group)
    later = lax.axis_index("ctx") >= group
    fill_slots(group, rank, pays, slots)
    base = per * HD
    for j in range(per):
        rows = slice(j * HD, (j + 1) * HD)
        state = jnp.zeros((HD, HD), F32)
        if carried:
            state = jnp.where(later, carry[rows, :].astype(F32), state)
        prefixes[0, rows, :] = state.astype(BF16)
        for k in range(group - 1):
            state = decay_row(slots, k, base, j) * state + slots[k, rows, :].astype(F32)
            prefixes[k + 1, rows, :] = state.astype(BF16)
    for s in range(group):
        outs[s][...] = prefixes[rank ^ s]


def intra_kernel(heads, tri_ref, bias_ref, ld_ref, q_ref, ka_ref, va_ref, gate_ref, gain_ref, *outs):
    intra_ref, qa_ref, gain_out, decay_out = outs
    ld = ld_ref[...]
    tri = tri_ref[...]
    bias = bias_ref[...]
    cum = lax.dot_general(tri, ld, NT, precision=HIGH, preferred_element_type=F32)
    cum_t = lax.dot_general(ld, tri, NT, precision=HIGH, preferred_element_type=F32)
    decay_out[...] = jnp.exp(cum)
    for h in range(heads):
        cols = head_cols(h)
        qa = silu16(q_ref[:, cols])
        qa_ref[:, cols] = qa
        scores = lax.dot_general(qa, ka_ref[:, cols], NT, preferred_element_type=F32)
        decay = jnp.exp((cum[:, h : h + 1] - cum_t[h : h + 1, :]) + bias)
        weights = (scores * decay).astype(BF16)
        intra_ref[:, cols] = jnp.dot(weights, va_ref[:, cols], preferred_element_type=F32)
        gate = 1.0 / (1.0 + jnp.exp(-gate_ref[:, cols].astype(F32)))
        gain_out[:, cols] = gate * gain_ref[:, cols]


def inter_kernel(group, heads, decay_ref, qa_ref, intra_ref, *rest):
    parts, (lin_ref, squares_ref, states) = rest[:group], rest[group:]
    tokens = qa_ref.shape[0]
    per = heads // group
    rank = my_rank(group)
    for s in range(group):
        states[dyn(rank ^ s, per * HD), :] = parts[s][...]
    decay = decay_ref[...]
    acc = jnp.zeros((tokens, HD), F32)
    for h in range(heads):
        cols = head_cols(h)
        state = states[h * HD : (h + 1) * HD, :]
        inter = jnp.dot(qa_ref[:, cols], state, preferred_element_type=F32)
        lin = intra_ref[:, cols] + inter * decay[:, h : h + 1]
        lin_ref[:, cols] = lin
        acc += lin * lin
    ones = jnp.ones((8, HD), F32)
    squares_ref[...] = lax.dot_general(ones, acc, NT, precision=HIGH, preferred_element_type=F32)


def add_kernel(a_ref, b_ref, out_ref):
    out_ref[...] = a_ref[...] + b_ref[...]


def mixed_kernel(heads, columns, lin_ref, gain_ref, *rest):
    squares, out_ref = rest[:-1], rest[-1]
    total = squares[0][...]
    for part in squares[1:]:
        total = total + part[...]
    inv = jnp.transpose(lax.rsqrt(total / columns + EPS))[:, 0:1]
    for h in range(heads):
        cols = head_cols(h)
        out_ref[:, cols] = (lin_ref[:, cols] * inv * gain_ref[:, cols]).astype(BF16)


def softmax_kernel(count, group, block, g, kv_heads, order_ref, q_ref, *rest):
    chunks, (out_ref, done_ref, kv, bias_ref) = rest[:group], rest[-4:]
    done_ref[...] = jnp.zeros_like(done_ref)
    tokens = q_ref.shape[0]
    heads = q_ref.shape[1] // HD
    me = lax.axis_index("ctx")
    rank, mine = lax.rem(me, group), lax.div(me, group)
    groups = count // group
    for i in range(count):
        s, d = divmod(i, groups)
        place = lax.rem(mine + groups - d, groups) * group + (rank ^ s)
        rows = slice(d * tokens, (d + 1) * tokens)
        kv[dyn(place, tokens), :HD] = chunks[s][rows, head_cols(g)]
        kv[dyn(place, tokens), HD:] = chunks[s][rows, head_cols(kv_heads + g)]
    first = order_ref[0] * tokens
    scale = math.log2(math.e) / math.sqrt(HD)
    blocks = count * tokens // block
    pack = 2 if heads % 2 == 0 else 1

    def allowed(start):
        qpos = first + lax.broadcasted_iota(jnp.int32, (tokens, block), 0)
        kpos = start + lax.broadcasted_iota(jnp.int32, (tokens, block), 1)
        return jnp.where(kpos <= qpos, 0.0, -1e30)

    def query(h):
        return jnp.concatenate([q_ref[:, head_cols(h + i)] for i in range(pack)], axis=0)

    def store(h, value):
        for i in range(pack):
            out_ref[:, head_cols(h + i)] = value[i * tokens : (i + 1) * tokens]

    def scores(h, start):
        keys = kv[pl.ds(start, block), :HD]
        raw = lax.dot_general(query(h), keys, NT, preferred_element_type=F32)
        return raw.reshape(pack, tokens, block) + bias_ref[...][None]

    def weigh(start, probs):
        values = kv[pl.ds(start, block), HD:]
        flat = probs.astype(BF16).reshape(pack * tokens, block)
        return jnp.dot(flat, values, preferred_element_type=F32)

    if blocks == 1:
        bias_ref[...] = allowed(0)
        for h in range(0, heads, pack):
            raw = scores(h, 0)
            top = jnp.max(raw, axis=-1, keepdims=True)
            probs = jnp.exp2((raw - top) * scale)
            den = jnp.sum(probs, axis=-1, keepdims=True).reshape(pack * tokens, 1)
            store(h, (weigh(0, probs) / den).astype(BF16))
        return

    reach = lax.div(first + tokens - 1, block) + 1
    for h in range(0, heads, pack):

        def step(i, carry):
            top, den, acc = carry
            start = pl.multiple_of(i * block, block)
            bias_ref[...] = allowed(start)
            raw = scores(h, start)
            new = jnp.maximum(top, jnp.max(raw, axis=-1, keepdims=True))
            alpha = jnp.exp2((top - new) * scale)
            probs = jnp.exp2((raw - new) * scale)
            den = den * alpha + jnp.sum(probs, axis=-1, keepdims=True)
            acc = acc * alpha.reshape(pack * tokens, 1) + weigh(start, probs)
            return new, den, acc

        top, den, acc = lax.fori_loop(
            0,
            reach,
            step,
            (
                jnp.full((pack, tokens, 1), -1e30, F32),
                jnp.zeros((pack, tokens, 1), F32),
                jnp.zeros((pack * tokens, HD), F32),
            ),
        )
        store(h, (acc / den.reshape(pack * tokens, 1)).astype(BF16))


def call(
    kernel, name, outs, args, scratch=(), flops=0, exps=0, limit=16, specs=None, after=(), **more
):
    size = sum(math.prod(x.shape) * x.dtype.itemsize for x in list(args) + list(outs))
    more.setdefault("out_specs", [VMEM for _ in outs])
    specs = list(specs or [VMEM for _ in args]) + [HBM for _ in after]
    count = len(args)

    def run(*refs):
        kernel(*refs[:count], *refs[count + len(after) :])

    return pl.pallas_call(
        run,
        name=name,
        out_shape=list(outs),
        in_specs=specs,
        scratch_shapes=list(scratch),
        cost_estimate=pl.CostEstimate(flops=flops, bytes_accessed=size, transcendentals=exps),
        compiler_params=pltpu.CompilerParams(vmem_limit_bytes=limit * MIB),
        **more,
    )(*args, *after)


def body(q_lin, k_lin, v_lin, log_decay, gate, norm_gain, queries, keys, values, order):
    tokens, width = q_lin.shape
    heads = log_decay.shape[0]
    kv_width = keys.shape[1]
    kv_heads = kv_width // HD
    n, nh = lax.axis_size("ctx"), lax.axis_size("head")
    group = 4 if n % 4 == 0 else 2 if n % 2 == 0 else 1
    groups = n // group
    per = heads // group
    rows = per * HD + 16
    cube = tokens * width * HD
    shape = jax.ShapeDtypeStruct

    def swap(x, s):
        return lax.ppermute(x, "ctx", [(c, c ^ s) for c in range(n)])

    def swap_all(xs):
        return [xs[0]] + [swap(xs[s], s) for s in range(1, group)]

    def ahead(x, d):
        return lax.ppermute(x, "ctx", [(c, (c + d * group) % n) for c in range(n)])

    tri, bias = call(
        triangle_kernel, "triangle", [shape((tokens, tokens), F32)] * 2, (), flops=1 << 31
    )
    kv = jnp.concatenate([keys, values], axis=1)
    far = [ahead(kv, d) for d in range(1, groups)]

    *pays, ka, va = call(
        functools.partial(state_kernel, group, heads),
        "block_states",
        [shape((rows, HD), BF16)] * group + [shape((tokens, width), BF16)] * 2,
        (tri, log_decay, k_lin, v_lin),
        [pltpu.VMEM((heads * HD, HD), BF16), pltpu.VMEM((group * 16, HD), F32)],
        flops=4 * cube,
        exps=2 * tokens * width,
    )
    pays = swap_all(pays)
    intra, qa, gain, decay = call(
        functools.partial(intra_kernel, heads),
        "intra_block",
        [
            shape((tokens, width), F32),
            shape((tokens, width), BF16),
            shape((tokens, width), F32),
            shape((tokens, heads), F32),
        ],
        (tri, bias, log_decay, q_lin, ka, va, gate, norm_gain.reshape(1, width)),
        flops=4 * cube,
        exps=4 * tokens * width,
    )

    slots = pltpu.VMEM((group, rows, HD), BF16)
    carry = ()
    if groups > 1:
        (total,) = call(
            functools.partial(total_kernel, group, per),
            "group_state",
            [shape((rows, HD), BF16)],
            pays,
            [slots],
            flops=2 * per * HD * HD * group,
            after=(intra, *far),
        )
        before = ahead(total, 1)
        shift = 1
        while shift < groups - 1:
            mine = lax.div(lax.axis_index("ctx"), group)
            later = jnp.where(mine >= 1, before, 0).astype(F32)
            earlier = ahead(later.astype(BF16), shift)
            earlier = jnp.where(mine >= shift + 1, earlier, 0).astype(F32)
            step = later[per * HD :][:per] + later[per * HD + 8 :][:per]
            prior = earlier[per * HD :][:per] + earlier[per * HD + 8 :][:per]
            state = later[: per * HD] + jnp.repeat(step, HD, axis=0) * earlier[: per * HD]
            both = jnp.where(mine >= shift + 1, step * prior, step)
            high = both.astype(BF16).astype(F32)
            pad = jnp.zeros((8 - per, HD), F32)
            before = jnp.concatenate([state, high, pad, both - high, pad], axis=0).astype(BF16)
            shift *= 2
        carry = (before,)
    prefixes = call(
        functools.partial(prefix_kernel, group, per, bool(carry)),
        "prefix_states",
        [shape((per * HD, HD), BF16)] * group,
        (*pays, *carry),
        [slots, pltpu.VMEM((group, per * HD, HD), BF16)],
        flops=2 * per * HD * HD * group,
    )
    prefixes = swap_all(prefixes)

    (own,) = call(
        stack_kernel,
        "stack_keys_values",
        [shape((groups * tokens, kv.shape[1]), BF16)],
        (kv, *far),
        after=(intra,),
        limit=16 + 4 * n * tokens * kv.shape[1] // MIB,
    )
    chunks = [own] + [swap(own, s) for s in (1, 2) if s < group]
    if group == 4:
        half = own.shape[0] // 2
        chunks.append(jnp.concatenate([swap(chunks[1][:half], 2), swap(chunks[2][half:], 1)]))
    span = n * tokens
    block = min(span, 1024)
    share = width // kv_heads

    def attend(g, *done):
        columns = pl.BlockSpec((tokens, share), functools.partial(lambda g, i: (0, g), g))
        held = [pl.BlockSpec(x.shape, lambda i: (0, 0)) for x in chunks]
        return call(
            functools.partial(softmax_kernel, n, group, block, g, kv_heads),
            "softmax_attention",
            [shape((tokens, width), BF16), shape((8, HD), F32)],
            (order, queries, *chunks, *done),
            [pltpu.VMEM((span, 2 * HD), BF16), pltpu.VMEM((tokens, block), F32)],
            flops=4 * tokens * share * span,
            exps=tokens * span * share // HD,
            limit=16 + 6 * span * 2 * kv_width // MIB,
            specs=[pl.BlockSpec(memory_space=pltpu.SMEM), columns, *held, *[HBM for _ in done]],
            out_specs=[columns, pl.BlockSpec((8, HD), lambda i: (0, 0))],
            grid=(1,),
            input_output_aliases={2 + group: 0} if done else {},
        )

    attended, marks = (), []
    for g in range(kv_heads):
        *attended, mark = attend(g, *attended)
        marks.append(mark)

    lin, squares = call(
        functools.partial(inter_kernel, group, heads),
        "inter_block",
        [shape((tokens, width), F32), shape((8, tokens), F32)],
        (decay, qa, intra, *prefixes),
        [pltpu.VMEM((heads * HD, HD), BF16)],
        flops=2 * cube,
    )
    if nh & (nh - 1) == 0:
        parts, shift = [squares], 1
        while shift < nh:
            held = parts[0]
            if len(parts) > 1:
                (held,) = call(add_kernel, "add", [shape((8, tokens), F32)], parts, after=marks[:1])
            parts = [held, lax.ppermute(held, "head", [(i, i ^ shift) for i in range(nh)])]
            shift *= 2
    else:
        turns = [[(i, (i + d) % nh) for i in range(nh)] for d in range(1, nh)]
        parts = [squares] + [lax.ppermute(squares, "head", turn) for turn in turns]
    (mixed,) = call(
        functools.partial(mixed_kernel, heads, float(width * nh)),
        "gated_norm",
        [shape((tokens, width), BF16)],
        (lin, gain, *parts),
        flops=4 * tokens * width,
        after=marks,
    )
    return (mixed, attended[0])


def solution(mesh):
    return jax.shard_map(
        body,
        mesh=mesh,
        in_specs=(
            P("ctx", "head"),
            P("ctx", "head"),
            P("ctx", "head"),
            P("head", "ctx"),
            P("ctx", "head"),
            P("head"),
            P("ctx", "head"),
            P("ctx", "head"),
            P("ctx", "head"),
            P("ctx"),
        ),
        out_specs=(P("ctx", "head"), P("ctx", "head")),
        check_vma=False,
    )
```

```python
import functools
import math

import jax
import jax.numpy as jnp
from jax import lax
from jax.experimental import pallas as pl
from jax.experimental.pallas import tpu as pltpu
from jax.sharding import PartitionSpec as P

HD = 128
EPS = 1e-06
HIGH = lax.Precision.HIGHEST
F32 = jnp.float32
BF16 = jnp.bfloat16
NT = (((1,), (1,)), ((), ()))
TN = (((0,), (0,)), ((), ()))
MIB = 1 << 20
VMEM = pl.BlockSpec(memory_space=pltpu.VMEM)
HBM = pl.BlockSpec(memory_space=pltpu.HBM)


def silu16(x):
    x = x.astype(F32)
    return (x / (1.0 + jnp.exp(-x))).astype(BF16)


def lower_ones(size):
    rows = lax.broadcasted_iota(jnp.int32, (size, size), 0)
    cols = lax.broadcasted_iota(jnp.int32, (size, size), 1)
    return rows >= cols


def head_cols(h):
    return slice(h * HD, (h + 1) * HD)


def my_rank(group):
    return lax.rem(lax.axis_index("ctx"), group)


def dyn(index, size):
    return pl.ds(pl.multiple_of(index * size, size), size)


def triangle_kernel(ones_ref, bias_ref):
    lower = lower_ones(ones_ref.shape[0])
    ones_ref[...] = lower.astype(F32)
    bias_ref[...] = jnp.where(lower, 0.0, -1e30)


def state_kernel(group, heads, tri_ref, ld_ref, k_ref, v_ref, *rest):
    outs, (ka_ref, va_ref, states, totals) = rest[:group], rest[group:]
    tokens = k_ref.shape[0]
    per = heads // group
    rank = my_rank(group)
    ld = ld_ref[...]
    cum = lax.dot_general(tri_ref[...], ld, NT, precision=HIGH, preferred_element_type=F32)
    weight = jnp.exp(cum[tokens - 1 : tokens, :] - cum)
    total = jnp.broadcast_to(jnp.exp(jnp.sum(ld, axis=1, keepdims=True)), (heads, HD))
    high = total.astype(BF16).astype(F32)
    low = total - high
    totals[...] = jnp.zeros_like(totals)
    for k in range(group):
        totals[k * 16 : k * 16 + per, :] = high[k * per : (k + 1) * per]
        totals[k * 16 + 8 : k * 16 + 8 + per, :] = low[k * per : (k + 1) * per]
    for h in range(heads):
        ka = silu16(k_ref[:, head_cols(h)])
        va = silu16(v_ref[:, head_cols(h)])
        ka_ref[:, head_cols(h)] = ka
        va_ref[:, head_cols(h)] = va
        kdec = ka.astype(F32) * weight[:, h : h + 1]
        khigh = kdec.astype(BF16)
        klow = (kdec - khigh.astype(F32)).astype(BF16)
        state = lax.dot_general(khigh, va, TN, preferred_element_type=F32)
        state += lax.dot_general(klow, va, TN, preferred_element_type=F32)
        states[h * HD : (h + 1) * HD, :] = state.astype(BF16)
    for s in range(group):
        dest = rank ^ s
        outs[s][: per * HD, :] = states[dyn(dest, per * HD), :]
        outs[s][per * HD :, :] = totals[dyn(dest, 16), :].astype(BF16)


def beside_kernel(keys, values, out):
    width = keys.shape[1]
    out[:, :width] = keys[...]
    out[:, width:] = values[...]


def stack_kernel(*refs):
    tokens = refs[0].shape[0]
    for i, part in enumerate(refs[:-1]):
        refs[-1][i * tokens : (i + 1) * tokens, :] = part[...]


def decay_row(slots, k, base, j):
    tail = slots[k, base : base + 16, :].astype(F32)
    return tail[j : j + 1] + tail[8 + j : 9 + j]


def fill_slots(group, rank, pays, slots):
    for s in range(group):
        slots[rank ^ s] = pays[s][...]


def total_kernel(group, per, *refs):
    pays, out, slots = refs[:group], refs[group], refs[group + 1]
    fill_slots(group, my_rank(group), pays, slots)
    base = per * HD
    tails = []
    for j in range(per):
        state = slots[0, j * HD : (j + 1) * HD, :].astype(F32)
        whole = decay_row(slots, 0, base, j)
        for k in range(1, group):
            decay = decay_row(slots, k, base, j)
            state = decay * state + slots[k, j * HD : (j + 1) * HD, :].astype(F32)
            whole = whole * decay
        out[j * HD : (j + 1) * HD, :] = state.astype(BF16)
        tails.append(whole)
    pad = [jnp.zeros((8 - per, HD), F32)] if per < 8 else []
    total = jnp.concatenate(tails + pad, axis=0)
    high = total.astype(BF16).astype(F32)
    out[base:, :] = jnp.concatenate([high, total - high], axis=0).astype(BF16)


def prefix_kernel(group, per, carried, *refs):
    pays, refs = refs[:group], refs[group:]
    carry = None
    if carried:
        carry, refs = refs[0], refs[1:]
    outs, slots, prefixes = refs[:group], refs[group], refs[group + 1]
    rank = my_rank(group)
    later = lax.axis_index("ctx") >= group
    fill_slots(group, rank, pays, slots)
    base = per * HD
    for j in range(per):
        rows = slice(j * HD, (j + 1) * HD)
        state = jnp.zeros((HD, HD), F32)
        if carried:
            state = jnp.where(later, carry[rows, :].astype(F32), state)
        prefixes[0, rows, :] = state.astype(BF16)
        for k in range(group - 1):
            state = decay_row(slots, k, base, j) * state + slots[k, rows, :].astype(F32)
            prefixes[k + 1, rows, :] = state.astype(BF16)
    for s in range(group):
        outs[s][...] = prefixes[rank ^ s]


def intra_kernel(heads, tri_ref, bias_ref, ld_ref, q_ref, ka_ref, va_ref, gate_ref, gain_ref, *outs):
    intra_ref, qa_ref, gain_out, decay_out = outs
    ld = ld_ref[...]
    tri = tri_ref[...]
    bias = bias_ref[...]
    cum = lax.dot_general(tri, ld, NT, precision=HIGH, preferred_element_type=F32)
    cum_t = lax.dot_general(ld, tri, NT, precision=HIGH, preferred_element_type=F32)
    decay_out[...] = jnp.exp(cum)
    for h in range(heads):
        cols = head_cols(h)
        qa = silu16(q_ref[:, cols])
        qa_ref[:, cols] = qa
        scores = lax.dot_general(qa, ka_ref[:, cols], NT, preferred_element_type=F32)
        decay = jnp.exp((cum[:, h : h + 1] - cum_t[h : h + 1, :]) + bias)
        weights = (scores * decay).astype(BF16)
        intra_ref[:, cols] = jnp.dot(weights, va_ref[:, cols], preferred_element_type=F32)
        gate = 1.0 / (1.0 + jnp.exp(-gate_ref[:, cols].astype(F32)))
        gain_out[:, cols] = gate * gain_ref[:, cols]


def inter_kernel(group, heads, decay_ref, qa_ref, intra_ref, *rest):
    parts, (lin_ref, squares_ref, states) = rest[:group], rest[group:]
    tokens = qa_ref.shape[0]
    per = heads // group
    rank = my_rank(group)
    for s in range(group):
        states[dyn(rank ^ s, per * HD), :] = parts[s][...]
    decay = decay_ref[...]
    acc = jnp.zeros((tokens, HD), F32)
    for h in range(heads):
        cols = head_cols(h)
        state = states[h * HD : (h + 1) * HD, :]
        inter = jnp.dot(qa_ref[:, cols], state, preferred_element_type=F32)
        lin = intra_ref[:, cols] + inter * decay[:, h : h + 1]
        lin_ref[:, cols] = lin
        acc += lin * lin
    ones = jnp.ones((8, HD), F32)
    squares_ref[...] = lax.dot_general(ones, acc, NT, precision=HIGH, preferred_element_type=F32)


def add_kernel(a_ref, b_ref, out_ref):
    out_ref[...] = a_ref[...] + b_ref[...]


def mixed_kernel(heads, columns, lin_ref, gain_ref, *rest):
    squares, out_ref = rest[:-1], rest[-1]
    total = squares[0][...]
    for part in squares[1:]:
        total = total + part[...]
    inv = jnp.transpose(lax.rsqrt(total / columns + EPS))[:, 0:1]
    for h in range(heads):
        cols = head_cols(h)
        out_ref[:, cols] = (lin_ref[:, cols] * inv * gain_ref[:, cols]).astype(BF16)


def softmax_bias(group, sides, order_ref, bias):
    tokens, span = bias.shape[0], bias.shape[1] // 2
    groups = span // tokens
    me = lax.axis_index("ctx")
    rank, mine = lax.rem(me, group), lax.div(me, group)
    qpos = order_ref[0] * tokens + lax.broadcasted_iota(jnp.int32, (tokens, tokens), 0)
    kpos = lax.broadcasted_iota(jnp.int32, (tokens, tokens), 1)
    for i, s in enumerate(sides):
        for d in range(groups):
            place = lax.rem(mine + groups - d, groups) * group + (rank ^ s)
            at = i * span + d * tokens
            bias[:, at : at + tokens] = jnp.where(place * tokens + kpos <= qpos, 0.0, -1e30)


def softmax_values(held, g, kv_heads, values):
    span = held[0].shape[0]
    values[:, HD:] = jnp.ones((2 * span, HD), BF16)
    for i, ref in enumerate(held):
        values[i * span : (i + 1) * span, :HD] = ref[:, head_cols(kv_heads + g)]


def softmax_scores(query, held, g, bias):
    raw = [
        lax.dot_general(query, ref[:, head_cols(g)], NT, preferred_element_type=F32) for ref in held
    ]
    raw = jnp.concatenate(raw, axis=1)
    raw = raw.reshape(-1, *bias.shape) + bias[...][None]
    return raw.reshape(-1, bias.shape[1])


def stacked(ref, columns):
    return jnp.concatenate([ref[:, cols] for cols in columns], axis=0)


SCORE = math.log2(math.e) / math.sqrt(HD)


def softmax_first_kernel(group, sides, kv_heads, pack, order_ref, q_ref, a_ref, b_ref, *rest):
    acc_ref, tops, (values, bias) = rest[0], rest[1:-2], rest[-2:]
    tokens = q_ref.shape[0]
    share = q_ref.shape[1] // HD // kv_heads
    softmax_bias(group, sides, order_ref, bias)
    for g in range(kv_heads):
        softmax_values((a_ref, b_ref), g, kv_heads, values)
        for j in range(0, share, pack):
            heads = range(g * share + j, g * share + j + pack)
            raw = softmax_scores(stacked(q_ref, map(head_cols, heads)), (a_ref, b_ref), g, bias)
            top = jnp.max(raw, axis=-1, keepdims=True)
            probs = jnp.exp2((raw - top) * SCORE).astype(BF16)
            acc = jnp.dot(probs, values[...], preferred_element_type=F32)
            for i, h in enumerate(heads):
                rows = slice(i * tokens, (i + 1) * tokens)
                acc_ref[:, 2 * h * HD : 2 * (h + 1) * HD] = acc[rows]
                tops[g][:, j + i : j + i + 1] = top[rows]


def softmax_last_kernel(group, sides, g, kv_heads, pack, order_ref, q_ref, a_ref, b_ref, *rest):
    acc_ref, top_ref = rest[:2]
    out_ref, done_ref, values, bias = rest[-4:]
    tokens = q_ref.shape[0]
    done_ref[...] = jnp.zeros_like(done_ref)
    softmax_bias(group, sides, order_ref, bias)
    softmax_values((a_ref, b_ref), g, kv_heads, values)
    for j in range(0, q_ref.shape[1] // HD, pack):
        heads = range(j, j + pack)
        raw = softmax_scores(stacked(q_ref, map(head_cols, heads)), (a_ref, b_ref), g, bias)
        old = stacked(top_ref, [slice(h, h + 1) for h in heads])
        top = jnp.maximum(old, jnp.max(raw, axis=-1, keepdims=True))
        probs = jnp.exp2((raw - top) * SCORE).astype(BF16)
        acc = jnp.dot(probs, values[...], preferred_element_type=F32)
        held = stacked(acc_ref, [slice(2 * h * HD, 2 * (h + 1) * HD) for h in heads])
        acc += held * jnp.exp2((old - top) * SCORE)
        out = (acc[:, :HD] / acc[:, HD:]).astype(BF16)
        for i, h in enumerate(heads):
            out_ref[:, head_cols(h)] = out[i * tokens : (i + 1) * tokens]


def call(
    kernel, name, outs, args, scratch=(), flops=0, exps=0, limit=16, specs=None, after=(), **more
):
    size = sum(math.prod(x.shape) * x.dtype.itemsize for x in list(args) + list(outs))
    more.setdefault("out_specs", [VMEM for _ in outs])
    specs = list(specs or [VMEM for _ in args]) + [HBM for _ in after]
    count = len(args)

    def run(*refs):
        kernel(*refs[:count], *refs[count + len(after) :])

    return pl.pallas_call(
        run,
        name=name,
        out_shape=list(outs),
        in_specs=specs,
        scratch_shapes=list(scratch),
        cost_estimate=pl.CostEstimate(flops=flops, bytes_accessed=size, transcendentals=exps),
        compiler_params=pltpu.CompilerParams(vmem_limit_bytes=limit * MIB),
        **more,
    )(*args, *after)


def body(q_lin, k_lin, v_lin, log_decay, gate, norm_gain, queries, keys, values, order):
    tokens, width = q_lin.shape
    heads = log_decay.shape[0]
    kv_width = keys.shape[1]
    kv_heads = kv_width // HD
    n, nh = lax.axis_size("ctx"), lax.axis_size("head")
    group = 4
    groups = n // group
    per = heads // group
    rows = per * HD + 16
    cube = tokens * width * HD
    shape = jax.ShapeDtypeStruct

    def swap(x, s):
        return lax.ppermute(x, "ctx", [(c, c ^ s) for c in range(n)])

    def swap_all(xs):
        return [xs[0]] + [swap(xs[s], s) for s in range(1, group)]

    def ahead(x, d):
        return lax.ppermute(x, "ctx", [(c, (c + d * group) % n) for c in range(n)])

    tri, bias = call(
        triangle_kernel, "triangle", [shape((tokens, tokens), F32)] * 2, (), flops=1 << 31
    )
    (kv,) = call(
        beside_kernel,
        "keys_beside_values",
        [shape((tokens, 2 * kv_width), BF16)],
        (keys, values),
        after=(tri,),
    )
    far = [ahead(kv, d) for d in range(1, groups)]

    *pays, ka, va = call(
        functools.partial(state_kernel, group, heads),
        "block_states",
        [shape((rows, HD), BF16)] * group + [shape((tokens, width), BF16)] * 2,
        (tri, log_decay, k_lin, v_lin),
        [pltpu.VMEM((heads * HD, HD), BF16), pltpu.VMEM((group * 16, HD), F32)],
        flops=4 * cube,
        exps=2 * tokens * width,
    )
    pays = swap_all(pays)
    intra, qa, gain, decay = call(
        functools.partial(intra_kernel, heads),
        "intra_block",
        [
            shape((tokens, width), F32),
            shape((tokens, width), BF16),
            shape((tokens, width), F32),
            shape((tokens, heads), F32),
        ],
        (tri, bias, log_decay, q_lin, ka, va, gate, norm_gain.reshape(1, width)),
        flops=4 * cube,
        exps=4 * tokens * width,
        after=far,
    )

    slots = pltpu.VMEM((group, rows, HD), BF16)
    carry = ()
    if groups > 1:
        (total,) = call(
            functools.partial(total_kernel, group, per),
            "group_state",
            [shape((rows, HD), BF16)],
            pays,
            [slots],
            flops=2 * per * HD * HD * group,
            after=(intra,),
        )
        before = ahead(total, 1)
        shift = 1
        while shift < groups - 1:
            mine = lax.div(lax.axis_index("ctx"), group)
            later = jnp.where(mine >= 1, before, 0).astype(F32)
            earlier = ahead(later.astype(BF16), shift)
            earlier = jnp.where(mine >= shift + 1, earlier, 0).astype(F32)
            step = later[per * HD :][:per] + later[per * HD + 8 :][:per]
            prior = earlier[per * HD :][:per] + earlier[per * HD + 8 :][:per]
            state = later[: per * HD] + jnp.repeat(step, HD, axis=0) * earlier[: per * HD]
            both = jnp.where(mine >= shift + 1, step * prior, step)
            high = both.astype(BF16).astype(F32)
            pad = jnp.zeros((8 - per, HD), F32)
            before = jnp.concatenate([state, high, pad, both - high, pad], axis=0).astype(BF16)
            shift *= 2
        carry = (before,)
    prefixes = call(
        functools.partial(prefix_kernel, group, per, bool(carry)),
        "prefix_states",
        [shape((per * HD, HD), BF16)] * group,
        (*pays, *carry),
        [slots, pltpu.VMEM((group, per * HD, HD), BF16)],
        flops=1 << 33,
    )
    prefixes = swap_all(prefixes)

    (own,) = call(
        stack_kernel,
        "stack_keys_values",
        [shape((groups * tokens, kv.shape[1]), BF16)],
        (kv, *far),
        after=(total,) if groups > 1 else (intra,),
        flops=1 << 32,
    )
    near, side = swap(own, 1), swap(own, 2)
    half = own.shape[0] // 2
    across = jnp.concatenate([swap(near[:half], 2), swap(side[half:], 1)])
    share = width // kv_heads
    pack = 2 if share // HD % 2 == 0 else 1
    span = 2 * own.shape[0]
    scratch = [pltpu.VMEM((span, 2 * HD), BF16), pltpu.VMEM((tokens, span), F32)]
    room = 24 + 16 * span * tokens * 4 // MIB
    smem = pl.BlockSpec(memory_space=pltpu.SMEM)
    acc, *tops = call(
        functools.partial(softmax_first_kernel, group, (0, 1), kv_heads, pack),
        "softmax_first",
        [shape((tokens, 2 * width), F32)] + [shape((tokens, share // HD), F32)] * kv_heads,
        (order, queries, own, near),
        scratch,
        flops=4 * tokens * width * span,
        exps=tokens * span * width // HD,
        limit=room,
        specs=[smem] + [VMEM] * 3,
    )
    attended, marks = (), []
    for g in range(kv_heads):

        def columns(size, g=g):
            return pl.BlockSpec((tokens, size), lambda i: (0, g))

        def whole(x):
            return pl.BlockSpec(x.shape, lambda i: (0, 0))

        *attended, mark = call(
            functools.partial(softmax_last_kernel, group, (2, 3), g, kv_heads, pack),
            "softmax_last",
            [shape((tokens, width), BF16), shape((8, HD), F32)],
            (order, queries, side, across, acc, tops[g], *attended),
            scratch,
            flops=4 * tokens * share * span,
            exps=tokens * span * share // HD,
            limit=room,
            specs=[smem, columns(share), whole(side), whole(across)]
            + [columns(2 * share), whole(tops[g])]
            + [HBM for _ in attended],
            out_specs=[columns(share), pl.BlockSpec((8, HD), lambda i: (0, 0))],
            grid=(1,),
            input_output_aliases={6: 0} if attended else {},
        )
        marks.append(mark)

    lin, squares = call(
        functools.partial(inter_kernel, group, heads),
        "inter_block",
        [shape((tokens, width), F32), shape((8, tokens), F32)],
        (decay, qa, intra, *prefixes),
        [pltpu.VMEM((heads * HD, HD), BF16)],
        flops=2 * cube,
        after=tops[:1],
    )
    if nh & (nh - 1) == 0:
        parts, shift = [squares], 1
        while shift < nh:
            held = parts[0]
            if len(parts) > 1:
                (held,) = call(add_kernel, "add", [shape((8, tokens), F32)], parts, after=marks[:1])
            parts = [held, lax.ppermute(held, "head", [(i, i ^ shift) for i in range(nh)])]
            shift *= 2
    else:
        turns = [[(i, (i + d) % nh) for i in range(nh)] for d in range(1, nh)]
        parts = [squares] + [lax.ppermute(squares, "head", turn) for turn in turns]
    (mixed,) = call(
        functools.partial(mixed_kernel, heads, float(width * nh)),
        "gated_norm",
        [shape((tokens, width), BF16)],
        (lin, gain, *parts),
        flops=4 * tokens * width,
        after=marks,
    )
    return (mixed, attended[0])


def solution(mesh):
    return jax.shard_map(
        body,
        mesh=mesh,
        in_specs=(
            P("ctx", "head"),
            P("ctx", "head"),
            P("ctx", "head"),
            P("head", "ctx"),
            P("ctx", "head"),
            P("head"),
            P("ctx", "head"),
            P("ctx", "head"),
            P("ctx", "head"),
            P("ctx"),
        ),
        out_specs=(P("ctx", "head"), P("ctx", "head")),
        check_vma=False,
    )
```

```python
import functools
import math

import jax
import jax.numpy as jnp
from jax import lax
from jax.experimental import pallas as pl
from jax.experimental.pallas import tpu as pltpu
from jax.sharding import PartitionSpec as P

HD = 128
EPS = 1e-06
HIGH = lax.Precision.HIGHEST
F32 = jnp.float32
BF16 = jnp.bfloat16
NT = (((1,), (1,)), ((), ()))
TN = (((0,), (0,)), ((), ()))
MIB = 1 << 20
VMEM = pl.BlockSpec(memory_space=pltpu.VMEM)
HBM = pl.BlockSpec(memory_space=pltpu.HBM)


def silu16(x):
    x = x.astype(F32)
    return (x / (1.0 + jnp.exp(-x))).astype(BF16)


def lower_ones(size):
    rows = lax.broadcasted_iota(jnp.int32, (size, size), 0)
    cols = lax.broadcasted_iota(jnp.int32, (size, size), 1)
    return rows >= cols


def head_cols(h):
    return slice(h * HD, (h + 1) * HD)


def my_rank(group):
    return lax.rem(lax.axis_index("ctx"), group)


def dyn(index, size):
    return pl.ds(pl.multiple_of(index * size, size), size)


def triangle_kernel(ones_ref, bias_ref):
    lower = lower_ones(ones_ref.shape[0])
    ones_ref[...] = lower.astype(F32)
    bias_ref[...] = jnp.where(lower, 0.0, -1e30)


def state_kernel(group, heads, tri_ref, ld_ref, k_ref, v_ref, *rest):
    outs, (ka_ref, va_ref, states, totals) = rest[:group], rest[group:]
    tokens = k_ref.shape[0]
    per = heads // group
    rank = my_rank(group)
    ld = ld_ref[...]
    cum = lax.dot_general(tri_ref[...], ld, NT, precision=HIGH, preferred_element_type=F32)
    weight = jnp.exp(cum[tokens - 1 : tokens, :] - cum)
    total = jnp.broadcast_to(jnp.exp(jnp.sum(ld, axis=1, keepdims=True)), (heads, HD))
    high = total.astype(BF16).astype(F32)
    low = total - high
    totals[...] = jnp.zeros_like(totals)
    for k in range(group):
        totals[k * 16 : k * 16 + per, :] = high[k * per : (k + 1) * per]
        totals[k * 16 + 8 : k * 16 + 8 + per, :] = low[k * per : (k + 1) * per]
    for h in range(heads):
        ka = silu16(k_ref[:, head_cols(h)])
        va = silu16(v_ref[:, head_cols(h)])
        ka_ref[:, head_cols(h)] = ka
        va_ref[:, head_cols(h)] = va
        kdec = ka.astype(F32) * weight[:, h : h + 1]
        khigh = kdec.astype(BF16)
        klow = (kdec - khigh.astype(F32)).astype(BF16)
        state = lax.dot_general(khigh, va, TN, preferred_element_type=F32)
        state += lax.dot_general(klow, va, TN, preferred_element_type=F32)
        states[h * HD : (h + 1) * HD, :] = state.astype(BF16)
    for s in range(group):
        dest = rank ^ s
        outs[s][: per * HD, :] = states[dyn(dest, per * HD), :]
        outs[s][per * HD :, :] = totals[dyn(dest, 16), :].astype(BF16)


def beside_kernel(keys, values, out):
    width = keys.shape[1]
    out[:, :width] = keys[...]
    out[:, width:] = values[...]


def stack_kernel(*refs):
    tokens = refs[0].shape[0]
    for i, part in enumerate(refs[:-1]):
        refs[-1][i * tokens : (i + 1) * tokens, :] = part[...]


def halves_kernel(a_ref, b_ref, a_out, b_out):
    half = a_out.shape[0]
    a_out[...] = a_ref[:half, :]
    b_out[...] = b_ref[half:, :]


def decay_row(slots, k, base, j):
    tail = slots[k, base : base + 16, :].astype(F32)
    return tail[j : j + 1] + tail[8 + j : 9 + j]


def sent(group):
    return [0, *range(group - 1, 0, -1)]


def fill_slots(group, rank, pays, slots):
    for s, pay in zip(sent(group), pays):
        slots[rank ^ s] = pay[...]


def total_kernel(group, per, *refs):
    pays, out, slots = refs[:group], refs[group], refs[group + 1]
    fill_slots(group, my_rank(group), pays, slots)
    base = per * HD
    tails = []
    for j in range(per):
        state = slots[0, j * HD : (j + 1) * HD, :].astype(F32)
        whole = decay_row(slots, 0, base, j)
        for k in range(1, group):
            decay = decay_row(slots, k, base, j)
            state = decay * state + slots[k, j * HD : (j + 1) * HD, :].astype(F32)
            whole = whole * decay
        out[j * HD : (j + 1) * HD, :] = state.astype(BF16)
        tails.append(whole)
    pad = [jnp.zeros((8 - per, HD), F32)] if per < 8 else []
    total = jnp.concatenate(tails + pad, axis=0)
    high = total.astype(BF16).astype(F32)
    out[base:, :] = jnp.concatenate([high, total - high], axis=0).astype(BF16)


def prefix_kernel(group, per, carried, *refs):
    pays, refs = refs[:group], refs[group:]
    carry = None
    if carried:
        carry, refs = refs[0], refs[1:]
    outs, slots, prefixes = refs[:group], refs[group], refs[group + 1]
    rank = my_rank(group)
    later = lax.axis_index("ctx") >= group
    fill_slots(group, rank, pays, slots)
    base = per * HD
    for j in range(per):
        rows = slice(j * HD, (j + 1) * HD)
        state = jnp.zeros((HD, HD), F32)
        if carried:
            state = jnp.where(later, carry[rows, :].astype(F32), state)
        prefixes[0, rows, :] = state.astype(BF16)
        for k in range(group - 1):
            state = decay_row(slots, k, base, j) * state + slots[k, rows, :].astype(F32)
            prefixes[k + 1, rows, :] = state.astype(BF16)
    for s in range(group):
        outs[s][...] = prefixes[rank ^ s]


def intra_kernel(heads, tri_ref, bias_ref, ld_ref, q_ref, ka_ref, va_ref, gate_ref, gain_ref, *outs):
    intra_ref, qa_ref, gain_out, decay_out = outs
    ld = ld_ref[...]
    tri = tri_ref[...]
    bias = bias_ref[...]
    cum = lax.dot_general(tri, ld, NT, precision=HIGH, preferred_element_type=F32)
    cum_t = lax.dot_general(ld, tri, NT, precision=HIGH, preferred_element_type=F32)
    decay_out[...] = jnp.exp(cum)
    for h in range(heads):
        cols = head_cols(h)
        qa = silu16(q_ref[:, cols])
        qa_ref[:, cols] = qa
        scores = lax.dot_general(qa, ka_ref[:, cols], NT, preferred_element_type=F32)
        decay = jnp.exp((cum[:, h : h + 1] - cum_t[h : h + 1, :]) + bias)
        weights = (scores * decay).astype(BF16)
        intra_ref[:, cols] = jnp.dot(weights, va_ref[:, cols], preferred_element_type=F32)
        gate = 1.0 / (1.0 + jnp.exp(-gate_ref[:, cols].astype(F32)))
        gain_out[:, cols] = gate * gain_ref[:, cols]


def inter_kernel(group, heads, decay_ref, qa_ref, intra_ref, *rest):
    parts, (lin_ref, squares_ref, states) = rest[:group], rest[group:]
    tokens = qa_ref.shape[0]
    per = heads // group
    rank = my_rank(group)
    for s, part in zip(sent(group), parts):
        states[dyn(rank ^ s, per * HD), :] = part[...]
    decay = decay_ref[...]
    acc = jnp.zeros((tokens, HD), F32)
    for h in range(heads):
        cols = head_cols(h)
        state = states[h * HD : (h + 1) * HD, :]
        inter = jnp.dot(qa_ref[:, cols], state, preferred_element_type=F32)
        lin = intra_ref[:, cols] + inter * decay[:, h : h + 1]
        lin_ref[:, cols] = lin
        acc += lin * lin
    ones = jnp.ones((8, HD), F32)
    squares_ref[...] = lax.dot_general(ones, acc, NT, precision=HIGH, preferred_element_type=F32)


def add_kernel(a_ref, b_ref, out_ref):
    out_ref[...] = a_ref[...] + b_ref[...]


def mixed_kernel(heads, columns, lin_ref, gain_ref, *rest):
    squares, out_ref = rest[:-1], rest[-1]
    total = squares[0][...]
    for part in squares[1:]:
        total = total + part[...]
    inv = jnp.transpose(lax.rsqrt(total / columns + EPS))[:, 0:1]
    for h in range(heads):
        cols = head_cols(h)
        out_ref[:, cols] = (lin_ref[:, cols] * inv * gain_ref[:, cols]).astype(BF16)


def softmax_bias(group, sides, order_ref, bias):
    tokens, span = bias.shape[0], bias.shape[1] // 2
    groups = span // tokens
    me = lax.axis_index("ctx")
    rank, mine = lax.rem(me, group), lax.div(me, group)
    qpos = order_ref[0] * tokens + lax.broadcasted_iota(jnp.int32, (tokens, tokens), 0)
    kpos = lax.broadcasted_iota(jnp.int32, (tokens, tokens), 1)
    for i, s in enumerate(sides):
        for d in range(groups):
            place = lax.rem(mine + groups - d, groups) * group + (rank ^ s)
            at = i * span + d * tokens
            bias[:, at : at + tokens] = jnp.where(place * tokens + kpos <= qpos, 0.0, -1e30)


def softmax_values(held, g, kv_heads, values):
    span = held[0].shape[0]
    values[:, HD:] = jnp.ones((2 * span, HD), BF16)
    for i, ref in enumerate(held):
        values[i * span : (i + 1) * span, :HD] = ref[:, head_cols(kv_heads + g)]


def softmax_scores(query, held, g, bias):
    raw = [
        lax.dot_general(query, ref[:, head_cols(g)], NT, preferred_element_type=F32) for ref in held
    ]
    raw = jnp.concatenate(raw, axis=1)
    raw = raw.reshape(-1, *bias.shape) + bias[...][None]
    return raw.reshape(-1, bias.shape[1])


def stacked(ref, columns):
    return jnp.concatenate([ref[:, cols] for cols in columns], axis=0)


SCORE = math.log2(math.e) / math.sqrt(HD)


def softmax_first_kernel(group, sides, kv_heads, pack, order_ref, q_ref, a_ref, b_ref, *rest):
    acc_ref, tops, (values, bias) = rest[0], rest[1:-2], rest[-2:]
    tokens = q_ref.shape[0]
    share = q_ref.shape[1] // HD // kv_heads
    softmax_bias(group, sides, order_ref, bias)
    for g in range(kv_heads):
        softmax_values((a_ref, b_ref), g, kv_heads, values)
        for j in range(0, share, pack):
            heads = range(g * share + j, g * share + j + pack)
            raw = softmax_scores(stacked(q_ref, map(head_cols, heads)), (a_ref, b_ref), g, bias)
            top = jnp.max(raw, axis=-1, keepdims=True)
            probs = jnp.exp2((raw - top) * SCORE).astype(BF16)
            acc = jnp.dot(probs, values[...], preferred_element_type=F32)
            for i, h in enumerate(heads):
                rows = slice(i * tokens, (i + 1) * tokens)
                acc_ref[:, 2 * h * HD : 2 * (h + 1) * HD] = acc[rows]
                tops[g][:, j + i : j + i + 1] = top[rows]


def softmax_last_kernel(group, sides, kv_heads, pack, order_ref, q_ref, a_ref, b_ref, *rest):
    acc_ref, tops, (out_ref, done_ref, values, bias) = rest[0], rest[1:-4], rest[-4:]
    tokens = q_ref.shape[0]
    share = q_ref.shape[1] // HD // kv_heads
    done_ref[...] = jnp.zeros_like(done_ref)
    softmax_bias(group, sides, order_ref, bias)
    for g in range(kv_heads):
        softmax_values((a_ref, b_ref), g, kv_heads, values)
        for j in range(0, share, pack):
            heads = range(g * share + j, g * share + j + pack)
            raw = softmax_scores(stacked(q_ref, map(head_cols, heads)), (a_ref, b_ref), g, bias)
            old = stacked(tops[g], [slice(j + i, j + i + 1) for i in range(pack)])
            top = jnp.maximum(old, jnp.max(raw, axis=-1, keepdims=True))
            probs = jnp.exp2((raw - top) * SCORE).astype(BF16)
            acc = jnp.dot(probs, values[...], preferred_element_type=F32)
            held = stacked(acc_ref, [slice(2 * h * HD, 2 * (h + 1) * HD) for h in heads])
            acc += held * jnp.exp2((old - top) * SCORE)
            out = (acc[:, :HD] / acc[:, HD:]).astype(BF16)
            for i, h in enumerate(heads):
                out_ref[:, head_cols(h)] = out[i * tokens : (i + 1) * tokens]


def call(
    kernel, name, outs, args, scratch=(), flops=0, exps=0, limit=16, specs=None, after=(), **more
):
    size = sum(math.prod(x.shape) * x.dtype.itemsize for x in list(args) + list(outs))
    more.setdefault("out_specs", [VMEM for _ in outs])
    specs = list(specs or [VMEM for _ in args]) + [HBM for _ in after]
    count = len(args)

    def run(*refs):
        kernel(*refs[:count], *refs[count + len(after) :])

    return pl.pallas_call(
        run,
        name=name,
        out_shape=list(outs),
        in_specs=specs,
        scratch_shapes=list(scratch),
        cost_estimate=pl.CostEstimate(flops=flops, bytes_accessed=size, transcendentals=exps),
        compiler_params=pltpu.CompilerParams(vmem_limit_bytes=limit * MIB),
        **more,
    )(*args, *after)


def body(q_lin, k_lin, v_lin, log_decay, gate, norm_gain, queries, keys, values, order):
    tokens, width = q_lin.shape
    heads = log_decay.shape[0]
    kv_width = keys.shape[1]
    kv_heads = kv_width // HD
    n, nh = lax.axis_size("ctx"), lax.axis_size("head")
    group = 4
    groups = n // group
    per = heads // group
    rows = per * HD + 16
    cube = tokens * width * HD
    shape = jax.ShapeDtypeStruct

    def swap(x, s):
        return lax.ppermute(x, "ctx", [(c, c ^ s) for c in range(n)])

    def swap_all(xs):
        return [swap(xs[s], s) if s else xs[s] for s in sent(group)]

    def ahead(x, d):
        return lax.ppermute(x, "ctx", [(c, (c + d * group) % n) for c in range(n)])

    tri, bias = call(
        triangle_kernel, "triangle", [shape((tokens, tokens), F32)] * 2, (), flops=1 << 31
    )
    (kv,) = call(
        beside_kernel,
        "keys_beside_values",
        [shape((tokens, 2 * kv_width), BF16)],
        (keys, values),
        after=(tri,),
    )
    far = [ahead(kv, d) for d in range(1, groups)]

    *pays, ka, va = call(
        functools.partial(state_kernel, group, heads),
        "block_states",
        [shape((rows, HD), BF16)] * group + [shape((tokens, width), BF16)] * 2,
        (tri, log_decay, k_lin, v_lin),
        [pltpu.VMEM((heads * HD, HD), BF16), pltpu.VMEM((group * 16, HD), F32)],
        flops=4 * cube,
        exps=2 * tokens * width,
    )
    pays = swap_all(pays)
    intra, qa, gain, decay = call(
        functools.partial(intra_kernel, heads),
        "intra_block",
        [
            shape((tokens, width), F32),
            shape((tokens, width), BF16),
            shape((tokens, width), F32),
            shape((tokens, heads), F32),
        ],
        (tri, bias, log_decay, q_lin, ka, va, gate, norm_gain.reshape(1, width)),
        flops=4 * cube,
        exps=4 * tokens * width,
        after=far,
    )

    slots = pltpu.VMEM((group, rows, HD), BF16)
    carry = ()
    if groups > 1:
        (total,) = call(
            functools.partial(total_kernel, group, per),
            "group_state",
            [shape((rows, HD), BF16)],
            pays,
            [slots],
            flops=2 * per * HD * HD * group,
            after=(intra,),
        )
        before = ahead(total, 1)
        shift = 1
        while shift < groups - 1:
            mine = lax.div(lax.axis_index("ctx"), group)
            later = jnp.where(mine >= 1, before, 0).astype(F32)
            earlier = ahead(later.astype(BF16), shift)
            earlier = jnp.where(mine >= shift + 1, earlier, 0).astype(F32)
            step = later[per * HD :][:per] + later[per * HD + 8 :][:per]
            prior = earlier[per * HD :][:per] + earlier[per * HD + 8 :][:per]
            state = later[: per * HD] + jnp.repeat(step, HD, axis=0) * earlier[: per * HD]
            both = jnp.where(mine >= shift + 1, step * prior, step)
            high = both.astype(BF16).astype(F32)
            pad = jnp.zeros((8 - per, HD), F32)
            before = jnp.concatenate([state, high, pad, both - high, pad], axis=0).astype(BF16)
            shift *= 2
        carry = (before,)
    prefixes = call(
        functools.partial(prefix_kernel, group, per, bool(carry)),
        "prefix_states",
        [shape((per * HD, HD), BF16)] * group,
        (*pays, *carry),
        [slots, pltpu.VMEM((group, per * HD, HD), BF16)],
        flops=1 << 33,
    )
    prefixes = swap_all(prefixes)

    (own,) = call(
        stack_kernel,
        "stack_keys_values",
        [shape((groups * tokens, kv.shape[1]), BF16)],
        (kv, *far),
        after=(total,) if groups > 1 else (intra,),
        flops=1 << 32,
    )
    near, side = swap(own, 1), swap(own, 2)
    share = width // kv_heads
    pack = 2 if share // HD % 2 == 0 else 1
    span = 2 * own.shape[0]
    scratch = [pltpu.VMEM((span, 2 * HD), BF16), pltpu.VMEM((tokens, span), F32)]
    room = 24 + 16 * span * tokens * 4 // MIB
    smem = pl.BlockSpec(memory_space=pltpu.SMEM)
    acc, *tops = call(
        functools.partial(softmax_first_kernel, group, (0, 1), kv_heads, pack),
        "softmax_first",
        [shape((tokens, 2 * width), F32)] + [shape((tokens, share // HD), F32)] * kv_heads,
        (order, queries, own, near),
        scratch,
        flops=4 * tokens * width * span,
        exps=tokens * span * width // HD,
        limit=room,
        specs=[smem] + [VMEM] * 3,
    )
    half = shape((own.shape[0] // 2, own.shape[1]), BF16)
    upper, under = call(halves_kernel, "sent_on", [half] * 2, (near, side), after=tops[:1])
    across = jnp.concatenate([swap(upper, 2), swap(under, 1)])
    attended, mark = call(
        functools.partial(softmax_last_kernel, group, (2, 3), kv_heads, pack),
        "softmax_last",
        [shape((tokens, width), BF16), shape((8, HD), F32)],
        (order, queries, side, across, acc, *tops),
        scratch,
        flops=4 * tokens * width * span,
        exps=tokens * span * width // HD,
        limit=room,
        specs=[smem] + [VMEM] * (4 + kv_heads),
    )

    lin, squares = call(
        functools.partial(inter_kernel, group, heads),
        "inter_block",
        [shape((tokens, width), F32), shape((8, tokens), F32)],
        (decay, qa, intra, *prefixes),
        [pltpu.VMEM((heads * HD, HD), BF16)],
        flops=2 * cube,
        after=tops[:1],
    )
    if nh & (nh - 1) == 0:
        parts, shift = [squares], 1
        while shift < nh:
            held = parts[0]
            if len(parts) > 1:
                (held,) = call(add_kernel, "add", [shape((8, tokens), F32)], parts, after=(mark,))
            parts = [held, lax.ppermute(held, "head", [(i, i ^ shift) for i in range(nh)])]
            shift *= 2
    else:
        turns = [[(i, (i + d) % nh) for i in range(nh)] for d in range(1, nh)]
        parts = [squares] + [lax.ppermute(squares, "head", turn) for turn in turns]
    (mixed,) = call(
        functools.partial(mixed_kernel, heads, float(width * nh)),
        "gated_norm",
        [shape((tokens, width), BF16)],
        (lin, gain, *parts),
        flops=4 * tokens * width,
        after=(mark,),
    )
    return (mixed, attended)


def solution(mesh):
    return jax.shard_map(
        body,
        mesh=mesh,
        in_specs=(
            P("ctx", "head"),
            P("ctx", "head"),
            P("ctx", "head"),
            P("head", "ctx"),
            P("ctx", "head"),
            P("head"),
            P("ctx", "head"),
            P("ctx", "head"),
            P("ctx", "head"),
            P("ctx"),
        ),
        out_specs=(P("ctx", "head"), P("ctx", "head")),
        check_vma=False,
    )
```

```python
import functools
import math

import jax
import jax.numpy as jnp
from jax import lax
from jax.experimental import pallas as pl
from jax.experimental.pallas import tpu as pltpu
from jax.sharding import PartitionSpec as P

HD = 128
EPS = 1e-06
HIGH = lax.Precision.HIGHEST
F32 = jnp.float32
BF16 = jnp.bfloat16
NT = (((1,), (1,)), ((), ()))
TN = (((0,), (0,)), ((), ()))
MIB = 1 << 20
VMEM = pl.BlockSpec(memory_space=pltpu.VMEM)
HBM = pl.BlockSpec(memory_space=pltpu.HBM)


def silu16(x):
    x = x.astype(F32)
    return (x / (1.0 + jnp.exp(-x))).astype(BF16)


def lower_ones(size):
    rows = lax.broadcasted_iota(jnp.int32, (size, size), 0)
    cols = lax.broadcasted_iota(jnp.int32, (size, size), 1)
    return rows >= cols


def head_cols(h):
    return slice(h * HD, (h + 1) * HD)


def my_rank(group):
    return lax.rem(lax.axis_index("ctx"), group)


def dyn(index, size):
    return pl.ds(pl.multiple_of(index * size, size), size)


def triangle_kernel(ones_ref, bias_ref):
    lower = lower_ones(ones_ref.shape[0])
    ones_ref[...] = lower.astype(F32)
    bias_ref[...] = jnp.where(lower, 0.0, -1e30)


def state_kernel(group, heads, tri_ref, ld_ref, k_ref, v_ref, *rest):
    outs, (ka_ref, va_ref, states, totals) = rest[:group], rest[group:]
    tokens = k_ref.shape[0]
    per = heads // group
    rank = my_rank(group)
    ld = ld_ref[...]
    cum = lax.dot_general(tri_ref[...], ld, NT, precision=HIGH, preferred_element_type=F32)
    weight = jnp.exp(cum[tokens - 1 : tokens, :] - cum)
    total = jnp.broadcast_to(jnp.exp(jnp.sum(ld, axis=1, keepdims=True)), (heads, HD))
    high = total.astype(BF16).astype(F32)
    low = total - high
    totals[...] = jnp.zeros_like(totals)
    for k in range(group):
        totals[k * 16 : k * 16 + per, :] = high[k * per : (k + 1) * per]
        totals[k * 16 + 8 : k * 16 + 8 + per, :] = low[k * per : (k + 1) * per]
    for h in range(heads):
        ka = silu16(k_ref[:, head_cols(h)])
        va = silu16(v_ref[:, head_cols(h)])
        ka_ref[:, head_cols(h)] = ka
        va_ref[:, head_cols(h)] = va
        kdec = ka.astype(F32) * weight[:, h : h + 1]
        khigh = kdec.astype(BF16)
        klow = (kdec - khigh.astype(F32)).astype(BF16)
        state = lax.dot_general(khigh, va, TN, preferred_element_type=F32)
        state += lax.dot_general(klow, va, TN, preferred_element_type=F32)
        states[h * HD : (h + 1) * HD, :] = state.astype(BF16)
    for s in range(group):
        dest = rank ^ s
        outs[s][: per * HD, :] = states[dyn(dest, per * HD), :]
        outs[s][per * HD :, :] = totals[dyn(dest, 16), :].astype(BF16)


def beside_kernel(keys, values, out):
    width = keys.shape[1]
    out[:, :width] = keys[...]
    out[:, width:] = values[...]


def stack_kernel(*refs):
    tokens = refs[0].shape[0]
    for i, part in enumerate(refs[:-1]):
        refs[-1][i * tokens : (i + 1) * tokens, :] = part[...]


def halves_kernel(a_ref, b_ref, a_out, b_out):
    half = a_out.shape[0]
    a_out[...] = a_ref[:half, :]
    b_out[...] = b_ref[half:, :]


def decay_row(slots, k, base, j):
    tail = slots[k, base : base + 16, :].astype(F32)
    return tail[j : j + 1] + tail[8 + j : 9 + j]


def sent(group):
    return [0, *range(group - 1, 0, -1)]


def fill_slots(group, rank, pays, slots):
    for s, pay in zip(sent(group), pays):
        slots[rank ^ s] = pay[...]


def total_kernel(group, per, *refs):
    pays, out, slots = refs[:group], refs[group], refs[group + 1]
    fill_slots(group, my_rank(group), pays, slots)
    base = per * HD
    tails = []
    for j in range(per):
        state = slots[0, j * HD : (j + 1) * HD, :].astype(F32)
        whole = decay_row(slots, 0, base, j)
        for k in range(1, group):
            decay = decay_row(slots, k, base, j)
            state = decay * state + slots[k, j * HD : (j + 1) * HD, :].astype(F32)
            whole = whole * decay
        out[j * HD : (j + 1) * HD, :] = state.astype(BF16)
        tails.append(whole)
    pad = [jnp.zeros((8 - per, HD), F32)] if per < 8 else []
    total = jnp.concatenate(tails + pad, axis=0)
    high = total.astype(BF16).astype(F32)
    out[base:, :] = jnp.concatenate([high, total - high], axis=0).astype(BF16)


def prefix_kernel(group, per, carried, *refs):
    pays, refs = refs[:group], refs[group:]
    carry = None
    if carried:
        carry, refs = refs[0], refs[1:]
    outs, slots, prefixes = refs[:group], refs[group], refs[group + 1]
    rank = my_rank(group)
    later = lax.axis_index("ctx") >= group
    fill_slots(group, rank, pays, slots)
    base = per * HD
    for j in range(per):
        rows = slice(j * HD, (j + 1) * HD)
        state = jnp.zeros((HD, HD), F32)
        if carried:
            state = jnp.where(later, carry[rows, :].astype(F32), state)
        prefixes[0, rows, :] = state.astype(BF16)
        for k in range(group - 1):
            state = decay_row(slots, k, base, j) * state + slots[k, rows, :].astype(F32)
            prefixes[k + 1, rows, :] = state.astype(BF16)
    for s in range(group):
        outs[s][...] = prefixes[rank ^ s]


def intra_kernel(heads, tri_ref, bias_ref, ld_ref, q_ref, ka_ref, va_ref, gate_ref, gain_ref, *outs):
    intra_ref, qa_ref, gain_out, decay_out = outs
    ld = ld_ref[...]
    tri = tri_ref[...]
    bias = bias_ref[...]
    cum = lax.dot_general(tri, ld, NT, precision=HIGH, preferred_element_type=F32)
    cum_t = lax.dot_general(ld, tri, NT, precision=HIGH, preferred_element_type=F32)
    decay_out[...] = jnp.exp(cum)
    for h in range(heads):
        cols = head_cols(h)
        qa = silu16(q_ref[:, cols])
        qa_ref[:, cols] = qa
        scores = lax.dot_general(qa, ka_ref[:, cols], NT, preferred_element_type=F32)
        decay = jnp.exp((cum[:, h : h + 1] - cum_t[h : h + 1, :]) + bias)
        weights = (scores * decay).astype(BF16)
        intra_ref[:, cols] = jnp.dot(weights, va_ref[:, cols], preferred_element_type=F32)
        gate = 1.0 / (1.0 + jnp.exp(-gate_ref[:, cols].astype(F32)))
        gain_out[:, cols] = gate * gain_ref[:, cols]


def inter_kernel(group, heads, decay_ref, qa_ref, intra_ref, *rest):
    parts, (lin_ref, squares_ref, states) = rest[:group], rest[group:]
    tokens = qa_ref.shape[0]
    per = heads // group
    rank = my_rank(group)
    for s, part in zip(sent(group), parts):
        states[dyn(rank ^ s, per * HD), :] = part[...]
    decay = decay_ref[...]
    acc = jnp.zeros((tokens, HD), F32)
    for h in range(heads):
        cols = head_cols(h)
        state = states[h * HD : (h + 1) * HD, :]
        inter = jnp.dot(qa_ref[:, cols], state, preferred_element_type=F32)
        lin = intra_ref[:, cols] + inter * decay[:, h : h + 1]
        lin_ref[:, cols] = lin
        acc += lin * lin
    ones = jnp.ones((8, HD), F32)
    squares_ref[...] = lax.dot_general(ones, acc, NT, precision=HIGH, preferred_element_type=F32)


def mixed_kernel(heads, columns, lin_ref, gain_ref, *rest):
    squares, out_ref = rest[:-1], rest[-1]
    total = squares[0][...]
    for part in squares[1:]:
        total = total + part[...]
    inv = jnp.transpose(lax.rsqrt(total / columns + EPS))[:, 0:1]
    for h in range(heads):
        cols = head_cols(h)
        out_ref[:, cols] = (lin_ref[:, cols] * inv * gain_ref[:, cols]).astype(BF16)


def softmax_bias(group, sides, order_ref, bias):
    tokens, span = bias.shape[0], bias.shape[1] // len(sides)
    groups = span // tokens
    me = lax.axis_index("ctx")
    rank, mine = lax.rem(me, group), lax.div(me, group)
    qpos = order_ref[0] * tokens + lax.broadcasted_iota(jnp.int32, (tokens, tokens), 0)
    kpos = lax.broadcasted_iota(jnp.int32, (tokens, tokens), 1)
    for i, s in enumerate(sides):
        for d in range(groups):
            place = lax.rem(mine + groups - d, groups) * group + (rank ^ s)
            at = i * span + d * tokens
            bias[:, at : at + tokens] = jnp.where(place * tokens + kpos <= qpos, 0.0, -1e30)


def softmax_values(held, g, kv_heads, values):
    span = held[0].shape[0]
    values[:, HD:] = jnp.ones((span * len(held), HD), BF16)
    for i, ref in enumerate(held):
        values[i * span : (i + 1) * span, :HD] = ref[:, head_cols(kv_heads + g)]


def softmax_scores(query, held, g, bias):
    raw = [
        lax.dot_general(query, ref[:, head_cols(g)], NT, preferred_element_type=F32) for ref in held
    ]
    raw = jnp.concatenate(raw, axis=1)
    raw = raw.reshape(-1, *bias.shape) + bias[...][None]
    return raw.reshape(-1, bias.shape[1])


def stacked(ref, columns):
    return jnp.concatenate([ref[:, cols] for cols in columns], axis=0)


SCORE = math.log2(math.e) / math.sqrt(HD)


def softmax_first_kernel(group, sides, kv_heads, pack, order_ref, q_ref, *rest):
    arrays, rest = rest[: len(sides)], rest[len(sides) :]
    acc_ref, tops, (values, bias) = rest[0], rest[1:-2], rest[-2:]
    tokens = q_ref.shape[0]
    share = q_ref.shape[1] // HD // kv_heads
    softmax_bias(group, sides, order_ref, bias)
    for g in range(kv_heads):
        softmax_values(arrays, g, kv_heads, values)
        for j in range(0, share, pack):
            heads = range(g * share + j, g * share + j + pack)
            raw = softmax_scores(stacked(q_ref, map(head_cols, heads)), arrays, g, bias)
            top = jnp.max(raw, axis=-1, keepdims=True)
            probs = jnp.exp2((raw - top) * SCORE).astype(BF16)
            acc = jnp.dot(probs, values[...], preferred_element_type=F32)
            for i, h in enumerate(heads):
                rows = slice(i * tokens, (i + 1) * tokens)
                acc_ref[:, 2 * h * HD : 2 * (h + 1) * HD] = acc[rows]
                tops[g][:, j + i : j + i + 1] = top[rows]


def softmax_last_kernel(group, sides, kv_heads, pack, order_ref, q_ref, *rest):
    arrays, rest = rest[: len(sides)], rest[len(sides) :]
    acc_ref, tops, (out_ref, done_ref, values, bias) = rest[0], rest[1:-4], rest[-4:]
    tokens = q_ref.shape[0]
    share = q_ref.shape[1] // HD // kv_heads
    done_ref[...] = jnp.zeros_like(done_ref)
    softmax_bias(group, sides, order_ref, bias)
    for g in range(kv_heads):
        softmax_values(arrays, g, kv_heads, values)
        for j in range(0, share, pack):
            heads = range(g * share + j, g * share + j + pack)
            raw = softmax_scores(stacked(q_ref, map(head_cols, heads)), arrays, g, bias)
            old = stacked(tops[g], [slice(j + i, j + i + 1) for i in range(pack)])
            top = jnp.maximum(old, jnp.max(raw, axis=-1, keepdims=True))
            probs = jnp.exp2((raw - top) * SCORE).astype(BF16)
            acc = jnp.dot(probs, values[...], preferred_element_type=F32)
            held = stacked(acc_ref, [slice(2 * h * HD, 2 * (h + 1) * HD) for h in heads])
            acc += held * jnp.exp2((old - top) * SCORE)
            out = (acc[:, :HD] / acc[:, HD:]).astype(BF16)
            for i, h in enumerate(heads):
                out_ref[:, head_cols(h)] = out[i * tokens : (i + 1) * tokens]


def call(
    kernel, name, outs, args, scratch=(), flops=0, exps=0, limit=16, specs=None, after=(), **more
):
    size = sum(math.prod(x.shape) * x.dtype.itemsize for x in list(args) + list(outs))
    more.setdefault("out_specs", [VMEM for _ in outs])
    specs = list(specs or [VMEM for _ in args]) + [HBM for _ in after]
    count = len(args)

    def run(*refs):
        kernel(*refs[:count], *refs[count + len(after) :])

    return pl.pallas_call(
        run,
        name=name,
        out_shape=list(outs),
        in_specs=specs,
        scratch_shapes=list(scratch),
        cost_estimate=pl.CostEstimate(flops=flops, bytes_accessed=size, transcendentals=exps),
        compiler_params=pltpu.CompilerParams(vmem_limit_bytes=limit * MIB),
        **more,
    )(*args, *after)


def body(q_lin, k_lin, v_lin, log_decay, gate, norm_gain, queries, keys, values, order):
    tokens, width = q_lin.shape
    heads = log_decay.shape[0]
    kv_width = keys.shape[1]
    kv_heads = kv_width // HD
    n, nh = lax.axis_size("ctx"), lax.axis_size("head")
    group = 4
    groups = n // group
    per = heads // group
    rows = per * HD + 16
    cube = tokens * width * HD
    shape = jax.ShapeDtypeStruct

    def swap(x, s):
        return lax.ppermute(x, "ctx", [(c, c ^ s) for c in range(n)])

    def swap_all(xs):
        return [swap(xs[s], s) if s else xs[s] for s in sent(group)]

    def ahead(x, d):
        return lax.ppermute(x, "ctx", [(c, (c + d * group) % n) for c in range(n)])

    tri, bias = call(
        triangle_kernel, "triangle", [shape((tokens, tokens), F32)] * 2, (), flops=1 << 31
    )
    (kv,) = call(
        beside_kernel,
        "keys_beside_values",
        [shape((tokens, 2 * kv_width), BF16)],
        (keys, values),
        after=(tri,),
    )
    far = [ahead(kv, d) for d in range(1, groups)]

    *pays, ka, va = call(
        functools.partial(state_kernel, group, heads),
        "block_states",
        [shape((rows, HD), BF16)] * group + [shape((tokens, width), BF16)] * 2,
        (tri, log_decay, k_lin, v_lin),
        [pltpu.VMEM((heads * HD, HD), BF16), pltpu.VMEM((group * 16, HD), F32)],
        flops=4 * cube,
        exps=2 * tokens * width,
    )
    pays = swap_all(pays)
    intra, qa, gain, decay = call(
        functools.partial(intra_kernel, heads),
        "intra_block",
        [
            shape((tokens, width), F32),
            shape((tokens, width), BF16),
            shape((tokens, width), F32),
            shape((tokens, heads), F32),
        ],
        (tri, bias, log_decay, q_lin, ka, va, gate, norm_gain.reshape(1, width)),
        flops=4 * cube,
        exps=4 * tokens * width,
        after=far,
    )

    slots = pltpu.VMEM((group, rows, HD), BF16)
    carry = ()
    if groups > 1:
        (total,) = call(
            functools.partial(total_kernel, group, per),
            "group_state",
            [shape((rows, HD), BF16)],
            pays,
            [slots],
            flops=2 * per * HD * HD * group,
            after=(intra,),
        )
        before = ahead(total, 1)
        shift = 1
        while shift < groups - 1:
            mine = lax.div(lax.axis_index("ctx"), group)
            later = jnp.where(mine >= 1, before, 0).astype(F32)
            earlier = ahead(later.astype(BF16), shift)
            earlier = jnp.where(mine >= shift + 1, earlier, 0).astype(F32)
            step = later[per * HD :][:per] + later[per * HD + 8 :][:per]
            prior = earlier[per * HD :][:per] + earlier[per * HD + 8 :][:per]
            state = later[: per * HD] + jnp.repeat(step, HD, axis=0) * earlier[: per * HD]
            both = jnp.where(mine >= shift + 1, step * prior, step)
            high = both.astype(BF16).astype(F32)
            pad = jnp.zeros((8 - per, HD), F32)
            before = jnp.concatenate([state, high, pad, both - high, pad], axis=0).astype(BF16)
            shift *= 2
        carry = (before,)
    prefixes = call(
        functools.partial(prefix_kernel, group, per, bool(carry)),
        "prefix_states",
        [shape((per * HD, HD), BF16)] * group,
        (*pays, *carry),
        [slots, pltpu.VMEM((group, per * HD, HD), BF16)],
        flops=1 << 33,
    )
    prefixes = swap_all(prefixes)

    (own,) = call(
        stack_kernel,
        "stack_keys_values",
        [shape((groups * tokens, kv.shape[1]), BF16)],
        (kv, *far),
        after=(total,) if groups > 1 else (intra,),
        flops=1 << 32,
    )
    side, near = swap(own, 2), swap(own, 1)
    half = shape((own.shape[0] // 2, own.shape[1]), BF16)
    upper, under = call(halves_kernel, "sent_on", [half] * 2, (side, near))
    across = jnp.concatenate([swap(upper, 1), swap(under, 2)])
    share = width // kv_heads
    pack = 2 if share // HD % 2 == 0 else 1
    span = own.shape[0]
    room = 24 + 48 * span * tokens * 4 // MIB
    smem = pl.BlockSpec(memory_space=pltpu.SMEM)

    def scratch(count):
        keys = count * span
        return [pltpu.VMEM((keys, 2 * HD), BF16), pltpu.VMEM((tokens, keys), F32)]

    acc, *tops = call(
        functools.partial(softmax_first_kernel, group, (0, 2, 1), kv_heads, pack),
        "softmax_first",
        [shape((tokens, 2 * width), F32)] + [shape((tokens, share // HD), F32)] * kv_heads,
        (order, queries, own, side, near),
        scratch(3),
        flops=12 * tokens * width * span,
        exps=3 * tokens * span * width // HD,
        limit=room,
        specs=[smem] + [VMEM] * 4,
    )
    attended, mark = call(
        functools.partial(softmax_last_kernel, group, (3,), kv_heads, pack),
        "softmax_last",
        [shape((tokens, width), BF16), shape((8, HD), F32)],
        (order, queries, across, acc, *tops),
        scratch(1),
        flops=4 * tokens * width * span,
        exps=tokens * span * width // HD,
        limit=room,
        specs=[smem] + [VMEM] * (3 + kv_heads),
    )

    lin, squares = call(
        functools.partial(inter_kernel, group, heads),
        "inter_block",
        [shape((tokens, width), F32), shape((8, tokens), F32)],
        (decay, qa, intra, *prefixes),
        [pltpu.VMEM((heads * HD, HD), BF16)],
        flops=2 * cube,
        after=tops[:1],
    )
    if nh & (nh - 1) == 0:
        turns = [[(i, i ^ d) for i in range(nh)] for d in range(nh - 1, 0, -1)]
    else:
        turns = [[(i, (i + d) % nh) for i in range(nh)] for d in range(1, nh)]
    parts = [squares] + [lax.ppermute(squares, "head", turn) for turn in turns]
    (mixed,) = call(
        functools.partial(mixed_kernel, heads, float(width * nh)),
        "gated_norm",
        [shape((tokens, width), BF16)],
        (lin, gain, *parts),
        flops=4 * tokens * width,
        after=(mark,),
    )
    return (mixed, attended)


def solution(mesh):
    return jax.shard_map(
        body,
        mesh=mesh,
        in_specs=(
            P("ctx", "head"),
            P("ctx", "head"),
            P("ctx", "head"),
            P("head", "ctx"),
            P("ctx", "head"),
            P("head"),
            P("ctx", "head"),
            P("ctx", "head"),
            P("ctx", "head"),
            P("ctx"),
        ),
        out_specs=(P("ctx", "head"), P("ctx", "head")),
        check_vma=False,
    )
```

```python
import functools
import math

import jax
import jax.numpy as jnp
from jax import lax
from jax.experimental import pallas as pl
from jax.experimental.pallas import tpu as pltpu
from jax.sharding import PartitionSpec as P

HD = 128
EPS = 1e-06
HIGH = lax.Precision.HIGHEST
F32 = jnp.float32
BF16 = jnp.bfloat16
NT = (((1,), (1,)), ((), ()))
TN = (((0,), (0,)), ((), ()))
MIB = 1 << 20
VMEM = pl.BlockSpec(memory_space=pltpu.VMEM)
HBM = pl.BlockSpec(memory_space=pltpu.HBM)


def inverse(x):
    guess = pl.reciprocal(x, approx=True)
    return guess * (2.0 - x * guess)


def sigmoid(x):
    return inverse(1.0 + jnp.exp(-x))


def silu16(x):
    x = x.astype(F32)
    return (x * sigmoid(x)).astype(BF16)


def lower_ones(size):
    rows = lax.broadcasted_iota(jnp.int32, (size, size), 0)
    cols = lax.broadcasted_iota(jnp.int32, (size, size), 1)
    return rows >= cols


def head_cols(h):
    return slice(h * HD, (h + 1) * HD)


def my_rank(group):
    return lax.rem(lax.axis_index("ctx"), group)


def dyn(index, size):
    return pl.ds(pl.multiple_of(index * size, size), size)


def triangle_kernel(ones_ref, bias_ref):
    lower = lower_ones(ones_ref.shape[0])
    ones_ref[...] = lower.astype(F32)
    bias_ref[...] = jnp.where(lower, 0.0, -1e30)


def state_kernel(group, heads, tri_ref, ld_ref, k_ref, v_ref, *rest):
    outs, (ka_ref, va_ref, states, totals) = rest[:group], rest[group:]
    tokens = k_ref.shape[0]
    per = heads // group
    rank = my_rank(group)
    ld = ld_ref[...]
    cum = lax.dot_general(tri_ref[...], ld, NT, precision=HIGH, preferred_element_type=F32)
    weight = jnp.exp(cum[tokens - 1 : tokens, :] - cum)
    total = jnp.broadcast_to(jnp.exp(jnp.sum(ld, axis=1, keepdims=True)), (heads, HD))
    high = total.astype(BF16).astype(F32)
    low = total - high
    totals[...] = jnp.zeros_like(totals)
    for k in range(group):
        totals[k * 16 : k * 16 + per, :] = high[k * per : (k + 1) * per]
        totals[k * 16 + 8 : k * 16 + 8 + per, :] = low[k * per : (k + 1) * per]
    for h in range(heads):
        ka = silu16(k_ref[:, head_cols(h)])
        va = silu16(v_ref[:, head_cols(h)])
        ka_ref[:, head_cols(h)] = ka
        va_ref[:, head_cols(h)] = va
        kdec = ka.astype(F32) * weight[:, h : h + 1]
        khigh = kdec.astype(BF16)
        klow = (kdec - khigh.astype(F32)).astype(BF16)
        state = lax.dot_general(khigh, va, TN, preferred_element_type=F32)
        state += lax.dot_general(klow, va, TN, preferred_element_type=F32)
        states[h * HD : (h + 1) * HD, :] = state.astype(BF16)
    for s in range(group):
        dest = rank ^ s
        outs[s][: per * HD, :] = states[dyn(dest, per * HD), :]
        outs[s][per * HD :, :] = totals[dyn(dest, 16), :].astype(BF16)


def beside_kernel(keys, values, out):
    width = keys.shape[1]
    out[:, :width] = keys[...]
    out[:, width:] = values[...]


def stack_kernel(*refs):
    tokens = refs[0].shape[0]
    for i, part in enumerate(refs[:-1]):
        refs[-1][i * tokens : (i + 1) * tokens, :] = part[...]


def halves_kernel(a_ref, b_ref, a_out, b_out):
    half = a_out.shape[0]
    a_out[...] = a_ref[:half, :]
    b_out[...] = b_ref[half:, :]


def decay_row(slots, k, base, j):
    tail = slots[k, base : base + 16, :].astype(F32)
    return tail[j : j + 1] + tail[8 + j : 9 + j]


def sent(group):
    return [0, *range(group - 1, 0, -1)]


def fill_slots(group, rank, pays, slots):
    for s, pay in zip(sent(group), pays):
        slots[rank ^ s] = pay[...]


def total_kernel(group, per, *refs):
    pays, out, slots = refs[:group], refs[group], refs[group + 1]
    fill_slots(group, my_rank(group), pays, slots)
    base = per * HD
    tails = []
    for j in range(per):
        state = slots[0, j * HD : (j + 1) * HD, :].astype(F32)
        whole = decay_row(slots, 0, base, j)
        for k in range(1, group):
            decay = decay_row(slots, k, base, j)
            state = decay * state + slots[k, j * HD : (j + 1) * HD, :].astype(F32)
            whole = whole * decay
        out[j * HD : (j + 1) * HD, :] = state.astype(BF16)
        tails.append(whole)
    pad = [jnp.zeros((8 - per, HD), F32)] if per < 8 else []
    total = jnp.concatenate(tails + pad, axis=0)
    high = total.astype(BF16).astype(F32)
    out[base:, :] = jnp.concatenate([high, total - high], axis=0).astype(BF16)


def prefix_kernel(group, per, carried, *refs):
    pays, refs = refs[:group], refs[group:]
    carry = None
    if carried:
        carry, refs = refs[0], refs[1:]
    outs, slots, prefixes = refs[:group], refs[group], refs[group + 1]
    rank = my_rank(group)
    later = lax.axis_index("ctx") >= group
    fill_slots(group, rank, pays, slots)
    base = per * HD
    for j in range(per):
        rows = slice(j * HD, (j + 1) * HD)
        state = jnp.zeros((HD, HD), F32)
        if carried:
            state = jnp.where(later, carry[rows, :].astype(F32), state)
        prefixes[0, rows, :] = state.astype(BF16)
        for k in range(group - 1):
            state = decay_row(slots, k, base, j) * state + slots[k, rows, :].astype(F32)
            prefixes[k + 1, rows, :] = state.astype(BF16)
    for s in range(group):
        outs[s][...] = prefixes[rank ^ s]


def intra_kernel(heads, tri_ref, bias_ref, ld_ref, q_ref, ka_ref, va_ref, gate_ref, gain_ref, *outs):
    intra_ref, qa_ref, gain_out, decay_out = outs
    ld = ld_ref[...]
    tri = tri_ref[...]
    bias = bias_ref[...]
    cum = lax.dot_general(tri, ld, NT, precision=HIGH, preferred_element_type=F32)
    cum_t = lax.dot_general(ld, tri, NT, precision=HIGH, preferred_element_type=F32)
    decay_out[...] = jnp.exp(cum)
    for h in range(heads):
        cols = head_cols(h)
        qa = silu16(q_ref[:, cols])
        qa_ref[:, cols] = qa
        scores = lax.dot_general(qa, ka_ref[:, cols], NT, preferred_element_type=F32)
        decay = jnp.exp((cum[:, h : h + 1] - cum_t[h : h + 1, :]) + bias)
        weights = (scores * decay).astype(BF16)
        intra_ref[:, cols] = jnp.dot(weights, va_ref[:, cols], preferred_element_type=F32)
        gain_out[:, cols] = sigmoid(gate_ref[:, cols].astype(F32)) * gain_ref[:, cols]


def inter_kernel(group, heads, decay_ref, qa_ref, intra_ref, *rest):
    parts, (lin_ref, squares_ref, states) = rest[:group], rest[group:]
    tokens = qa_ref.shape[0]
    per = heads // group
    rank = my_rank(group)
    for s, part in zip(sent(group), parts):
        states[dyn(rank ^ s, per * HD), :] = part[...]
    decay = decay_ref[...]
    acc = jnp.zeros((tokens, HD), F32)
    for h in range(heads):
        cols = head_cols(h)
        state = states[h * HD : (h + 1) * HD, :]
        inter = jnp.dot(qa_ref[:, cols], state, preferred_element_type=F32)
        lin = intra_ref[:, cols] + inter * decay[:, h : h + 1]
        lin_ref[:, cols] = lin
        acc += lin * lin
    ones = jnp.ones((8, HD), F32)
    squares_ref[...] = lax.dot_general(ones, acc, NT, precision=HIGH, preferred_element_type=F32)


def results_kernel(columns, parts, attended_ref, lin_ref, gain_ref, *rest):
    squares, (mixed_out, attended_out, mixed_ref, sems) = rest[:-4], rest[-4:]
    first = pltpu.make_async_copy(attended_ref, attended_out, sems.at[parts])
    first.start()
    total = squares[0][...]
    for part in squares[1:]:
        total = total + part[...]
    inv = jnp.transpose(lax.rsqrt(total / columns + EPS))[:, 0:1]
    width = lin_ref.shape[1] // parts
    copies = []
    for i in range(parts):
        cols = slice(i * width, (i + 1) * width)
        mixed_ref[:, cols] = (lin_ref[:, cols] * inv * gain_ref[:, cols]).astype(BF16)
        copies.append(
            pltpu.make_async_copy(mixed_ref.at[:, cols], mixed_out.at[:, cols], sems.at[i])
        )
        copies[-1].start()
    for copy in copies:
        copy.wait()
    first.wait()


def softmax_bias(group, sides, order_ref, bias):
    tokens, span = bias.shape[0], bias.shape[1] // len(sides)
    groups = span // tokens
    me = lax.axis_index("ctx")
    rank, mine = lax.rem(me, group), lax.div(me, group)
    qpos = order_ref[0] * tokens + lax.broadcasted_iota(jnp.int32, (tokens, tokens), 0)
    kpos = lax.broadcasted_iota(jnp.int32, (tokens, tokens), 1)
    for i, s in enumerate(sides):
        for d in range(groups):
            place = lax.rem(mine + groups - d, groups) * group + (rank ^ s)
            at = i * span + d * tokens
            bias[:, at : at + tokens] = jnp.where(place * tokens + kpos <= qpos, 0.0, -1e30)


def softmax_values(held, g, kv_heads, values):
    span = held[0].shape[0]
    values[:, HD:] = jnp.ones((span * len(held), HD), BF16)
    for i, ref in enumerate(held):
        values[i * span : (i + 1) * span, :HD] = ref[:, head_cols(kv_heads + g)]


def softmax_scores(query, held, g, bias):
    raw = [
        lax.dot_general(query, ref[:, head_cols(g)], NT, preferred_element_type=F32) for ref in held
    ]
    raw = jnp.concatenate(raw, axis=1)
    raw = raw.reshape(-1, *bias.shape) + bias[...][None]
    return raw.reshape(-1, bias.shape[1])


def stacked(ref, columns):
    return jnp.concatenate([ref[:, cols] for cols in columns], axis=0)


SCORE = math.log2(math.e) / math.sqrt(HD)


def softmax_first_kernel(group, sides, kv_heads, pack, order_ref, q_ref, *rest):
    arrays, rest = rest[: len(sides)], rest[len(sides) :]
    acc_ref, tops, (values, bias) = rest[0], rest[1:-2], rest[-2:]
    tokens = q_ref.shape[0]
    share = q_ref.shape[1] // HD // kv_heads
    softmax_bias(group, sides, order_ref, bias)
    for g in range(kv_heads):
        softmax_values(arrays, g, kv_heads, values)
        for j in range(0, share, pack):
            heads = range(g * share + j, g * share + j + pack)
            raw = softmax_scores(stacked(q_ref, map(head_cols, heads)), arrays, g, bias)
            top = jnp.max(raw, axis=-1, keepdims=True)
            probs = jnp.exp2((raw - top) * SCORE).astype(BF16)
            acc = jnp.dot(probs, values[...], preferred_element_type=F32)
            for i, h in enumerate(heads):
                rows = slice(i * tokens, (i + 1) * tokens)
                acc_ref[:, 2 * h * HD : 2 * (h + 1) * HD] = acc[rows]
                tops[g][:, j + i : j + i + 1] = top[rows]


def softmax_last_kernel(group, sides, kv_heads, pack, order_ref, q_ref, *rest):
    arrays, rest = rest[: len(sides)], rest[len(sides) :]
    acc_ref, tops, (out_ref, values, bias) = rest[0], rest[1:-3], rest[-3:]
    tokens = q_ref.shape[0]
    share = q_ref.shape[1] // HD // kv_heads
    softmax_bias(group, sides, order_ref, bias)
    for g in range(kv_heads):
        softmax_values(arrays, g, kv_heads, values)
        for j in range(0, share, pack):
            heads = range(g * share + j, g * share + j + pack)
            raw = softmax_scores(stacked(q_ref, map(head_cols, heads)), arrays, g, bias)
            old = stacked(tops[g], [slice(j + i, j + i + 1) for i in range(pack)])
            top = jnp.maximum(old, jnp.max(raw, axis=-1, keepdims=True))
            probs = jnp.exp2((raw - top) * SCORE).astype(BF16)
            acc = jnp.dot(probs, values[...], preferred_element_type=F32)
            held = stacked(acc_ref, [slice(2 * h * HD, 2 * (h + 1) * HD) for h in heads])
            acc += held * jnp.exp2((old - top) * SCORE)
            out = (acc[:, :HD] * inverse(acc[:, HD:])).astype(BF16)
            for i, h in enumerate(heads):
                out_ref[:, head_cols(h)] = out[i * tokens : (i + 1) * tokens]


def call(
    kernel, name, outs, args, scratch=(), flops=0, exps=0, limit=16, specs=None, after=(), **more
):
    size = sum(math.prod(x.shape) * x.dtype.itemsize for x in list(args) + list(outs))
    more.setdefault("out_specs", [VMEM for _ in outs])
    specs = list(specs or [VMEM for _ in args]) + [HBM for _ in after]
    count = len(args)

    def run(*refs):
        kernel(*refs[:count], *refs[count + len(after) :])

    return pl.pallas_call(
        run,
        name=name,
        out_shape=list(outs),
        in_specs=specs,
        scratch_shapes=list(scratch),
        cost_estimate=pl.CostEstimate(flops=flops, bytes_accessed=size, transcendentals=exps),
        compiler_params=pltpu.CompilerParams(vmem_limit_bytes=limit * MIB),
        **more,
    )(*args, *after)


def body(q_lin, k_lin, v_lin, log_decay, gate, norm_gain, queries, keys, values, order):
    tokens, width = q_lin.shape
    heads = log_decay.shape[0]
    kv_width = keys.shape[1]
    kv_heads = kv_width // HD
    n, nh = lax.axis_size("ctx"), lax.axis_size("head")
    group = 4
    groups = n // group
    per = heads // group
    rows = per * HD + 16
    cube = tokens * width * HD
    shape = jax.ShapeDtypeStruct

    def swap(x, s):
        return lax.ppermute(x, "ctx", [(c, c ^ s) for c in range(n)])

    def swap_all(xs):
        return [swap(xs[s], s) if s else xs[s] for s in sent(group)]

    def ahead(x, d):
        return lax.ppermute(x, "ctx", [(c, (c + d * group) % n) for c in range(n)])

    tri, bias = call(
        triangle_kernel, "triangle", [shape((tokens, tokens), F32)] * 2, (), flops=1 << 31
    )
    (kv,) = call(
        beside_kernel,
        "keys_beside_values",
        [shape((tokens, 2 * kv_width), BF16)],
        (keys, values),
        after=(tri,),
    )
    far = [ahead(kv, d) for d in range(1, groups)]

    *pays, ka, va = call(
        functools.partial(state_kernel, group, heads),
        "block_states",
        [shape((rows, HD), BF16)] * group + [shape((tokens, width), BF16)] * 2,
        (tri, log_decay, k_lin, v_lin),
        [pltpu.VMEM((heads * HD, HD), BF16), pltpu.VMEM((group * 16, HD), F32)],
        flops=4 * cube,
        exps=2 * tokens * width,
    )
    pays = swap_all(pays)
    intra, qa, gain, decay = call(
        functools.partial(intra_kernel, heads),
        "intra_block",
        [
            shape((tokens, width), F32),
            shape((tokens, width), BF16),
            shape((tokens, width), F32),
            shape((tokens, heads), F32),
        ],
        (tri, bias, log_decay, q_lin, ka, va, gate, norm_gain.reshape(1, width)),
        flops=4 * cube,
        exps=4 * tokens * width,
        after=far,
    )

    slots = pltpu.VMEM((group, rows, HD), BF16)
    carry = ()
    if groups > 1:
        (total,) = call(
            functools.partial(total_kernel, group, per),
            "group_state",
            [shape((rows, HD), BF16)],
            pays,
            [slots],
            flops=2 * per * HD * HD * group,
            after=(intra,),
        )
        before = ahead(total, 1)
        shift = 1
        while shift < groups - 1:
            mine = lax.div(lax.axis_index("ctx"), group)
            later = jnp.where(mine >= 1, before, 0).astype(F32)
            earlier = ahead(later.astype(BF16), shift)
            earlier = jnp.where(mine >= shift + 1, earlier, 0).astype(F32)
            step = later[per * HD :][:per] + later[per * HD + 8 :][:per]
            prior = earlier[per * HD :][:per] + earlier[per * HD + 8 :][:per]
            state = later[: per * HD] + jnp.repeat(step, HD, axis=0) * earlier[: per * HD]
            both = jnp.where(mine >= shift + 1, step * prior, step)
            high = both.astype(BF16).astype(F32)
            pad = jnp.zeros((8 - per, HD), F32)
            before = jnp.concatenate([state, high, pad, both - high, pad], axis=0).astype(BF16)
            shift *= 2
        carry = (before,)
    prefixes = call(
        functools.partial(prefix_kernel, group, per, bool(carry)),
        "prefix_states",
        [shape((per * HD, HD), BF16)] * group,
        (*pays, *carry),
        [slots, pltpu.VMEM((group, per * HD, HD), BF16)],
        flops=1 << 33,
    )
    prefixes = swap_all(prefixes)

    (own,) = call(
        stack_kernel,
        "stack_keys_values",
        [shape((groups * tokens, kv.shape[1]), BF16)],
        (kv, *far),
        after=(total,) if groups > 1 else (intra,),
        flops=1 << 32,
    )
    side, near = swap(own, 2), swap(own, 1)
    half = shape((own.shape[0] // 2, own.shape[1]), BF16)
    upper, under = call(halves_kernel, "sent_on", [half] * 2, (side, near))
    across = jnp.concatenate([swap(upper, 1), swap(under, 2)])
    share = width // kv_heads
    pack = 2 if share // HD % 2 == 0 else 1
    span = own.shape[0]
    room = 24 + 48 * span * tokens * 4 // MIB
    smem = pl.BlockSpec(memory_space=pltpu.SMEM)

    def scratch(count):
        keys = count * span
        return [pltpu.VMEM((keys, 2 * HD), BF16), pltpu.VMEM((tokens, keys), F32)]

    acc, *tops = call(
        functools.partial(softmax_first_kernel, group, (0, 2, 1), kv_heads, pack),
        "softmax_first",
        [shape((tokens, 2 * width), F32)] + [shape((tokens, share // HD), F32)] * kv_heads,
        (order, queries, own, side, near),
        scratch(3),
        flops=12 * tokens * width * span,
        exps=3 * tokens * span * width // HD,
        limit=room,
        specs=[smem] + [VMEM] * 4,
    )
    (attended,) = call(
        functools.partial(softmax_last_kernel, group, (3,), kv_heads, pack),
        "softmax_last",
        [shape((tokens, width), BF16)],
        (order, queries, across, acc, *tops),
        scratch(1),
        flops=4 * tokens * width * span,
        exps=tokens * span * width // HD,
        limit=room,
        specs=[smem] + [VMEM] * (3 + kv_heads),
    )

    lin, squares = call(
        functools.partial(inter_kernel, group, heads),
        "inter_block",
        [shape((tokens, width), F32), shape((8, tokens), F32)],
        (decay, qa, intra, *prefixes),
        [pltpu.VMEM((heads * HD, HD), BF16)],
        flops=2 * cube,
        after=tops[:1],
    )
    if nh & (nh - 1) == 0:
        turns = [[(i, i ^ d) for i in range(nh)] for d in range(nh - 1, 0, -1)]
    else:
        turns = [[(i, (i + d) % nh) for i in range(nh)] for d in range(1, nh)]
    parts = [squares] + [lax.ppermute(squares, "head", turn) for turn in turns]
    pieces = 4 if width % (4 * HD) == 0 else 1
    return call(
        functools.partial(results_kernel, float(width * nh), pieces),
        "results",
        [shape((tokens, width), BF16)] * 2,
        (attended, lin, gain, *parts),
        [pltpu.VMEM((tokens, width), BF16), pltpu.SemaphoreType.DMA((pieces + 1,))],
        flops=4 * tokens * width,
        out_specs=[HBM] * 2,
    )


def solution(mesh):
    return jax.shard_map(
        body,
        mesh=mesh,
        in_specs=(
            P("ctx", "head"),
            P("ctx", "head"),
            P("ctx", "head"),
            P("head", "ctx"),
            P("ctx", "head"),
            P("head"),
            P("ctx", "head"),
            P("ctx", "head"),
            P("ctx", "head"),
            P("ctx"),
        ),
        out_specs=(P("ctx", "head"), P("ctx", "head")),
        check_vma=False,
    )
```

```python
import functools
import math

import jax
import jax.numpy as jnp
from jax import lax
from jax.experimental import pallas as pl
from jax.experimental.pallas import tpu as pltpu
from jax.sharding import PartitionSpec as P

HD = 128
EPS = 1e-06
HIGH = lax.Precision.HIGHEST
F32 = jnp.float32
BF16 = jnp.bfloat16
NT = (((1,), (1,)), ((), ()))
TN = (((0,), (0,)), ((), ()))
MIB = 1 << 20
VMEM = pl.BlockSpec(memory_space=pltpu.VMEM)
HBM = pl.BlockSpec(memory_space=pltpu.HBM)


def inverse(x):
    guess = pl.reciprocal(x, approx=True)
    return guess * (2.0 - x * guess)


def silu16(x):
    x = x.astype(F32)
    return (x / (1.0 + jnp.exp(-x))).astype(BF16)


def lower_ones(size):
    rows = lax.broadcasted_iota(jnp.int32, (size, size), 0)
    cols = lax.broadcasted_iota(jnp.int32, (size, size), 1)
    return rows >= cols


def head_cols(h):
    return slice(h * HD, (h + 1) * HD)


def my_rank(group):
    return lax.rem(lax.axis_index("ctx"), group)


def dyn(index, size):
    return pl.ds(pl.multiple_of(index * size, size), size)


def triangle_kernel(ones_ref, bias_ref):
    lower = lower_ones(ones_ref.shape[0])
    ones_ref[...] = lower.astype(F32)
    bias_ref[...] = jnp.where(lower, 0.0, -1e30)


def state_kernel(group, heads, tri_ref, ld_ref, k_ref, v_ref, *rest):
    outs, (ka_ref, va_ref, states, totals) = rest[:group], rest[group:]
    tokens = k_ref.shape[0]
    per = heads // group
    rank = my_rank(group)
    ld = ld_ref[...]
    cum = lax.dot_general(tri_ref[...], ld, NT, precision=HIGH, preferred_element_type=F32)
    weight = jnp.exp(cum[tokens - 1 : tokens, :] - cum)
    total = jnp.broadcast_to(jnp.exp(jnp.sum(ld, axis=1, keepdims=True)), (heads, HD))
    high = total.astype(BF16).astype(F32)
    low = total - high
    totals[...] = jnp.zeros_like(totals)
    for k in range(group):
        totals[k * 16 : k * 16 + per, :] = high[k * per : (k + 1) * per]
        totals[k * 16 + 8 : k * 16 + 8 + per, :] = low[k * per : (k + 1) * per]
    for h in range(heads):
        ka = silu16(k_ref[:, head_cols(h)])
        va = silu16(v_ref[:, head_cols(h)])
        ka_ref[:, head_cols(h)] = ka
        va_ref[:, head_cols(h)] = va
        kdec = ka.astype(F32) * weight[:, h : h + 1]
        khigh = kdec.astype(BF16)
        klow = (kdec - khigh.astype(F32)).astype(BF16)
        state = lax.dot_general(khigh, va, TN, preferred_element_type=F32)
        state += lax.dot_general(klow, va, TN, preferred_element_type=F32)
        states[h * HD : (h + 1) * HD, :] = state.astype(BF16)
    for s in range(group):
        dest = rank ^ s
        outs[s][: per * HD, :] = states[dyn(dest, per * HD), :]
        outs[s][per * HD :, :] = totals[dyn(dest, 16), :].astype(BF16)


def beside_kernel(keys, values, out):
    width = keys.shape[1]
    out[:, :width] = keys[...]
    out[:, width:] = values[...]


def stack_kernel(*refs):
    tokens = refs[0].shape[0]
    for i, part in enumerate(refs[:-1]):
        refs[-1][i * tokens : (i + 1) * tokens, :] = part[...]


def halves_kernel(a_ref, b_ref, a_out, b_out):
    half = a_out.shape[0]
    a_out[...] = a_ref[:half, :]
    b_out[...] = b_ref[half:, :]


def decay_row(slots, k, base, j):
    tail = slots[k, base : base + 16, :].astype(F32)
    return tail[j : j + 1] + tail[8 + j : 9 + j]


def sent(group):
    return [0, *range(group - 1, 0, -1)]


def fill_slots(group, rank, pays, slots):
    for s, pay in zip(sent(group), pays):
        slots[rank ^ s] = pay[...]


def total_kernel(group, per, *refs):
    pays, out, slots = refs[:group], refs[group], refs[group + 1]
    fill_slots(group, my_rank(group), pays, slots)
    base = per * HD
    tails = []
    for j in range(per):
        state = slots[0, j * HD : (j + 1) * HD, :].astype(F32)
        whole = decay_row(slots, 0, base, j)
        for k in range(1, group):
            decay = decay_row(slots, k, base, j)
            state = decay * state + slots[k, j * HD : (j + 1) * HD, :].astype(F32)
            whole = whole * decay
        out[j * HD : (j + 1) * HD, :] = state.astype(BF16)
        tails.append(whole)
    pad = [jnp.zeros((8 - per, HD), F32)] if per < 8 else []
    total = jnp.concatenate(tails + pad, axis=0)
    high = total.astype(BF16).astype(F32)
    out[base:, :] = jnp.concatenate([high, total - high], axis=0).astype(BF16)


def prefix_kernel(group, per, carried, *refs):
    pays, refs = refs[:group], refs[group:]
    carry = None
    if carried:
        carry, refs = refs[0], refs[1:]
    outs, slots, prefixes = refs[:group], refs[group], refs[group + 1]
    rank = my_rank(group)
    later = lax.axis_index("ctx") >= group
    fill_slots(group, rank, pays, slots)
    base = per * HD
    for j in range(per):
        rows = slice(j * HD, (j + 1) * HD)
        state = jnp.zeros((HD, HD), F32)
        if carried:
            state = jnp.where(later, carry[rows, :].astype(F32), state)
        prefixes[0, rows, :] = state.astype(BF16)
        for k in range(group - 1):
            state = decay_row(slots, k, base, j) * state + slots[k, rows, :].astype(F32)
            prefixes[k + 1, rows, :] = state.astype(BF16)
    for s in range(group):
        outs[s][...] = prefixes[rank ^ s]


def intra_kernel(heads, tri_ref, bias_ref, ld_ref, q_ref, ka_ref, va_ref, gate_ref, gain_ref, *outs):
    intra_ref, qa_ref, gain_out, decay_out = outs
    ld = ld_ref[...]
    tri = tri_ref[...]
    bias = bias_ref[...]
    cum = lax.dot_general(tri, ld, NT, precision=HIGH, preferred_element_type=F32)
    cum_t = lax.dot_general(ld, tri, NT, precision=HIGH, preferred_element_type=F32)
    decay_out[...] = jnp.exp(cum)
    for h in range(heads):
        cols = head_cols(h)
        qa = silu16(q_ref[:, cols])
        qa_ref[:, cols] = qa
        scores = lax.dot_general(qa, ka_ref[:, cols], NT, preferred_element_type=F32)
        decay = jnp.exp((cum[:, h : h + 1] - cum_t[h : h + 1, :]) + bias)
        weights = (scores * decay).astype(BF16)
        intra_ref[:, cols] = jnp.dot(weights, va_ref[:, cols], preferred_element_type=F32)
        gate = 1.0 / (1.0 + jnp.exp(-gate_ref[:, cols].astype(F32)))
        gain_out[:, cols] = gate * gain_ref[:, cols]


def inter_kernel(group, heads, decay_ref, qa_ref, intra_ref, *rest):
    parts, (lin_ref, squares_ref, states) = rest[:group], rest[group:]
    tokens = qa_ref.shape[0]
    per = heads // group
    rank = my_rank(group)
    for s, part in zip(sent(group), parts):
        states[dyn(rank ^ s, per * HD), :] = part[...]
    decay = decay_ref[...]
    acc = jnp.zeros((tokens, HD), F32)
    for h in range(heads):
        cols = head_cols(h)
        state = states[h * HD : (h + 1) * HD, :]
        inter = jnp.dot(qa_ref[:, cols], state, preferred_element_type=F32)
        lin = intra_ref[:, cols] + inter * decay[:, h : h + 1]
        lin_ref[:, cols] = lin
        acc += lin * lin
    ones = jnp.ones((8, HD), F32)
    squares_ref[...] = lax.dot_general(ones, acc, NT, precision=HIGH, preferred_element_type=F32)


def results_kernel(columns, parts, attended_ref, lin_ref, gain_ref, *rest):
    squares, (mixed_out, attended_out, mixed_ref, sems) = rest[:-4], rest[-4:]
    first = pltpu.make_async_copy(attended_ref, attended_out, sems.at[parts])
    first.start()
    total = squares[0][...]
    for part in squares[1:]:
        total = total + part[...]
    inv = jnp.transpose(lax.rsqrt(total / columns + EPS))[:, 0:1]
    width = lin_ref.shape[1] // parts
    copies = []
    for i in range(parts):
        cols = slice(i * width, (i + 1) * width)
        mixed_ref[:, cols] = (lin_ref[:, cols] * inv * gain_ref[:, cols]).astype(BF16)
        copies.append(
            pltpu.make_async_copy(mixed_ref.at[:, cols], mixed_out.at[:, cols], sems.at[i])
        )
        copies[-1].start()
    for copy in copies:
        copy.wait()
    first.wait()


def softmax_bias(group, sides, order_ref, bias):
    tokens, span = bias.shape[0], bias.shape[1] // len(sides)
    groups = span // tokens
    me = lax.axis_index("ctx")
    rank, mine = lax.rem(me, group), lax.div(me, group)
    qpos = order_ref[0] * tokens + lax.broadcasted_iota(jnp.int32, (tokens, tokens), 0)
    kpos = lax.broadcasted_iota(jnp.int32, (tokens, tokens), 1)
    for i, s in enumerate(sides):
        for d in range(groups):
            place = lax.rem(mine + groups - d, groups) * group + (rank ^ s)
            at = i * span + d * tokens
            bias[:, at : at + tokens] = jnp.where(place * tokens + kpos <= qpos, 0.0, -1e30)


def softmax_values(held, g, kv_heads, values):
    span = held[0].shape[0]
    values[:, HD:] = jnp.ones((span * len(held), HD), BF16)
    for i, ref in enumerate(held):
        values[i * span : (i + 1) * span, :HD] = ref[:, head_cols(kv_heads + g)]


def softmax_scores(query, held, g, bias):
    raw = [
        lax.dot_general(query, ref[:, head_cols(g)], NT, preferred_element_type=F32) for ref in held
    ]
    raw = jnp.concatenate(raw, axis=1)
    raw = raw.reshape(-1, *bias.shape) + bias[...][None]
    return raw.reshape(-1, bias.shape[1])


def stacked(ref, columns):
    return jnp.concatenate([ref[:, cols] for cols in columns], axis=0)


SCORE = math.log2(math.e) / math.sqrt(HD)


def softmax_first_kernel(group, sides, kv_heads, pack, order_ref, q_ref, *rest):
    arrays, rest = rest[: len(sides)], rest[len(sides) :]
    acc_ref, tops, (values, bias) = rest[0], rest[1:-2], rest[-2:]
    tokens = q_ref.shape[0]
    share = q_ref.shape[1] // HD // kv_heads
    softmax_bias(group, sides, order_ref, bias)
    for g in range(kv_heads):
        softmax_values(arrays, g, kv_heads, values)
        for j in range(0, share, pack):
            heads = range(g * share + j, g * share + j + pack)
            raw = softmax_scores(stacked(q_ref, map(head_cols, heads)), arrays, g, bias)
            top = jnp.max(raw, axis=-1, keepdims=True)
            probs = jnp.exp2((raw - top) * SCORE).astype(BF16)
            acc = jnp.dot(probs, values[...], preferred_element_type=F32)
            for i, h in enumerate(heads):
                rows = slice(i * tokens, (i + 1) * tokens)
                acc_ref[:, 2 * h * HD : 2 * (h + 1) * HD] = acc[rows]
                tops[g][:, j + i : j + i + 1] = top[rows]


def softmax_last_kernel(group, sides, kv_heads, pack, order_ref, q_ref, *rest):
    arrays, rest = rest[: len(sides)], rest[len(sides) :]
    acc_ref, tops, (out_ref, values, bias) = rest[0], rest[1:-3], rest[-3:]
    tokens = q_ref.shape[0]
    share = q_ref.shape[1] // HD // kv_heads
    softmax_bias(group, sides, order_ref, bias)
    for g in range(kv_heads):
        softmax_values(arrays, g, kv_heads, values)
        for j in range(0, share, pack):
            heads = range(g * share + j, g * share + j + pack)
            raw = softmax_scores(stacked(q_ref, map(head_cols, heads)), arrays, g, bias)
            old = stacked(tops[g], [slice(j + i, j + i + 1) for i in range(pack)])
            top = jnp.maximum(old, jnp.max(raw, axis=-1, keepdims=True))
            probs = jnp.exp2((raw - top) * SCORE).astype(BF16)
            acc = jnp.dot(probs, values[...], preferred_element_type=F32)
            held = stacked(acc_ref, [slice(2 * h * HD, 2 * (h + 1) * HD) for h in heads])
            acc += held * jnp.exp2((old - top) * SCORE)
            out = (acc[:, :HD] * inverse(acc[:, HD:])).astype(BF16)
            for i, h in enumerate(heads):
                out_ref[:, head_cols(h)] = out[i * tokens : (i + 1) * tokens]


def call(
    kernel, name, outs, args, scratch=(), flops=0, exps=0, limit=16, specs=None, after=(), **more
):
    size = sum(math.prod(x.shape) * x.dtype.itemsize for x in list(args) + list(outs))
    more.setdefault("out_specs", [VMEM for _ in outs])
    specs = list(specs or [VMEM for _ in args]) + [HBM for _ in after]
    count = len(args)

    def run(*refs):
        kernel(*refs[:count], *refs[count + len(after) :])

    return pl.pallas_call(
        run,
        name=name,
        out_shape=list(outs),
        in_specs=specs,
        scratch_shapes=list(scratch),
        cost_estimate=pl.CostEstimate(flops=flops, bytes_accessed=size, transcendentals=exps),
        compiler_params=pltpu.CompilerParams(vmem_limit_bytes=limit * MIB),
        **more,
    )(*args, *after)


def body(q_lin, k_lin, v_lin, log_decay, gate, norm_gain, queries, keys, values, order):
    tokens, width = q_lin.shape
    heads = log_decay.shape[0]
    kv_width = keys.shape[1]
    kv_heads = kv_width // HD
    n, nh = lax.axis_size("ctx"), lax.axis_size("head")
    group = 4
    groups = n // group
    per = heads // group
    rows = per * HD + 16
    cube = tokens * width * HD
    shape = jax.ShapeDtypeStruct

    def swap(x, s):
        return lax.ppermute(x, "ctx", [(c, c ^ s) for c in range(n)])

    def swap_all(xs):
        return [swap(xs[s], s) if s else xs[s] for s in sent(group)]

    def ahead(x, d):
        return lax.ppermute(x, "ctx", [(c, (c + d * group) % n) for c in range(n)])

    tri, bias = call(
        triangle_kernel, "triangle", [shape((tokens, tokens), F32)] * 2, (), flops=1 << 31
    )
    (kv,) = call(
        beside_kernel,
        "keys_beside_values",
        [shape((tokens, 2 * kv_width), BF16)],
        (keys, values),
        after=(tri,),
    )
    far = [ahead(kv, d) for d in range(1, groups)]

    *pays, ka, va = call(
        functools.partial(state_kernel, group, heads),
        "block_states",
        [shape((rows, HD), BF16)] * group + [shape((tokens, width), BF16)] * 2,
        (tri, log_decay, k_lin, v_lin),
        [pltpu.VMEM((heads * HD, HD), BF16), pltpu.VMEM((group * 16, HD), F32)],
        flops=4 * cube,
        exps=2 * tokens * width,
    )
    pays = swap_all(pays)
    intra, qa, gain, decay = call(
        functools.partial(intra_kernel, heads),
        "intra_block",
        [
            shape((tokens, width), F32),
            shape((tokens, width), BF16),
            shape((tokens, width), F32),
            shape((tokens, heads), F32),
        ],
        (tri, bias, log_decay, q_lin, ka, va, gate, norm_gain.reshape(1, width)),
        flops=4 * cube,
        exps=4 * tokens * width,
        after=far,
    )

    slots = pltpu.VMEM((group, rows, HD), BF16)
    carry = ()
    if groups > 1:
        (total,) = call(
            functools.partial(total_kernel, group, per),
            "group_state",
            [shape((rows, HD), BF16)],
            pays,
            [slots],
            flops=2 * per * HD * HD * group,
            after=(intra,),
        )
        before = ahead(total, 1)
        shift = 1
        while shift < groups - 1:
            mine = lax.div(lax.axis_index("ctx"), group)
            later = jnp.where(mine >= 1, before, 0).astype(F32)
            earlier = ahead(later.astype(BF16), shift)
            earlier = jnp.where(mine >= shift + 1, earlier, 0).astype(F32)
            step = later[per * HD :][:per] + later[per * HD + 8 :][:per]
            prior = earlier[per * HD :][:per] + earlier[per * HD + 8 :][:per]
            state = later[: per * HD] + jnp.repeat(step, HD, axis=0) * earlier[: per * HD]
            both = jnp.where(mine >= shift + 1, step * prior, step)
            high = both.astype(BF16).astype(F32)
            pad = jnp.zeros((8 - per, HD), F32)
            before = jnp.concatenate([state, high, pad, both - high, pad], axis=0).astype(BF16)
            shift *= 2
        carry = (before,)
    prefixes = call(
        functools.partial(prefix_kernel, group, per, bool(carry)),
        "prefix_states",
        [shape((per * HD, HD), BF16)] * group,
        (*pays, *carry),
        [slots, pltpu.VMEM((group, per * HD, HD), BF16)],
        flops=2 * per * HD * HD * group,
    )
    prefixes = swap_all(prefixes)

    (own,) = call(
        stack_kernel,
        "stack_keys_values",
        [shape((groups * tokens, kv.shape[1]), BF16)],
        (kv, *far),
        after=(intra,),
    )
    side, near = swap(own, 2), swap(own, 1)
    half = shape((own.shape[0] // 2, own.shape[1]), BF16)
    upper, under = call(halves_kernel, "sent_on", [half] * 2, (side, near))
    across = jnp.concatenate([swap(upper, 1), swap(under, 2)])
    share = width // kv_heads
    pack = 2 if share // HD % 2 == 0 else 1
    span = own.shape[0]
    room = 24 + 48 * span * tokens * 4 // MIB
    smem = pl.BlockSpec(memory_space=pltpu.SMEM)

    def scratch(count):
        keys = count * span
        return [pltpu.VMEM((keys, 2 * HD), BF16), pltpu.VMEM((tokens, keys), F32)]

    acc, *tops = call(
        functools.partial(softmax_first_kernel, group, (0, 2, 1), kv_heads, pack),
        "softmax_first",
        [shape((tokens, 2 * width), F32)] + [shape((tokens, share // HD), F32)] * kv_heads,
        (order, queries, own, side, near),
        scratch(3),
        flops=12 * tokens * width * span,
        exps=3 * tokens * span * width // HD,
        limit=room,
        specs=[smem] + [VMEM] * 4,
    )
    (attended,) = call(
        functools.partial(softmax_last_kernel, group, (3,), kv_heads, pack),
        "softmax_last",
        [shape((tokens, width), BF16)],
        (order, queries, across, acc, *tops),
        scratch(1),
        flops=4 * tokens * width * span,
        exps=tokens * span * width // HD,
        limit=room,
        specs=[smem] + [VMEM] * (3 + kv_heads),
    )

    lin, squares = call(
        functools.partial(inter_kernel, group, heads),
        "inter_block",
        [shape((tokens, width), F32), shape((8, tokens), F32)],
        (decay, qa, intra, *prefixes),
        [pltpu.VMEM((heads * HD, HD), BF16)],
        flops=2 * cube,
        after=tops[:1],
    )
    if nh & (nh - 1) == 0:
        turns = [[(i, i ^ d) for i in range(nh)] for d in range(nh - 1, 0, -1)]
    else:
        turns = [[(i, (i + d) % nh) for i in range(nh)] for d in range(1, nh)]
    parts = [squares] + [lax.ppermute(squares, "head", turn) for turn in turns]
    pieces = 4 if width % (4 * HD) == 0 else 1
    return call(
        functools.partial(results_kernel, float(width * nh), pieces),
        "results",
        [shape((tokens, width), BF16)] * 2,
        (attended, lin, gain, *parts),
        [pltpu.VMEM((tokens, width), BF16), pltpu.SemaphoreType.DMA((pieces + 1,))],
        flops=4 * tokens * width,
        out_specs=[HBM] * 2,
    )


def solution(mesh):
    return jax.shard_map(
        body,
        mesh=mesh,
        in_specs=(
            P("ctx", "head"),
            P("ctx", "head"),
            P("ctx", "head"),
            P("head", "ctx"),
            P("ctx", "head"),
            P("head"),
            P("ctx", "head"),
            P("ctx", "head"),
            P("ctx", "head"),
            P("ctx"),
        ),
        out_specs=(P("ctx", "head"), P("ctx", "head")),
        check_vma=False,
    )
```

```python
import functools
import math

import jax
import jax.numpy as jnp
from jax import lax
from jax.experimental import pallas as pl
from jax.experimental.pallas import tpu as pltpu
from jax.sharding import PartitionSpec as P

HD = 128
EPS = 1e-06
HIGH = lax.Precision.HIGHEST
F32 = jnp.float32
BF16 = jnp.bfloat16
NT = (((1,), (1,)), ((), ()))
TN = (((0,), (0,)), ((), ()))
MIB = 1 << 20
VMEM = pl.BlockSpec(memory_space=pltpu.VMEM)
HBM = pl.BlockSpec(memory_space=pltpu.HBM)


def inverse(x):
    guess = pl.reciprocal(x, approx=True)
    return guess * (2.0 - x * guess)


def silu16(x):
    x = x.astype(F32)
    return (x / (1.0 + jnp.exp(-x))).astype(BF16)


def lower_ones(size):
    rows = lax.broadcasted_iota(jnp.int32, (size, size), 0)
    cols = lax.broadcasted_iota(jnp.int32, (size, size), 1)
    return rows >= cols


def head_cols(h):
    return slice(h * HD, (h + 1) * HD)


def my_rank(group):
    return lax.rem(lax.axis_index("ctx"), group)


def dyn(index, size):
    return pl.ds(pl.multiple_of(index * size, size), size)


def triangle_kernel(ones_ref, bias_ref):
    lower = lower_ones(ones_ref.shape[0])
    ones_ref[...] = lower.astype(F32)
    bias_ref[...] = jnp.where(lower, 0.0, -1e30)


def state_kernel(group, heads, tri_ref, ld_ref, k_ref, v_ref, *rest):
    outs, (ka_ref, va_ref, states, totals) = rest[:group], rest[group:]
    tokens = k_ref.shape[0]
    per = heads // group
    rank = my_rank(group)
    ld = ld_ref[...]
    cum = lax.dot_general(tri_ref[...], ld, NT, precision=HIGH, preferred_element_type=F32)
    weight = jnp.exp(cum[tokens - 1 : tokens, :] - cum)
    total = jnp.broadcast_to(jnp.exp(jnp.sum(ld, axis=1, keepdims=True)), (heads, HD))
    high = total.astype(BF16).astype(F32)
    low = total - high
    totals[...] = jnp.zeros_like(totals)
    for k in range(group):
        totals[k * 16 : k * 16 + per, :] = high[k * per : (k + 1) * per]
        totals[k * 16 + 8 : k * 16 + 8 + per, :] = low[k * per : (k + 1) * per]
    for h in range(heads):
        ka = silu16(k_ref[:, head_cols(h)])
        va = silu16(v_ref[:, head_cols(h)])
        ka_ref[:, head_cols(h)] = ka
        va_ref[:, head_cols(h)] = va
        kdec = ka.astype(F32) * weight[:, h : h + 1]
        khigh = kdec.astype(BF16)
        klow = (kdec - khigh.astype(F32)).astype(BF16)
        state = lax.dot_general(khigh, va, TN, preferred_element_type=F32)
        state += lax.dot_general(klow, va, TN, preferred_element_type=F32)
        states[h * HD : (h + 1) * HD, :] = state.astype(BF16)
    for s in range(group):
        dest = rank ^ s
        outs[s][: per * HD, :] = states[dyn(dest, per * HD), :]
        outs[s][per * HD :, :] = totals[dyn(dest, 16), :].astype(BF16)


def beside_kernel(keys, values, out):
    width = keys.shape[1]
    out[:, :width] = keys[...]
    out[:, width:] = values[...]


def stack_kernel(*refs):
    tokens = refs[0].shape[0]
    for i, part in enumerate(refs[:-1]):
        refs[-1][i * tokens : (i + 1) * tokens, :] = part[...]


def halves_kernel(a_ref, b_ref, a_out, b_out):
    half = a_out.shape[0]
    a_out[...] = a_ref[:half, :]
    b_out[...] = b_ref[half:, :]


def decay_row(slots, k, base, j):
    tail = slots[k, base : base + 16, :].astype(F32)
    return tail[j : j + 1] + tail[8 + j : 9 + j]


def sent(group):
    return [0, *range(group - 1, 0, -1)]


def fill_slots(group, rank, pays, slots):
    for s, pay in zip(sent(group), pays):
        slots[rank ^ s] = pay[...]


def total_kernel(group, per, *refs):
    pays, out, slots = refs[:group], refs[group], refs[group + 1]
    fill_slots(group, my_rank(group), pays, slots)
    base = per * HD
    tails = []
    for j in range(per):
        state = slots[0, j * HD : (j + 1) * HD, :].astype(F32)
        whole = decay_row(slots, 0, base, j)
        for k in range(1, group):
            decay = decay_row(slots, k, base, j)
            state = decay * state + slots[k, j * HD : (j + 1) * HD, :].astype(F32)
            whole = whole * decay
        out[j * HD : (j + 1) * HD, :] = state.astype(BF16)
        tails.append(whole)
    pad = [jnp.zeros((8 - per, HD), F32)] if per < 8 else []
    total = jnp.concatenate(tails + pad, axis=0)
    high = total.astype(BF16).astype(F32)
    out[base:, :] = jnp.concatenate([high, total - high], axis=0).astype(BF16)


def prefix_kernel(group, per, carried, *refs):
    pays, refs = refs[:group], refs[group:]
    carry = None
    if carried:
        carry, refs = refs[0], refs[1:]
    outs, slots, prefixes = refs[:group], refs[group], refs[group + 1]
    rank = my_rank(group)
    later = lax.axis_index("ctx") >= group
    fill_slots(group, rank, pays, slots)
    base = per * HD
    for j in range(per):
        rows = slice(j * HD, (j + 1) * HD)
        state = jnp.zeros((HD, HD), F32)
        if carried:
            state = jnp.where(later, carry[rows, :].astype(F32), state)
        prefixes[0, rows, :] = state.astype(BF16)
        for k in range(group - 1):
            state = decay_row(slots, k, base, j) * state + slots[k, rows, :].astype(F32)
            prefixes[k + 1, rows, :] = state.astype(BF16)
    for s in range(group):
        outs[s][...] = prefixes[rank ^ s]


def intra_kernel(heads, tri_ref, bias_ref, ld_ref, q_ref, ka_ref, va_ref, gate_ref, gain_ref, *outs):
    intra_ref, qa_ref, gain_out, decay_out = outs
    ld = ld_ref[...]
    tri = tri_ref[...]
    bias = bias_ref[...]
    cum = lax.dot_general(tri, ld, NT, precision=HIGH, preferred_element_type=F32)
    cum_t = lax.dot_general(ld, tri, NT, precision=HIGH, preferred_element_type=F32)
    decay_out[...] = jnp.exp(cum)
    for h in range(heads):
        cols = head_cols(h)
        qa = silu16(q_ref[:, cols])
        qa_ref[:, cols] = qa
        scores = lax.dot_general(qa, ka_ref[:, cols], NT, preferred_element_type=F32)
        decay = jnp.exp((cum[:, h : h + 1] - cum_t[h : h + 1, :]) + bias)
        weights = (scores * decay).astype(BF16)
        intra_ref[:, cols] = jnp.dot(weights, va_ref[:, cols], preferred_element_type=F32)
        gate = 1.0 / (1.0 + jnp.exp(-gate_ref[:, cols].astype(F32)))
        gain_out[:, cols] = gate * gain_ref[:, cols]


def inter_kernel(group, heads, decay_ref, qa_ref, intra_ref, *rest):
    parts, (lin_ref, squares_ref, states) = rest[:group], rest[group:]
    tokens = qa_ref.shape[0]
    per = heads // group
    rank = my_rank(group)
    for s, part in zip(sent(group), parts):
        states[dyn(rank ^ s, per * HD), :] = part[...]
    decay = decay_ref[...]
    acc = jnp.zeros((tokens, HD), F32)
    for h in range(heads):
        cols = head_cols(h)
        state = states[h * HD : (h + 1) * HD, :]
        inter = jnp.dot(qa_ref[:, cols], state, preferred_element_type=F32)
        lin = intra_ref[:, cols] + inter * decay[:, h : h + 1]
        lin_ref[:, cols] = lin
        acc += lin * lin
    ones = jnp.ones((8, HD), F32)
    squares_ref[...] = lax.dot_general(ones, acc, NT, precision=HIGH, preferred_element_type=F32)


def results_kernel(columns, parts, attended_ref, lin_ref, gain_ref, *rest):
    squares, (mixed_out, attended_out, mixed_ref, sems) = rest[:-4], rest[-4:]
    first = pltpu.make_async_copy(attended_ref, attended_out, sems.at[parts])
    first.start()
    total = squares[0][...]
    for part in squares[1:]:
        total = total + part[...]
    inv = jnp.transpose(lax.rsqrt(total / columns + EPS))[:, 0:1]
    width = lin_ref.shape[1] // parts
    copies = []
    for i in range(parts):
        cols = slice(i * width, (i + 1) * width)
        mixed_ref[:, cols] = (lin_ref[:, cols] * inv * gain_ref[:, cols]).astype(BF16)
        copies.append(
            pltpu.make_async_copy(mixed_ref.at[:, cols], mixed_out.at[:, cols], sems.at[i])
        )
        copies[-1].start()
    for copy in copies:
        copy.wait()
    first.wait()


def softmax_bias(group, sides, order_ref, bias):
    tokens, span = bias.shape[0], bias.shape[1] // len(sides)
    groups = span // tokens
    me = lax.axis_index("ctx")
    rank, mine = lax.rem(me, group), lax.div(me, group)
    qpos = order_ref[0] * tokens + lax.broadcasted_iota(jnp.int32, (tokens, tokens), 0)
    kpos = lax.broadcasted_iota(jnp.int32, (tokens, tokens), 1)
    for i, s in enumerate(sides):
        for d in range(groups):
            place = lax.rem(mine + groups - d, groups) * group + (rank ^ s)
            at = i * span + d * tokens
            bias[:, at : at + tokens] = jnp.where(place * tokens + kpos <= qpos, 0.0, -1e30)


def softmax_values(held, g, kv_heads, values):
    span = held[0].shape[0]
    values[:, HD:] = jnp.ones((span * len(held), HD), BF16)
    for i, ref in enumerate(held):
        values[i * span : (i + 1) * span, :HD] = ref[:, head_cols(kv_heads + g)]


def softmax_scores(query, held, g, bias):
    raw = [
        lax.dot_general(query, ref[:, head_cols(g)], NT, preferred_element_type=F32) for ref in held
    ]
    raw = jnp.concatenate(raw, axis=1)
    raw = raw.reshape(-1, *bias.shape) + bias[...][None]
    return raw.reshape(-1, bias.shape[1])


def stacked(ref, columns):
    return jnp.concatenate([ref[:, cols] for cols in columns], axis=0)


SCORE = math.log2(math.e) / math.sqrt(HD)


def softmax_first_kernel(group, sides, kv_heads, pack, order_ref, q_ref, *rest):
    arrays, rest = rest[: len(sides)], rest[len(sides) :]
    acc_ref, tops, (values, bias) = rest[0], rest[1:-2], rest[-2:]
    tokens = q_ref.shape[0]
    share = q_ref.shape[1] // HD // kv_heads
    softmax_bias(group, sides, order_ref, bias)
    for g in range(kv_heads):
        softmax_values(arrays, g, kv_heads, values)
        for j in range(0, share, pack):
            heads = range(g * share + j, g * share + j + pack)
            raw = softmax_scores(stacked(q_ref, map(head_cols, heads)), arrays, g, bias)
            top = jnp.max(raw, axis=-1, keepdims=True)
            probs = jnp.exp2((raw - top) * SCORE).astype(BF16)
            acc = jnp.dot(probs, values[...], preferred_element_type=F32)
            for i, h in enumerate(heads):
                rows = slice(i * tokens, (i + 1) * tokens)
                acc_ref[:, 2 * h * HD : 2 * (h + 1) * HD] = acc[rows]
                tops[g][:, j + i : j + i + 1] = top[rows]


def softmax_last_kernel(group, sides, kv_heads, pack, order_ref, q_ref, *rest):
    arrays, rest = rest[: len(sides)], rest[len(sides) :]
    acc_ref, tops, (out_ref, values, bias) = rest[0], rest[1:-3], rest[-3:]
    tokens = q_ref.shape[0]
    share = q_ref.shape[1] // HD // kv_heads
    softmax_bias(group, sides, order_ref, bias)
    for g in range(kv_heads):
        softmax_values(arrays, g, kv_heads, values)
        for j in range(0, share, pack):
            heads = range(g * share + j, g * share + j + pack)
            raw = softmax_scores(stacked(q_ref, map(head_cols, heads)), arrays, g, bias)
            old = stacked(tops[g], [slice(j + i, j + i + 1) for i in range(pack)])
            top = jnp.maximum(old, jnp.max(raw, axis=-1, keepdims=True))
            probs = jnp.exp2((raw - top) * SCORE).astype(BF16)
            acc = jnp.dot(probs, values[...], preferred_element_type=F32)
            held = stacked(acc_ref, [slice(2 * h * HD, 2 * (h + 1) * HD) for h in heads])
            acc += held * jnp.exp2((old - top) * SCORE)
            out = (acc[:, :HD] * inverse(acc[:, HD:])).astype(BF16)
            for i, h in enumerate(heads):
                out_ref[:, head_cols(h)] = out[i * tokens : (i + 1) * tokens]


def call(
    kernel, name, outs, args, scratch=(), flops=0, exps=0, limit=16, specs=None, after=(), **more
):
    size = sum(math.prod(x.shape) * x.dtype.itemsize for x in list(args) + list(outs))
    more.setdefault("out_specs", [VMEM for _ in outs])
    specs = list(specs or [VMEM for _ in args]) + [HBM for _ in after]
    count = len(args)

    def run(*refs):
        kernel(*refs[:count], *refs[count + len(after) :])

    return pl.pallas_call(
        run,
        name=name,
        out_shape=list(outs),
        in_specs=specs,
        scratch_shapes=list(scratch),
        cost_estimate=pl.CostEstimate(flops=flops, bytes_accessed=size, transcendentals=exps),
        compiler_params=pltpu.CompilerParams(vmem_limit_bytes=limit * MIB),
        **more,
    )(*args, *after)


def body(q_lin, k_lin, v_lin, log_decay, gate, norm_gain, queries, keys, values, order):
    tokens, width = q_lin.shape
    heads = log_decay.shape[0]
    kv_width = keys.shape[1]
    kv_heads = kv_width // HD
    n, nh = lax.axis_size("ctx"), lax.axis_size("head")
    group = 4
    groups = n // group
    per = heads // group
    rows = per * HD + 16
    cube = tokens * width * HD
    shape = jax.ShapeDtypeStruct

    def swap(x, s):
        return lax.ppermute(x, "ctx", [(c, c ^ s) for c in range(n)])

    def swap_all(xs):
        return [swap(xs[s], s) if s else xs[s] for s in sent(group)]

    def ahead(x, d):
        return lax.ppermute(x, "ctx", [(c, (c + d * group) % n) for c in range(n)])

    tri, bias = call(
        triangle_kernel, "triangle", [shape((tokens, tokens), F32)] * 2, (), flops=1 << 31
    )
    (kv,) = call(
        beside_kernel,
        "keys_beside_values",
        [shape((tokens, 2 * kv_width), BF16)],
        (keys, values),
        after=(tri,),
    )
    far = [ahead(kv, d) for d in range(1, groups)]

    *pays, ka, va = call(
        functools.partial(state_kernel, group, heads),
        "block_states",
        [shape((rows, HD), BF16)] * group + [shape((tokens, width), BF16)] * 2,
        (tri, log_decay, k_lin, v_lin),
        [pltpu.VMEM((heads * HD, HD), BF16), pltpu.VMEM((group * 16, HD), F32)],
        flops=4 * cube,
        exps=2 * tokens * width,
    )
    pays = swap_all(pays)
    intra, qa, gain, decay = call(
        functools.partial(intra_kernel, heads),
        "intra_block",
        [
            shape((tokens, width), F32),
            shape((tokens, width), BF16),
            shape((tokens, width), F32),
            shape((tokens, heads), F32),
        ],
        (tri, bias, log_decay, q_lin, ka, va, gate, norm_gain.reshape(1, width)),
        flops=4 * cube,
        exps=4 * tokens * width,
    )

    slots = pltpu.VMEM((group, rows, HD), BF16)
    carry = ()
    if groups > 1:
        (total,) = call(
            functools.partial(total_kernel, group, per),
            "group_state",
            [shape((rows, HD), BF16)],
            pays,
            [slots],
            flops=2 * per * HD * HD * group,
            after=(intra,),
        )
        before = ahead(total, 1)
        shift = 1
        while shift < groups - 1:
            mine = lax.div(lax.axis_index("ctx"), group)
            later = jnp.where(mine >= 1, before, 0).astype(F32)
            earlier = ahead(later.astype(BF16), shift)
            earlier = jnp.where(mine >= shift + 1, earlier, 0).astype(F32)
            step = later[per * HD :][:per] + later[per * HD + 8 :][:per]
            prior = earlier[per * HD :][:per] + earlier[per * HD + 8 :][:per]
            state = later[: per * HD] + jnp.repeat(step, HD, axis=0) * earlier[: per * HD]
            both = jnp.where(mine >= shift + 1, step * prior, step)
            high = both.astype(BF16).astype(F32)
            pad = jnp.zeros((8 - per, HD), F32)
            before = jnp.concatenate([state, high, pad, both - high, pad], axis=0).astype(BF16)
            shift *= 2
        carry = (before,)
    prefixes = call(
        functools.partial(prefix_kernel, group, per, bool(carry)),
        "prefix_states",
        [shape((per * HD, HD), BF16)] * group,
        (*pays, *carry),
        [slots, pltpu.VMEM((group, per * HD, HD), BF16)],
        flops=1 << 33,
    )
    prefixes = swap_all(prefixes)

    (own,) = call(
        stack_kernel,
        "stack_keys_values",
        [shape((groups * tokens, kv.shape[1]), BF16)],
        (kv, *far),
        after=(total,) if groups > 1 else (intra,),
        flops=1 << 32,
    )
    side, near = swap(own, 2), swap(own, 1)
    half = shape((own.shape[0] // 2, own.shape[1]), BF16)
    upper, under = call(halves_kernel, "sent_on", [half] * 2, (side, near))
    across = jnp.concatenate([swap(upper, 1), swap(under, 2)])
    share = width // kv_heads
    pack = 2 if share // HD % 2 == 0 else 1
    span = own.shape[0]
    room = 24 + 48 * span * tokens * 4 // MIB
    smem = pl.BlockSpec(memory_space=pltpu.SMEM)

    def scratch(count):
        keys = count * span
        return [pltpu.VMEM((keys, 2 * HD), BF16), pltpu.VMEM((tokens, keys), F32)]

    acc, *tops = call(
        functools.partial(softmax_first_kernel, group, (0, 2, 1), kv_heads, pack),
        "softmax_first",
        [shape((tokens, 2 * width), F32)] + [shape((tokens, share // HD), F32)] * kv_heads,
        (order, queries, own, side, near),
        scratch(3),
        flops=12 * tokens * width * span,
        exps=3 * tokens * span * width // HD,
        limit=room,
        specs=[smem] + [VMEM] * 4,
    )
    (attended,) = call(
        functools.partial(softmax_last_kernel, group, (3,), kv_heads, pack),
        "softmax_last",
        [shape((tokens, width), BF16)],
        (order, queries, across, acc, *tops),
        scratch(1),
        flops=4 * tokens * width * span,
        exps=tokens * span * width // HD,
        limit=room,
        specs=[smem] + [VMEM] * (3 + kv_heads),
    )

    lin, squares = call(
        functools.partial(inter_kernel, group, heads),
        "inter_block",
        [shape((tokens, width), F32), shape((8, tokens), F32)],
        (decay, qa, intra, *prefixes),
        [pltpu.VMEM((heads * HD, HD), BF16)],
        flops=2 * cube,
        after=tops[:1],
    )
    if nh & (nh - 1) == 0:
        turns = [[(i, i ^ d) for i in range(nh)] for d in range(nh - 1, 0, -1)]
    else:
        turns = [[(i, (i + d) % nh) for i in range(nh)] for d in range(1, nh)]
    parts = [squares] + [lax.ppermute(squares, "head", turn) for turn in turns]
    pieces = 4 if width % (4 * HD) == 0 else 1
    return call(
        functools.partial(results_kernel, float(width * nh), pieces),
        "results",
        [shape((tokens, width), BF16)] * 2,
        (attended, lin, gain, *parts),
        [pltpu.VMEM((tokens, width), BF16), pltpu.SemaphoreType.DMA((pieces + 1,))],
        flops=4 * tokens * width,
        out_specs=[HBM] * 2,
    )


def solution(mesh):
    return jax.shard_map(
        body,
        mesh=mesh,
        in_specs=(
            P("ctx", "head"),
            P("ctx", "head"),
            P("ctx", "head"),
            P("head", "ctx"),
            P("ctx", "head"),
            P("head"),
            P("ctx", "head"),
            P("ctx", "head"),
            P("ctx", "head"),
            P("ctx"),
        ),
        out_specs=(P("ctx", "head"), P("ctx", "head")),
        check_vma=False,
    )
```

```python
import functools
import math

import jax
import jax.numpy as jnp
from jax import lax
from jax.experimental import pallas as pl
from jax.experimental.pallas import tpu as pltpu
from jax.sharding import PartitionSpec as P

HD = 128
EPS = 1e-06
HIGH = lax.Precision.HIGHEST
F32 = jnp.float32
BF16 = jnp.bfloat16
NT = (((1,), (1,)), ((), ()))
TN = (((0,), (0,)), ((), ()))
MIB = 1 << 20
VMEM = pl.BlockSpec(memory_space=pltpu.VMEM)
HBM = pl.BlockSpec(memory_space=pltpu.HBM)


def inverse(x):
    guess = pl.reciprocal(x, approx=True)
    return guess * (2.0 - x * guess)


def silu16(x):
    x = x.astype(F32)
    return (x / (1.0 + jnp.exp(-x))).astype(BF16)


def lower_ones(size):
    rows = lax.broadcasted_iota(jnp.int32, (size, size), 0)
    cols = lax.broadcasted_iota(jnp.int32, (size, size), 1)
    return rows >= cols


def head_cols(h):
    return slice(h * HD, (h + 1) * HD)


def my_rank(group):
    return lax.rem(lax.axis_index("ctx"), group)


def dyn(index, size):
    return pl.ds(pl.multiple_of(index * size, size), size)


def triangle_kernel(ones_ref, bias_ref):
    lower = lower_ones(ones_ref.shape[0])
    ones_ref[...] = lower.astype(F32)
    bias_ref[...] = jnp.where(lower, 0.0, -1e30)


def decay_weights(tri_ref, ld_ref):
    ld = ld_ref[...]
    cum = lax.dot_general(tri_ref[...], ld, NT, precision=HIGH, preferred_element_type=F32)
    return jnp.exp(cum[-1:, :] - cum), jnp.exp(jnp.sum(ld, axis=1, keepdims=True))


def owner_states(k, per, weight, total, k_ref, v_ref, out):
    for j in range(per):
        h = k * per + j
        ka = silu16(k_ref[:, head_cols(h)])
        va = silu16(v_ref[:, head_cols(h)])
        kdec = ka.astype(F32) * weight[:, h : h + 1]
        khigh = kdec.astype(BF16)
        klow = (kdec - khigh.astype(F32)).astype(BF16)
        state = lax.dot_general(khigh, va, TN, preferred_element_type=F32)
        state += lax.dot_general(klow, va, TN, preferred_element_type=F32)
        out[j * HD : (j + 1) * HD, :] = state.astype(BF16)
    mine = jnp.broadcast_to(total[k * per : (k + 1) * per], (per, HD))
    high = mine.astype(BF16).astype(F32)
    pad = [jnp.zeros((8 - per, HD), F32)] if per < 8 else []
    tail = jnp.concatenate([high, *pad, mine - high, *pad], axis=0)
    out[per * HD :, :] = tail.astype(BF16)


def first_state_kernel(group, per, first, tri_ref, ld_ref, k_ref, v_ref, out_ref):
    weight, total = decay_weights(tri_ref, ld_ref)
    dest = my_rank(group) ^ first
    for k in range(group):
        pl.when(dest == k)(
            functools.partial(owner_states, k, per, weight, total, k_ref, v_ref, out_ref)
        )


def other_states_kernel(group, per, first, others, tri_ref, ld_ref, k_ref, v_ref, *rest):
    outs, payloads = rest[:-1], rest[-1]
    weight, total = decay_weights(tri_ref, ld_ref)
    rank = my_rank(group)
    for k in range(group):
        pl.when((rank ^ first) != k)(
            functools.partial(owner_states, k, per, weight, total, k_ref, v_ref, payloads.at[k])
        )
    for s, out in zip(others, outs):
        out[...] = payloads[rank ^ s]


def beside_kernel(keys, values, out):
    width = keys.shape[1]
    out[:, :width] = keys[...]
    out[:, width:] = values[...]


def stack_kernel(*refs):
    tokens = refs[0].shape[0]
    for i, part in enumerate(refs[:-1]):
        refs[-1][i * tokens : (i + 1) * tokens, :] = part[...]


def halves_kernel(a_ref, b_ref, a_out, b_out):
    half = a_out.shape[0]
    a_out[...] = a_ref[:half, :]
    b_out[...] = b_ref[half:, :]


def decay_row(slots, k, base, j):
    tail = slots[k, base : base + 16, :].astype(F32)
    return tail[j : j + 1] + tail[8 + j : 9 + j]


def fill_slots(order, rank, pays, slots):
    for s, pay in zip(order, pays):
        slots[rank ^ s] = pay[...]


def total_kernel(group, per, order, *refs):
    pays, out, slots = refs[:group], refs[group], refs[group + 1]
    fill_slots(order, my_rank(group), pays, slots)
    base = per * HD
    tails = []
    for j in range(per):
        state = slots[0, j * HD : (j + 1) * HD, :].astype(F32)
        whole = decay_row(slots, 0, base, j)
        for k in range(1, group):
            decay = decay_row(slots, k, base, j)
            state = decay * state + slots[k, j * HD : (j + 1) * HD, :].astype(F32)
            whole = whole * decay
        out[j * HD : (j + 1) * HD, :] = state.astype(BF16)
        tails.append(whole)
    pad = [jnp.zeros((8 - per, HD), F32)] if per < 8 else []
    total = jnp.concatenate(tails + pad, axis=0)
    high = total.astype(BF16).astype(F32)
    out[base:, :] = jnp.concatenate([high, total - high], axis=0).astype(BF16)


def prefix_kernel(group, per, order, carried, *refs):
    pays, refs = refs[:group], refs[group:]
    carry = None
    if carried:
        carry, refs = refs[0], refs[1:]
    outs, slots, prefixes = refs[:group], refs[group], refs[group + 1]
    rank = my_rank(group)
    later = lax.axis_index("ctx") >= group
    fill_slots(order, rank, pays, slots)
    base = per * HD
    for j in range(per):
        rows = slice(j * HD, (j + 1) * HD)
        state = jnp.zeros((HD, HD), F32)
        if carried:
            state = jnp.where(later, carry[rows, :].astype(F32), state)
        prefixes[0, rows, :] = state.astype(BF16)
        for k in range(group - 1):
            state = decay_row(slots, k, base, j) * state + slots[k, rows, :].astype(F32)
            prefixes[k + 1, rows, :] = state.astype(BF16)
    for s in range(group):
        outs[s][...] = prefixes[rank ^ s]


def intra_kernel(heads, tri_ref, bias_ref, ld_ref, q_ref, k_ref, v_ref, gate_ref, gain_ref, *outs):
    intra_ref, qa_ref, gain_out, decay_out = outs
    ld = ld_ref[...]
    tri = tri_ref[...]
    bias = bias_ref[...]
    cum = lax.dot_general(tri, ld, NT, precision=HIGH, preferred_element_type=F32)
    cum_t = lax.dot_general(ld, tri, NT, precision=HIGH, preferred_element_type=F32)
    decay_out[...] = jnp.exp(cum)
    for h in range(heads):
        cols = head_cols(h)
        qa = silu16(q_ref[:, cols])
        qa_ref[:, cols] = qa
        ka = silu16(k_ref[:, cols])
        va = silu16(v_ref[:, cols])
        scores = lax.dot_general(qa, ka, NT, preferred_element_type=F32)
        decay = jnp.exp((cum[:, h : h + 1] - cum_t[h : h + 1, :]) + bias)
        weights = (scores * decay).astype(BF16)
        intra_ref[:, cols] = jnp.dot(weights, va, preferred_element_type=F32)
        gate = 1.0 / (1.0 + jnp.exp(-gate_ref[:, cols].astype(F32)))
        gain_out[:, cols] = gate * gain_ref[:, cols]


def inter_kernel(group, heads, order, decay_ref, qa_ref, intra_ref, *rest):
    parts, (lin_ref, squares_ref, states) = rest[:group], rest[group:]
    tokens = qa_ref.shape[0]
    per = heads // group
    rank = my_rank(group)
    for s, part in zip(order, parts):
        states[dyn(rank ^ s, per * HD), :] = part[...]
    decay = decay_ref[...]
    acc = jnp.zeros((tokens, HD), F32)
    for h in range(heads):
        cols = head_cols(h)
        state = states[h * HD : (h + 1) * HD, :]
        inter = jnp.dot(qa_ref[:, cols], state, preferred_element_type=F32)
        lin = intra_ref[:, cols] + inter * decay[:, h : h + 1]
        lin_ref[:, cols] = lin
        acc += lin * lin
    ones = jnp.ones((8, HD), F32)
    squares_ref[...] = lax.dot_general(ones, acc, NT, precision=HIGH, preferred_element_type=F32)


def results_kernel(columns, parts, attended_ref, lin_ref, gain_ref, *rest):
    squares, (mixed_out, attended_out, mixed_ref, sems) = rest[:-4], rest[-4:]
    first = pltpu.make_async_copy(attended_ref, attended_out, sems.at[parts])
    first.start()
    total = squares[0][...]
    for part in squares[1:]:
        total = total + part[...]
    inv = jnp.transpose(lax.rsqrt(total / columns + EPS))[:, 0:1]
    width = lin_ref.shape[1] // parts
    copies = []
    for i in range(parts):
        cols = slice(i * width, (i + 1) * width)
        mixed_ref[:, cols] = (lin_ref[:, cols] * inv * gain_ref[:, cols]).astype(BF16)
        copies.append(
            pltpu.make_async_copy(mixed_ref.at[:, cols], mixed_out.at[:, cols], sems.at[i])
        )
        copies[-1].start()
    for copy in copies:
        copy.wait()
    first.wait()


def softmax_bias(group, sides, order_ref, bias):
    tokens, span = bias.shape[0], bias.shape[1] // len(sides)
    groups = span // tokens
    me = lax.axis_index("ctx")
    rank, mine = lax.rem(me, group), lax.div(me, group)
    qpos = order_ref[0] * tokens + lax.broadcasted_iota(jnp.int32, (tokens, tokens), 0)
    kpos = lax.broadcasted_iota(jnp.int32, (tokens, tokens), 1)
    for i, s in enumerate(sides):
        for d in range(groups):
            place = lax.rem(mine + groups - d, groups) * group + (rank ^ s)
            at = i * span + d * tokens
            bias[:, at : at + tokens] = jnp.where(place * tokens + kpos <= qpos, 0.0, -1e30)


def softmax_values(held, g, kv_heads, values):
    span = held[0].shape[0]
    values[:, HD:] = jnp.ones((span * len(held), HD), BF16)
    for i, ref in enumerate(held):
        values[i * span : (i + 1) * span, :HD] = ref[:, head_cols(kv_heads + g)]


def softmax_scores(query, held, g, bias):
    raw = [
        lax.dot_general(query, ref[:, head_cols(g)], NT, preferred_element_type=F32) for ref in held
    ]
    raw = jnp.concatenate(raw, axis=1)
    raw = raw.reshape(-1, *bias.shape) + bias[...][None]
    return raw.reshape(-1, bias.shape[1])


def stacked(ref, columns):
    return jnp.concatenate([ref[:, cols] for cols in columns], axis=0)


SCORE = math.log2(math.e) / math.sqrt(HD)


def softmax_first_kernel(group, sides, kv_heads, pack, order_ref, q_ref, *rest):
    arrays, rest = rest[: len(sides)], rest[len(sides) :]
    acc_ref, tops, (values, bias) = rest[0], rest[1:-2], rest[-2:]
    tokens = q_ref.shape[0]
    share = q_ref.shape[1] // HD // kv_heads
    softmax_bias(group, sides, order_ref, bias)
    for g in range(kv_heads):
        softmax_values(arrays, g, kv_heads, values)
        for j in range(0, share, pack):
            heads = range(g * share + j, g * share + j + pack)
            raw = softmax_scores(stacked(q_ref, map(head_cols, heads)), arrays, g, bias)
            top = jnp.max(raw, axis=-1, keepdims=True)
            probs = jnp.exp2((raw - top) * SCORE).astype(BF16)
            acc = jnp.dot(probs, values[...], preferred_element_type=F32)
            for i, h in enumerate(heads):
                rows = slice(i * tokens, (i + 1) * tokens)
                acc_ref[:, 2 * h * HD : 2 * (h + 1) * HD] = acc[rows]
                tops[g][:, j + i : j + i + 1] = top[rows]


def softmax_last_kernel(group, sides, kv_heads, pack, order_ref, q_ref, *rest):
    arrays, rest = rest[: len(sides)], rest[len(sides) :]
    acc_ref, tops, (out_ref, values, bias) = rest[0], rest[1:-3], rest[-3:]
    tokens = q_ref.shape[0]
    share = q_ref.shape[1] // HD // kv_heads
    softmax_bias(group, sides, order_ref, bias)
    for g in range(kv_heads):
        softmax_values(arrays, g, kv_heads, values)
        for j in range(0, share, pack):
            heads = range(g * share + j, g * share + j + pack)
            raw = softmax_scores(stacked(q_ref, map(head_cols, heads)), arrays, g, bias)
            old = stacked(tops[g], [slice(j + i, j + i + 1) for i in range(pack)])
            top = jnp.maximum(old, jnp.max(raw, axis=-1, keepdims=True))
            probs = jnp.exp2((raw - top) * SCORE).astype(BF16)
            acc = jnp.dot(probs, values[...], preferred_element_type=F32)
            held = stacked(acc_ref, [slice(2 * h * HD, 2 * (h + 1) * HD) for h in heads])
            acc += held * jnp.exp2((old - top) * SCORE)
            out = (acc[:, :HD] * inverse(acc[:, HD:])).astype(BF16)
            for i, h in enumerate(heads):
                out_ref[:, head_cols(h)] = out[i * tokens : (i + 1) * tokens]


def call(
    kernel, name, outs, args, scratch=(), flops=0, exps=0, limit=16, specs=None, after=(), **more
):
    size = sum(math.prod(x.shape) * x.dtype.itemsize for x in list(args) + list(outs))
    more.setdefault("out_specs", [VMEM for _ in outs])
    specs = list(specs or [VMEM for _ in args]) + [HBM for _ in after]
    count = len(args)

    def run(*refs):
        kernel(*refs[:count], *refs[count + len(after) :])

    return pl.pallas_call(
        run,
        name=name,
        out_shape=list(outs),
        in_specs=specs,
        scratch_shapes=list(scratch),
        cost_estimate=pl.CostEstimate(flops=flops, bytes_accessed=size, transcendentals=exps),
        compiler_params=pltpu.CompilerParams(vmem_limit_bytes=limit * MIB),
        **more,
    )(*args, *after)


def body(q_lin, k_lin, v_lin, log_decay, gate, norm_gain, queries, keys, values, order):
    tokens, width = q_lin.shape
    heads = log_decay.shape[0]
    kv_width = keys.shape[1]
    kv_heads = kv_width // HD
    n, nh = lax.axis_size("ctx"), lax.axis_size("head")
    group = 4
    groups = n // group
    per = heads // group
    rows = per * HD + 16
    cube = tokens * width * HD
    shape = jax.ShapeDtypeStruct

    def swap(x, s):
        return lax.ppermute(x, "ctx", [(c, c ^ s) for c in range(n)])

    def ahead(x, d):
        return lax.ppermute(x, "ctx", [(c, (c + d * group) % n) for c in range(n)])

    tri, bias = call(
        triangle_kernel, "triangle", [shape((tokens, tokens), F32)] * 2, (), flops=1 << 31
    )
    (kv,) = call(
        beside_kernel,
        "keys_beside_values",
        [shape((tokens, 2 * kv_width), BF16)],
        (keys, values),
        after=(tri,),
    )
    far = [ahead(kv, d) for d in range(1, groups)]

    to, back = (0, 2, 3, 1), (0, 3, 2, 1)
    others = [s for s in to if s != to[1]]
    payload = shape((rows, HD), BF16)
    (early,) = call(
        functools.partial(first_state_kernel, group, per, to[1]),
        "first_states",
        [payload],
        (tri, log_decay, k_lin, v_lin),
        flops=4 * cube // group,
        exps=2 * tokens * width // group,
    )
    late = call(
        functools.partial(other_states_kernel, group, per, to[1], others),
        "other_states",
        [payload] * len(others),
        (tri, log_decay, k_lin, v_lin),
        [pltpu.VMEM((group, rows, HD), BF16)],
        flops=4 * cube,
        exps=2 * tokens * width,
    )
    pays = {to[1]: early, **dict(zip(others, late))}
    pays = [swap(pays[s], s) if s else pays[s] for s in to]

    intra, qa, gain, decay = call(
        functools.partial(intra_kernel, heads),
        "intra_block",
        [
            shape((tokens, width), F32),
            shape((tokens, width), BF16),
            shape((tokens, width), F32),
            shape((tokens, heads), F32),
        ],
        (tri, bias, log_decay, q_lin, k_lin, v_lin, gate, norm_gain.reshape(1, width)),
        flops=4 * cube,
        exps=4 * tokens * width,
    )

    slots = pltpu.VMEM((group, rows, HD), BF16)
    carry = ()
    if groups > 1:
        (total,) = call(
            functools.partial(total_kernel, group, per, to),
            "group_state",
            [shape((rows, HD), BF16)],
            pays,
            [slots],
            flops=2 * per * HD * HD * group,
            after=(intra,),
        )
        before = ahead(total, 1)
        shift = 1
        while shift < groups - 1:
            mine = lax.div(lax.axis_index("ctx"), group)
            later = jnp.where(mine >= 1, before, 0).astype(F32)
            earlier = ahead(later.astype(BF16), shift)
            earlier = jnp.where(mine >= shift + 1, earlier, 0).astype(F32)
            step = later[per * HD :][:per] + later[per * HD + 8 :][:per]
            prior = earlier[per * HD :][:per] + earlier[per * HD + 8 :][:per]
            state = later[: per * HD] + jnp.repeat(step, HD, axis=0) * earlier[: per * HD]
            both = jnp.where(mine >= shift + 1, step * prior, step)
            high = both.astype(BF16).astype(F32)
            pad = jnp.zeros((8 - per, HD), F32)
            before = jnp.concatenate([state, high, pad, both - high, pad], axis=0).astype(BF16)
            shift *= 2
        carry = (before,)
    prefixes = call(
        functools.partial(prefix_kernel, group, per, to, bool(carry)),
        "prefix_states",
        [shape((per * HD, HD), BF16)] * group,
        (*pays, *carry),
        [slots, pltpu.VMEM((group, per * HD, HD), BF16)],
        flops=1 << 33,
    )
    prefixes = [swap(prefixes[s], s) if s else prefixes[s] for s in back]

    (own,) = call(
        stack_kernel,
        "stack_keys_values",
        [shape((groups * tokens, kv.shape[1]), BF16)],
        (kv, *far),
        after=(total,) if groups > 1 else (intra,),
        flops=1 << 32,
    )
    side, near = swap(own, 2), swap(own, 1)
    share = width // kv_heads
    pack = 2 if share // HD % 2 == 0 else 1
    span = own.shape[0]
    room = 24 + 48 * span * tokens * 4 // MIB
    smem = pl.BlockSpec(memory_space=pltpu.SMEM)

    def scratch(count):
        keys = count * span
        return [pltpu.VMEM((keys, 2 * HD), BF16), pltpu.VMEM((tokens, keys), F32)]

    acc, *tops = call(
        functools.partial(softmax_first_kernel, group, (0, 2, 1), kv_heads, pack),
        "softmax_first",
        [shape((tokens, 2 * width), F32)] + [shape((tokens, share // HD), F32)] * kv_heads,
        (order, queries, own, side, near),
        scratch(3),
        flops=12 * tokens * width * span,
        exps=3 * tokens * span * width // HD,
        limit=room,
        specs=[smem] + [VMEM] * 4,
    )
    half = shape((own.shape[0] // 2, own.shape[1]), BF16)
    upper, under = call(halves_kernel, "sent_on", [half] * 2, (side, near), after=tops[:1])
    across = jnp.concatenate([swap(upper, 1), swap(under, 2)])
    (attended,) = call(
        functools.partial(softmax_last_kernel, group, (3,), kv_heads, pack),
        "softmax_last",
        [shape((tokens, width), BF16)],
        (order, queries, across, acc, *tops),
        scratch(1),
        flops=4 * tokens * width * span,
        exps=tokens * span * width // HD,
        limit=room,
        specs=[smem] + [VMEM] * (3 + kv_heads),
    )

    lin, squares = call(
        functools.partial(inter_kernel, group, heads, back),
        "inter_block",
        [shape((tokens, width), F32), shape((8, tokens), F32)],
        (decay, qa, intra, *prefixes),
        [pltpu.VMEM((heads * HD, HD), BF16)],
        flops=2 * cube,
        after=tops[:1],
    )
    if nh & (nh - 1) == 0:
        turns = [[(i, i ^ d) for i in range(nh)] for d in range(nh - 1, 0, -1)]
    else:
        turns = [[(i, (i + d) % nh) for i in range(nh)] for d in range(1, nh)]
    parts = [squares] + [lax.ppermute(squares, "head", turn) for turn in turns]
    pieces = 4 if width % (4 * HD) == 0 else 1
    return call(
        functools.partial(results_kernel, float(width * nh), pieces),
        "results",
        [shape((tokens, width), BF16)] * 2,
        (attended, lin, gain, *parts),
        [pltpu.VMEM((tokens, width), BF16), pltpu.SemaphoreType.DMA((pieces + 1,))],
        flops=4 * tokens * width,
        out_specs=[HBM] * 2,
    )


def solution(mesh):
    return jax.shard_map(
        body,
        mesh=mesh,
        in_specs=(
            P("ctx", "head"),
            P("ctx", "head"),
            P("ctx", "head"),
            P("head", "ctx"),
            P("ctx", "head"),
            P("head"),
            P("ctx", "head"),
            P("ctx", "head"),
            P("ctx", "head"),
            P("ctx"),
        ),
        out_specs=(P("ctx", "head"), P("ctx", "head")),
        check_vma=False,
    )
```

```python
import functools
import math

import jax
import jax.numpy as jnp
from jax import lax
from jax.experimental import pallas as pl
from jax.experimental.pallas import tpu as pltpu
from jax.sharding import PartitionSpec as P

HD = 128
EPS = 1e-06
HIGH = lax.Precision.HIGHEST
F32 = jnp.float32
BF16 = jnp.bfloat16
NT = (((1,), (1,)), ((), ()))
TN = (((0,), (0,)), ((), ()))
MIB = 1 << 20
VMEM = pl.BlockSpec(memory_space=pltpu.VMEM)
HBM = pl.BlockSpec(memory_space=pltpu.HBM)


def inverse(x):
    guess = pl.reciprocal(x, approx=True)
    return guess * (2.0 - x * guess)


def silu16(x):
    x = x.astype(F32)
    return (x / (1.0 + jnp.exp(-x))).astype(BF16)


def lower_ones(size):
    rows = lax.broadcasted_iota(jnp.int32, (size, size), 0)
    cols = lax.broadcasted_iota(jnp.int32, (size, size), 1)
    return rows >= cols


def head_cols(h):
    return slice(h * HD, (h + 1) * HD)


def my_rank(group):
    return lax.rem(lax.axis_index("ctx"), group)


def dyn(index, size):
    return pl.ds(pl.multiple_of(index * size, size), size)


def triangle_kernel(ones_ref, bias_ref):
    lower = lower_ones(ones_ref.shape[0])
    ones_ref[...] = lower.astype(F32)
    bias_ref[...] = jnp.where(lower, 0.0, -1e30)


def decay_weights(tri_ref, ld_ref):
    ld = ld_ref[...]
    cum = lax.dot_general(tri_ref[...], ld, NT, precision=HIGH, preferred_element_type=F32)
    return jnp.exp(cum[-1:, :] - cum), jnp.exp(jnp.sum(ld, axis=1, keepdims=True))


def owner_states(k, per, weight, total, k_ref, v_ref, out):
    for j in range(per):
        h = k * per + j
        ka = silu16(k_ref[:, head_cols(h)])
        va = silu16(v_ref[:, head_cols(h)])
        kdec = ka.astype(F32) * weight[:, h : h + 1]
        khigh = kdec.astype(BF16)
        klow = (kdec - khigh.astype(F32)).astype(BF16)
        state = lax.dot_general(khigh, va, TN, preferred_element_type=F32)
        state += lax.dot_general(klow, va, TN, preferred_element_type=F32)
        out[j * HD : (j + 1) * HD, :] = state.astype(BF16)
    mine = jnp.broadcast_to(total[k * per : (k + 1) * per], (per, HD))
    high = mine.astype(BF16).astype(F32)
    pad = [jnp.zeros((8 - per, HD), F32)] if per < 8 else []
    tail = jnp.concatenate([high, *pad, mine - high, *pad], axis=0)
    out[per * HD :, :] = tail.astype(BF16)


def first_state_kernel(group, per, first, tri_ref, ld_ref, k_ref, v_ref, out_ref):
    weight, total = decay_weights(tri_ref, ld_ref)
    dest = my_rank(group) ^ first
    for k in range(group):
        pl.when(dest == k)(
            functools.partial(owner_states, k, per, weight, total, k_ref, v_ref, out_ref)
        )


def other_states_kernel(group, per, first, others, tri_ref, ld_ref, k_ref, v_ref, *rest):
    outs, payloads = rest[:-1], rest[-1]
    weight, total = decay_weights(tri_ref, ld_ref)
    rank = my_rank(group)
    for k in range(group):
        pl.when((rank ^ first) != k)(
            functools.partial(owner_states, k, per, weight, total, k_ref, v_ref, payloads.at[k])
        )
    for s, out in zip(others, outs):
        out[...] = payloads[rank ^ s]


def beside_kernel(keys, values, out):
    width = keys.shape[1]
    out[:, :width] = keys[...]
    out[:, width:] = values[...]


def stack_kernel(*refs):
    tokens = refs[0].shape[0]
    for i, part in enumerate(refs[:-1]):
        refs[-1][i * tokens : (i + 1) * tokens, :] = part[...]


def halves_kernel(a_ref, b_ref, a_out, b_out):
    half = a_out.shape[0]
    a_out[...] = a_ref[:half, :]
    b_out[...] = b_ref[half:, :]


def decay_row(slots, k, base, j):
    tail = slots[k, base : base + 16, :].astype(F32)
    return tail[j : j + 1] + tail[8 + j : 9 + j]


def fill_slots(order, rank, pays, slots):
    for s, pay in zip(order, pays):
        slots[rank ^ s] = pay[...]


def total_kernel(group, per, order, *refs):
    pays, out, slots = refs[:group], refs[group], refs[group + 1]
    fill_slots(order, my_rank(group), pays, slots)
    base = per * HD
    tails = []
    for j in range(per):
        state = slots[0, j * HD : (j + 1) * HD, :].astype(F32)
        whole = decay_row(slots, 0, base, j)
        for k in range(1, group):
            decay = decay_row(slots, k, base, j)
            state = decay * state + slots[k, j * HD : (j + 1) * HD, :].astype(F32)
            whole = whole * decay
        out[j * HD : (j + 1) * HD, :] = state.astype(BF16)
        tails.append(whole)
    pad = [jnp.zeros((8 - per, HD), F32)] if per < 8 else []
    total = jnp.concatenate(tails + pad, axis=0)
    high = total.astype(BF16).astype(F32)
    out[base:, :] = jnp.concatenate([high, total - high], axis=0).astype(BF16)


def prefix_kernel(group, per, order, carried, *refs):
    pays, refs = refs[:group], refs[group:]
    carry = None
    if carried:
        carry, refs = refs[0], refs[1:]
    outs, slots, prefixes = refs[:group], refs[group], refs[group + 1]
    rank = my_rank(group)
    later = lax.axis_index("ctx") >= group
    fill_slots(order, rank, pays, slots)
    base = per * HD
    for j in range(per):
        rows = slice(j * HD, (j + 1) * HD)
        state = jnp.zeros((HD, HD), F32)
        if carried:
            state = jnp.where(later, carry[rows, :].astype(F32), state)
        prefixes[0, rows, :] = state.astype(BF16)
        for k in range(group - 1):
            state = decay_row(slots, k, base, j) * state + slots[k, rows, :].astype(F32)
            prefixes[k + 1, rows, :] = state.astype(BF16)
    for s in range(group):
        outs[s][...] = prefixes[rank ^ s]


def intra_kernel(heads, tri_ref, bias_ref, ld_ref, q_ref, k_ref, v_ref, *outs):
    intra_ref, qa_ref, decay_out = outs
    ld = ld_ref[...]
    tri = tri_ref[...]
    bias = bias_ref[...]
    cum = lax.dot_general(tri, ld, NT, precision=HIGH, preferred_element_type=F32)
    cum_t = lax.dot_general(ld, tri, NT, precision=HIGH, preferred_element_type=F32)
    decay_out[...] = jnp.exp(cum)
    for h in range(heads):
        cols = head_cols(h)
        qa = silu16(q_ref[:, cols])
        qa_ref[:, cols] = qa
        ka = silu16(k_ref[:, cols])
        va = silu16(v_ref[:, cols])
        scores = lax.dot_general(qa, ka, NT, preferred_element_type=F32)
        decay = jnp.exp((cum[:, h : h + 1] - cum_t[h : h + 1, :]) + bias)
        weights = (scores * decay).astype(BF16)
        intra_ref[:, cols] = jnp.dot(weights, va, preferred_element_type=F32)


def gate_kernel(heads, gate_ref, gain_ref, out_ref):
    for h in range(heads):
        cols = head_cols(h)
        gate = 1.0 / (1.0 + jnp.exp(-gate_ref[:, cols].astype(F32)))
        out_ref[:, cols] = gate * gain_ref[:, cols]


def inter_kernel(group, heads, order, decay_ref, qa_ref, intra_ref, *rest):
    parts, (lin_ref, squares_ref, states) = rest[:group], rest[group:]
    tokens = qa_ref.shape[0]
    per = heads // group
    rank = my_rank(group)
    for s, part in zip(order, parts):
        states[dyn(rank ^ s, per * HD), :] = part[...]
    decay = decay_ref[...]
    acc = jnp.zeros((tokens, HD), F32)
    for h in range(heads):
        cols = head_cols(h)
        state = states[h * HD : (h + 1) * HD, :]
        inter = jnp.dot(qa_ref[:, cols], state, preferred_element_type=F32)
        lin = intra_ref[:, cols] + inter * decay[:, h : h + 1]
        lin_ref[:, cols] = lin
        acc += lin * lin
    ones = jnp.ones((8, HD), F32)
    squares_ref[...] = lax.dot_general(ones, acc, NT, precision=HIGH, preferred_element_type=F32)


def results_kernel(columns, parts, attended_ref, lin_ref, gain_ref, *rest):
    squares, (mixed_out, attended_out, mixed_ref, sems) = rest[:-4], rest[-4:]
    first = pltpu.make_async_copy(attended_ref, attended_out, sems.at[parts])
    first.start()
    total = squares[0][...]
    for part in squares[1:]:
        total = total + part[...]
    inv = jnp.transpose(lax.rsqrt(total / columns + EPS))[:, 0:1]
    width = lin_ref.shape[1] // parts
    copies = []
    for i in range(parts):
        cols = slice(i * width, (i + 1) * width)
        mixed_ref[:, cols] = (lin_ref[:, cols] * inv * gain_ref[:, cols]).astype(BF16)
        copies.append(
            pltpu.make_async_copy(mixed_ref.at[:, cols], mixed_out.at[:, cols], sems.at[i])
        )
        copies[-1].start()
    for copy in copies:
        copy.wait()
    first.wait()


def softmax_bias(group, sides, order_ref, bias):
    tokens, span = bias.shape[0], bias.shape[1] // len(sides)
    groups = span // tokens
    me = lax.axis_index("ctx")
    rank, mine = lax.rem(me, group), lax.div(me, group)
    qpos = order_ref[0] * tokens + lax.broadcasted_iota(jnp.int32, (tokens, tokens), 0)
    kpos = lax.broadcasted_iota(jnp.int32, (tokens, tokens), 1)
    for i, s in enumerate(sides):
        for d in range(groups):
            place = lax.rem(mine + groups - d, groups) * group + (rank ^ s)
            at = i * span + d * tokens
            bias[:, at : at + tokens] = jnp.where(place * tokens + kpos <= qpos, 0.0, -1e30)


def softmax_values(held, g, kv_heads, values):
    span = held[0].shape[0]
    values[:, HD:] = jnp.ones((span * len(held), HD), BF16)
    for i, ref in enumerate(held):
        values[i * span : (i + 1) * span, :HD] = ref[:, head_cols(kv_heads + g)]


def softmax_scores(query, held, g, bias):
    raw = [
        lax.dot_general(query, ref[:, head_cols(g)], NT, preferred_element_type=F32) for ref in held
    ]
    raw = jnp.concatenate(raw, axis=1)
    raw = raw.reshape(-1, *bias.shape) + bias[...][None]
    return raw.reshape(-1, bias.shape[1])


def stacked(ref, columns):
    return jnp.concatenate([ref[:, cols] for cols in columns], axis=0)


SCORE = math.log2(math.e) / math.sqrt(HD)


def softmax_first_kernel(group, sides, kv_heads, pack, order_ref, q_ref, *rest):
    arrays, rest = rest[: len(sides)], rest[len(sides) :]
    acc_ref, tops, (values, bias) = rest[0], rest[1:-2], rest[-2:]
    tokens = q_ref.shape[0]
    share = q_ref.shape[1] // HD // kv_heads
    softmax_bias(group, sides, order_ref, bias)
    for g in range(kv_heads):
        softmax_values(arrays, g, kv_heads, values)
        for j in range(0, share, pack):
            heads = range(g * share + j, g * share + j + pack)
            raw = softmax_scores(stacked(q_ref, map(head_cols, heads)), arrays, g, bias)
            top = jnp.max(raw, axis=-1, keepdims=True)
            probs = jnp.exp2((raw - top) * SCORE).astype(BF16)
            acc = jnp.dot(probs, values[...], preferred_element_type=F32)
            for i, h in enumerate(heads):
                rows = slice(i * tokens, (i + 1) * tokens)
                acc_ref[:, 2 * h * HD : 2 * (h + 1) * HD] = acc[rows]
                tops[g][:, j + i : j + i + 1] = top[rows]


def softmax_last_kernel(group, sides, kv_heads, pack, order_ref, q_ref, *rest):
    arrays, rest = rest[: len(sides)], rest[len(sides) :]
    acc_ref, tops, (out_ref, values, bias) = rest[0], rest[1:-3], rest[-3:]
    tokens = q_ref.shape[0]
    share = q_ref.shape[1] // HD // kv_heads
    softmax_bias(group, sides, order_ref, bias)
    for g in range(kv_heads):
        softmax_values(arrays, g, kv_heads, values)
        for j in range(0, share, pack):
            heads = range(g * share + j, g * share + j + pack)
            raw = softmax_scores(stacked(q_ref, map(head_cols, heads)), arrays, g, bias)
            old = stacked(tops[g], [slice(j + i, j + i + 1) for i in range(pack)])
            top = jnp.maximum(old, jnp.max(raw, axis=-1, keepdims=True))
            probs = jnp.exp2((raw - top) * SCORE).astype(BF16)
            acc = jnp.dot(probs, values[...], preferred_element_type=F32)
            held = stacked(acc_ref, [slice(2 * h * HD, 2 * (h + 1) * HD) for h in heads])
            acc += held * jnp.exp2((old - top) * SCORE)
            out = (acc[:, :HD] * inverse(acc[:, HD:])).astype(BF16)
            for i, h in enumerate(heads):
                out_ref[:, head_cols(h)] = out[i * tokens : (i + 1) * tokens]


def call(
    kernel,
    name,
    outs,
    args,
    scratch=(),
    flops=0,
    exps=0,
    size=None,
    limit=16,
    specs=None,
    after=(),
    **more,
):
    if size is None:
        size = sum(math.prod(x.shape) * x.dtype.itemsize for x in list(args) + list(outs))
    more.setdefault("out_specs", [VMEM for _ in outs])
    specs = list(specs or [VMEM for _ in args]) + [HBM for _ in after]
    count = len(args)

    def run(*refs):
        kernel(*refs[:count], *refs[count + len(after) :])

    return pl.pallas_call(
        run,
        name=name,
        out_shape=list(outs),
        in_specs=specs,
        scratch_shapes=list(scratch),
        cost_estimate=pl.CostEstimate(flops=flops, bytes_accessed=size, transcendentals=exps),
        compiler_params=pltpu.CompilerParams(vmem_limit_bytes=limit * MIB),
        **more,
    )(*args, *after)


def body(q_lin, k_lin, v_lin, log_decay, gate, norm_gain, queries, keys, values, order):
    tokens, width = q_lin.shape
    heads = log_decay.shape[0]
    kv_width = keys.shape[1]
    kv_heads = kv_width // HD
    n, nh = lax.axis_size("ctx"), lax.axis_size("head")
    group = 4
    groups = n // group
    per = heads // group
    rows = per * HD + 16
    cube = tokens * width * HD
    shape = jax.ShapeDtypeStruct

    def swap(x, s):
        return lax.ppermute(x, "ctx", [(c, c ^ s) for c in range(n)])

    def ahead(x, d):
        return lax.ppermute(x, "ctx", [(c, (c + d * group) % n) for c in range(n)])

    tri, bias = call(
        triangle_kernel, "triangle", [shape((tokens, tokens), F32)] * 2, (), flops=1 << 31
    )
    to, back = (0, 2, 3, 1), (0, 3, 2, 1)
    others = [s for s in to if s != to[1]]
    payload = shape((rows, HD), BF16)
    (early,) = call(
        functools.partial(first_state_kernel, group, per, to[1]),
        "first_states",
        [payload],
        (tri, log_decay, k_lin, v_lin),
        flops=4 * cube // group,
        exps=2 * tokens * width // group,
    )
    (kv,) = call(
        beside_kernel,
        "keys_beside_values",
        [shape((tokens, 2 * kv_width), BF16)],
        (keys, values),
        after=(early,),
    )
    far = [ahead(kv, d) for d in range(1, groups)]

    late = call(
        functools.partial(other_states_kernel, group, per, to[1], others),
        "other_states",
        [payload] * len(others),
        (tri, log_decay, k_lin, v_lin),
        [pltpu.VMEM((group, rows, HD), BF16)],
        flops=1 << 32,
        exps=2 * tokens * width,
    )
    pays = {to[1]: early, **dict(zip(others, late))}
    pays = [swap(pays[s], s) if s else pays[s] for s in to]

    (gain,) = call(
        functools.partial(gate_kernel, heads),
        "gate_gain",
        [shape((tokens, width), F32)],
        (gate, norm_gain.reshape(1, width)),
        flops=1 << 32,
        exps=tokens * width,
        after=far,
    )

    slots = pltpu.VMEM((group, rows, HD), BF16)
    carry = ()
    if groups > 1:
        (total,) = call(
            functools.partial(total_kernel, group, per, to),
            "group_state",
            [shape((rows, HD), BF16)],
            pays,
            [slots],
            flops=2 * per * HD * HD * group,
            after=(gain,),
        )
        before = ahead(total, 1)
        shift = 1
        while shift < groups - 1:
            mine = lax.div(lax.axis_index("ctx"), group)
            later = jnp.where(mine >= 1, before, 0).astype(F32)
            earlier = ahead(later.astype(BF16), shift)
            earlier = jnp.where(mine >= shift + 1, earlier, 0).astype(F32)
            step = later[per * HD :][:per] + later[per * HD + 8 :][:per]
            prior = earlier[per * HD :][:per] + earlier[per * HD + 8 :][:per]
            state = later[: per * HD] + jnp.repeat(step, HD, axis=0) * earlier[: per * HD]
            both = jnp.where(mine >= shift + 1, step * prior, step)
            high = both.astype(BF16).astype(F32)
            pad = jnp.zeros((8 - per, HD), F32)
            before = jnp.concatenate([state, high, pad, both - high, pad], axis=0).astype(BF16)
            shift *= 2
        carry = (before,)
    intra, qa, decay = call(
        functools.partial(intra_kernel, heads),
        "intra_block",
        [shape((tokens, width), F32), shape((tokens, width), BF16), shape((tokens, heads), F32)],
        (tri, bias, log_decay, q_lin, k_lin, v_lin),
        flops=4 * cube,
        exps=4 * tokens * width,
        after=(total,) if groups > 1 else (),
    )
    prefixes = call(
        functools.partial(prefix_kernel, group, per, to, bool(carry)),
        "prefix_states",
        [shape((per * HD, HD), BF16)] * group,
        (*pays, *carry),
        [slots, pltpu.VMEM((group, per * HD, HD), BF16)],
        flops=1 << 33,
        after=(intra,),
    )
    prefixes = [swap(prefixes[s], s) if s else prefixes[s] for s in back]

    (own,) = call(
        stack_kernel,
        "stack_keys_values",
        [shape((groups * tokens, kv.shape[1]), BF16)],
        (kv, *far),
        after=(total,) if groups > 1 else (),
        flops=1 << 32,
    )
    side, near = swap(own, 2), swap(own, 1)
    share = width // kv_heads
    pack = 2 if share // HD % 2 == 0 else 1
    span = own.shape[0]
    room = 24 + 48 * span * tokens * 4 // MIB
    smem = pl.BlockSpec(memory_space=pltpu.SMEM)

    def scratch(count):
        keys = count * span
        return [pltpu.VMEM((keys, 2 * HD), BF16), pltpu.VMEM((tokens, keys), F32)]

    acc, *tops = call(
        functools.partial(softmax_first_kernel, group, (0, 2, 1), kv_heads, pack),
        "softmax_first",
        [shape((tokens, 2 * width), F32)] + [shape((tokens, share // HD), F32)] * kv_heads,
        (order, queries, own, side, near),
        scratch(3),
        flops=12 * tokens * width * span,
        exps=3 * tokens * span * width // HD,
        limit=room,
        specs=[smem] + [VMEM] * 4,
    )
    half = shape((own.shape[0] // 2, own.shape[1]), BF16)
    upper, under = call(halves_kernel, "sent_on", [half] * 2, (side, near))
    across = jnp.concatenate([swap(upper, 1), swap(under, 2)])
    (attended,) = call(
        functools.partial(softmax_last_kernel, group, (3,), kv_heads, pack),
        "softmax_last",
        [shape((tokens, width), BF16)],
        (order, queries, across, acc, *tops),
        scratch(1),
        flops=4 * tokens * width * span,
        exps=tokens * span * width // HD,
        limit=room,
        specs=[smem] + [VMEM] * (3 + kv_heads),
    )

    lin, squares = call(
        functools.partial(inter_kernel, group, heads, back),
        "inter_block",
        [shape((tokens, width), F32), shape((8, tokens), F32)],
        (decay, qa, intra, *prefixes),
        [pltpu.VMEM((heads * HD, HD), BF16)],
        flops=2 * cube,
        after=tops[:1],
    )
    if nh & (nh - 1) == 0:
        turns = [[(i, i ^ d) for i in range(nh)] for d in range(nh - 1, 0, -1)]
    else:
        turns = [[(i, (i + d) % nh) for i in range(nh)] for d in range(1, nh)]
    parts = [squares] + [lax.ppermute(squares, "head", turn) for turn in turns]
    pieces = 4 if width % (4 * HD) == 0 else 1
    return call(
        functools.partial(results_kernel, float(width * nh), pieces),
        "results",
        [shape((tokens, width), BF16)] * 2,
        (attended, lin, gain, *parts),
        [pltpu.VMEM((tokens, width), BF16), pltpu.SemaphoreType.DMA((pieces + 1,))],
        flops=4 * tokens * width,
        out_specs=[HBM] * 2,
    )


def solution(mesh):
    return jax.shard_map(
        body,
        mesh=mesh,
        in_specs=(
            P("ctx", "head"),
            P("ctx", "head"),
            P("ctx", "head"),
            P("head", "ctx"),
            P("ctx", "head"),
            P("head"),
            P("ctx", "head"),
            P("ctx", "head"),
            P("ctx", "head"),
            P("ctx"),
        ),
        out_specs=(P("ctx", "head"), P("ctx", "head")),
        check_vma=False,
    )
```

```python
import functools
import math

import jax
import jax.numpy as jnp
from jax import lax
from jax.experimental import pallas as pl
from jax.experimental.pallas import tpu as pltpu
from jax.sharding import PartitionSpec as P

HD = 128
EPS = 1e-06
HIGH = lax.Precision.HIGHEST
F32 = jnp.float32
BF16 = jnp.bfloat16
NT = (((1,), (1,)), ((), ()))
TN = (((0,), (0,)), ((), ()))
MIB = 1 << 20
VMEM = pl.BlockSpec(memory_space=pltpu.VMEM)
HBM = pl.BlockSpec(memory_space=pltpu.HBM)


def inverse(x):
    guess = pl.reciprocal(x, approx=True)
    return guess * (2.0 - x * guess)


def silu16(x):
    x = x.astype(F32)
    return (x / (1.0 + jnp.exp(-x))).astype(BF16)


def lower_ones(size):
    rows = lax.broadcasted_iota(jnp.int32, (size, size), 0)
    cols = lax.broadcasted_iota(jnp.int32, (size, size), 1)
    return rows >= cols


def head_cols(h):
    return slice(h * HD, (h + 1) * HD)


def my_rank(group):
    return lax.rem(lax.axis_index("ctx"), group)


def dyn(index, size):
    return pl.ds(pl.multiple_of(index * size, size), size)


def triangle_kernel(ones_ref, bias_ref):
    lower = lower_ones(ones_ref.shape[0])
    ones_ref[...] = lower.astype(F32)
    bias_ref[...] = jnp.where(lower, 0.0, -1e30)


def decay_weights(tri_ref, ld_ref):
    ld = ld_ref[...]
    cum = lax.dot_general(tri_ref[...], ld, NT, precision=HIGH, preferred_element_type=F32)
    return jnp.exp(cum[-1:, :] - cum), jnp.exp(jnp.sum(ld, axis=1, keepdims=True))


def owner_states(k, per, weight, total, k_ref, v_ref, out):
    for j in range(per):
        h = k * per + j
        ka = silu16(k_ref[:, head_cols(h)])
        va = silu16(v_ref[:, head_cols(h)])
        kdec = ka.astype(F32) * weight[:, h : h + 1]
        khigh = kdec.astype(BF16)
        klow = (kdec - khigh.astype(F32)).astype(BF16)
        state = lax.dot_general(khigh, va, TN, preferred_element_type=F32)
        state += lax.dot_general(klow, va, TN, preferred_element_type=F32)
        out[j * HD : (j + 1) * HD, :] = state.astype(BF16)
    mine = jnp.broadcast_to(total[k * per : (k + 1) * per], (per, HD))
    high = mine.astype(BF16).astype(F32)
    pad = [jnp.zeros((8 - per, HD), F32)] if per < 8 else []
    tail = jnp.concatenate([high, *pad, mine - high, *pad], axis=0)
    out[per * HD :, :] = tail.astype(BF16)


def state_kernel(group, per, s, tri_ref, ld_ref, k_ref, v_ref, out_ref):
    weight, total = decay_weights(tri_ref, ld_ref)
    dest = my_rank(group) ^ s
    for k in range(group):
        pl.when(dest == k)(
            functools.partial(owner_states, k, per, weight, total, k_ref, v_ref, out_ref)
        )


def beside_kernel(keys, values, out):
    width = keys.shape[1]
    out[:, :width] = keys[...]
    out[:, width:] = values[...]


def stack_kernel(*refs):
    tokens = refs[0].shape[0]
    for i, part in enumerate(refs[:-1]):
        refs[-1][i * tokens : (i + 1) * tokens, :] = part[...]


def halves_kernel(a_ref, b_ref, a_out, b_out):
    half = a_out.shape[0]
    a_out[...] = a_ref[:half, :]
    b_out[...] = b_ref[half:, :]


def decay_row(slots, k, base, j):
    tail = slots[k, base : base + 16, :].astype(F32)
    return tail[j : j + 1] + tail[8 + j : 9 + j]


def fill_slots(order, rank, pays, slots):
    for s, pay in zip(order, pays):
        slots[rank ^ s] = pay[...]


def total_kernel(group, per, order, *refs):
    pays, out, slots = refs[:group], refs[group], refs[group + 1]
    fill_slots(order, my_rank(group), pays, slots)
    base = per * HD
    tails = []
    for j in range(per):
        state = slots[0, j * HD : (j + 1) * HD, :].astype(F32)
        whole = decay_row(slots, 0, base, j)
        for k in range(1, group):
            decay = decay_row(slots, k, base, j)
            state = decay * state + slots[k, j * HD : (j + 1) * HD, :].astype(F32)
            whole = whole * decay
        out[j * HD : (j + 1) * HD, :] = state.astype(BF16)
        tails.append(whole)
    pad = [jnp.zeros((8 - per, HD), F32)] if per < 8 else []
    total = jnp.concatenate(tails + pad, axis=0)
    high = total.astype(BF16).astype(F32)
    out[base:, :] = jnp.concatenate([high, total - high], axis=0).astype(BF16)


def prefix_kernel(group, per, order, carried, *refs):
    pays, refs = refs[:group], refs[group:]
    carry = None
    if carried:
        carry, refs = refs[0], refs[1:]
    outs, slots, prefixes = refs[:group], refs[group], refs[group + 1]
    rank = my_rank(group)
    later = lax.axis_index("ctx") >= group
    fill_slots(order, rank, pays, slots)
    base = per * HD
    for j in range(per):
        rows = slice(j * HD, (j + 1) * HD)
        state = jnp.zeros((HD, HD), F32)
        if carried:
            state = jnp.where(later, carry[rows, :].astype(F32), state)
        prefixes[0, rows, :] = state.astype(BF16)
        for k in range(group - 1):
            state = decay_row(slots, k, base, j) * state + slots[k, rows, :].astype(F32)
            prefixes[k + 1, rows, :] = state.astype(BF16)
    for s in range(group):
        outs[s][...] = prefixes[rank ^ s]


def intra_kernel(heads, tri_ref, bias_ref, ld_ref, q_ref, k_ref, v_ref, gate_ref, gain_ref, *outs):
    intra_ref, qa_ref, gain_out, decay_out = outs
    ld = ld_ref[...]
    tri = tri_ref[...]
    bias = bias_ref[...]
    cum = lax.dot_general(tri, ld, NT, precision=HIGH, preferred_element_type=F32)
    cum_t = lax.dot_general(ld, tri, NT, precision=HIGH, preferred_element_type=F32)
    decay_out[...] = jnp.exp(cum)
    for h in range(heads):
        cols = head_cols(h)
        qa = silu16(q_ref[:, cols])
        qa_ref[:, cols] = qa
        ka = silu16(k_ref[:, cols])
        va = silu16(v_ref[:, cols])
        scores = lax.dot_general(qa, ka, NT, preferred_element_type=F32)
        decay = jnp.exp((cum[:, h : h + 1] - cum_t[h : h + 1, :]) + bias)
        weights = (scores * decay).astype(BF16)
        intra_ref[:, cols] = jnp.dot(weights, va, preferred_element_type=F32)
        gate = 1.0 / (1.0 + jnp.exp(-gate_ref[:, cols].astype(F32)))
        gain_out[:, cols] = gate * gain_ref[:, cols]


def inter_kernel(group, heads, order, decay_ref, qa_ref, intra_ref, *rest):
    parts, (lin_ref, squares_ref, states) = rest[:group], rest[group:]
    tokens = qa_ref.shape[0]
    per = heads // group
    rank = my_rank(group)
    for s, part in zip(order, parts):
        states[dyn(rank ^ s, per * HD), :] = part[...]
    decay = decay_ref[...]
    acc = jnp.zeros((tokens, HD), F32)
    for h in range(heads):
        cols = head_cols(h)
        state = states[h * HD : (h + 1) * HD, :]
        inter = jnp.dot(qa_ref[:, cols], state, preferred_element_type=F32)
        lin = intra_ref[:, cols] + inter * decay[:, h : h + 1]
        lin_ref[:, cols] = lin
        acc += lin * lin
    ones = jnp.ones((8, HD), F32)
    squares_ref[...] = lax.dot_general(ones, acc, NT, precision=HIGH, preferred_element_type=F32)


def results_kernel(columns, parts, attended_ref, lin_ref, gain_ref, *rest):
    squares, (mixed_out, attended_out, mixed_ref, sems) = rest[:-4], rest[-4:]
    first = pltpu.make_async_copy(attended_ref, attended_out, sems.at[parts])
    first.start()
    total = squares[0][...]
    for part in squares[1:]:
        total = total + part[...]
    inv = jnp.transpose(lax.rsqrt(total / columns + EPS))[:, 0:1]
    width = lin_ref.shape[1] // parts
    copies = []
    for i in range(parts):
        cols = slice(i * width, (i + 1) * width)
        mixed_ref[:, cols] = (lin_ref[:, cols] * inv * gain_ref[:, cols]).astype(BF16)
        copies.append(
            pltpu.make_async_copy(mixed_ref.at[:, cols], mixed_out.at[:, cols], sems.at[i])
        )
        copies[-1].start()
    for copy in copies:
        copy.wait()
    first.wait()


def softmax_bias(group, sides, order_ref, bias):
    tokens, span = bias.shape[0], bias.shape[1] // len(sides)
    groups = span // tokens
    me = lax.axis_index("ctx")
    rank, mine = lax.rem(me, group), lax.div(me, group)
    qpos = order_ref[0] * tokens + lax.broadcasted_iota(jnp.int32, (tokens, tokens), 0)
    kpos = lax.broadcasted_iota(jnp.int32, (tokens, tokens), 1)
    for i, s in enumerate(sides):
        for d in range(groups):
            place = lax.rem(mine + groups - d, groups) * group + (rank ^ s)
            at = i * span + d * tokens
            bias[:, at : at + tokens] = jnp.where(place * tokens + kpos <= qpos, 0.0, -1e30)


def softmax_values(held, g, kv_heads, values):
    span = held[0].shape[0]
    values[:, HD:] = jnp.ones((span * len(held), HD), BF16)
    for i, ref in enumerate(held):
        values[i * span : (i + 1) * span, :HD] = ref[:, head_cols(kv_heads + g)]


def softmax_scores(query, held, g, bias):
    raw = [
        lax.dot_general(query, ref[:, head_cols(g)], NT, preferred_element_type=F32) for ref in held
    ]
    raw = jnp.concatenate(raw, axis=1)
    raw = raw.reshape(-1, *bias.shape) + bias[...][None]
    return raw.reshape(-1, bias.shape[1])


def stacked(ref, columns):
    return jnp.concatenate([ref[:, cols] for cols in columns], axis=0)


SCORE = math.log2(math.e) / math.sqrt(HD)


def softmax_first_kernel(group, sides, kv_heads, pack, order_ref, q_ref, *rest):
    arrays, rest = rest[: len(sides)], rest[len(sides) :]
    acc_ref, tops, (values, bias) = rest[0], rest[1:-2], rest[-2:]
    tokens = q_ref.shape[0]
    share = q_ref.shape[1] // HD // kv_heads
    softmax_bias(group, sides, order_ref, bias)
    for g in range(kv_heads):
        softmax_values(arrays, g, kv_heads, values)
        for j in range(0, share, pack):
            heads = range(g * share + j, g * share + j + pack)
            raw = softmax_scores(stacked(q_ref, map(head_cols, heads)), arrays, g, bias)
            top = jnp.max(raw, axis=-1, keepdims=True)
            probs = jnp.exp2((raw - top) * SCORE).astype(BF16)
            acc = jnp.dot(probs, values[...], preferred_element_type=F32)
            for i, h in enumerate(heads):
                rows = slice(i * tokens, (i + 1) * tokens)
                acc_ref[:, 2 * h * HD : 2 * (h + 1) * HD] = acc[rows]
                tops[g][:, j + i : j + i + 1] = top[rows]


def softmax_last_kernel(group, sides, kv_heads, pack, order_ref, q_ref, *rest):
    arrays, rest = rest[: len(sides)], rest[len(sides) :]
    acc_ref, tops, (out_ref, values, bias) = rest[0], rest[1:-3], rest[-3:]
    tokens = q_ref.shape[0]
    share = q_ref.shape[1] // HD // kv_heads
    softmax_bias(group, sides, order_ref, bias)
    for g in range(kv_heads):
        softmax_values(arrays, g, kv_heads, values)
        for j in range(0, share, pack):
            heads = range(g * share + j, g * share + j + pack)
            raw = softmax_scores(stacked(q_ref, map(head_cols, heads)), arrays, g, bias)
            old = stacked(tops[g], [slice(j + i, j + i + 1) for i in range(pack)])
            top = jnp.maximum(old, jnp.max(raw, axis=-1, keepdims=True))
            probs = jnp.exp2((raw - top) * SCORE).astype(BF16)
            acc = jnp.dot(probs, values[...], preferred_element_type=F32)
            held = stacked(acc_ref, [slice(2 * h * HD, 2 * (h + 1) * HD) for h in heads])
            acc += held * jnp.exp2((old - top) * SCORE)
            out = (acc[:, :HD] * inverse(acc[:, HD:])).astype(BF16)
            for i, h in enumerate(heads):
                out_ref[:, head_cols(h)] = out[i * tokens : (i + 1) * tokens]


def call(
    kernel, name, outs, args, scratch=(), flops=0, exps=0, limit=16, specs=None, after=(), **more
):
    size = sum(math.prod(x.shape) * x.dtype.itemsize for x in list(args) + list(outs))
    more.setdefault("out_specs", [VMEM for _ in outs])
    specs = list(specs or [VMEM for _ in args]) + [HBM for _ in after]
    count = len(args)

    def run(*refs):
        kernel(*refs[:count], *refs[count + len(after) :])

    return pl.pallas_call(
        run,
        name=name,
        out_shape=list(outs),
        in_specs=specs,
        scratch_shapes=list(scratch),
        cost_estimate=pl.CostEstimate(flops=flops, bytes_accessed=size, transcendentals=exps),
        compiler_params=pltpu.CompilerParams(vmem_limit_bytes=limit * MIB),
        **more,
    )(*args, *after)


def body(q_lin, k_lin, v_lin, log_decay, gate, norm_gain, queries, keys, values, order):
    tokens, width = q_lin.shape
    heads = log_decay.shape[0]
    kv_width = keys.shape[1]
    kv_heads = kv_width // HD
    n, nh = lax.axis_size("ctx"), lax.axis_size("head")
    group = 4
    groups = n // group
    per = heads // group
    rows = per * HD + 16
    cube = tokens * width * HD
    shape = jax.ShapeDtypeStruct

    def swap(x, s):
        return lax.ppermute(x, "ctx", [(c, c ^ s) for c in range(n)])

    def ahead(x, d):
        return lax.ppermute(x, "ctx", [(c, (c + d * group) % n) for c in range(n)])

    tri, bias = call(
        triangle_kernel, "triangle", [shape((tokens, tokens), F32)] * 2, (), flops=1 << 31
    )
    (kv,) = call(
        beside_kernel,
        "keys_beside_values",
        [shape((tokens, 2 * kv_width), BF16)],
        (keys, values),
        after=(tri,),
    )
    far = [ahead(kv, d) for d in range(1, groups)]

    to, back = (0, 2, 3, 1), (0, 3, 2, 1)

    def states(s):
        return call(
            functools.partial(state_kernel, group, per, s),
            "states_%d" % s,
            [shape((rows, HD), BF16)],
            (tri, log_decay, k_lin, v_lin),
            flops=4 * cube // group,
            exps=2 * tokens * width // group,
        )[0]

    pays = {s: swap(states(s), s) for s in to[1:]}
    pays[0] = states(0)
    pays = [pays[s] for s in to]

    intra, qa, gain, decay = call(
        functools.partial(intra_kernel, heads),
        "intra_block",
        [
            shape((tokens, width), F32),
            shape((tokens, width), BF16),
            shape((tokens, width), F32),
            shape((tokens, heads), F32),
        ],
        (tri, bias, log_decay, q_lin, k_lin, v_lin, gate, norm_gain.reshape(1, width)),
        flops=4 * cube,
        exps=4 * tokens * width,
    )

    slots = pltpu.VMEM((group, rows, HD), BF16)
    carry = ()
    if groups > 1:
        (total,) = call(
            functools.partial(total_kernel, group, per, to),
            "group_state",
            [shape((rows, HD), BF16)],
            pays,
            [slots],
            flops=2 * per * HD * HD * group,
            after=(intra,),
        )
        before = ahead(total, 1)
        shift = 1
        while shift < groups - 1:
            mine = lax.div(lax.axis_index("ctx"), group)
            later = jnp.where(mine >= 1, before, 0).astype(F32)
            earlier = ahead(later.astype(BF16), shift)
            earlier = jnp.where(mine >= shift + 1, earlier, 0).astype(F32)
            step = later[per * HD :][:per] + later[per * HD + 8 :][:per]
            prior = earlier[per * HD :][:per] + earlier[per * HD + 8 :][:per]
            state = later[: per * HD] + jnp.repeat(step, HD, axis=0) * earlier[: per * HD]
            both = jnp.where(mine >= shift + 1, step * prior, step)
            high = both.astype(BF16).astype(F32)
            pad = jnp.zeros((8 - per, HD), F32)
            before = jnp.concatenate([state, high, pad, both - high, pad], axis=0).astype(BF16)
            shift *= 2
        carry = (before,)
    prefixes = call(
        functools.partial(prefix_kernel, group, per, to, bool(carry)),
        "prefix_states",
        [shape((per * HD, HD), BF16)] * group,
        (*pays, *carry),
        [slots, pltpu.VMEM((group, per * HD, HD), BF16)],
        flops=1 << 33,
    )
    prefixes = [swap(prefixes[s], s) if s else prefixes[s] for s in back]

    (own,) = call(
        stack_kernel,
        "stack_keys_values",
        [shape((groups * tokens, kv.shape[1]), BF16)],
        (kv, *far),
        after=(total,) if groups > 1 else (intra,),
        flops=1 << 32,
    )
    side, near = swap(own, 2), swap(own, 1)
    share = width // kv_heads
    pack = 2 if share // HD % 2 == 0 else 1
    span = own.shape[0]
    room = 24 + 48 * span * tokens * 4 // MIB
    smem = pl.BlockSpec(memory_space=pltpu.SMEM)

    def scratch(count):
        keys = count * span
        return [pltpu.VMEM((keys, 2 * HD), BF16), pltpu.VMEM((tokens, keys), F32)]

    acc, *tops = call(
        functools.partial(softmax_first_kernel, group, (0, 2, 1), kv_heads, pack),
        "softmax_first",
        [shape((tokens, 2 * width), F32)] + [shape((tokens, share // HD), F32)] * kv_heads,
        (order, queries, own, side, near),
        scratch(3),
        flops=12 * tokens * width * span,
        exps=3 * tokens * span * width // HD,
        limit=room,
        specs=[smem] + [VMEM] * 4,
    )
    half = shape((own.shape[0] // 2, own.shape[1]), BF16)
    upper, under = call(halves_kernel, "sent_on", [half] * 2, (side, near))
    across = jnp.concatenate([swap(upper, 1), swap(under, 2)])
    (attended,) = call(
        functools.partial(softmax_last_kernel, group, (3,), kv_heads, pack),
        "softmax_last",
        [shape((tokens, width), BF16)],
        (order, queries, across, acc, *tops),
        scratch(1),
        flops=4 * tokens * width * span,
        exps=tokens * span * width // HD,
        limit=room,
        specs=[smem] + [VMEM] * (3 + kv_heads),
    )

    lin, squares = call(
        functools.partial(inter_kernel, group, heads, back),
        "inter_block",
        [shape((tokens, width), F32), shape((8, tokens), F32)],
        (decay, qa, intra, *prefixes),
        [pltpu.VMEM((heads * HD, HD), BF16)],
        flops=2 * cube,
        after=tops[:1],
    )
    if nh & (nh - 1) == 0:
        turns = [[(i, i ^ d) for i in range(nh)] for d in range(nh - 1, 0, -1)]
    else:
        turns = [[(i, (i + d) % nh) for i in range(nh)] for d in range(1, nh)]
    parts = [squares] + [lax.ppermute(squares, "head", turn) for turn in turns]
    pieces = 4 if width % (4 * HD) == 0 else 1
    return call(
        functools.partial(results_kernel, float(width * nh), pieces),
        "results",
        [shape((tokens, width), BF16)] * 2,
        (attended, lin, gain, *parts),
        [pltpu.VMEM((tokens, width), BF16), pltpu.SemaphoreType.DMA((pieces + 1,))],
        flops=4 * tokens * width,
        out_specs=[HBM] * 2,
    )


def solution(mesh):
    return jax.shard_map(
        body,
        mesh=mesh,
        in_specs=(
            P("ctx", "head"),
            P("ctx", "head"),
            P("ctx", "head"),
            P("head", "ctx"),
            P("ctx", "head"),
            P("head"),
            P("ctx", "head"),
            P("ctx", "head"),
            P("ctx", "head"),
            P("ctx"),
        ),
        out_specs=(P("ctx", "head"), P("ctx", "head")),
        check_vma=False,
    )
```

```python
import functools
import math

import jax
import jax.numpy as jnp
from jax import lax
from jax.experimental import pallas as pl
from jax.experimental.pallas import tpu as pltpu
from jax.sharding import PartitionSpec as P

HD = 128
EPS = 1e-06
HIGH = lax.Precision.HIGHEST
F32 = jnp.float32
BF16 = jnp.bfloat16
NT = (((1,), (1,)), ((), ()))
TN = (((0,), (0,)), ((), ()))
MIB = 1 << 20
VMEM = pl.BlockSpec(memory_space=pltpu.VMEM)
HBM = pl.BlockSpec(memory_space=pltpu.HBM)


def inverse(x):
    guess = pl.reciprocal(x, approx=True)
    return guess * (2.0 - x * guess)


def silu16(x):
    x = x.astype(F32)
    return (x / (1.0 + jnp.exp(-x))).astype(BF16)


def lower_ones(size):
    rows = lax.broadcasted_iota(jnp.int32, (size, size), 0)
    cols = lax.broadcasted_iota(jnp.int32, (size, size), 1)
    return rows >= cols


def head_cols(h):
    return slice(h * HD, (h + 1) * HD)


def my_rank(group):
    return lax.rem(lax.axis_index("ctx"), group)


def dyn(index, size):
    return pl.ds(pl.multiple_of(index * size, size), size)


def triangle_kernel(ones_ref, bias_ref):
    lower = lower_ones(ones_ref.shape[0])
    ones_ref[...] = lower.astype(F32)
    bias_ref[...] = jnp.where(lower, 0.0, -1e30)


def decay_weights(tri_ref, ld_ref):
    ld = ld_ref[...]
    cum = lax.dot_general(tri_ref[...], ld, NT, precision=HIGH, preferred_element_type=F32)
    return jnp.exp(cum[-1:, :] - cum), jnp.exp(jnp.sum(ld, axis=1, keepdims=True))


def owner_states(k, per, weight, total, k_ref, v_ref, out):
    for j in range(per):
        h = k * per + j
        ka = silu16(k_ref[:, head_cols(h)])
        va = silu16(v_ref[:, head_cols(h)])
        kdec = ka.astype(F32) * weight[:, h : h + 1]
        khigh = kdec.astype(BF16)
        klow = (kdec - khigh.astype(F32)).astype(BF16)
        state = lax.dot_general(khigh, va, TN, preferred_element_type=F32)
        state += lax.dot_general(klow, va, TN, preferred_element_type=F32)
        out[j * HD : (j + 1) * HD, :] = state.astype(BF16)
    mine = jnp.broadcast_to(total[k * per : (k + 1) * per], (per, HD))
    high = mine.astype(BF16).astype(F32)
    pad = [jnp.zeros((8 - per, HD), F32)] if per < 8 else []
    tail = jnp.concatenate([high, *pad, mine - high, *pad], axis=0)
    out[per * HD :, :] = tail.astype(BF16)


def state_kernel(group, per, s, tri_ref, ld_ref, k_ref, v_ref, out_ref):
    weight, total = decay_weights(tri_ref, ld_ref)
    dest = my_rank(group) ^ s
    for k in range(group):
        pl.when(dest == k)(
            functools.partial(owner_states, k, per, weight, total, k_ref, v_ref, out_ref)
        )


def beside_kernel(keys, values, out):
    width = keys.shape[1]
    out[:, :width] = keys[...]
    out[:, width:] = values[...]


def stack_kernel(*refs):
    tokens = refs[0].shape[0]
    for i, part in enumerate(refs[:-1]):
        refs[-1][i * tokens : (i + 1) * tokens, :] = part[...]


def halves_kernel(a_ref, b_ref, a_out, b_out):
    half = a_out.shape[0]
    a_out[...] = a_ref[:half, :]
    b_out[...] = b_ref[half:, :]


def decay_row(slots, k, base, j):
    tail = slots[k, base : base + 16, :].astype(F32)
    return tail[j : j + 1] + tail[8 + j : 9 + j]


def fill_slots(order, rank, pays, slots):
    for s, pay in zip(order, pays):
        slots[rank ^ s] = pay[...]


def total_kernel(group, per, order, *refs):
    pays, out, slots = refs[:group], refs[group], refs[group + 1]
    fill_slots(order, my_rank(group), pays, slots)
    base = per * HD
    tails = []
    for j in range(per):
        state = slots[0, j * HD : (j + 1) * HD, :].astype(F32)
        whole = decay_row(slots, 0, base, j)
        for k in range(1, group):
            decay = decay_row(slots, k, base, j)
            state = decay * state + slots[k, j * HD : (j + 1) * HD, :].astype(F32)
            whole = whole * decay
        out[j * HD : (j + 1) * HD, :] = state.astype(BF16)
        tails.append(whole)
    pad = [jnp.zeros((8 - per, HD), F32)] if per < 8 else []
    total = jnp.concatenate(tails + pad, axis=0)
    high = total.astype(BF16).astype(F32)
    out[base:, :] = jnp.concatenate([high, total - high], axis=0).astype(BF16)


def prefix_kernel(group, per, order, carried, *refs):
    pays, refs = refs[:group], refs[group:]
    carry = None
    if carried:
        carry, refs = refs[0], refs[1:]
    outs, slots, prefixes = refs[:group], refs[group], refs[group + 1]
    rank = my_rank(group)
    later = lax.axis_index("ctx") >= group
    fill_slots(order, rank, pays, slots)
    base = per * HD
    for j in range(per):
        rows = slice(j * HD, (j + 1) * HD)
        state = jnp.zeros((HD, HD), F32)
        if carried:
            state = jnp.where(later, carry[rows, :].astype(F32), state)
        prefixes[0, rows, :] = state.astype(BF16)
        for k in range(group - 1):
            state = decay_row(slots, k, base, j) * state + slots[k, rows, :].astype(F32)
            prefixes[k + 1, rows, :] = state.astype(BF16)
    for s in range(group):
        outs[s][...] = prefixes[rank ^ s]


def intra_kernel(heads, tri_ref, bias_ref, ld_ref, q_ref, k_ref, v_ref, gate_ref, gain_ref, *outs):
    intra_ref, qa_ref, gain_out, decay_out = outs
    ld = ld_ref[...]
    tri = tri_ref[...]
    bias = bias_ref[...]
    cum = lax.dot_general(tri, ld, NT, precision=HIGH, preferred_element_type=F32)
    cum_t = lax.dot_general(ld, tri, NT, precision=HIGH, preferred_element_type=F32)
    decay_out[...] = jnp.exp(cum)
    for h in range(heads):
        cols = head_cols(h)
        qa = silu16(q_ref[:, cols])
        qa_ref[:, cols] = qa
        ka = silu16(k_ref[:, cols])
        va = silu16(v_ref[:, cols])
        scores = lax.dot_general(qa, ka, NT, preferred_element_type=F32)
        decay = jnp.exp((cum[:, h : h + 1] - cum_t[h : h + 1, :]) + bias)
        weights = (scores * decay).astype(BF16)
        intra_ref[:, cols] = jnp.dot(weights, va, preferred_element_type=F32)
        gate = 1.0 / (1.0 + jnp.exp(-gate_ref[:, cols].astype(F32)))
        gain_out[:, cols] = gate * gain_ref[:, cols]


def inter_kernel(group, heads, order, decay_ref, qa_ref, intra_ref, *rest):
    parts, (lin_ref, squares_ref, states) = rest[:group], rest[group:]
    tokens = qa_ref.shape[0]
    per = heads // group
    rank = my_rank(group)
    for s, part in zip(order, parts):
        states[dyn(rank ^ s, per * HD), :] = part[...]
    decay = decay_ref[...]
    acc = jnp.zeros((tokens, HD), F32)
    for h in range(heads):
        cols = head_cols(h)
        state = states[h * HD : (h + 1) * HD, :]
        inter = jnp.dot(qa_ref[:, cols], state, preferred_element_type=F32)
        lin = intra_ref[:, cols] + inter * decay[:, h : h + 1]
        lin_ref[:, cols] = lin
        acc += lin * lin
    ones = jnp.ones((8, HD), F32)
    squares_ref[...] = lax.dot_general(ones, acc, NT, precision=HIGH, preferred_element_type=F32)


def results_kernel(columns, parts, attended_ref, lin_ref, gain_ref, *rest):
    squares, (mixed_out, attended_out, mixed_ref, sems) = rest[:-4], rest[-4:]
    first = pltpu.make_async_copy(attended_ref, attended_out, sems.at[parts])
    first.start()
    total = squares[0][...]
    for part in squares[1:]:
        total = total + part[...]
    inv = jnp.transpose(lax.rsqrt(total / columns + EPS))[:, 0:1]
    width = lin_ref.shape[1] // parts
    copies = []
    for i in range(parts):
        cols = slice(i * width, (i + 1) * width)
        mixed_ref[:, cols] = (lin_ref[:, cols] * inv * gain_ref[:, cols]).astype(BF16)
        copies.append(
            pltpu.make_async_copy(mixed_ref.at[:, cols], mixed_out.at[:, cols], sems.at[i])
        )
        copies[-1].start()
    for copy in copies:
        copy.wait()
    first.wait()


def softmax_bias(group, sides, order_ref, bias):
    tokens, span = bias.shape[0], bias.shape[1] // len(sides)
    groups = span // tokens
    me = lax.axis_index("ctx")
    rank, mine = lax.rem(me, group), lax.div(me, group)
    qpos = order_ref[0] * tokens + lax.broadcasted_iota(jnp.int32, (tokens, tokens), 0)
    kpos = lax.broadcasted_iota(jnp.int32, (tokens, tokens), 1)
    for i, s in enumerate(sides):
        for d in range(groups):
            place = lax.rem(mine + groups - d, groups) * group + (rank ^ s)
            at = i * span + d * tokens
            bias[:, at : at + tokens] = jnp.where(place * tokens + kpos <= qpos, 0.0, -1e30)


def softmax_values(held, g, kv_heads, values):
    span = held[0].shape[0]
    values[:, HD:] = jnp.ones((span * len(held), HD), BF16)
    for i, ref in enumerate(held):
        values[i * span : (i + 1) * span, :HD] = ref[:, head_cols(kv_heads + g)]


def softmax_scores(query, held, g, bias):
    raw = [
        lax.dot_general(query, ref[:, head_cols(g)], NT, preferred_element_type=F32) for ref in held
    ]
    raw = jnp.concatenate(raw, axis=1)
    raw = raw.reshape(-1, *bias.shape) + bias[...][None]
    return raw.reshape(-1, bias.shape[1])


def stacked(ref, columns):
    return jnp.concatenate([ref[:, cols] for cols in columns], axis=0)


SCORE = math.log2(math.e) / math.sqrt(HD)


def softmax_first_kernel(group, sides, kv_heads, pack, order_ref, q_ref, *rest):
    arrays, rest = rest[: len(sides)], rest[len(sides) :]
    acc_ref, tops, (values, bias) = rest[0], rest[1:-2], rest[-2:]
    tokens = q_ref.shape[0]
    share = q_ref.shape[1] // HD // kv_heads
    softmax_bias(group, sides, order_ref, bias)
    for g in range(kv_heads):
        softmax_values(arrays, g, kv_heads, values)
        for j in range(0, share, pack):
            heads = range(g * share + j, g * share + j + pack)
            raw = softmax_scores(stacked(q_ref, map(head_cols, heads)), arrays, g, bias)
            top = jnp.max(raw, axis=-1, keepdims=True)
            probs = jnp.exp2((raw - top) * SCORE).astype(BF16)
            acc = jnp.dot(probs, values[...], preferred_element_type=F32)
            for i, h in enumerate(heads):
                rows = slice(i * tokens, (i + 1) * tokens)
                acc_ref[:, 2 * h * HD : 2 * (h + 1) * HD] = acc[rows]
                tops[g][:, j + i : j + i + 1] = top[rows]


def softmax_last_kernel(group, sides, kv_heads, pack, order_ref, q_ref, *rest):
    arrays, rest = rest[: len(sides)], rest[len(sides) :]
    acc_ref, tops, (out_ref, values, bias) = rest[0], rest[1:-3], rest[-3:]
    tokens = q_ref.shape[0]
    share = q_ref.shape[1] // HD // kv_heads
    softmax_bias(group, sides, order_ref, bias)
    for g in range(kv_heads):
        softmax_values(arrays, g, kv_heads, values)
        for j in range(0, share, pack):
            heads = range(g * share + j, g * share + j + pack)
            raw = softmax_scores(stacked(q_ref, map(head_cols, heads)), arrays, g, bias)
            old = stacked(tops[g], [slice(j + i, j + i + 1) for i in range(pack)])
            top = jnp.maximum(old, jnp.max(raw, axis=-1, keepdims=True))
            probs = jnp.exp2((raw - top) * SCORE).astype(BF16)
            acc = jnp.dot(probs, values[...], preferred_element_type=F32)
            held = stacked(acc_ref, [slice(2 * h * HD, 2 * (h + 1) * HD) for h in heads])
            acc += held * jnp.exp2((old - top) * SCORE)
            out = (acc[:, :HD] * inverse(acc[:, HD:])).astype(BF16)
            for i, h in enumerate(heads):
                out_ref[:, head_cols(h)] = out[i * tokens : (i + 1) * tokens]


def call(
    kernel, name, outs, args, scratch=(), flops=0, exps=0, limit=16, specs=None, after=(), **more
):
    size = sum(math.prod(x.shape) * x.dtype.itemsize for x in list(args) + list(outs))
    more.setdefault("out_specs", [VMEM for _ in outs])
    specs = list(specs or [VMEM for _ in args]) + [HBM for _ in after]
    count = len(args)

    def run(*refs):
        kernel(*refs[:count], *refs[count + len(after) :])

    return pl.pallas_call(
        run,
        name=name,
        out_shape=list(outs),
        in_specs=specs,
        scratch_shapes=list(scratch),
        cost_estimate=pl.CostEstimate(flops=flops, bytes_accessed=size, transcendentals=exps),
        compiler_params=pltpu.CompilerParams(vmem_limit_bytes=limit * MIB),
        **more,
    )(*args, *after)


def body(q_lin, k_lin, v_lin, log_decay, gate, norm_gain, queries, keys, values, order):
    tokens, width = q_lin.shape
    heads = log_decay.shape[0]
    kv_width = keys.shape[1]
    kv_heads = kv_width // HD
    n, nh = lax.axis_size("ctx"), lax.axis_size("head")
    group = 4
    groups = n // group
    per = heads // group
    rows = per * HD + 16
    cube = tokens * width * HD
    shape = jax.ShapeDtypeStruct

    def swap(x, s):
        return lax.ppermute(x, "ctx", [(c, c ^ s) for c in range(n)])

    def ahead(x, d):
        return lax.ppermute(x, "ctx", [(c, (c + d * group) % n) for c in range(n)])

    tri, bias = call(
        triangle_kernel, "triangle", [shape((tokens, tokens), F32)] * 2, (), flops=1 << 31
    )
    (kv,) = call(
        beside_kernel,
        "keys_beside_values",
        [shape((tokens, 2 * kv_width), BF16)],
        (keys, values),
        after=(tri,),
    )
    far = [ahead(kv, d) for d in range(1, groups)]

    to, back = (0, 2, 1, 3), (0, 3, 2, 1)

    def states(s):
        return call(
            functools.partial(state_kernel, group, per, s),
            "states_%d" % s,
            [shape((rows, HD), BF16)],
            (tri, log_decay, k_lin, v_lin),
            flops=4 * cube // group,
            exps=2 * tokens * width // group,
        )[0]

    pays = {s: swap(states(s), s) for s in to[1:]}
    pays[0] = states(0)
    pays = [pays[s] for s in to]

    intra, qa, gain, decay = call(
        functools.partial(intra_kernel, heads),
        "intra_block",
        [
            shape((tokens, width), F32),
            shape((tokens, width), BF16),
            shape((tokens, width), F32),
            shape((tokens, heads), F32),
        ],
        (tri, bias, log_decay, q_lin, k_lin, v_lin, gate, norm_gain.reshape(1, width)),
        flops=4 * cube,
        exps=4 * tokens * width,
    )

    slots = pltpu.VMEM((group, rows, HD), BF16)
    carry = ()
    if groups > 1:
        (total,) = call(
            functools.partial(total_kernel, group, per, to),
            "group_state",
            [shape((rows, HD), BF16)],
            pays,
            [slots],
            flops=2 * per * HD * HD * group,
            after=(intra,),
        )
        before = ahead(total, 1)
        shift = 1
        while shift < groups - 1:
            mine = lax.div(lax.axis_index("ctx"), group)
            later = jnp.where(mine >= 1, before, 0).astype(F32)
            earlier = ahead(later.astype(BF16), shift)
            earlier = jnp.where(mine >= shift + 1, earlier, 0).astype(F32)
            step = later[per * HD :][:per] + later[per * HD + 8 :][:per]
            prior = earlier[per * HD :][:per] + earlier[per * HD + 8 :][:per]
            state = later[: per * HD] + jnp.repeat(step, HD, axis=0) * earlier[: per * HD]
            both = jnp.where(mine >= shift + 1, step * prior, step)
            high = both.astype(BF16).astype(F32)
            pad = jnp.zeros((8 - per, HD), F32)
            before = jnp.concatenate([state, high, pad, both - high, pad], axis=0).astype(BF16)
            shift *= 2
        carry = (before,)
    prefixes = call(
        functools.partial(prefix_kernel, group, per, to, bool(carry)),
        "prefix_states",
        [shape((per * HD, HD), BF16)] * group,
        (*pays, *carry),
        [slots, pltpu.VMEM((group, per * HD, HD), BF16)],
        flops=1 << 33,
    )
    prefixes = [swap(prefixes[s], s) if s else prefixes[s] for s in back]

    (own,) = call(
        stack_kernel,
        "stack_keys_values",
        [shape((groups * tokens, kv.shape[1]), BF16)],
        (kv, *far),
        after=(total,) if groups > 1 else (intra,),
        flops=1 << 32,
    )
    side, near = swap(own, 2), swap(own, 1)
    share = width // kv_heads
    pack = 2 if share // HD % 2 == 0 else 1
    span = own.shape[0]
    room = 24 + 48 * span * tokens * 4 // MIB
    smem = pl.BlockSpec(memory_space=pltpu.SMEM)

    def scratch(count):
        keys = count * span
        return [pltpu.VMEM((keys, 2 * HD), BF16), pltpu.VMEM((tokens, keys), F32)]

    acc, *tops = call(
        functools.partial(softmax_first_kernel, group, (0, 2, 1), kv_heads, pack),
        "softmax_first",
        [shape((tokens, 2 * width), F32)] + [shape((tokens, share // HD), F32)] * kv_heads,
        (order, queries, own, side, near),
        scratch(3),
        flops=12 * tokens * width * span,
        exps=3 * tokens * span * width // HD,
        limit=room,
        specs=[smem] + [VMEM] * 4,
    )
    half = shape((own.shape[0] // 2, own.shape[1]), BF16)
    upper, under = call(halves_kernel, "sent_on", [half] * 2, (side, near))
    across = jnp.concatenate([swap(upper, 1), swap(under, 2)])
    (attended,) = call(
        functools.partial(softmax_last_kernel, group, (3,), kv_heads, pack),
        "softmax_last",
        [shape((tokens, width), BF16)],
        (order, queries, across, acc, *tops),
        scratch(1),
        flops=4 * tokens * width * span,
        exps=tokens * span * width // HD,
        limit=room,
        specs=[smem] + [VMEM] * (3 + kv_heads),
    )

    lin, squares = call(
        functools.partial(inter_kernel, group, heads, back),
        "inter_block",
        [shape((tokens, width), F32), shape((8, tokens), F32)],
        (decay, qa, intra, *prefixes),
        [pltpu.VMEM((heads * HD, HD), BF16)],
        flops=2 * cube,
        after=tops[:1],
    )
    if nh & (nh - 1) == 0:
        turns = [[(i, i ^ d) for i in range(nh)] for d in range(nh - 1, 0, -1)]
    else:
        turns = [[(i, (i + d) % nh) for i in range(nh)] for d in range(1, nh)]
    parts = [squares] + [lax.ppermute(squares, "head", turn) for turn in turns]
    pieces = 4 if width % (4 * HD) == 0 else 1
    return call(
        functools.partial(results_kernel, float(width * nh), pieces),
        "results",
        [shape((tokens, width), BF16)] * 2,
        (attended, lin, gain, *parts),
        [pltpu.VMEM((tokens, width), BF16), pltpu.SemaphoreType.DMA((pieces + 1,))],
        flops=4 * tokens * width,
        out_specs=[HBM] * 2,
    )


def solution(mesh):
    return jax.shard_map(
        body,
        mesh=mesh,
        in_specs=(
            P("ctx", "head"),
            P("ctx", "head"),
            P("ctx", "head"),
            P("head", "ctx"),
            P("ctx", "head"),
            P("head"),
            P("ctx", "head"),
            P("ctx", "head"),
            P("ctx", "head"),
            P("ctx"),
        ),
        out_specs=(P("ctx", "head"), P("ctx", "head")),
        check_vma=False,
    )
```

```python
import functools
import math

import jax
import jax.numpy as jnp
from jax import lax
from jax.experimental import pallas as pl
from jax.experimental.pallas import tpu as pltpu
from jax.sharding import PartitionSpec as P

HD = 128
EPS = 1e-06
HIGH = lax.Precision.HIGHEST
F32 = jnp.float32
BF16 = jnp.bfloat16
NT = (((1,), (1,)), ((), ()))
TN = (((0,), (0,)), ((), ()))
MIB = 1 << 20
VMEM = pl.BlockSpec(memory_space=pltpu.VMEM)
HBM = pl.BlockSpec(memory_space=pltpu.HBM)


def inverse(x):
    guess = pl.reciprocal(x, approx=True)
    return guess * (2.0 - x * guess)


def silu16(x):
    x = x.astype(F32)
    return (x / (1.0 + jnp.exp(-x))).astype(BF16)


def lower_ones(size):
    rows = lax.broadcasted_iota(jnp.int32, (size, size), 0)
    cols = lax.broadcasted_iota(jnp.int32, (size, size), 1)
    return rows >= cols


def head_cols(h):
    return slice(h * HD, (h + 1) * HD)


def my_rank(group):
    return lax.rem(lax.axis_index("ctx"), group)


def dyn(index, size):
    return pl.ds(pl.multiple_of(index * size, size), size)


def triangle_kernel(ones_ref, bias_ref):
    lower = lower_ones(ones_ref.shape[0])
    ones_ref[...] = lower.astype(F32)
    bias_ref[...] = jnp.where(lower, 0.0, -1e30)


def decay_weights(tri_ref, ld_ref):
    ld = ld_ref[...]
    cum = lax.dot_general(tri_ref[...], ld, NT, precision=HIGH, preferred_element_type=F32)
    return jnp.exp(cum[-1:, :] - cum), jnp.exp(jnp.sum(ld, axis=1, keepdims=True))


def owner_states(k, per, weight, total, k_ref, v_ref, out):
    for j in range(per):
        h = k * per + j
        ka = silu16(k_ref[:, head_cols(h)])
        va = silu16(v_ref[:, head_cols(h)])
        kdec = ka.astype(F32) * weight[:, h : h + 1]
        khigh = kdec.astype(BF16)
        klow = (kdec - khigh.astype(F32)).astype(BF16)
        state = lax.dot_general(khigh, va, TN, preferred_element_type=F32)
        state += lax.dot_general(klow, va, TN, preferred_element_type=F32)
        out[j * HD : (j + 1) * HD, :] = state.astype(BF16)
    mine = jnp.broadcast_to(total[k * per : (k + 1) * per], (per, HD))
    high = mine.astype(BF16).astype(F32)
    pad = [jnp.zeros((8 - per, HD), F32)] if per < 8 else []
    tail = jnp.concatenate([high, *pad, mine - high, *pad], axis=0)
    out[per * HD :, :] = tail.astype(BF16)


def state_kernel(group, per, s, tri_ref, ld_ref, k_ref, v_ref, out_ref):
    weight, total = decay_weights(tri_ref, ld_ref)
    dest = my_rank(group) ^ s
    for k in range(group):
        pl.when(dest == k)(
            functools.partial(owner_states, k, per, weight, total, k_ref, v_ref, out_ref)
        )


def beside_kernel(keys, values, out):
    width = keys.shape[1]
    out[:, :width] = keys[...]
    out[:, width:] = values[...]


def stack_kernel(*refs):
    tokens = refs[0].shape[0]
    for i, part in enumerate(refs[:-1]):
        refs[-1][i * tokens : (i + 1) * tokens, :] = part[...]


def halves_kernel(a_ref, b_ref, a_out, b_out):
    half = a_out.shape[0]
    a_out[...] = a_ref[:half, :]
    b_out[...] = b_ref[half:, :]


def decay_row(slots, k, base, j):
    tail = slots[k, base : base + 16, :].astype(F32)
    return tail[j : j + 1] + tail[8 + j : 9 + j]


def fill_slots(order, rank, pays, slots):
    for s, pay in zip(order, pays):
        slots[rank ^ s] = pay[...]


def total_kernel(group, per, order, *refs):
    pays, out, slots = refs[:group], refs[group], refs[group + 1]
    fill_slots(order, my_rank(group), pays, slots)
    base = per * HD
    tails = []
    for j in range(per):
        state = slots[0, j * HD : (j + 1) * HD, :].astype(F32)
        whole = decay_row(slots, 0, base, j)
        for k in range(1, group):
            decay = decay_row(slots, k, base, j)
            state = decay * state + slots[k, j * HD : (j + 1) * HD, :].astype(F32)
            whole = whole * decay
        out[j * HD : (j + 1) * HD, :] = state.astype(BF16)
        tails.append(whole)
    pad = [jnp.zeros((8 - per, HD), F32)] if per < 8 else []
    total = jnp.concatenate(tails + pad, axis=0)
    high = total.astype(BF16).astype(F32)
    out[base:, :] = jnp.concatenate([high, total - high], axis=0).astype(BF16)


def prefix_kernel(group, per, order, carried, *refs):
    pays, refs = refs[:group], refs[group:]
    carry = None
    if carried:
        carry, refs = refs[0], refs[1:]
    outs, slots, prefixes = refs[:group], refs[group], refs[group + 1]
    rank = my_rank(group)
    later = lax.axis_index("ctx") >= group
    fill_slots(order, rank, pays, slots)
    base = per * HD
    for j in range(per):
        rows = slice(j * HD, (j + 1) * HD)
        state = jnp.zeros((HD, HD), F32)
        if carried:
            state = jnp.where(later, carry[rows, :].astype(F32), state)
        prefixes[0, rows, :] = state.astype(BF16)
        for k in range(group - 1):
            state = decay_row(slots, k, base, j) * state + slots[k, rows, :].astype(F32)
            prefixes[k + 1, rows, :] = state.astype(BF16)
    for s in range(group):
        outs[s][...] = prefixes[rank ^ s]


def intra_kernel(heads, tri_ref, bias_ref, ld_ref, q_ref, k_ref, v_ref, gate_ref, gain_ref, *outs):
    intra_ref, qa_ref, gain_out, decay_out = outs
    ld = ld_ref[...]
    tri = tri_ref[...]
    bias = bias_ref[...]
    cum = lax.dot_general(tri, ld, NT, precision=HIGH, preferred_element_type=F32)
    cum_t = lax.dot_general(ld, tri, NT, precision=HIGH, preferred_element_type=F32)
    decay_out[...] = jnp.exp(cum)
    for h in range(heads):
        cols = head_cols(h)
        qa = silu16(q_ref[:, cols])
        qa_ref[:, cols] = qa
        ka = silu16(k_ref[:, cols])
        va = silu16(v_ref[:, cols])
        scores = lax.dot_general(qa, ka, NT, preferred_element_type=F32)
        decay = jnp.exp((cum[:, h : h + 1] - cum_t[h : h + 1, :]) + bias)
        weights = (scores * decay).astype(BF16)
        intra_ref[:, cols] = jnp.dot(weights, va, preferred_element_type=F32)
        gate = 1.0 / (1.0 + jnp.exp(-gate_ref[:, cols].astype(F32)))
        gain_out[:, cols] = gate * gain_ref[:, cols]


def inter_kernel(group, heads, order, decay_ref, qa_ref, intra_ref, *rest):
    parts, (lin_ref, squares_ref, states) = rest[:group], rest[group:]
    tokens = qa_ref.shape[0]
    per = heads // group
    rank = my_rank(group)
    for s, part in zip(order, parts):
        states[dyn(rank ^ s, per * HD), :] = part[...]
    decay = decay_ref[...]
    acc = jnp.zeros((tokens, HD), F32)
    for h in range(heads):
        cols = head_cols(h)
        state = states[h * HD : (h + 1) * HD, :]
        inter = jnp.dot(qa_ref[:, cols], state, preferred_element_type=F32)
        lin = intra_ref[:, cols] + inter * decay[:, h : h + 1]
        lin_ref[:, cols] = lin
        acc += lin * lin
    ones = jnp.ones((8, HD), F32)
    squares_ref[...] = lax.dot_general(ones, acc, NT, precision=HIGH, preferred_element_type=F32)


def results_kernel(columns, parts, attended_ref, lin_ref, gain_ref, *rest):
    squares, (mixed_out, attended_out, mixed_ref, sems) = rest[:-4], rest[-4:]
    first = pltpu.make_async_copy(attended_ref, attended_out, sems.at[parts])
    first.start()
    total = squares[0][...]
    for part in squares[1:]:
        total = total + part[...]
    inv = jnp.transpose(lax.rsqrt(total / columns + EPS))[:, 0:1]
    width = lin_ref.shape[1] // parts
    copies = []
    for i in range(parts):
        cols = slice(i * width, (i + 1) * width)
        mixed_ref[:, cols] = (lin_ref[:, cols] * inv * gain_ref[:, cols]).astype(BF16)
        copies.append(
            pltpu.make_async_copy(mixed_ref.at[:, cols], mixed_out.at[:, cols], sems.at[i])
        )
        copies[-1].start()
    for copy in copies:
        copy.wait()
    first.wait()


def softmax_bias(group, sides, order_ref, bias):
    tokens, span = bias.shape[0], bias.shape[1] // len(sides)
    groups = span // tokens
    me = lax.axis_index("ctx")
    rank, mine = lax.rem(me, group), lax.div(me, group)
    qpos = order_ref[0] * tokens + lax.broadcasted_iota(jnp.int32, (tokens, tokens), 0)
    kpos = lax.broadcasted_iota(jnp.int32, (tokens, tokens), 1)
    for i, s in enumerate(sides):
        for d in range(groups):
            place = lax.rem(mine + groups - d, groups) * group + (rank ^ s)
            at = i * span + d * tokens
            bias[:, at : at + tokens] = jnp.where(place * tokens + kpos <= qpos, 0.0, -1e30)


def softmax_values(held, g, kv_heads, values):
    span = held[0].shape[0]
    values[:, HD:] = jnp.ones((span * len(held), HD), BF16)
    for i, ref in enumerate(held):
        values[i * span : (i + 1) * span, :HD] = ref[:, head_cols(kv_heads + g)]


def softmax_scores(query, held, g, bias):
    raw = [
        lax.dot_general(query, ref[:, head_cols(g)], NT, preferred_element_type=F32) for ref in held
    ]
    raw = jnp.concatenate(raw, axis=1)
    raw = raw.reshape(-1, *bias.shape) + bias[...][None]
    return raw.reshape(-1, bias.shape[1])


def stacked(ref, columns):
    return jnp.concatenate([ref[:, cols] for cols in columns], axis=0)


SCORE = math.log2(math.e) / math.sqrt(HD)


def softmax_first_kernel(group, sides, kv_heads, pack, order_ref, q_ref, *rest):
    arrays, rest = rest[: len(sides)], rest[len(sides) :]
    acc_ref, tops, (values, bias) = rest[0], rest[1:-2], rest[-2:]
    tokens = q_ref.shape[0]
    share = q_ref.shape[1] // HD // kv_heads
    softmax_bias(group, sides, order_ref, bias)
    for g in range(kv_heads):
        softmax_values(arrays, g, kv_heads, values)
        for j in range(0, share, pack):
            heads = range(g * share + j, g * share + j + pack)
            raw = softmax_scores(stacked(q_ref, map(head_cols, heads)), arrays, g, bias)
            top = jnp.max(raw, axis=-1, keepdims=True)
            probs = jnp.exp2((raw - top) * SCORE).astype(BF16)
            acc = jnp.dot(probs, values[...], preferred_element_type=F32)
            for i, h in enumerate(heads):
                rows = slice(i * tokens, (i + 1) * tokens)
                acc_ref[:, 2 * h * HD : 2 * (h + 1) * HD] = acc[rows]
                tops[g][:, j + i : j + i + 1] = top[rows]


def softmax_last_kernel(group, sides, kv_heads, pack, order_ref, q_ref, *rest):
    arrays, rest = rest[: len(sides)], rest[len(sides) :]
    acc_ref, tops, (out_ref, values, bias) = rest[0], rest[1:-3], rest[-3:]
    tokens = q_ref.shape[0]
    share = q_ref.shape[1] // HD // kv_heads
    softmax_bias(group, sides, order_ref, bias)
    for g in range(kv_heads):
        softmax_values(arrays, g, kv_heads, values)
        for j in range(0, share, pack):
            heads = range(g * share + j, g * share + j + pack)
            raw = softmax_scores(stacked(q_ref, map(head_cols, heads)), arrays, g, bias)
            old = stacked(tops[g], [slice(j + i, j + i + 1) for i in range(pack)])
            top = jnp.maximum(old, jnp.max(raw, axis=-1, keepdims=True))
            probs = jnp.exp2((raw - top) * SCORE).astype(BF16)
            acc = jnp.dot(probs, values[...], preferred_element_type=F32)
            held = stacked(acc_ref, [slice(2 * h * HD, 2 * (h + 1) * HD) for h in heads])
            acc += held * jnp.exp2((old - top) * SCORE)
            out = (acc[:, :HD] * inverse(acc[:, HD:])).astype(BF16)
            for i, h in enumerate(heads):
                out_ref[:, head_cols(h)] = out[i * tokens : (i + 1) * tokens]


def call(
    kernel, name, outs, args, scratch=(), flops=0, exps=0, limit=16, specs=None, after=(), **more
):
    size = sum(math.prod(x.shape) * x.dtype.itemsize for x in list(args) + list(outs))
    more.setdefault("out_specs", [VMEM for _ in outs])
    specs = list(specs or [VMEM for _ in args]) + [HBM for _ in after]
    count = len(args)

    def run(*refs):
        kernel(*refs[:count], *refs[count + len(after) :])

    return pl.pallas_call(
        run,
        name=name,
        out_shape=list(outs),
        in_specs=specs,
        scratch_shapes=list(scratch),
        cost_estimate=pl.CostEstimate(flops=flops, bytes_accessed=size, transcendentals=exps),
        compiler_params=pltpu.CompilerParams(vmem_limit_bytes=limit * MIB),
        **more,
    )(*args, *after)


def body(q_lin, k_lin, v_lin, log_decay, gate, norm_gain, queries, keys, values, order):
    tokens, width = q_lin.shape
    heads = log_decay.shape[0]
    kv_width = keys.shape[1]
    kv_heads = kv_width // HD
    n, nh = lax.axis_size("ctx"), lax.axis_size("head")
    group = 4
    groups = n // group
    per = heads // group
    rows = per * HD + 16
    cube = tokens * width * HD
    shape = jax.ShapeDtypeStruct

    def swap(x, s):
        return lax.ppermute(x, "ctx", [(c, c ^ s) for c in range(n)])

    def ahead(x, d):
        return lax.ppermute(x, "ctx", [(c, (c + d * group) % n) for c in range(n)])

    tri, bias = call(
        triangle_kernel, "triangle", [shape((tokens, tokens), F32)] * 2, (), flops=1 << 31
    )
    (kv,) = call(
        beside_kernel,
        "keys_beside_values",
        [shape((tokens, 2 * kv_width), BF16)],
        (keys, values),
        after=(tri,),
    )
    far = [ahead(kv, d) for d in range(1, groups)]

    to, back = (0, 2, 1, 3), (0, 3, 2, 1)

    def states(s):
        return call(
            functools.partial(state_kernel, group, per, s),
            "states_%d" % s,
            [shape((rows, HD), BF16)],
            (tri, log_decay, k_lin, v_lin),
            flops=4 * cube // group,
            exps=2 * tokens * width // group,
        )[0]

    pays = {s: swap(states(s), s) for s in to[1:]}
    pays[0] = states(0)
    pays = [pays[s] for s in to]

    intra, qa, gain, decay = call(
        functools.partial(intra_kernel, heads),
        "intra_block",
        [
            shape((tokens, width), F32),
            shape((tokens, width), BF16),
            shape((tokens, width), F32),
            shape((tokens, heads), F32),
        ],
        (tri, bias, log_decay, q_lin, k_lin, v_lin, gate, norm_gain.reshape(1, width)),
        flops=4 * cube,
        exps=4 * tokens * width,
        after=far,
    )

    slots = pltpu.VMEM((group, rows, HD), BF16)
    carry = ()
    if groups > 1:
        (total,) = call(
            functools.partial(total_kernel, group, per, to),
            "group_state",
            [shape((rows, HD), BF16)],
            pays,
            [slots],
            flops=2 * per * HD * HD * group,
            after=(intra,),
        )
        before = ahead(total, 1)
        shift = 1
        while shift < groups - 1:
            mine = lax.div(lax.axis_index("ctx"), group)
            later = jnp.where(mine >= 1, before, 0).astype(F32)
            earlier = ahead(later.astype(BF16), shift)
            earlier = jnp.where(mine >= shift + 1, earlier, 0).astype(F32)
            step = later[per * HD :][:per] + later[per * HD + 8 :][:per]
            prior = earlier[per * HD :][:per] + earlier[per * HD + 8 :][:per]
            state = later[: per * HD] + jnp.repeat(step, HD, axis=0) * earlier[: per * HD]
            both = jnp.where(mine >= shift + 1, step * prior, step)
            high = both.astype(BF16).astype(F32)
            pad = jnp.zeros((8 - per, HD), F32)
            before = jnp.concatenate([state, high, pad, both - high, pad], axis=0).astype(BF16)
            shift *= 2
        carry = (before,)
    prefixes = call(
        functools.partial(prefix_kernel, group, per, to, bool(carry)),
        "prefix_states",
        [shape((per * HD, HD), BF16)] * group,
        (*pays, *carry),
        [slots, pltpu.VMEM((group, per * HD, HD), BF16)],
        flops=1 << 33,
    )
    prefixes = [swap(prefixes[s], s) if s else prefixes[s] for s in back]

    (own,) = call(
        stack_kernel,
        "stack_keys_values",
        [shape((groups * tokens, kv.shape[1]), BF16)],
        (kv, *far),
        after=(total,) if groups > 1 else (intra,),
        flops=1 << 32,
    )
    side, near = swap(own, 2), swap(own, 1)
    share = width // kv_heads
    pack = 2 if share // HD % 2 == 0 else 1
    span = own.shape[0]
    room = 24 + 48 * span * tokens * 4 // MIB
    smem = pl.BlockSpec(memory_space=pltpu.SMEM)

    def scratch(count):
        keys = count * span
        return [pltpu.VMEM((keys, 2 * HD), BF16), pltpu.VMEM((tokens, keys), F32)]

    acc, *tops = call(
        functools.partial(softmax_first_kernel, group, (0, 2, 1), kv_heads, pack),
        "softmax_first",
        [shape((tokens, 2 * width), F32)] + [shape((tokens, share // HD), F32)] * kv_heads,
        (order, queries, own, side, near),
        scratch(3),
        flops=12 * tokens * width * span,
        exps=3 * tokens * span * width // HD,
        limit=room,
        specs=[smem] + [VMEM] * 4,
    )
    half = shape((own.shape[0] // 2, own.shape[1]), BF16)
    upper, under = call(halves_kernel, "sent_on", [half] * 2, (side, near))
    across = jnp.concatenate([swap(upper, 1), swap(under, 2)])
    (attended,) = call(
        functools.partial(softmax_last_kernel, group, (3,), kv_heads, pack),
        "softmax_last",
        [shape((tokens, width), BF16)],
        (order, queries, across, acc, *tops),
        scratch(1),
        flops=4 * tokens * width * span,
        exps=tokens * span * width // HD,
        limit=room,
        specs=[smem] + [VMEM] * (3 + kv_heads),
    )

    lin, squares = call(
        functools.partial(inter_kernel, group, heads, back),
        "inter_block",
        [shape((tokens, width), F32), shape((8, tokens), F32)],
        (decay, qa, intra, *prefixes),
        [pltpu.VMEM((heads * HD, HD), BF16)],
        flops=2 * cube,
        after=tops[:1],
    )
    if nh & (nh - 1) == 0:
        turns = [[(i, i ^ d) for i in range(nh)] for d in range(nh - 1, 0, -1)]
    else:
        turns = [[(i, (i + d) % nh) for i in range(nh)] for d in range(1, nh)]
    parts = [squares] + [lax.ppermute(squares, "head", turn) for turn in turns]
    pieces = 4 if width % (4 * HD) == 0 else 1
    return call(
        functools.partial(results_kernel, float(width * nh), pieces),
        "results",
        [shape((tokens, width), BF16)] * 2,
        (attended, lin, gain, *parts),
        [pltpu.VMEM((tokens, width), BF16), pltpu.SemaphoreType.DMA((pieces + 1,))],
        flops=4 * tokens * width,
        out_specs=[HBM] * 2,
    )


def solution(mesh):
    return jax.shard_map(
        body,
        mesh=mesh,
        in_specs=(
            P("ctx", "head"),
            P("ctx", "head"),
            P("ctx", "head"),
            P("head", "ctx"),
            P("ctx", "head"),
            P("head"),
            P("ctx", "head"),
            P("ctx", "head"),
            P("ctx", "head"),
            P("ctx"),
        ),
        out_specs=(P("ctx", "head"), P("ctx", "head")),
        check_vma=False,
    )
```

```python
import functools
import math

import jax
import jax.numpy as jnp
from jax import lax
from jax.experimental import pallas as pl
from jax.experimental.pallas import tpu as pltpu
from jax.sharding import PartitionSpec as P

HD = 128
EPS = 1e-06
HIGH = lax.Precision.HIGHEST
F32 = jnp.float32
BF16 = jnp.bfloat16
NT = (((1,), (1,)), ((), ()))
TN = (((0,), (0,)), ((), ()))
MIB = 1 << 20
VMEM = pl.BlockSpec(memory_space=pltpu.VMEM)
HBM = pl.BlockSpec(memory_space=pltpu.HBM)


def inverse(x):
    guess = pl.reciprocal(x, approx=True)
    return guess * (2.0 - x * guess)


def silu16(x):
    x = x.astype(F32)
    return (x / (1.0 + jnp.exp(-x))).astype(BF16)


def lower_ones(size):
    rows = lax.broadcasted_iota(jnp.int32, (size, size), 0)
    cols = lax.broadcasted_iota(jnp.int32, (size, size), 1)
    return rows >= cols


def head_cols(h):
    return slice(h * HD, (h + 1) * HD)


def my_rank(group):
    return lax.rem(lax.axis_index("ctx"), group)


def dyn(index, size):
    return pl.ds(pl.multiple_of(index * size, size), size)


def triangle_kernel(ones_ref, bias_ref):
    lower = lower_ones(ones_ref.shape[0])
    ones_ref[...] = lower.astype(F32)
    bias_ref[...] = jnp.where(lower, 0.0, -1e30)


def decay_weights(tri_ref, ld_ref):
    ld = ld_ref[...]
    cum = lax.dot_general(tri_ref[...], ld, NT, precision=HIGH, preferred_element_type=F32)
    return jnp.exp(cum[-1:, :] - cum), jnp.exp(jnp.sum(ld, axis=1, keepdims=True))


def owner_states(k, per, weight, total, k_ref, v_ref, out):
    for j in range(per):
        h = k * per + j
        ka = silu16(k_ref[:, head_cols(h)])
        va = silu16(v_ref[:, head_cols(h)])
        kdec = ka.astype(F32) * weight[:, h : h + 1]
        khigh = kdec.astype(BF16)
        klow = (kdec - khigh.astype(F32)).astype(BF16)
        state = lax.dot_general(khigh, va, TN, preferred_element_type=F32)
        state += lax.dot_general(klow, va, TN, preferred_element_type=F32)
        out[j * HD : (j + 1) * HD, :] = state.astype(BF16)
    mine = jnp.broadcast_to(total[k * per : (k + 1) * per], (per, HD))
    high = mine.astype(BF16).astype(F32)
    pad = [jnp.zeros((8 - per, HD), F32)] if per < 8 else []
    tail = jnp.concatenate([high, *pad, mine - high, *pad], axis=0)
    out[per * HD :, :] = tail.astype(BF16)


def state_kernel(group, per, s, tri_ref, ld_ref, k_ref, v_ref, out_ref):
    weight, total = decay_weights(tri_ref, ld_ref)
    dest = my_rank(group) ^ s
    for k in range(group):
        pl.when(dest == k)(
            functools.partial(owner_states, k, per, weight, total, k_ref, v_ref, out_ref)
        )


def beside_kernel(keys, values, out):
    width = keys.shape[1]
    out[:, :width] = keys[...]
    out[:, width:] = values[...]


def stack_kernel(*refs):
    tokens = refs[0].shape[0]
    for i, part in enumerate(refs[:-1]):
        refs[-1][i * tokens : (i + 1) * tokens, :] = part[...]


def halves_kernel(a_ref, b_ref, a_out, b_out):
    half = a_out.shape[0]
    a_out[...] = a_ref[:half, :]
    b_out[...] = b_ref[half:, :]


def decay_row(slots, k, base, j):
    tail = slots[k, base : base + 16, :].astype(F32)
    return tail[j : j + 1] + tail[8 + j : 9 + j]


def fill_slots(order, rank, pays, slots):
    for s, pay in zip(order, pays):
        slots[rank ^ s] = pay[...]


def total_kernel(group, per, order, *refs):
    pays, out, slots = refs[:group], refs[group], refs[group + 1]
    fill_slots(order, my_rank(group), pays, slots)
    base = per * HD
    tails = []
    for j in range(per):
        state = slots[0, j * HD : (j + 1) * HD, :].astype(F32)
        whole = decay_row(slots, 0, base, j)
        for k in range(1, group):
            decay = decay_row(slots, k, base, j)
            state = decay * state + slots[k, j * HD : (j + 1) * HD, :].astype(F32)
            whole = whole * decay
        out[j * HD : (j + 1) * HD, :] = state.astype(BF16)
        tails.append(whole)
    pad = [jnp.zeros((8 - per, HD), F32)] if per < 8 else []
    total = jnp.concatenate(tails + pad, axis=0)
    high = total.astype(BF16).astype(F32)
    out[base:, :] = jnp.concatenate([high, total - high], axis=0).astype(BF16)


def prefix_kernel(group, per, order, carried, *refs):
    pays, refs = refs[:group], refs[group:]
    ends = []
    if carried:
        ends, refs = refs[: group - 1], refs[group - 1 :]
    carry = None
    if carried:
        carry, refs = refs[0], refs[1:]
    outs, slots, prefixes = refs[:group], refs[group], refs[group + 1]
    rank = my_rank(group)
    later = lax.axis_index("ctx") >= group
    fill_slots(order, rank, pays, slots)
    if carried:
        last = lax.axis_index("ctx") >= lax.axis_size("ctx") - group
        pl.when(last)(functools.partial(fill_slots, order[1:], rank, ends, slots))
    base = per * HD
    for j in range(per):
        rows = slice(j * HD, (j + 1) * HD)
        state = jnp.zeros((HD, HD), F32)
        if carried:
            state = jnp.where(later, carry[rows, :].astype(F32), state)
        prefixes[0, rows, :] = state.astype(BF16)
        for k in range(group - 1):
            state = decay_row(slots, k, base, j) * state + slots[k, rows, :].astype(F32)
            prefixes[k + 1, rows, :] = state.astype(BF16)
    for s in range(group):
        outs[s][...] = prefixes[rank ^ s]


def intra_kernel(heads, tri_ref, bias_ref, ld_ref, q_ref, k_ref, v_ref, *outs):
    intra_ref, qa_ref, decay_out = outs
    ld = ld_ref[...]
    tri = tri_ref[...]
    bias = bias_ref[...]
    cum = lax.dot_general(tri, ld, NT, precision=HIGH, preferred_element_type=F32)
    cum_t = lax.dot_general(ld, tri, NT, precision=HIGH, preferred_element_type=F32)
    decay_out[...] = jnp.exp(cum)
    for h in range(heads):
        cols = head_cols(h)
        qa = silu16(q_ref[:, cols])
        qa_ref[:, cols] = qa
        ka = silu16(k_ref[:, cols])
        va = silu16(v_ref[:, cols])
        scores = lax.dot_general(qa, ka, NT, preferred_element_type=F32)
        decay = jnp.exp((cum[:, h : h + 1] - cum_t[h : h + 1, :]) + bias)
        weights = (scores * decay).astype(BF16)
        intra_ref[:, cols] = jnp.dot(weights, va, preferred_element_type=F32)


def gate_kernel(heads, gate_ref, gain_ref, out_ref):
    for h in range(heads):
        cols = head_cols(h)
        gate = 1.0 / (1.0 + jnp.exp(-gate_ref[:, cols].astype(F32)))
        out_ref[:, cols] = gate * gain_ref[:, cols]


def inter_kernel(group, heads, order, decay_ref, qa_ref, intra_ref, *rest):
    parts, (lin_ref, squares_ref, states) = rest[:group], rest[group:]
    tokens = qa_ref.shape[0]
    per = heads // group
    rank = my_rank(group)
    for s, part in zip(order, parts):
        states[dyn(rank ^ s, per * HD), :] = part[...]
    decay = decay_ref[...]
    acc = jnp.zeros((tokens, HD), F32)
    for h in range(heads):
        cols = head_cols(h)
        state = states[h * HD : (h + 1) * HD, :]
        inter = jnp.dot(qa_ref[:, cols], state, preferred_element_type=F32)
        lin = intra_ref[:, cols] + inter * decay[:, h : h + 1]
        lin_ref[:, cols] = lin
        acc += lin * lin
    ones = jnp.ones((8, HD), F32)
    squares_ref[...] = lax.dot_general(ones, acc, NT, precision=HIGH, preferred_element_type=F32)


def results_kernel(columns, parts, attended_ref, lin_ref, gain_ref, *rest):
    squares, (mixed_out, attended_out, mixed_ref, sems) = rest[:-4], rest[-4:]
    first = pltpu.make_async_copy(attended_ref, attended_out, sems.at[parts])
    first.start()
    total = squares[0][...]
    for part in squares[1:]:
        total = total + part[...]
    inv = jnp.transpose(lax.rsqrt(total / columns + EPS))[:, 0:1]
    width = lin_ref.shape[1] // parts
    copies = []
    for i in range(parts):
        cols = slice(i * width, (i + 1) * width)
        mixed_ref[:, cols] = (lin_ref[:, cols] * inv * gain_ref[:, cols]).astype(BF16)
        copies.append(
            pltpu.make_async_copy(mixed_ref.at[:, cols], mixed_out.at[:, cols], sems.at[i])
        )
        copies[-1].start()
    for copy in copies:
        copy.wait()
    first.wait()


def softmax_bias(group, sides, order_ref, bias):
    tokens, span = bias.shape[0], bias.shape[1] // len(sides)
    groups = span // tokens
    me = lax.axis_index("ctx")
    rank, mine = lax.rem(me, group), lax.div(me, group)
    qpos = order_ref[0] * tokens + lax.broadcasted_iota(jnp.int32, (tokens, tokens), 0)
    kpos = lax.broadcasted_iota(jnp.int32, (tokens, tokens), 1)
    for i, s in enumerate(sides):
        for d in range(groups):
            place = lax.rem(mine + groups - d, groups) * group + (rank ^ s)
            at = i * span + d * tokens
            bias[:, at : at + tokens] = jnp.where(place * tokens + kpos <= qpos, 0.0, -1e30)


def softmax_values(held, g, kv_heads, values):
    span = held[0].shape[0]
    values[:, HD:] = jnp.ones((span * len(held), HD), BF16)
    for i, ref in enumerate(held):
        values[i * span : (i + 1) * span, :HD] = ref[:, head_cols(kv_heads + g)]


def softmax_scores(query, held, g, bias):
    raw = [
        lax.dot_general(query, ref[:, head_cols(g)], NT, preferred_element_type=F32) for ref in held
    ]
    raw = jnp.concatenate(raw, axis=1)
    raw = raw.reshape(-1, *bias.shape) + bias[...][None]
    return raw.reshape(-1, bias.shape[1])


def stacked(ref, columns):
    return jnp.concatenate([ref[:, cols] for cols in columns], axis=0)


SCORE = math.log2(math.e) / math.sqrt(HD)


def softmax_first_kernel(group, sides, kv_heads, pack, order_ref, q_ref, *rest):
    arrays, rest = rest[: len(sides)], rest[len(sides) :]
    acc_ref, tops, (values, bias) = rest[0], rest[1:-2], rest[-2:]
    tokens = q_ref.shape[0]
    share = q_ref.shape[1] // HD // kv_heads
    softmax_bias(group, sides, order_ref, bias)
    for g in range(kv_heads):
        softmax_values(arrays, g, kv_heads, values)
        for j in range(0, share, pack):
            heads = range(g * share + j, g * share + j + pack)
            raw = softmax_scores(stacked(q_ref, map(head_cols, heads)), arrays, g, bias)
            top = jnp.max(raw, axis=-1, keepdims=True)
            probs = jnp.exp2((raw - top) * SCORE).astype(BF16)
            acc = jnp.dot(probs, values[...], preferred_element_type=F32)
            for i, h in enumerate(heads):
                rows = slice(i * tokens, (i + 1) * tokens)
                acc_ref[:, 2 * h * HD : 2 * (h + 1) * HD] = acc[rows]
                tops[g][:, j + i : j + i + 1] = top[rows]


def softmax_last_kernel(group, sides, kv_heads, pack, order_ref, q_ref, *rest):
    arrays, rest = rest[: len(sides)], rest[len(sides) :]
    acc_ref, tops, (out_ref, values, bias) = rest[0], rest[1:-3], rest[-3:]
    tokens = q_ref.shape[0]
    share = q_ref.shape[1] // HD // kv_heads
    softmax_bias(group, sides, order_ref, bias)
    for g in range(kv_heads):
        softmax_values(arrays, g, kv_heads, values)
        for j in range(0, share, pack):
            heads = range(g * share + j, g * share + j + pack)
            raw = softmax_scores(stacked(q_ref, map(head_cols, heads)), arrays, g, bias)
            old = stacked(tops[g], [slice(j + i, j + i + 1) for i in range(pack)])
            top = jnp.maximum(old, jnp.max(raw, axis=-1, keepdims=True))
            probs = jnp.exp2((raw - top) * SCORE).astype(BF16)
            acc = jnp.dot(probs, values[...], preferred_element_type=F32)
            held = stacked(acc_ref, [slice(2 * h * HD, 2 * (h + 1) * HD) for h in heads])
            acc += held * jnp.exp2((old - top) * SCORE)
            out = (acc[:, :HD] * inverse(acc[:, HD:])).astype(BF16)
            for i, h in enumerate(heads):
                out_ref[:, head_cols(h)] = out[i * tokens : (i + 1) * tokens]


def call(
    kernel, name, outs, args, scratch=(), flops=0, exps=0, limit=16, specs=None, after=(), **more
):
    size = sum(math.prod(x.shape) * x.dtype.itemsize for x in list(args) + list(outs))
    more.setdefault("out_specs", [VMEM for _ in outs])
    specs = list(specs or [VMEM for _ in args]) + [HBM for _ in after]
    count = len(args)

    def run(*refs):
        kernel(*refs[:count], *refs[count + len(after) :])

    return pl.pallas_call(
        run,
        name=name,
        out_shape=list(outs),
        in_specs=specs,
        scratch_shapes=list(scratch),
        cost_estimate=pl.CostEstimate(flops=flops, bytes_accessed=size, transcendentals=exps),
        compiler_params=pltpu.CompilerParams(vmem_limit_bytes=limit * MIB),
        **more,
    )(*args, *after)


def body(q_lin, k_lin, v_lin, log_decay, gate, norm_gain, queries, keys, values, order):
    tokens, width = q_lin.shape
    heads = log_decay.shape[0]
    kv_width = keys.shape[1]
    kv_heads = kv_width // HD
    n, nh = lax.axis_size("ctx"), lax.axis_size("head")
    group = 4
    groups = n // group
    per = heads // group
    rows = per * HD + 16
    cube = tokens * width * HD
    shape = jax.ShapeDtypeStruct

    def swap(x, s):
        return lax.ppermute(x, "ctx", [(c, c ^ s) for c in range(n)])

    def ahead(x, d):
        return lax.ppermute(x, "ctx", [(c, (c + d * group) % n) for c in range(n)])

    tri, bias = call(
        triangle_kernel, "triangle", [shape((tokens, tokens), F32)] * 2, (), flops=1 << 31
    )
    (kv,) = call(
        beside_kernel,
        "keys_beside_values",
        [shape((tokens, 2 * kv_width), BF16)],
        (keys, values),
        after=(tri,),
    )
    far = [ahead(kv, d) for d in range(1, groups)]

    to, back = (0, 2, 1, 3), (0, 3, 2, 1)

    def states(s):
        return call(
            functools.partial(state_kernel, group, per, s),
            "states_%d" % s,
            [shape((rows, HD), BF16)],
            (tri, log_decay, k_lin, v_lin),
            flops=4 * cube // group,
            exps=2 * tokens * width // group,
        )[0]

    split = n - group if groups > 1 else n

    def swap_among(x, s, first, last):
        return lax.ppermute(x, "ctx", [(c, c ^ s) for c in range(first, last)])

    added = {s: states(s) for s in to[1:]}
    mine = states(0)
    pays = [mine] + [swap_among(added[s], s, 0, split) for s in to[1:]]
    ends = [swap_among(added[s], s, split, n) for s in to[1:]] if groups > 1 else []

    (gain,) = call(
        functools.partial(gate_kernel, heads),
        "gate_gain",
        [shape((tokens, width), F32)],
        (gate, norm_gain.reshape(1, width)),
        flops=1 << 30,
        exps=tokens * width,
        after=far,
    )

    slots = pltpu.VMEM((group, rows, HD), BF16)
    carry = ()
    if groups > 1:
        (total,) = call(
            functools.partial(total_kernel, group, per, to),
            "group_state",
            [shape((rows, HD), BF16)],
            pays,
            [slots],
            flops=2 * per * HD * HD * group,
            after=(gain,),
        )
        before = ahead(total, 1)
        shift = 1
        while shift < groups - 1:
            mine = lax.div(lax.axis_index("ctx"), group)
            later = jnp.where(mine >= 1, before, 0).astype(F32)
            earlier = ahead(later.astype(BF16), shift)
            earlier = jnp.where(mine >= shift + 1, earlier, 0).astype(F32)
            step = later[per * HD :][:per] + later[per * HD + 8 :][:per]
            prior = earlier[per * HD :][:per] + earlier[per * HD + 8 :][:per]
            state = later[: per * HD] + jnp.repeat(step, HD, axis=0) * earlier[: per * HD]
            both = jnp.where(mine >= shift + 1, step * prior, step)
            high = both.astype(BF16).astype(F32)
            pad = jnp.zeros((8 - per, HD), F32)
            before = jnp.concatenate([state, high, pad, both - high, pad], axis=0).astype(BF16)
            shift *= 2
        carry = (before,)
    intra, qa, decay = call(
        functools.partial(intra_kernel, heads),
        "intra_block",
        [shape((tokens, width), F32), shape((tokens, width), BF16), shape((tokens, heads), F32)],
        (tri, bias, log_decay, q_lin, k_lin, v_lin),
        flops=4 * cube,
        exps=4 * tokens * width,
        after=(total,) if groups > 1 else (),
    )
    prefixes = call(
        functools.partial(prefix_kernel, group, per, to, bool(carry)),
        "prefix_states",
        [shape((per * HD, HD), BF16)] * group,
        (*pays, *ends, *carry),
        [slots, pltpu.VMEM((group, per * HD, HD), BF16)],
        flops=1 << 33,
        after=(intra,),
    )
    prefixes = [swap(prefixes[s], s) if s else prefixes[s] for s in back]

    (own,) = call(
        stack_kernel,
        "stack_keys_values",
        [shape((groups * tokens, kv.shape[1]), BF16)],
        (kv, *far),
        after=(total,) if groups > 1 else (),
        flops=1 << 32,
    )
    side, near = swap(own, 2), swap(own, 1)
    share = width // kv_heads
    pack = 2 if share // HD % 2 == 0 else 1
    span = own.shape[0]
    room = 24 + 48 * span * tokens * 4 // MIB
    smem = pl.BlockSpec(memory_space=pltpu.SMEM)

    def scratch(count):
        keys = count * span
        return [pltpu.VMEM((keys, 2 * HD), BF16), pltpu.VMEM((tokens, keys), F32)]

    acc, *tops = call(
        functools.partial(softmax_first_kernel, group, (0, 2, 1), kv_heads, pack),
        "softmax_first",
        [shape((tokens, 2 * width), F32)] + [shape((tokens, share // HD), F32)] * kv_heads,
        (order, queries, own, side, near),
        scratch(3),
        flops=12 * tokens * width * span,
        exps=3 * tokens * span * width // HD,
        limit=room,
        specs=[smem] + [VMEM] * 4,
    )
    half = shape((own.shape[0] // 2, own.shape[1]), BF16)
    upper, under = call(halves_kernel, "sent_on", [half] * 2, (side, near))
    across = jnp.concatenate([swap(upper, 1), swap(under, 2)])
    (attended,) = call(
        functools.partial(softmax_last_kernel, group, (3,), kv_heads, pack),
        "softmax_last",
        [shape((tokens, width), BF16)],
        (order, queries, across, acc, *tops),
        scratch(1),
        flops=4 * tokens * width * span,
        exps=tokens * span * width // HD,
        limit=room,
        specs=[smem] + [VMEM] * (3 + kv_heads),
    )

    lin, squares = call(
        functools.partial(inter_kernel, group, heads, back),
        "inter_block",
        [shape((tokens, width), F32), shape((8, tokens), F32)],
        (decay, qa, intra, *prefixes),
        [pltpu.VMEM((heads * HD, HD), BF16)],
        flops=2 * cube,
        after=tops[:1],
    )
    if nh & (nh - 1) == 0:
        turns = [[(i, i ^ d) for i in range(nh)] for d in range(nh - 1, 0, -1)]
    else:
        turns = [[(i, (i + d) % nh) for i in range(nh)] for d in range(1, nh)]
    parts = [squares] + [lax.ppermute(squares, "head", turn) for turn in turns]
    pieces = 4 if width % (4 * HD) == 0 else 1
    return call(
        functools.partial(results_kernel, float(width * nh), pieces),
        "results",
        [shape((tokens, width), BF16)] * 2,
        (attended, lin, gain, *parts),
        [pltpu.VMEM((tokens, width), BF16), pltpu.SemaphoreType.DMA((pieces + 1,))],
        flops=4 * tokens * width,
        out_specs=[HBM] * 2,
    )


def solution(mesh):
    return jax.shard_map(
        body,
        mesh=mesh,
        in_specs=(
            P("ctx", "head"),
            P("ctx", "head"),
            P("ctx", "head"),
            P("head", "ctx"),
            P("ctx", "head"),
            P("head"),
            P("ctx", "head"),
            P("ctx", "head"),
            P("ctx", "head"),
            P("ctx"),
        ),
        out_specs=(P("ctx", "head"), P("ctx", "head")),
        check_vma=False,
    )
```

```python
import functools
import math

import jax
import jax.numpy as jnp
from jax import lax
from jax.experimental import pallas as pl
from jax.experimental.pallas import tpu as pltpu
from jax.sharding import PartitionSpec as P

HD = 128
EPS = 1e-06
HIGH = lax.Precision.HIGHEST
F32 = jnp.float32
BF16 = jnp.bfloat16
NT = (((1,), (1,)), ((), ()))
TN = (((0,), (0,)), ((), ()))
MIB = 1 << 20
VMEM = pl.BlockSpec(memory_space=pltpu.VMEM)
HBM = pl.BlockSpec(memory_space=pltpu.HBM)


def inverse(x):
    guess = pl.reciprocal(x, approx=True)
    return guess * (2.0 - x * guess)


def silu16(x):
    x = x.astype(F32)
    return (x / (1.0 + jnp.exp(-x))).astype(BF16)


def lower_ones(size):
    rows = lax.broadcasted_iota(jnp.int32, (size, size), 0)
    cols = lax.broadcasted_iota(jnp.int32, (size, size), 1)
    return rows >= cols


def head_cols(h):
    return slice(h * HD, (h + 1) * HD)


def my_rank(group):
    return lax.rem(lax.axis_index("ctx"), group)


def dyn(index, size):
    return pl.ds(pl.multiple_of(index * size, size), size)


def triangle_kernel(ones_ref, bias_ref):
    lower = lower_ones(ones_ref.shape[0])
    ones_ref[...] = lower.astype(F32)
    bias_ref[...] = jnp.where(lower, 0.0, -1e30)


def decay_weights(tri_ref, ld_ref):
    ld = ld_ref[...]
    cum = lax.dot_general(tri_ref[...], ld, NT, precision=HIGH, preferred_element_type=F32)
    return jnp.exp(cum[-1:, :] - cum), jnp.exp(jnp.sum(ld, axis=1, keepdims=True))


def owner_states(k, per, weight, total, k_ref, v_ref, out):
    for j in range(per):
        h = k * per + j
        ka = silu16(k_ref[:, head_cols(h)])
        va = silu16(v_ref[:, head_cols(h)])
        kdec = ka.astype(F32) * weight[:, h : h + 1]
        khigh = kdec.astype(BF16)
        klow = (kdec - khigh.astype(F32)).astype(BF16)
        state = lax.dot_general(khigh, va, TN, preferred_element_type=F32)
        state += lax.dot_general(klow, va, TN, preferred_element_type=F32)
        out[j * HD : (j + 1) * HD, :] = state.astype(BF16)
    mine = jnp.broadcast_to(total[k * per : (k + 1) * per], (per, HD))
    high = mine.astype(BF16).astype(F32)
    pad = [jnp.zeros((8 - per, HD), F32)] if per < 8 else []
    tail = jnp.concatenate([high, *pad, mine - high, *pad], axis=0)
    out[per * HD :, :] = tail.astype(BF16)


def state_kernel(group, per, s, tri_ref, ld_ref, k_ref, v_ref, out_ref):
    weight, total = decay_weights(tri_ref, ld_ref)
    dest = my_rank(group) ^ s
    for k in range(group):
        pl.when(dest == k)(
            functools.partial(owner_states, k, per, weight, total, k_ref, v_ref, out_ref)
        )


def beside_kernel(keys, values, out):
    width = keys.shape[1]
    out[:, :width] = keys[...]
    out[:, width:] = values[...]


def stack_kernel(*refs):
    tokens = refs[0].shape[0]
    for i, part in enumerate(refs[:-1]):
        refs[-1][i * tokens : (i + 1) * tokens, :] = part[...]


def halves_kernel(a_ref, b_ref, a_out, b_out):
    half = a_out.shape[0]
    a_out[...] = a_ref[:half, :]
    b_out[...] = b_ref[half:, :]


def decay_row(slots, k, base, j):
    tail = slots[k, base : base + 16, :].astype(F32)
    return tail[j : j + 1] + tail[8 + j : 9 + j]


def fill_slots(order, rank, pays, slots):
    for s, pay in zip(order, pays):
        slots[rank ^ s] = pay[...]


def total_kernel(group, per, order, *refs):
    pays, out, slots = refs[:group], refs[group], refs[group + 1]
    fill_slots(order, my_rank(group), pays, slots)
    base = per * HD
    tails = []
    for j in range(per):
        state = slots[0, j * HD : (j + 1) * HD, :].astype(F32)
        whole = decay_row(slots, 0, base, j)
        for k in range(1, group):
            decay = decay_row(slots, k, base, j)
            state = decay * state + slots[k, j * HD : (j + 1) * HD, :].astype(F32)
            whole = whole * decay
        out[j * HD : (j + 1) * HD, :] = state.astype(BF16)
        tails.append(whole)
    pad = [jnp.zeros((8 - per, HD), F32)] if per < 8 else []
    total = jnp.concatenate(tails + pad, axis=0)
    high = total.astype(BF16).astype(F32)
    out[base:, :] = jnp.concatenate([high, total - high], axis=0).astype(BF16)


def prefix_kernel(group, per, order, carried, *refs):
    pays, refs = refs[:group], refs[group:]
    carry = None
    if carried:
        carry, refs = refs[0], refs[1:]
    outs, slots, prefixes = refs[:group], refs[group], refs[group + 1]
    rank = my_rank(group)
    later = lax.axis_index("ctx") >= group
    fill_slots(order, rank, pays, slots)
    base = per * HD
    for j in range(per):
        rows = slice(j * HD, (j + 1) * HD)
        state = jnp.zeros((HD, HD), F32)
        if carried:
            state = jnp.where(later, carry[rows, :].astype(F32), state)
        prefixes[0, rows, :] = state.astype(BF16)
        for k in range(group - 1):
            state = decay_row(slots, k, base, j) * state + slots[k, rows, :].astype(F32)
            prefixes[k + 1, rows, :] = state.astype(BF16)
    for s in range(group):
        outs[s][...] = prefixes[rank ^ s]


def intra_kernel(heads, tri_ref, bias_ref, ld_ref, q_ref, k_ref, v_ref, gate_ref, gain_ref, *outs):
    intra_ref, qa_ref, gain_out, decay_out = outs
    ld = ld_ref[...]
    tri = tri_ref[...]
    bias = bias_ref[...]
    cum = lax.dot_general(tri, ld, NT, precision=HIGH, preferred_element_type=F32)
    cum_t = lax.dot_general(ld, tri, NT, precision=HIGH, preferred_element_type=F32)
    decay_out[...] = jnp.exp(cum)
    for h in range(heads):
        cols = head_cols(h)
        qa = silu16(q_ref[:, cols])
        qa_ref[:, cols] = qa
        ka = silu16(k_ref[:, cols])
        va = silu16(v_ref[:, cols])
        scores = lax.dot_general(qa, ka, NT, preferred_element_type=F32)
        decay = jnp.exp((cum[:, h : h + 1] - cum_t[h : h + 1, :]) + bias)
        weights = (scores * decay).astype(BF16)
        intra_ref[:, cols] = jnp.dot(weights, va, preferred_element_type=F32)
        gate = 1.0 / (1.0 + jnp.exp(-gate_ref[:, cols].astype(F32)))
        gain_out[:, cols] = gate * gain_ref[:, cols]


def inter_kernel(group, heads, order, decay_ref, qa_ref, intra_ref, *rest):
    parts, (lin_ref, squares_ref, states) = rest[:group], rest[group:]
    tokens = qa_ref.shape[0]
    per = heads // group
    rank = my_rank(group)
    for s, part in zip(order, parts):
        states[dyn(rank ^ s, per * HD), :] = part[...]
    decay = decay_ref[...]
    acc = jnp.zeros((tokens, HD), F32)
    for h in range(heads):
        cols = head_cols(h)
        state = states[h * HD : (h + 1) * HD, :]
        inter = jnp.dot(qa_ref[:, cols], state, preferred_element_type=F32)
        lin = intra_ref[:, cols] + inter * decay[:, h : h + 1]
        lin_ref[:, cols] = lin
        acc += lin * lin
    ones = jnp.ones((8, HD), F32)
    squares_ref[...] = lax.dot_general(ones, acc, NT, precision=HIGH, preferred_element_type=F32)


def results_kernel(columns, parts, attended_ref, lin_ref, gain_ref, *rest):
    squares, (mixed_out, attended_out, mixed_ref, sems) = rest[:-4], rest[-4:]
    first = pltpu.make_async_copy(attended_ref, attended_out, sems.at[parts])
    first.start()
    total = squares[0][...]
    for part in squares[1:]:
        total = total + part[...]
    inv = jnp.transpose(lax.rsqrt(total / columns + EPS))[:, 0:1]
    width = lin_ref.shape[1] // parts
    copies = []
    for i in range(parts):
        cols = slice(i * width, (i + 1) * width)
        mixed_ref[:, cols] = (lin_ref[:, cols] * inv * gain_ref[:, cols]).astype(BF16)
        copies.append(
            pltpu.make_async_copy(mixed_ref.at[:, cols], mixed_out.at[:, cols], sems.at[i])
        )
        copies[-1].start()
    for copy in copies:
        copy.wait()
    first.wait()


def softmax_bias(group, sides, order_ref, bias):
    tokens, span = bias.shape[0], bias.shape[1] // len(sides)
    groups = span // tokens
    me = lax.axis_index("ctx")
    rank, mine = lax.rem(me, group), lax.div(me, group)
    qpos = order_ref[0] * tokens + lax.broadcasted_iota(jnp.int32, (tokens, tokens), 0)
    kpos = lax.broadcasted_iota(jnp.int32, (tokens, tokens), 1)
    for i, s in enumerate(sides):
        for d in range(groups):
            place = lax.rem(mine + groups - d, groups) * group + (rank ^ s)
            at = i * span + d * tokens
            bias[:, at : at + tokens] = jnp.where(place * tokens + kpos <= qpos, 0.0, -1e30)


def softmax_values(held, g, kv_heads, values):
    span = held[0].shape[0]
    values[:, HD:] = jnp.ones((span * len(held), HD), BF16)
    for i, ref in enumerate(held):
        values[i * span : (i + 1) * span, :HD] = ref[:, head_cols(kv_heads + g)]


def softmax_scores(query, held, g, bias):
    raw = [
        lax.dot_general(query, ref[:, head_cols(g)], NT, preferred_element_type=F32) for ref in held
    ]
    raw = jnp.concatenate(raw, axis=1)
    raw = raw.reshape(-1, *bias.shape) + bias[...][None]
    return raw.reshape(-1, bias.shape[1])


def stacked(ref, columns):
    return jnp.concatenate([ref[:, cols] for cols in columns], axis=0)


SCORE = math.log2(math.e) / math.sqrt(HD)


def softmax_first_kernel(group, sides, kv_heads, pack, order_ref, q_ref, *rest):
    arrays, rest = rest[: len(sides)], rest[len(sides) :]
    acc_ref, tops, (values, bias) = rest[0], rest[1:-2], rest[-2:]
    tokens = q_ref.shape[0]
    share = q_ref.shape[1] // HD // kv_heads
    softmax_bias(group, sides, order_ref, bias)
    for g in range(kv_heads):
        softmax_values(arrays, g, kv_heads, values)
        for j in range(0, share, pack):
            heads = range(g * share + j, g * share + j + pack)
            raw = softmax_scores(stacked(q_ref, map(head_cols, heads)), arrays, g, bias)
            top = jnp.max(raw, axis=-1, keepdims=True)
            probs = jnp.exp2((raw - top) * SCORE).astype(BF16)
            acc = jnp.dot(probs, values[...], preferred_element_type=F32)
            for i, h in enumerate(heads):
                rows = slice(i * tokens, (i + 1) * tokens)
                acc_ref[:, 2 * h * HD : 2 * (h + 1) * HD] = acc[rows]
                tops[g][:, j + i : j + i + 1] = top[rows]


def softmax_last_kernel(group, sides, kv_heads, pack, order_ref, q_ref, *rest):
    arrays, rest = rest[: len(sides)], rest[len(sides) :]
    acc_ref, tops, (out_ref, values, bias) = rest[0], rest[1:-3], rest[-3:]
    tokens = q_ref.shape[0]
    share = q_ref.shape[1] // HD // kv_heads
    softmax_bias(group, sides, order_ref, bias)
    for g in range(kv_heads):
        softmax_values(arrays, g, kv_heads, values)
        for j in range(0, share, pack):
            heads = range(g * share + j, g * share + j + pack)
            raw = softmax_scores(stacked(q_ref, map(head_cols, heads)), arrays, g, bias)
            old = stacked(tops[g], [slice(j + i, j + i + 1) for i in range(pack)])
            top = jnp.maximum(old, jnp.max(raw, axis=-1, keepdims=True))
            probs = jnp.exp2((raw - top) * SCORE).astype(BF16)
            acc = jnp.dot(probs, values[...], preferred_element_type=F32)
            held = stacked(acc_ref, [slice(2 * h * HD, 2 * (h + 1) * HD) for h in heads])
            acc += held * jnp.exp2((old - top) * SCORE)
            out = (acc[:, :HD] * inverse(acc[:, HD:])).astype(BF16)
            for i, h in enumerate(heads):
                out_ref[:, head_cols(h)] = out[i * tokens : (i + 1) * tokens]


def call(
    kernel, name, outs, args, scratch=(), flops=0, exps=0, limit=16, specs=None, after=(), **more
):
    size = sum(math.prod(x.shape) * x.dtype.itemsize for x in list(args) + list(outs))
    more.setdefault("out_specs", [VMEM for _ in outs])
    specs = list(specs or [VMEM for _ in args]) + [HBM for _ in after]
    count = len(args)

    def run(*refs):
        kernel(*refs[:count], *refs[count + len(after) :])

    return pl.pallas_call(
        run,
        name=name,
        out_shape=list(outs),
        in_specs=specs,
        scratch_shapes=list(scratch),
        cost_estimate=pl.CostEstimate(flops=flops, bytes_accessed=size, transcendentals=exps),
        compiler_params=pltpu.CompilerParams(vmem_limit_bytes=limit * MIB),
        **more,
    )(*args, *after)


def body(q_lin, k_lin, v_lin, log_decay, gate, norm_gain, queries, keys, values, order):
    tokens, width = q_lin.shape
    heads = log_decay.shape[0]
    kv_width = keys.shape[1]
    kv_heads = kv_width // HD
    n, nh = lax.axis_size("ctx"), lax.axis_size("head")
    group = 4
    groups = n // group
    per = heads // group
    rows = per * HD + 16
    cube = tokens * width * HD
    shape = jax.ShapeDtypeStruct

    def swap(x, s):
        return lax.ppermute(x, "ctx", [(c, c ^ s) for c in range(n)])

    def ahead(x, d):
        return lax.ppermute(x, "ctx", [(c, (c + d * group) % n) for c in range(n)])

    tri, bias = call(
        triangle_kernel, "triangle", [shape((tokens, tokens), F32)] * 2, (), flops=1 << 31
    )
    (kv,) = call(
        beside_kernel,
        "keys_beside_values",
        [shape((tokens, 2 * kv_width), BF16)],
        (keys, values),
        after=(tri,),
    )
    far = [ahead(kv, d) for d in range(1, groups)]

    to, back = (0, 2, 3, 1), (0, 3, 2, 1)

    def states(s):
        return call(
            functools.partial(state_kernel, group, per, s),
            "states_%d" % s,
            [shape((rows, HD), BF16)],
            (tri, log_decay, k_lin, v_lin),
            flops=4 * cube // group,
            exps=2 * tokens * width // group,
        )[0]

    pays = {s: swap(states(s), s) for s in to[1:]}
    pays[0] = states(0)
    pays = [pays[s] for s in to]

    intra, qa, gain, decay = call(
        functools.partial(intra_kernel, heads),
        "intra_block",
        [
            shape((tokens, width), F32),
            shape((tokens, width), BF16),
            shape((tokens, width), F32),
            shape((tokens, heads), F32),
        ],
        (tri, bias, log_decay, q_lin, k_lin, v_lin, gate, norm_gain.reshape(1, width)),
        flops=4 * cube,
        exps=4 * tokens * width,
        after=far,
    )

    slots = pltpu.VMEM((group, rows, HD), BF16)
    carry = ()
    if groups > 1:
        (total,) = call(
            functools.partial(total_kernel, group, per, to),
            "group_state",
            [shape((rows, HD), BF16)],
            pays,
            [slots],
            flops=2 * per * HD * HD * group,
            after=(intra,),
        )
        before = ahead(total, 1)
        shift = 1
        while shift < groups - 1:
            mine = lax.div(lax.axis_index("ctx"), group)
            later = jnp.where(mine >= 1, before, 0).astype(F32)
            earlier = ahead(later.astype(BF16), shift)
            earlier = jnp.where(mine >= shift + 1, earlier, 0).astype(F32)
            step = later[per * HD :][:per] + later[per * HD + 8 :][:per]
            prior = earlier[per * HD :][:per] + earlier[per * HD + 8 :][:per]
            state = later[: per * HD] + jnp.repeat(step, HD, axis=0) * earlier[: per * HD]
            both = jnp.where(mine >= shift + 1, step * prior, step)
            high = both.astype(BF16).astype(F32)
            pad = jnp.zeros((8 - per, HD), F32)
            before = jnp.concatenate([state, high, pad, both - high, pad], axis=0).astype(BF16)
            shift *= 2
        carry = (before,)
    prefixes = call(
        functools.partial(prefix_kernel, group, per, to, bool(carry)),
        "prefix_states",
        [shape((per * HD, HD), BF16)] * group,
        (*pays, *carry),
        [slots, pltpu.VMEM((group, per * HD, HD), BF16)],
        flops=1 << 33,
    )
    prefixes = [swap(prefixes[s], s) if s else prefixes[s] for s in back]

    (own,) = call(
        stack_kernel,
        "stack_keys_values",
        [shape((groups * tokens, kv.shape[1]), BF16)],
        (kv, *far),
        after=(total,) if groups > 1 else (intra,),
        flops=1 << 32,
    )
    side, near = swap(own, 2), swap(own, 1)
    share = width // kv_heads
    pack = 2 if share // HD % 2 == 0 else 1
    span = own.shape[0]
    room = 24 + 48 * span * tokens * 4 // MIB
    smem = pl.BlockSpec(memory_space=pltpu.SMEM)

    def scratch(count):
        keys = count * span
        return [pltpu.VMEM((keys, 2 * HD), BF16), pltpu.VMEM((tokens, keys), F32)]

    acc, *tops = call(
        functools.partial(softmax_first_kernel, group, (0, 2, 1), kv_heads, pack),
        "softmax_first",
        [shape((tokens, 2 * width), F32)] + [shape((tokens, share // HD), F32)] * kv_heads,
        (order, queries, own, side, near),
        scratch(3),
        flops=12 * tokens * width * span,
        exps=3 * tokens * span * width // HD,
        limit=room,
        specs=[smem] + [VMEM] * 4,
    )
    half = shape((own.shape[0] // 2, own.shape[1]), BF16)
    upper, under = call(halves_kernel, "sent_on", [half] * 2, (side, near))
    across = jnp.concatenate([swap(upper, 1), swap(under, 2)])
    (attended,) = call(
        functools.partial(softmax_last_kernel, group, (3,), kv_heads, pack),
        "softmax_last",
        [shape((tokens, width), BF16)],
        (order, queries, across, acc, *tops),
        scratch(1),
        flops=4 * tokens * width * span,
        exps=tokens * span * width // HD,
        limit=room,
        specs=[smem] + [VMEM] * (3 + kv_heads),
    )

    lin, squares = call(
        functools.partial(inter_kernel, group, heads, back),
        "inter_block",
        [shape((tokens, width), F32), shape((8, tokens), F32)],
        (decay, qa, intra, *prefixes),
        [pltpu.VMEM((heads * HD, HD), BF16)],
        flops=2 * cube,
        after=tops[:1],
    )
    if nh & (nh - 1) == 0:
        turns = [[(i, i ^ d) for i in range(nh)] for d in range(nh - 1, 0, -1)]
    else:
        turns = [[(i, (i + d) % nh) for i in range(nh)] for d in range(1, nh)]
    parts = [squares] + [lax.ppermute(squares, "head", turn) for turn in turns]
    pieces = 4 if width % (4 * HD) == 0 else 1
    return call(
        functools.partial(results_kernel, float(width * nh), pieces),
        "results",
        [shape((tokens, width), BF16)] * 2,
        (attended, lin, gain, *parts),
        [pltpu.VMEM((tokens, width), BF16), pltpu.SemaphoreType.DMA((pieces + 1,))],
        flops=4 * tokens * width,
        out_specs=[HBM] * 2,
    )


def solution(mesh):
    return jax.shard_map(
        body,
        mesh=mesh,
        in_specs=(
            P("ctx", "head"),
            P("ctx", "head"),
            P("ctx", "head"),
            P("head", "ctx"),
            P("ctx", "head"),
            P("head"),
            P("ctx", "head"),
            P("ctx", "head"),
            P("ctx", "head"),
            P("ctx"),
        ),
        out_specs=(P("ctx", "head"), P("ctx", "head")),
        check_vma=False,
    )
```

```python
import functools
import math

import jax
import jax.numpy as jnp
from jax import lax
from jax.experimental import pallas as pl
from jax.experimental.pallas import tpu as pltpu
from jax.sharding import PartitionSpec as P

HD = 128
EPS = 1e-06
HIGH = lax.Precision.HIGHEST
F32 = jnp.float32
BF16 = jnp.bfloat16
NT = (((1,), (1,)), ((), ()))
TN = (((0,), (0,)), ((), ()))
MIB = 1 << 20
VMEM = pl.BlockSpec(memory_space=pltpu.VMEM)
HBM = pl.BlockSpec(memory_space=pltpu.HBM)


def inverse(x):
    guess = pl.reciprocal(x, approx=True)
    return guess * (2.0 - x * guess)


def silu16(x):
    x = x.astype(F32)
    return (x / (1.0 + jnp.exp(-x))).astype(BF16)


def lower_ones(size):
    rows = lax.broadcasted_iota(jnp.int32, (size, size), 0)
    cols = lax.broadcasted_iota(jnp.int32, (size, size), 1)
    return rows >= cols


def head_cols(h):
    return slice(h * HD, (h + 1) * HD)


def my_rank(group):
    return lax.rem(lax.axis_index("ctx"), group)


def dyn(index, size):
    return pl.ds(pl.multiple_of(index * size, size), size)


def triangle_kernel(ones_ref, bias_ref):
    lower = lower_ones(ones_ref.shape[0])
    ones_ref[...] = lower.astype(F32)
    bias_ref[...] = jnp.where(lower, 0.0, -1e30)


def state_kernel(group, heads, tri_ref, ld_ref, k_ref, v_ref, *rest):
    outs, (ka_ref, va_ref, states, totals) = rest[:group], rest[group:]
    tokens = k_ref.shape[0]
    per = heads // group
    rank = my_rank(group)
    ld = ld_ref[...]
    cum = lax.dot_general(tri_ref[...], ld, NT, precision=HIGH, preferred_element_type=F32)
    weight = jnp.exp(cum[tokens - 1 : tokens, :] - cum)
    total = jnp.broadcast_to(jnp.exp(jnp.sum(ld, axis=1, keepdims=True)), (heads, HD))
    high = total.astype(BF16).astype(F32)
    low = total - high
    totals[...] = jnp.zeros_like(totals)
    for k in range(group):
        totals[k * 16 : k * 16 + per, :] = high[k * per : (k + 1) * per]
        totals[k * 16 + 8 : k * 16 + 8 + per, :] = low[k * per : (k + 1) * per]
    for h in range(heads):
        ka = silu16(k_ref[:, head_cols(h)])
        va = silu16(v_ref[:, head_cols(h)])
        ka_ref[:, head_cols(h)] = ka
        va_ref[:, head_cols(h)] = va
        kdec = ka.astype(F32) * weight[:, h : h + 1]
        khigh = kdec.astype(BF16)
        klow = (kdec - khigh.astype(F32)).astype(BF16)
        state = lax.dot_general(khigh, va, TN, preferred_element_type=F32)
        state += lax.dot_general(klow, va, TN, preferred_element_type=F32)
        states[h * HD : (h + 1) * HD, :] = state.astype(BF16)
    for s in range(group):
        dest = rank ^ s
        outs[s][: per * HD, :] = states[dyn(dest, per * HD), :]
        outs[s][per * HD :, :] = totals[dyn(dest, 16), :].astype(BF16)


def beside_kernel(keys, values, out):
    width = keys.shape[1]
    out[:, :width] = keys[...]
    out[:, width:] = values[...]


def stack_kernel(*refs):
    tokens = refs[0].shape[0]
    for i, part in enumerate(refs[:-1]):
        refs[-1][i * tokens : (i + 1) * tokens, :] = part[...]


def halves_kernel(a_ref, b_ref, a_out, b_out):
    half = a_out.shape[0]
    a_out[...] = a_ref[:half, :]
    b_out[...] = b_ref[half:, :]


def decay_row(slots, k, base, j):
    tail = slots[k, base : base + 16, :].astype(F32)
    return tail[j : j + 1] + tail[8 + j : 9 + j]


def sent(group):
    return [0, *range(group - 1, 0, -1)]


def fill_slots(group, rank, pays, slots):
    for s, pay in zip(sent(group), pays):
        slots[rank ^ s] = pay[...]


def total_kernel(group, per, *refs):
    pays, out, slots = refs[:group], refs[group], refs[group + 1]
    fill_slots(group, my_rank(group), pays, slots)
    base = per * HD
    tails = []
    for j in range(per):
        state = slots[0, j * HD : (j + 1) * HD, :].astype(F32)
        whole = decay_row(slots, 0, base, j)
        for k in range(1, group):
            decay = decay_row(slots, k, base, j)
            state = decay * state + slots[k, j * HD : (j + 1) * HD, :].astype(F32)
            whole = whole * decay
        out[j * HD : (j + 1) * HD, :] = state.astype(BF16)
        tails.append(whole)
    pad = [jnp.zeros((8 - per, HD), F32)] if per < 8 else []
    total = jnp.concatenate(tails + pad, axis=0)
    high = total.astype(BF16).astype(F32)
    out[base:, :] = jnp.concatenate([high, total - high], axis=0).astype(BF16)


def prefix_kernel(group, per, carried, *refs):
    pays, refs = refs[:group], refs[group:]
    carry = None
    if carried:
        carry, refs = refs[0], refs[1:]
    outs, slots, prefixes = refs[:group], refs[group], refs[group + 1]
    rank = my_rank(group)
    later = lax.axis_index("ctx") >= group
    fill_slots(group, rank, pays, slots)
    base = per * HD
    for j in range(per):
        rows = slice(j * HD, (j + 1) * HD)
        state = jnp.zeros((HD, HD), F32)
        if carried:
            state = jnp.where(later, carry[rows, :].astype(F32), state)
        prefixes[0, rows, :] = state.astype(BF16)
        for k in range(group - 1):
            state = decay_row(slots, k, base, j) * state + slots[k, rows, :].astype(F32)
            prefixes[k + 1, rows, :] = state.astype(BF16)
    for s in range(group):
        outs[s][...] = prefixes[rank ^ s]


def intra_kernel(heads, tri_ref, bias_ref, ld_ref, q_ref, ka_ref, va_ref, gate_ref, gain_ref, *outs):
    intra_ref, qa_ref, gain_out, decay_out = outs
    ld = ld_ref[...]
    tri = tri_ref[...]
    bias = bias_ref[...]
    cum = lax.dot_general(tri, ld, NT, precision=HIGH, preferred_element_type=F32)
    cum_t = lax.dot_general(ld, tri, NT, precision=HIGH, preferred_element_type=F32)
    decay_out[...] = jnp.exp(cum)
    for h in range(heads):
        cols = head_cols(h)
        qa = silu16(q_ref[:, cols])
        qa_ref[:, cols] = qa
        scores = lax.dot_general(qa, ka_ref[:, cols], NT, preferred_element_type=F32)
        decay = jnp.exp((cum[:, h : h + 1] - cum_t[h : h + 1, :]) + bias)
        weights = (scores * decay).astype(BF16)
        intra_ref[:, cols] = jnp.dot(weights, va_ref[:, cols], preferred_element_type=F32)
        gate = 1.0 / (1.0 + jnp.exp(-gate_ref[:, cols].astype(F32)))
        gain_out[:, cols] = gate * gain_ref[:, cols]


def inter_kernel(group, heads, decay_ref, qa_ref, intra_ref, *rest):
    parts, (lin_ref, squares_ref, states) = rest[:group], rest[group:]
    tokens = qa_ref.shape[0]
    per = heads // group
    rank = my_rank(group)
    for s, part in zip(sent(group), parts):
        states[dyn(rank ^ s, per * HD), :] = part[...]
    decay = decay_ref[...]
    acc = jnp.zeros((tokens, HD), F32)
    for h in range(heads):
        cols = head_cols(h)
        state = states[h * HD : (h + 1) * HD, :]
        inter = jnp.dot(qa_ref[:, cols], state, preferred_element_type=F32)
        lin = intra_ref[:, cols] + inter * decay[:, h : h + 1]
        lin_ref[:, cols] = lin
        acc += lin * lin
    ones = jnp.ones((8, HD), F32)
    squares_ref[...] = lax.dot_general(ones, acc, NT, precision=HIGH, preferred_element_type=F32)


def results_kernel(columns, parts, attended_ref, lin_ref, gain_ref, *rest):
    squares, (mixed_out, attended_out, mixed_ref, sems) = rest[:-4], rest[-4:]
    first = pltpu.make_async_copy(attended_ref, attended_out, sems.at[parts])
    first.start()
    total = squares[0][...]
    for part in squares[1:]:
        total = total + part[...]
    inv = jnp.transpose(lax.rsqrt(total / columns + EPS))[:, 0:1]
    width = lin_ref.shape[1] // parts
    copies = []
    for i in range(parts):
        cols = slice(i * width, (i + 1) * width)
        mixed_ref[:, cols] = (lin_ref[:, cols] * inv * gain_ref[:, cols]).astype(BF16)
        copies.append(
            pltpu.make_async_copy(mixed_ref.at[:, cols], mixed_out.at[:, cols], sems.at[i])
        )
        copies[-1].start()
    for copy in copies:
        copy.wait()
    first.wait()


def softmax_bias(group, sides, order_ref, bias):
    tokens, span = bias.shape[0], bias.shape[1] // len(sides)
    groups = span // tokens
    me = lax.axis_index("ctx")
    rank, mine = lax.rem(me, group), lax.div(me, group)
    qpos = order_ref[0] * tokens + lax.broadcasted_iota(jnp.int32, (tokens, tokens), 0)
    kpos = lax.broadcasted_iota(jnp.int32, (tokens, tokens), 1)
    for i, s in enumerate(sides):
        for d in range(groups):
            place = lax.rem(mine + groups - d, groups) * group + (rank ^ s)
            at = i * span + d * tokens
            bias[:, at : at + tokens] = jnp.where(place * tokens + kpos <= qpos, 0.0, -1e30)


def softmax_values(held, g, kv_heads, values):
    span = held[0].shape[0]
    values[:, HD:] = jnp.ones((span * len(held), HD), BF16)
    for i, ref in enumerate(held):
        values[i * span : (i + 1) * span, :HD] = ref[:, head_cols(kv_heads + g)]


def softmax_scores(query, held, g, bias):
    raw = [
        lax.dot_general(query, ref[:, head_cols(g)], NT, preferred_element_type=F32) for ref in held
    ]
    raw = jnp.concatenate(raw, axis=1)
    raw = raw.reshape(-1, *bias.shape) + bias[...][None]
    return raw.reshape(-1, bias.shape[1])


def stacked(ref, columns):
    return jnp.concatenate([ref[:, cols] for cols in columns], axis=0)


SCORE = math.log2(math.e) / math.sqrt(HD)


def softmax_first_kernel(group, sides, kv_heads, pack, order_ref, q_ref, *rest):
    arrays, rest = rest[: len(sides)], rest[len(sides) :]
    acc_ref, tops, (values, bias) = rest[0], rest[1:-2], rest[-2:]
    tokens = q_ref.shape[0]
    share = q_ref.shape[1] // HD // kv_heads
    softmax_bias(group, sides, order_ref, bias)
    for g in range(kv_heads):
        softmax_values(arrays, g, kv_heads, values)
        for j in range(0, share, pack):
            heads = range(g * share + j, g * share + j + pack)
            raw = softmax_scores(stacked(q_ref, map(head_cols, heads)), arrays, g, bias)
            top = jnp.max(raw, axis=-1, keepdims=True)
            probs = jnp.exp2((raw - top) * SCORE).astype(BF16)
            acc = jnp.dot(probs, values[...], preferred_element_type=F32)
            for i, h in enumerate(heads):
                rows = slice(i * tokens, (i + 1) * tokens)
                acc_ref[:, 2 * h * HD : 2 * (h + 1) * HD] = acc[rows]
                tops[g][:, head_cols(j + i)] = jnp.broadcast_to(top[rows], (tokens, HD))


def softmax_last_kernel(group, sides, kv_heads, pack, order_ref, q_ref, *rest):
    arrays, rest = rest[: len(sides)], rest[len(sides) :]
    acc_ref, tops, (out_ref, values, bias) = rest[0], rest[1:-3], rest[-3:]
    tokens = q_ref.shape[0]
    share = q_ref.shape[1] // HD // kv_heads
    softmax_bias(group, sides, order_ref, bias)
    for g in range(kv_heads):
        softmax_values(arrays, g, kv_heads, values)
        for j in range(0, share, pack):
            heads = range(g * share + j, g * share + j + pack)
            raw = softmax_scores(stacked(q_ref, map(head_cols, heads)), arrays, g, bias)
            old = stacked(tops[g], map(head_cols, range(j, j + pack)))
            top = jnp.maximum(old, jnp.max(raw, axis=-1, keepdims=True))
            spread = jnp.concatenate([top] * (raw.shape[1] // HD), axis=1)
            probs = jnp.exp2((raw - spread) * SCORE).astype(BF16)
            acc = jnp.dot(probs, values[...], preferred_element_type=F32)
            held = stacked(acc_ref, [slice(2 * h * HD, 2 * (h + 1) * HD) for h in heads])
            alpha = jnp.exp2((old - top) * SCORE)
            acc += held * jnp.concatenate([alpha, alpha], axis=1)
            out = (acc[:, :HD] * inverse(acc[:, HD:])).astype(BF16)
            for i, h in enumerate(heads):
                out_ref[:, head_cols(h)] = out[i * tokens : (i + 1) * tokens]


def call(
    kernel, name, outs, args, scratch=(), flops=0, exps=0, limit=16, specs=None, after=(), **more
):
    size = sum(math.prod(x.shape) * x.dtype.itemsize for x in list(args) + list(outs))
    more.setdefault("out_specs", [VMEM for _ in outs])
    specs = list(specs or [VMEM for _ in args]) + [HBM for _ in after]
    count = len(args)

    def run(*refs):
        kernel(*refs[:count], *refs[count + len(after) :])

    return pl.pallas_call(
        run,
        name=name,
        out_shape=list(outs),
        in_specs=specs,
        scratch_shapes=list(scratch),
        cost_estimate=pl.CostEstimate(flops=flops, bytes_accessed=size, transcendentals=exps),
        compiler_params=pltpu.CompilerParams(vmem_limit_bytes=limit * MIB),
        **more,
    )(*args, *after)


def body(q_lin, k_lin, v_lin, log_decay, gate, norm_gain, queries, keys, values, order):
    tokens, width = q_lin.shape
    heads = log_decay.shape[0]
    kv_width = keys.shape[1]
    kv_heads = kv_width // HD
    n, nh = lax.axis_size("ctx"), lax.axis_size("head")
    group = 4
    groups = n // group
    per = heads // group
    rows = per * HD + 16
    cube = tokens * width * HD
    shape = jax.ShapeDtypeStruct

    def swap(x, s):
        return lax.ppermute(x, "ctx", [(c, c ^ s) for c in range(n)])

    def swap_all(xs):
        return [swap(xs[s], s) if s else xs[s] for s in sent(group)]

    def ahead(x, d):
        return lax.ppermute(x, "ctx", [(c, (c + d * group) % n) for c in range(n)])

    tri, bias = call(
        triangle_kernel, "triangle", [shape((tokens, tokens), F32)] * 2, (), flops=1 << 31
    )
    (kv,) = call(
        beside_kernel,
        "keys_beside_values",
        [shape((tokens, 2 * kv_width), BF16)],
        (keys, values),
        after=(tri,),
    )
    far = [ahead(kv, d) for d in range(1, groups)]

    *pays, ka, va = call(
        functools.partial(state_kernel, group, heads),
        "block_states",
        [shape((rows, HD), BF16)] * group + [shape((tokens, width), BF16)] * 2,
        (tri, log_decay, k_lin, v_lin),
        [pltpu.VMEM((heads * HD, HD), BF16), pltpu.VMEM((group * 16, HD), F32)],
        flops=4 * cube,
        exps=2 * tokens * width,
    )
    pays = swap_all(pays)
    intra, qa, gain, decay = call(
        functools.partial(intra_kernel, heads),
        "intra_block",
        [
            shape((tokens, width), F32),
            shape((tokens, width), BF16),
            shape((tokens, width), F32),
            shape((tokens, heads), F32),
        ],
        (tri, bias, log_decay, q_lin, ka, va, gate, norm_gain.reshape(1, width)),
        flops=4 * cube,
        exps=4 * tokens * width,
    )

    slots = pltpu.VMEM((group, rows, HD), BF16)
    carry = ()
    if groups > 1:
        (total,) = call(
            functools.partial(total_kernel, group, per),
            "group_state",
            [shape((rows, HD), BF16)],
            pays,
            [slots],
            flops=2 * per * HD * HD * group,
            after=(intra,),
        )
        before = ahead(total, 1)
        shift = 1
        while shift < groups - 1:
            mine = lax.div(lax.axis_index("ctx"), group)
            later = jnp.where(mine >= 1, before, 0).astype(F32)
            earlier = ahead(later.astype(BF16), shift)
            earlier = jnp.where(mine >= shift + 1, earlier, 0).astype(F32)
            step = later[per * HD :][:per] + later[per * HD + 8 :][:per]
            prior = earlier[per * HD :][:per] + earlier[per * HD + 8 :][:per]
            state = later[: per * HD] + jnp.repeat(step, HD, axis=0) * earlier[: per * HD]
            both = jnp.where(mine >= shift + 1, step * prior, step)
            high = both.astype(BF16).astype(F32)
            pad = jnp.zeros((8 - per, HD), F32)
            before = jnp.concatenate([state, high, pad, both - high, pad], axis=0).astype(BF16)
            shift *= 2
        carry = (before,)
    prefixes = call(
        functools.partial(prefix_kernel, group, per, bool(carry)),
        "prefix_states",
        [shape((per * HD, HD), BF16)] * group,
        (*pays, *carry),
        [slots, pltpu.VMEM((group, per * HD, HD), BF16)],
        flops=1 << 33,
    )
    prefixes = swap_all(prefixes)

    (own,) = call(
        stack_kernel,
        "stack_keys_values",
        [shape((groups * tokens, kv.shape[1]), BF16)],
        (kv, *far),
        after=(total,) if groups > 1 else (intra,),
        flops=1 << 32,
    )
    side, near = swap(own, 2), swap(own, 1)
    half = shape((own.shape[0] // 2, own.shape[1]), BF16)
    upper, under = call(halves_kernel, "sent_on", [half] * 2, (side, near))
    across = jnp.concatenate([swap(upper, 1), swap(under, 2)])
    share = width // kv_heads
    pack = 2 if share // HD % 2 == 0 else 1
    span = own.shape[0]
    room = 24 + 48 * span * tokens * 4 // MIB
    smem = pl.BlockSpec(memory_space=pltpu.SMEM)

    def scratch(count):
        keys = count * span
        return [pltpu.VMEM((keys, 2 * HD), BF16), pltpu.VMEM((tokens, keys), F32)]

    acc, *tops = call(
        functools.partial(softmax_first_kernel, group, (0, 2, 1), kv_heads, pack),
        "softmax_first",
        [shape((tokens, 2 * width), F32)] + [shape((tokens, share), F32)] * kv_heads,
        (order, queries, own, side, near),
        scratch(3),
        flops=12 * tokens * width * span,
        exps=3 * tokens * span * width // HD,
        limit=room,
        specs=[smem] + [VMEM] * 4,
    )
    (attended,) = call(
        functools.partial(softmax_last_kernel, group, (3,), kv_heads, pack),
        "softmax_last",
        [shape((tokens, width), BF16)],
        (order, queries, across, acc, *tops),
        scratch(1),
        flops=4 * tokens * width * span,
        exps=tokens * span * width // HD,
        limit=room,
        specs=[smem] + [VMEM] * (3 + kv_heads),
    )

    lin, squares = call(
        functools.partial(inter_kernel, group, heads),
        "inter_block",
        [shape((tokens, width), F32), shape((8, tokens), F32)],
        (decay, qa, intra, *prefixes),
        [pltpu.VMEM((heads * HD, HD), BF16)],
        flops=2 * cube,
        after=tops[:1],
    )
    if nh & (nh - 1) == 0:
        turns = [[(i, i ^ d) for i in range(nh)] for d in range(nh - 1, 0, -1)]
    else:
        turns = [[(i, (i + d) % nh) for i in range(nh)] for d in range(1, nh)]
    parts = [squares] + [lax.ppermute(squares, "head", turn) for turn in turns]
    pieces = 4 if width % (4 * HD) == 0 else 1
    return call(
        functools.partial(results_kernel, float(width * nh), pieces),
        "results",
        [shape((tokens, width), BF16)] * 2,
        (attended, lin, gain, *parts),
        [pltpu.VMEM((tokens, width), BF16), pltpu.SemaphoreType.DMA((pieces + 1,))],
        flops=4 * tokens * width,
        out_specs=[HBM] * 2,
    )


def solution(mesh):
    return jax.shard_map(
        body,
        mesh=mesh,
        in_specs=(
            P("ctx", "head"),
            P("ctx", "head"),
            P("ctx", "head"),
            P("head", "ctx"),
            P("ctx", "head"),
            P("head"),
            P("ctx", "head"),
            P("ctx", "head"),
            P("ctx", "head"),
            P("ctx"),
        ),
        out_specs=(P("ctx", "head"), P("ctx", "head")),
        check_vma=False,
    )
```

```python
import functools
import math

import jax
import jax.numpy as jnp
from jax import lax
from jax.experimental import pallas as pl
from jax.experimental.pallas import tpu as pltpu
from jax.sharding import PartitionSpec as P

HD = 128
EPS = 1e-06
HIGH = lax.Precision.HIGHEST
F32 = jnp.float32
BF16 = jnp.bfloat16
NT = (((1,), (1,)), ((), ()))
MIB = 1 << 20
VMEM = pl.BlockSpec(memory_space=pltpu.VMEM)
HBM = pl.BlockSpec(memory_space=pltpu.HBM)


def inverse(x):
    guess = pl.reciprocal(x, approx=True)
    return guess * (2.0 - x * guess)


def silu16(x):
    x = x.astype(F32)
    return (x / (1.0 + jnp.exp(-x))).astype(BF16)


def lower_ones(size):
    rows = lax.broadcasted_iota(jnp.int32, (size, size), 0)
    cols = lax.broadcasted_iota(jnp.int32, (size, size), 1)
    return rows >= cols


def head_cols(h):
    return slice(h * HD, (h + 1) * HD)


def my_rank(group):
    return lax.rem(lax.axis_index("ctx"), group)


def dyn(index, size):
    return pl.ds(pl.multiple_of(index * size, size), size)


def triangle_kernel(ones_ref, bias_ref):
    lower = lower_ones(ones_ref.shape[0])
    ones_ref[...] = lower.astype(F32)
    bias_ref[...] = jnp.where(lower, 0.0, -1e30)


def state_kernel(group, heads, tri_ref, ld_ref, k_ref, v_ref, *rest):
    outs, (ka_ref, va_ref, states, totals) = rest[:group], rest[group:]
    tokens = k_ref.shape[0]
    per = heads // group
    rank = my_rank(group)
    ld = ld_ref[...]
    cum = lax.dot_general(ld, tri_ref[...], NT, precision=HIGH, preferred_element_type=F32)
    weight = jnp.exp(cum[:, tokens - 1 : tokens] - cum)
    total = jnp.broadcast_to(jnp.exp(jnp.sum(ld, axis=1, keepdims=True)), (heads, HD))
    high = total.astype(BF16).astype(F32)
    low = total - high
    totals[...] = jnp.zeros_like(totals)
    for k in range(group):
        totals[k * 16 : k * 16 + per, :] = high[k * per : (k + 1) * per]
        totals[k * 16 + 8 : k * 16 + 8 + per, :] = low[k * per : (k + 1) * per]
    for h in range(heads):
        ka = silu16(k_ref[:, head_cols(h)])
        va = silu16(v_ref[:, head_cols(h)])
        ka_ref[:, head_cols(h)] = ka
        va_ref[:, head_cols(h)] = va
        kdec = jnp.transpose(ka).astype(F32) * weight[h : h + 1, :]
        khigh = kdec.astype(BF16)
        klow = (kdec - khigh.astype(F32)).astype(BF16)
        state = jnp.dot(khigh, va, preferred_element_type=F32)
        state += jnp.dot(klow, va, preferred_element_type=F32)
        states[h * HD : (h + 1) * HD, :] = state.astype(BF16)
    for s in range(group):
        dest = rank ^ s
        outs[s][: per * HD, :] = states[dyn(dest, per * HD), :]
        outs[s][per * HD :, :] = totals[dyn(dest, 16), :].astype(BF16)


def beside_kernel(keys, values, out):
    width = keys.shape[1]
    out[:, :width] = keys[...]
    out[:, width:] = values[...]


def stack_kernel(*refs):
    tokens = refs[0].shape[0]
    for i, part in enumerate(refs[:-1]):
        refs[-1][i * tokens : (i + 1) * tokens, :] = part[...]


def halves_kernel(a_ref, b_ref, a_out, b_out):
    half = a_out.shape[0]
    a_out[...] = a_ref[:half, :]
    b_out[...] = b_ref[half:, :]


def decay_row(slots, k, base, j):
    tail = slots[k, base : base + 16, :].astype(F32)
    return tail[j : j + 1] + tail[8 + j : 9 + j]


def sent(group):
    return [0, *range(group - 1, 0, -1)]


def fill_slots(group, rank, pays, slots):
    for s, pay in zip(sent(group), pays):
        slots[rank ^ s] = pay[...]


def total_kernel(group, per, *refs):
    pays, out, slots = refs[:group], refs[group], refs[group + 1]
    fill_slots(group, my_rank(group), pays, slots)
    base = per * HD
    tails = []
    for j in range(per):
        state = slots[0, j * HD : (j + 1) * HD, :].astype(F32)
        whole = decay_row(slots, 0, base, j)
        for k in range(1, group):
            decay = decay_row(slots, k, base, j)
            state = decay * state + slots[k, j * HD : (j + 1) * HD, :].astype(F32)
            whole = whole * decay
        out[j * HD : (j + 1) * HD, :] = state.astype(BF16)
        tails.append(whole)
    pad = [jnp.zeros((8 - per, HD), F32)] if per < 8 else []
    total = jnp.concatenate(tails + pad, axis=0)
    high = total.astype(BF16).astype(F32)
    out[base:, :] = jnp.concatenate([high, total - high], axis=0).astype(BF16)


def prefix_kernel(group, per, carried, *refs):
    pays, refs = refs[:group], refs[group:]
    carry = None
    if carried:
        carry, refs = refs[0], refs[1:]
    outs, slots, prefixes = refs[:group], refs[group], refs[group + 1]
    rank = my_rank(group)
    later = lax.axis_index("ctx") >= group
    fill_slots(group, rank, pays, slots)
    base = per * HD
    for j in range(per):
        rows = slice(j * HD, (j + 1) * HD)
        state = jnp.zeros((HD, HD), F32)
        if carried:
            state = jnp.where(later, carry[rows, :].astype(F32), state)
        prefixes[0, rows, :] = state.astype(BF16)
        for k in range(group - 1):
            state = decay_row(slots, k, base, j) * state + slots[k, rows, :].astype(F32)
            prefixes[k + 1, rows, :] = state.astype(BF16)
    for s in range(group):
        outs[s][...] = prefixes[rank ^ s]


def intra_kernel(heads, tri_ref, bias_ref, ld_ref, q_ref, ka_ref, va_ref, gate_ref, gain_ref, *outs):
    intra_ref, qa_ref, gain_out, decay_out = outs
    ld = ld_ref[...]
    tri = tri_ref[...]
    bias = bias_ref[...]
    cum = lax.dot_general(tri, ld, NT, precision=HIGH, preferred_element_type=F32)
    cum_t = lax.dot_general(ld, tri, NT, precision=HIGH, preferred_element_type=F32)
    for h in range(heads):
        cols = head_cols(h)
        qa = silu16(q_ref[:, cols])
        qa_ref[:, cols] = qa
        decay_out[:, cols] = jnp.exp(jnp.broadcast_to(cum[:, h : h + 1], qa.shape))
        scores = lax.dot_general(qa, ka_ref[:, cols], NT, preferred_element_type=F32)
        decay = jnp.exp((cum[:, h : h + 1] - cum_t[h : h + 1, :]) + bias)
        weights = (scores * decay).astype(BF16)
        intra_ref[:, cols] = jnp.dot(weights, va_ref[:, cols], preferred_element_type=F32)
        gate = 1.0 / (1.0 + jnp.exp(-gate_ref[:, cols].astype(F32)))
        gain_out[:, cols] = gate * gain_ref[:, cols]


def inter_kernel(group, heads, decay_ref, qa_ref, intra_ref, *rest):
    parts, (lin_ref, squares_ref, states) = rest[:group], rest[group:]
    tokens = qa_ref.shape[0]
    per = heads // group
    rank = my_rank(group)
    for s, part in zip(sent(group), parts):
        states[dyn(rank ^ s, per * HD), :] = part[...]
    acc = jnp.zeros((tokens, HD), F32)
    for h in range(heads):
        cols = head_cols(h)
        state = states[h * HD : (h + 1) * HD, :]
        inter = jnp.dot(qa_ref[:, cols], state, preferred_element_type=F32)
        lin = intra_ref[:, cols] + inter * decay_ref[:, cols]
        lin_ref[:, cols] = lin
        acc += lin * lin
    ones = jnp.ones((8, HD), F32)
    squares_ref[...] = lax.dot_general(ones, acc, NT, precision=HIGH, preferred_element_type=F32)


def results_kernel(columns, parts, attended_ref, lin_ref, gain_ref, *rest):
    squares, (mixed_out, attended_out, mixed_ref, sems) = rest[:-4], rest[-4:]
    first = pltpu.make_async_copy(attended_ref, attended_out, sems.at[parts])
    first.start()
    total = squares[0][...]
    for part in squares[1:]:
        total = total + part[...]
    inv = jnp.transpose(lax.rsqrt(total / columns + EPS))[:, 0:1]
    width = lin_ref.shape[1] // parts
    copies = []
    for i in range(parts):
        cols = slice(i * width, (i + 1) * width)
        mixed_ref[:, cols] = (lin_ref[:, cols] * inv * gain_ref[:, cols]).astype(BF16)
        copies.append(
            pltpu.make_async_copy(mixed_ref.at[:, cols], mixed_out.at[:, cols], sems.at[i])
        )
        copies[-1].start()
    for copy in copies:
        copy.wait()
    first.wait()


def softmax_bias(group, sides, order_ref, bias):
    tokens, span = bias.shape[0], bias.shape[1] // len(sides)
    groups = span // tokens
    me = lax.axis_index("ctx")
    rank, mine = lax.rem(me, group), lax.div(me, group)
    qpos = order_ref[0] * tokens + lax.broadcasted_iota(jnp.int32, (tokens, tokens), 0)
    kpos = lax.broadcasted_iota(jnp.int32, (tokens, tokens), 1)
    for i, s in enumerate(sides):
        for d in range(groups):
            place = lax.rem(mine + groups - d, groups) * group + (rank ^ s)
            at = i * span + d * tokens
            bias[:, at : at + tokens] = jnp.where(place * tokens + kpos <= qpos, 0.0, -1e30)


def softmax_values(held, g, kv_heads, values):
    span = held[0].shape[0]
    values[:, HD:] = jnp.ones((span * len(held), HD), BF16)
    for i, ref in enumerate(held):
        values[i * span : (i + 1) * span, :HD] = ref[:, head_cols(kv_heads + g)]


def softmax_scores(query, held, g, bias):
    raw = [
        lax.dot_general(query, ref[:, head_cols(g)], NT, preferred_element_type=F32) for ref in held
    ]
    raw = jnp.concatenate(raw, axis=1)
    raw = raw.reshape(-1, *bias.shape) + bias[...][None]
    return raw.reshape(-1, bias.shape[1])


def stacked(ref, columns):
    return jnp.concatenate([ref[:, cols] for cols in columns], axis=0)


SCORE = math.log2(math.e) / math.sqrt(HD)


def softmax_first_kernel(group, sides, kv_heads, pack, order_ref, q_ref, *rest):
    arrays, rest = rest[: len(sides)], rest[len(sides) :]
    acc_ref, tops, (values, bias) = rest[0], rest[1:-2], rest[-2:]
    tokens = q_ref.shape[0]
    share = q_ref.shape[1] // HD // kv_heads
    softmax_bias(group, sides, order_ref, bias)
    for g in range(kv_heads):
        softmax_values(arrays, g, kv_heads, values)
        for j in range(0, share, pack):
            heads = range(g * share + j, g * share + j + pack)
            raw = softmax_scores(stacked(q_ref, map(head_cols, heads)), arrays, g, bias)
            top = jnp.max(raw, axis=-1, keepdims=True)
            probs = jnp.exp2((raw - top) * SCORE).astype(BF16)
            acc = jnp.dot(probs, values[...], preferred_element_type=F32)
            for i, h in enumerate(heads):
                rows = slice(i * tokens, (i + 1) * tokens)
                acc_ref[:, 2 * h * HD : 2 * (h + 1) * HD] = acc[rows]
                tops[g][:, head_cols(j + i)] = jnp.broadcast_to(top[rows], (tokens, HD))


def softmax_last_kernel(group, sides, kv_heads, pack, order_ref, q_ref, *rest):
    arrays, rest = rest[: len(sides)], rest[len(sides) :]
    acc_ref, tops, (out_ref, values, bias) = rest[0], rest[1:-3], rest[-3:]
    tokens = q_ref.shape[0]
    share = q_ref.shape[1] // HD // kv_heads
    softmax_bias(group, sides, order_ref, bias)
    for g in range(kv_heads):
        softmax_values(arrays, g, kv_heads, values)
        for j in range(0, share, pack):
            heads = range(g * share + j, g * share + j + pack)
            raw = softmax_scores(stacked(q_ref, map(head_cols, heads)), arrays, g, bias)
            old = stacked(tops[g], map(head_cols, range(j, j + pack)))
            top = jnp.maximum(old, jnp.max(raw, axis=-1, keepdims=True))
            spread = jnp.concatenate([top] * (raw.shape[1] // HD), axis=1)
            probs = jnp.exp2((raw - spread) * SCORE).astype(BF16)
            acc = jnp.dot(probs, values[...], preferred_element_type=F32)
            held = stacked(acc_ref, [slice(2 * h * HD, 2 * (h + 1) * HD) for h in heads])
            alpha = jnp.exp2((old - top) * SCORE)
            acc += held * jnp.concatenate([alpha, alpha], axis=1)
            out = (acc[:, :HD] * inverse(acc[:, HD:])).astype(BF16)
            for i, h in enumerate(heads):
                out_ref[:, head_cols(h)] = out[i * tokens : (i + 1) * tokens]


def call(
    kernel, name, outs, args, scratch=(), flops=0, exps=0, limit=16, specs=None, after=(), **more
):
    size = sum(math.prod(x.shape) * x.dtype.itemsize for x in list(args) + list(outs))
    more.setdefault("out_specs", [VMEM for _ in outs])
    specs = list(specs or [VMEM for _ in args]) + [HBM for _ in after]
    count = len(args)

    def run(*refs):
        kernel(*refs[:count], *refs[count + len(after) :])

    return pl.pallas_call(
        run,
        name=name,
        out_shape=list(outs),
        in_specs=specs,
        scratch_shapes=list(scratch),
        cost_estimate=pl.CostEstimate(flops=flops, bytes_accessed=size, transcendentals=exps),
        compiler_params=pltpu.CompilerParams(vmem_limit_bytes=limit * MIB),
        **more,
    )(*args, *after)


def body(q_lin, k_lin, v_lin, log_decay, gate, norm_gain, queries, keys, values, order):
    tokens, width = q_lin.shape
    heads = log_decay.shape[0]
    kv_width = keys.shape[1]
    kv_heads = kv_width // HD
    n, nh = lax.axis_size("ctx"), lax.axis_size("head")
    group = 4
    groups = n // group
    per = heads // group
    rows = per * HD + 16
    cube = tokens * width * HD
    shape = jax.ShapeDtypeStruct

    def swap(x, s):
        return lax.ppermute(x, "ctx", [(c, c ^ s) for c in range(n)])

    def swap_all(xs):
        return [swap(xs[s], s) if s else xs[s] for s in sent(group)]

    def ahead(x, d):
        return lax.ppermute(x, "ctx", [(c, (c + d * group) % n) for c in range(n)])

    tri, bias = call(
        triangle_kernel, "triangle", [shape((tokens, tokens), F32)] * 2, (), flops=1 << 31
    )
    (kv,) = call(
        beside_kernel,
        "keys_beside_values",
        [shape((tokens, 2 * kv_width), BF16)],
        (keys, values),
        after=(tri,),
    )
    far = [ahead(kv, d) for d in range(1, groups)]

    *pays, ka, va = call(
        functools.partial(state_kernel, group, heads),
        "block_states",
        [shape((rows, HD), BF16)] * group + [shape((tokens, width), BF16)] * 2,
        (tri, log_decay, k_lin, v_lin),
        [pltpu.VMEM((heads * HD, HD), BF16), pltpu.VMEM((group * 16, HD), F32)],
        flops=4 * cube,
        exps=2 * tokens * width,
    )
    pays = swap_all(pays)
    intra, qa, gain, decay = call(
        functools.partial(intra_kernel, heads),
        "intra_block",
        [
            shape((tokens, width), F32),
            shape((tokens, width), BF16),
            shape((tokens, width), F32),
            shape((tokens, width), F32),
        ],
        (tri, bias, log_decay, q_lin, ka, va, gate, norm_gain.reshape(1, width)),
        flops=4 * cube,
        exps=4 * tokens * width,
    )

    slots = pltpu.VMEM((group, rows, HD), BF16)
    carry = ()
    if groups > 1:
        (total,) = call(
            functools.partial(total_kernel, group, per),
            "group_state",
            [shape((rows, HD), BF16)],
            pays,
            [slots],
            flops=2 * per * HD * HD * group,
            after=(intra,),
        )
        before = ahead(total, 1)
        shift = 1
        while shift < groups - 1:
            mine = lax.div(lax.axis_index("ctx"), group)
            later = jnp.where(mine >= 1, before, 0).astype(F32)
            earlier = ahead(later.astype(BF16), shift)
            earlier = jnp.where(mine >= shift + 1, earlier, 0).astype(F32)
            step = later[per * HD :][:per] + later[per * HD + 8 :][:per]
            prior = earlier[per * HD :][:per] + earlier[per * HD + 8 :][:per]
            state = later[: per * HD] + jnp.repeat(step, HD, axis=0) * earlier[: per * HD]
            both = jnp.where(mine >= shift + 1, step * prior, step)
            high = both.astype(BF16).astype(F32)
            pad = jnp.zeros((8 - per, HD), F32)
            before = jnp.concatenate([state, high, pad, both - high, pad], axis=0).astype(BF16)
            shift *= 2
        carry = (before,)
    prefixes = call(
        functools.partial(prefix_kernel, group, per, bool(carry)),
        "prefix_states",
        [shape((per * HD, HD), BF16)] * group,
        (*pays, *carry),
        [slots, pltpu.VMEM((group, per * HD, HD), BF16)],
        flops=1 << 33,
    )
    prefixes = swap_all(prefixes)

    (own,) = call(
        stack_kernel,
        "stack_keys_values",
        [shape((groups * tokens, kv.shape[1]), BF16)],
        (kv, *far),
        after=(total,) if groups > 1 else (intra,),
        flops=1 << 32,
    )
    side, near = swap(own, 2), swap(own, 1)
    half = shape((own.shape[0] // 2, own.shape[1]), BF16)
    upper, under = call(halves_kernel, "sent_on", [half] * 2, (side, near))
    across = jnp.concatenate([swap(upper, 1), swap(under, 2)])
    share = width // kv_heads
    pack = 2 if share // HD % 2 == 0 else 1
    span = own.shape[0]
    room = 24 + 48 * span * tokens * 4 // MIB
    smem = pl.BlockSpec(memory_space=pltpu.SMEM)

    def scratch(count):
        keys = count * span
        return [pltpu.VMEM((keys, 2 * HD), BF16), pltpu.VMEM((tokens, keys), F32)]

    acc, *tops = call(
        functools.partial(softmax_first_kernel, group, (0, 2, 1), kv_heads, pack),
        "softmax_first",
        [shape((tokens, 2 * width), F32)] + [shape((tokens, share), F32)] * kv_heads,
        (order, queries, own, side, near),
        scratch(3),
        flops=12 * tokens * width * span,
        exps=3 * tokens * span * width // HD,
        limit=room,
        specs=[smem] + [VMEM] * 4,
    )
    (attended,) = call(
        functools.partial(softmax_last_kernel, group, (3,), kv_heads, pack),
        "softmax_last",
        [shape((tokens, width), BF16)],
        (order, queries, across, acc, *tops),
        scratch(1),
        flops=4 * tokens * width * span,
        exps=tokens * span * width // HD,
        limit=room,
        specs=[smem] + [VMEM] * (3 + kv_heads),
    )

    lin, squares = call(
        functools.partial(inter_kernel, group, heads),
        "inter_block",
        [shape((tokens, width), F32), shape((8, tokens), F32)],
        (decay, qa, intra, *prefixes),
        [pltpu.VMEM((heads * HD, HD), BF16)],
        flops=2 * cube,
        after=tops[:1],
    )
    if nh & (nh - 1) == 0:
        turns = [[(i, i ^ d) for i in range(nh)] for d in range(nh - 1, 0, -1)]
    else:
        turns = [[(i, (i + d) % nh) for i in range(nh)] for d in range(1, nh)]
    parts = [squares] + [lax.ppermute(squares, "head", turn) for turn in turns]
    pieces = 4 if width % (4 * HD) == 0 else 1
    return call(
        functools.partial(results_kernel, float(width * nh), pieces),
        "results",
        [shape((tokens, width), BF16)] * 2,
        (attended, lin, gain, *parts),
        [pltpu.VMEM((tokens, width), BF16), pltpu.SemaphoreType.DMA((pieces + 1,))],
        flops=4 * tokens * width,
        out_specs=[HBM] * 2,
    )


def solution(mesh):
    return jax.shard_map(
        body,
        mesh=mesh,
        in_specs=(
            P("ctx", "head"),
            P("ctx", "head"),
            P("ctx", "head"),
            P("head", "ctx"),
            P("ctx", "head"),
            P("head"),
            P("ctx", "head"),
            P("ctx", "head"),
            P("ctx", "head"),
            P("ctx"),
        ),
        out_specs=(P("ctx", "head"), P("ctx", "head")),
        check_vma=False,
    )
```

```python
import functools
import math

import jax
import jax.numpy as jnp
from jax import lax
from jax.experimental import pallas as pl
from jax.experimental.pallas import tpu as pltpu
from jax.sharding import PartitionSpec as P

HD = 128
EPS = 1e-06
HIGH = lax.Precision.HIGHEST
F32 = jnp.float32
BF16 = jnp.bfloat16
NT = (((1,), (1,)), ((), ()))
MIB = 1 << 20
VMEM = pl.BlockSpec(memory_space=pltpu.VMEM)
HBM = pl.BlockSpec(memory_space=pltpu.HBM)


def inverse(x):
    guess = pl.reciprocal(x, approx=True)
    return guess * (2.0 - x * guess)


def silu16(x):
    x = x.astype(F32)
    return (x / (1.0 + jnp.exp(-x))).astype(BF16)


def lower_ones(size):
    rows = lax.broadcasted_iota(jnp.int32, (size, size), 0)
    cols = lax.broadcasted_iota(jnp.int32, (size, size), 1)
    return rows >= cols


def head_cols(h):
    return slice(h * HD, (h + 1) * HD)


def my_rank(group):
    return lax.rem(lax.axis_index("ctx"), group)


def dyn(index, size):
    return pl.ds(pl.multiple_of(index * size, size), size)


def triangle_kernel(ones_ref, bias_ref):
    lower = lower_ones(ones_ref.shape[0])
    ones_ref[...] = lower.astype(F32)
    bias_ref[...] = jnp.where(lower, 0.0, -1e30)


def state_kernel(group, heads, tri_ref, ld_ref, k_ref, v_ref, *rest):
    outs, (ka_ref, va_ref, states, totals) = rest[:group], rest[group:]
    tokens = k_ref.shape[0]
    per = heads // group
    rank = my_rank(group)
    ld = ld_ref[...]
    cum = lax.dot_general(ld, tri_ref[...], NT, precision=HIGH, preferred_element_type=F32)
    weight = jnp.exp(cum[:, tokens - 1 : tokens] - cum)
    total = jnp.broadcast_to(jnp.exp(jnp.sum(ld, axis=1, keepdims=True)), (heads, HD))
    high = total.astype(BF16).astype(F32)
    low = total - high
    totals[...] = jnp.zeros_like(totals)
    for k in range(group):
        totals[k * 16 : k * 16 + per, :] = high[k * per : (k + 1) * per]
        totals[k * 16 + 8 : k * 16 + 8 + per, :] = low[k * per : (k + 1) * per]
    for h in range(heads):
        ka = silu16(k_ref[:, head_cols(h)])
        va = silu16(v_ref[:, head_cols(h)])
        ka_ref[:, head_cols(h)] = ka
        va_ref[:, head_cols(h)] = va
        kdec = jnp.transpose(ka).astype(F32) * weight[h : h + 1, :]
        khigh = kdec.astype(BF16)
        klow = (kdec - khigh.astype(F32)).astype(BF16)
        state = jnp.dot(khigh, va, preferred_element_type=F32)
        state += jnp.dot(klow, va, preferred_element_type=F32)
        states[h * HD : (h + 1) * HD, :] = state.astype(BF16)
    for s in range(group):
        dest = rank ^ s
        outs[s][: per * HD, :] = states[dyn(dest, per * HD), :]
        outs[s][per * HD :, :] = totals[dyn(dest, 16), :].astype(BF16)


def beside_kernel(keys, values, out):
    width = keys.shape[1]
    out[:, :width] = keys[...]
    out[:, width:] = values[...]


def stack_kernel(*refs):
    tokens = refs[0].shape[0]
    for i, part in enumerate(refs[:-1]):
        refs[-1][i * tokens : (i + 1) * tokens, :] = part[...]


def halves_kernel(a_ref, b_ref, a_out, b_out):
    half = a_out.shape[0]
    a_out[...] = a_ref[:half, :]
    b_out[...] = b_ref[half:, :]


def decay_row(slots, k, base, j):
    tail = slots[k, base : base + 16, :].astype(F32)
    return tail[j : j + 1] + tail[8 + j : 9 + j]


def fill_slots(order, rank, pays, slots):
    for s, pay in zip(order, pays):
        slots[rank ^ s] = pay[...]


def total_kernel(group, per, order, *refs):
    pays, out, slots = refs[:group], refs[group], refs[group + 1]
    fill_slots(order, my_rank(group), pays, slots)
    base = per * HD
    tails = []
    for j in range(per):
        state = slots[0, j * HD : (j + 1) * HD, :].astype(F32)
        whole = decay_row(slots, 0, base, j)
        for k in range(1, group):
            decay = decay_row(slots, k, base, j)
            state = decay * state + slots[k, j * HD : (j + 1) * HD, :].astype(F32)
            whole = whole * decay
        out[j * HD : (j + 1) * HD, :] = state.astype(BF16)
        tails.append(whole)
    pad = [jnp.zeros((8 - per, HD), F32)] if per < 8 else []
    total = jnp.concatenate(tails + pad, axis=0)
    high = total.astype(BF16).astype(F32)
    out[base:, :] = jnp.concatenate([high, total - high], axis=0).astype(BF16)


def prefix_kernel(group, per, order, carried, *refs):
    pays, refs = refs[:group], refs[group:]
    carry = None
    if carried:
        carry, refs = refs[0], refs[1:]
    outs, slots, prefixes = refs[:group], refs[group], refs[group + 1]
    rank = my_rank(group)
    later = lax.axis_index("ctx") >= group
    fill_slots(order, rank, pays, slots)
    base = per * HD
    for j in range(per):
        rows = slice(j * HD, (j + 1) * HD)
        state = jnp.zeros((HD, HD), F32)
        if carried:
            state = jnp.where(later, carry[rows, :].astype(F32), state)
        prefixes[0, rows, :] = state.astype(BF16)
        for k in range(group - 1):
            state = decay_row(slots, k, base, j) * state + slots[k, rows, :].astype(F32)
            prefixes[k + 1, rows, :] = state.astype(BF16)
    for s in range(group):
        outs[s][...] = prefixes[rank ^ s]


def intra_kernel(heads, tri_ref, bias_ref, ld_ref, q_ref, ka_ref, va_ref, gate_ref, gain_ref, *outs):
    intra_ref, qa_ref, gain_out, decay_out = outs
    ld = ld_ref[...]
    tri = tri_ref[...]
    bias = bias_ref[...]
    cum = lax.dot_general(tri, ld, NT, precision=HIGH, preferred_element_type=F32)
    cum_t = lax.dot_general(ld, tri, NT, precision=HIGH, preferred_element_type=F32)
    for h in range(heads):
        cols = head_cols(h)
        qa = silu16(q_ref[:, cols])
        qa_ref[:, cols] = qa
        decay_out[:, cols] = jnp.exp(jnp.broadcast_to(cum[:, h : h + 1], qa.shape))
        scores = lax.dot_general(qa, ka_ref[:, cols], NT, preferred_element_type=F32)
        decay = jnp.exp((cum[:, h : h + 1] - cum_t[h : h + 1, :]) + bias)
        weights = (scores * decay).astype(BF16)
        intra_ref[:, cols] = jnp.dot(weights, va_ref[:, cols], preferred_element_type=F32)
        gate = 1.0 / (1.0 + jnp.exp(-gate_ref[:, cols].astype(F32)))
        gain_out[:, cols] = gate * gain_ref[:, cols]


def inter_kernel(group, heads, order, decay_ref, qa_ref, intra_ref, *rest):
    parts, (lin_ref, squares_ref, states) = rest[:group], rest[group:]
    tokens = qa_ref.shape[0]
    per = heads // group
    rank = my_rank(group)
    for s, part in zip(order, parts):
        states[dyn(rank ^ s, per * HD), :] = part[...]
    acc = jnp.zeros((tokens, HD), F32)
    for h in range(heads):
        cols = head_cols(h)
        state = states[h * HD : (h + 1) * HD, :]
        inter = jnp.dot(qa_ref[:, cols], state, preferred_element_type=F32)
        lin = intra_ref[:, cols] + inter * decay_ref[:, cols]
        lin_ref[:, cols] = lin
        acc += lin * lin
    ones = jnp.ones((8, HD), F32)
    squares_ref[...] = lax.dot_general(ones, acc, NT, precision=HIGH, preferred_element_type=F32)


def results_kernel(columns, parts, attended_ref, lin_ref, gain_ref, *rest):
    squares, (mixed_out, attended_out, mixed_ref, sems) = rest[:-4], rest[-4:]
    first = pltpu.make_async_copy(attended_ref, attended_out, sems.at[parts])
    first.start()
    total = squares[0][...]
    for part in squares[1:]:
        total = total + part[...]
    inv = jnp.transpose(lax.rsqrt(total / columns + EPS))[:, 0:1]
    width = lin_ref.shape[1] // parts
    copies = []
    for i in range(parts):
        cols = slice(i * width, (i + 1) * width)
        mixed_ref[:, cols] = (lin_ref[:, cols] * inv * gain_ref[:, cols]).astype(BF16)
        copies.append(
            pltpu.make_async_copy(mixed_ref.at[:, cols], mixed_out.at[:, cols], sems.at[i])
        )
        copies[-1].start()
    for copy in copies:
        copy.wait()
    first.wait()


def softmax_bias(group, sides, order_ref, bias):
    tokens, span = bias.shape[0], bias.shape[1] // len(sides)
    groups = span // tokens
    me = lax.axis_index("ctx")
    rank, mine = lax.rem(me, group), lax.div(me, group)
    qpos = order_ref[0] * tokens + lax.broadcasted_iota(jnp.int32, (tokens, tokens), 0)
    kpos = lax.broadcasted_iota(jnp.int32, (tokens, tokens), 1)
    for i, s in enumerate(sides):
        for d in range(groups):
            place = lax.rem(mine + groups - d, groups) * group + (rank ^ s)
            at = i * span + d * tokens
            bias[:, at : at + tokens] = jnp.where(place * tokens + kpos <= qpos, 0.0, -1e30)


def softmax_values(held, g, kv_heads, values):
    span = held[0].shape[0]
    values[:, HD:] = jnp.ones((span * len(held), HD), BF16)
    for i, ref in enumerate(held):
        values[i * span : (i + 1) * span, :HD] = ref[:, head_cols(kv_heads + g)]


def softmax_scores(query, held, g, bias):
    raw = [
        lax.dot_general(query, ref[:, head_cols(g)], NT, preferred_element_type=F32) for ref in held
    ]
    raw = jnp.concatenate(raw, axis=1)
    raw = raw.reshape(-1, *bias.shape) + bias[...][None]
    return raw.reshape(-1, bias.shape[1])


def stacked(ref, columns):
    return jnp.concatenate([ref[:, cols] for cols in columns], axis=0)


SCORE = math.log2(math.e) / math.sqrt(HD)


def softmax_first_kernel(group, sides, kv_heads, pack, order_ref, q_ref, *rest):
    arrays, rest = rest[: len(sides)], rest[len(sides) :]
    acc_ref, tops, (values, bias) = rest[0], rest[1:-2], rest[-2:]
    tokens = q_ref.shape[0]
    share = q_ref.shape[1] // HD // kv_heads
    softmax_bias(group, sides, order_ref, bias)
    for g in range(kv_heads):
        softmax_values(arrays, g, kv_heads, values)
        for j in range(0, share, pack):
            heads = range(g * share + j, g * share + j + pack)
            raw = softmax_scores(stacked(q_ref, map(head_cols, heads)), arrays, g, bias)
            top = jnp.max(raw, axis=-1, keepdims=True)
            probs = jnp.exp2((raw - top) * SCORE).astype(BF16)
            acc = jnp.dot(probs, values[...], preferred_element_type=F32)
            for i, h in enumerate(heads):
                rows = slice(i * tokens, (i + 1) * tokens)
                acc_ref[:, 2 * h * HD : 2 * (h + 1) * HD] = acc[rows]
                tops[g][:, head_cols(j + i)] = jnp.broadcast_to(top[rows], (tokens, HD))


def softmax_last_kernel(group, sides, kv_heads, pack, order_ref, q_ref, *rest):
    arrays, rest = rest[: len(sides)], rest[len(sides) :]
    acc_ref, tops, (out_ref, values, bias) = rest[0], rest[1:-3], rest[-3:]
    tokens = q_ref.shape[0]
    share = q_ref.shape[1] // HD // kv_heads
    softmax_bias(group, sides, order_ref, bias)
    for g in range(kv_heads):
        softmax_values(arrays, g, kv_heads, values)
        for j in range(0, share, pack):
            heads = range(g * share + j, g * share + j + pack)
            raw = softmax_scores(stacked(q_ref, map(head_cols, heads)), arrays, g, bias)
            old = stacked(tops[g], map(head_cols, range(j, j + pack)))
            top = jnp.maximum(old, jnp.max(raw, axis=-1, keepdims=True))
            spread = jnp.concatenate([top] * (raw.shape[1] // HD), axis=1)
            probs = jnp.exp2((raw - spread) * SCORE).astype(BF16)
            acc = jnp.dot(probs, values[...], preferred_element_type=F32)
            held = stacked(acc_ref, [slice(2 * h * HD, 2 * (h + 1) * HD) for h in heads])
            alpha = jnp.exp2((old - top) * SCORE)
            acc += held * jnp.concatenate([alpha, alpha], axis=1)
            out = (acc[:, :HD] * inverse(acc[:, HD:])).astype(BF16)
            for i, h in enumerate(heads):
                out_ref[:, head_cols(h)] = out[i * tokens : (i + 1) * tokens]


def call(
    kernel, name, outs, args, scratch=(), flops=0, exps=0, limit=16, specs=None, after=(), **more
):
    size = sum(math.prod(x.shape) * x.dtype.itemsize for x in list(args) + list(outs))
    more.setdefault("out_specs", [VMEM for _ in outs])
    specs = list(specs or [VMEM for _ in args]) + [HBM for _ in after]
    count = len(args)

    def run(*refs):
        kernel(*refs[:count], *refs[count + len(after) :])

    return pl.pallas_call(
        run,
        name=name,
        out_shape=list(outs),
        in_specs=specs,
        scratch_shapes=list(scratch),
        cost_estimate=pl.CostEstimate(flops=flops, bytes_accessed=size, transcendentals=exps),
        compiler_params=pltpu.CompilerParams(vmem_limit_bytes=limit * MIB),
        **more,
    )(*args, *after)


def body(q_lin, k_lin, v_lin, log_decay, gate, norm_gain, queries, keys, values, order):
    tokens, width = q_lin.shape
    heads = log_decay.shape[0]
    kv_width = keys.shape[1]
    kv_heads = kv_width // HD
    n, nh = lax.axis_size("ctx"), lax.axis_size("head")
    group = 4
    groups = n // group
    per = heads // group
    rows = per * HD + 16
    cube = tokens * width * HD
    shape = jax.ShapeDtypeStruct

    def swap(x, s):
        return lax.ppermute(x, "ctx", [(c, c ^ s) for c in range(n)])

    to, back = (0, 2, 3, 1), (0, 3, 2, 1)

    def swap_all(xs, order):
        return [swap(xs[s], s) if s else xs[s] for s in order]

    def ahead(x, d):
        return lax.ppermute(x, "ctx", [(c, (c + d * group) % n) for c in range(n)])

    tri, bias = call(
        triangle_kernel, "triangle", [shape((tokens, tokens), F32)] * 2, (), flops=1 << 31
    )
    (kv,) = call(
        beside_kernel,
        "keys_beside_values",
        [shape((tokens, 2 * kv_width), BF16)],
        (keys, values),
        after=(tri,),
    )
    far = [ahead(kv, d) for d in range(1, groups)]

    *pays, ka, va = call(
        functools.partial(state_kernel, group, heads),
        "block_states",
        [shape((rows, HD), BF16)] * group + [shape((tokens, width), BF16)] * 2,
        (tri, log_decay, k_lin, v_lin),
        [pltpu.VMEM((heads * HD, HD), BF16), pltpu.VMEM((group * 16, HD), F32)],
        flops=4 * cube,
        exps=2 * tokens * width,
    )
    pays = swap_all(pays, to)
    intra, qa, gain, decay = call(
        functools.partial(intra_kernel, heads),
        "intra_block",
        [
            shape((tokens, width), F32),
            shape((tokens, width), BF16),
            shape((tokens, width), F32),
            shape((tokens, width), F32),
        ],
        (tri, bias, log_decay, q_lin, ka, va, gate, norm_gain.reshape(1, width)),
        flops=4 * cube,
        exps=4 * tokens * width,
    )

    slots = pltpu.VMEM((group, rows, HD), BF16)
    carry = ()
    if groups > 1:
        (total,) = call(
            functools.partial(total_kernel, group, per, to),
            "group_state",
            [shape((rows, HD), BF16)],
            pays,
            [slots],
            flops=2 * per * HD * HD * group,
            after=(intra,),
        )
        before = ahead(total, 1)
        shift = 1
        while shift < groups - 1:
            mine = lax.div(lax.axis_index("ctx"), group)
            later = jnp.where(mine >= 1, before, 0).astype(F32)
            earlier = ahead(later.astype(BF16), shift)
            earlier = jnp.where(mine >= shift + 1, earlier, 0).astype(F32)
            step = later[per * HD :][:per] + later[per * HD + 8 :][:per]
            prior = earlier[per * HD :][:per] + earlier[per * HD + 8 :][:per]
            state = later[: per * HD] + jnp.repeat(step, HD, axis=0) * earlier[: per * HD]
            both = jnp.where(mine >= shift + 1, step * prior, step)
            high = both.astype(BF16).astype(F32)
            pad = jnp.zeros((8 - per, HD), F32)
            before = jnp.concatenate([state, high, pad, both - high, pad], axis=0).astype(BF16)
            shift *= 2
        carry = (before,)
    prefixes = call(
        functools.partial(prefix_kernel, group, per, to, bool(carry)),
        "prefix_states",
        [shape((per * HD, HD), BF16)] * group,
        (*pays, *carry),
        [slots, pltpu.VMEM((group, per * HD, HD), BF16)],
        flops=1 << 33,
    )
    prefixes = swap_all(prefixes, back)

    (own,) = call(
        stack_kernel,
        "stack_keys_values",
        [shape((groups * tokens, kv.shape[1]), BF16)],
        (kv, *far),
        after=(total,) if groups > 1 else (intra,),
        flops=1 << 32,
    )
    side, near = swap(own, 2), swap(own, 1)
    half = shape((own.shape[0] // 2, own.shape[1]), BF16)
    upper, under = call(halves_kernel, "sent_on", [half] * 2, (side, near))
    across = jnp.concatenate([swap(upper, 1), swap(under, 2)])
    share = width // kv_heads
    pack = 2 if share // HD % 2 == 0 else 1
    span = own.shape[0]
    room = 24 + 48 * span * tokens * 4 // MIB
    smem = pl.BlockSpec(memory_space=pltpu.SMEM)

    def scratch(count):
        keys = count * span
        return [pltpu.VMEM((keys, 2 * HD), BF16), pltpu.VMEM((tokens, keys), F32)]

    acc, *tops = call(
        functools.partial(softmax_first_kernel, group, (0, 2, 1), kv_heads, pack),
        "softmax_first",
        [shape((tokens, 2 * width), F32)] + [shape((tokens, share), F32)] * kv_heads,
        (order, queries, own, side, near),
        scratch(3),
        flops=12 * tokens * width * span,
        exps=3 * tokens * span * width // HD,
        limit=room,
        specs=[smem] + [VMEM] * 4,
    )
    (attended,) = call(
        functools.partial(softmax_last_kernel, group, (3,), kv_heads, pack),
        "softmax_last",
        [shape((tokens, width), BF16)],
        (order, queries, across, acc, *tops),
        scratch(1),
        flops=4 * tokens * width * span,
        exps=tokens * span * width // HD,
        limit=room,
        specs=[smem] + [VMEM] * (3 + kv_heads),
    )

    lin, squares = call(
        functools.partial(inter_kernel, group, heads, back),
        "inter_block",
        [shape((tokens, width), F32), shape((8, tokens), F32)],
        (decay, qa, intra, *prefixes),
        [pltpu.VMEM((heads * HD, HD), BF16)],
        flops=2 * cube,
        after=tops[:1],
    )
    if nh & (nh - 1) == 0:
        turns = [[(i, i ^ d) for i in range(nh)] for d in range(nh - 1, 0, -1)]
    else:
        turns = [[(i, (i + d) % nh) for i in range(nh)] for d in range(1, nh)]
    parts = [squares] + [lax.ppermute(squares, "head", turn) for turn in turns]
    pieces = 4 if width % (4 * HD) == 0 else 1
    return call(
        functools.partial(results_kernel, float(width * nh), pieces),
        "results",
        [shape((tokens, width), BF16)] * 2,
        (attended, lin, gain, *parts),
        [pltpu.VMEM((tokens, width), BF16), pltpu.SemaphoreType.DMA((pieces + 1,))],
        flops=4 * tokens * width,
        out_specs=[HBM] * 2,
    )


def solution(mesh):
    return jax.shard_map(
        body,
        mesh=mesh,
        in_specs=(
            P("ctx", "head"),
            P("ctx", "head"),
            P("ctx", "head"),
            P("head", "ctx"),
            P("ctx", "head"),
            P("head"),
            P("ctx", "head"),
            P("ctx", "head"),
            P("ctx", "head"),
            P("ctx"),
        ),
        out_specs=(P("ctx", "head"), P("ctx", "head")),
        check_vma=False,
    )
```

```python
import functools
import math

import jax
import jax.numpy as jnp
from jax import lax
from jax.experimental import pallas as pl
from jax.experimental.pallas import tpu as pltpu
from jax.sharding import PartitionSpec as P

HD = 128
EPS = 1e-06
HIGH = lax.Precision.HIGHEST
F32 = jnp.float32
BF16 = jnp.bfloat16
NT = (((1,), (1,)), ((), ()))
MIB = 1 << 20
VMEM = pl.BlockSpec(memory_space=pltpu.VMEM)
HBM = pl.BlockSpec(memory_space=pltpu.HBM)


def inverse(x):
    guess = pl.reciprocal(x, approx=True)
    return guess * (2.0 - x * guess)


def silu16(x):
    x = x.astype(F32)
    return (x / (1.0 + jnp.exp(-x))).astype(BF16)


def lower_ones(size):
    rows = lax.broadcasted_iota(jnp.int32, (size, size), 0)
    cols = lax.broadcasted_iota(jnp.int32, (size, size), 1)
    return rows >= cols


def head_cols(h):
    return slice(h * HD, (h + 1) * HD)


def my_rank(group):
    return lax.rem(lax.axis_index("ctx"), group)


def dyn(index, size):
    return pl.ds(pl.multiple_of(index * size, size), size)


def triangle_kernel(ones_ref, bias_ref):
    lower = lower_ones(ones_ref.shape[0])
    ones_ref[...] = lower.astype(F32)
    bias_ref[...] = jnp.where(lower, 0.0, -1e30)


def state_kernel(group, heads, tri_ref, ld_ref, k_ref, v_ref, *rest):
    outs, (ka_ref, va_ref, states, totals) = rest[:group], rest[group:]
    tokens = k_ref.shape[0]
    per = heads // group
    rank = my_rank(group)
    ld = ld_ref[...]
    cum = lax.dot_general(ld, tri_ref[...], NT, precision=HIGH, preferred_element_type=F32)
    weight = jnp.exp(cum[:, tokens - 1 : tokens] - cum)
    total = jnp.broadcast_to(jnp.exp(jnp.sum(ld, axis=1, keepdims=True)), (heads, HD))
    high = total.astype(BF16).astype(F32)
    low = total - high
    totals[...] = jnp.zeros_like(totals)
    for k in range(group):
        totals[k * 16 : k * 16 + per, :] = high[k * per : (k + 1) * per]
        totals[k * 16 + 8 : k * 16 + 8 + per, :] = low[k * per : (k + 1) * per]
    for h in range(heads):
        ka = silu16(k_ref[:, head_cols(h)])
        va = silu16(v_ref[:, head_cols(h)])
        ka_ref[:, head_cols(h)] = ka
        va_ref[:, head_cols(h)] = va
        kdec = jnp.transpose(ka).astype(F32) * weight[h : h + 1, :]
        khigh = kdec.astype(BF16)
        klow = (kdec - khigh.astype(F32)).astype(BF16)
        state = jnp.dot(khigh, va, preferred_element_type=F32)
        state += jnp.dot(klow, va, preferred_element_type=F32)
        states[h * HD : (h + 1) * HD, :] = state.astype(BF16)
    for s in range(group):
        dest = rank ^ s
        outs[s][: per * HD, :] = states[dyn(dest, per * HD), :]
        outs[s][per * HD :, :] = totals[dyn(dest, 16), :].astype(BF16)


def beside_kernel(keys, values, out):
    width = keys.shape[1]
    out[:, :width] = keys[...]
    out[:, width:] = values[...]


def stack_kernel(*refs):
    tokens = refs[0].shape[0]
    for i, part in enumerate(refs[:-1]):
        refs[-1][i * tokens : (i + 1) * tokens, :] = part[...]


def halves_kernel(a_ref, b_ref, a_out, b_out):
    half = a_out.shape[0]
    a_out[...] = a_ref[:half, :]
    b_out[...] = b_ref[half:, :]


def decay_row(slots, k, base, j):
    tail = slots[k, base : base + 16, :].astype(F32)
    return tail[j : j + 1] + tail[8 + j : 9 + j]


def fill_slots(order, rank, pays, slots):
    for s, pay in zip(order, pays):
        slots[rank ^ s] = pay[...]


def total_kernel(group, per, order, *refs):
    pays, out, slots = refs[:group], refs[group], refs[group + 1]
    fill_slots(order, my_rank(group), pays, slots)
    base = per * HD
    tails = []
    for j in range(per):
        state = slots[0, j * HD : (j + 1) * HD, :].astype(F32)
        whole = decay_row(slots, 0, base, j)
        for k in range(1, group):
            decay = decay_row(slots, k, base, j)
            state = decay * state + slots[k, j * HD : (j + 1) * HD, :].astype(F32)
            whole = whole * decay
        out[j * HD : (j + 1) * HD, :] = state.astype(BF16)
        tails.append(whole)
    pad = [jnp.zeros((8 - per, HD), F32)] if per < 8 else []
    total = jnp.concatenate(tails + pad, axis=0)
    high = total.astype(BF16).astype(F32)
    out[base:, :] = jnp.concatenate([high, total - high], axis=0).astype(BF16)


def prefix_kernel(group, per, order, carried, *refs):
    pays, refs = refs[:group], refs[group:]
    carry = None
    if carried:
        carry, refs = refs[0], refs[1:]
    outs, slots, prefixes = refs[:group], refs[group], refs[group + 1]
    rank = my_rank(group)
    later = lax.axis_index("ctx") >= group
    fill_slots(order, rank, pays, slots)
    base = per * HD
    for j in range(per):
        rows = slice(j * HD, (j + 1) * HD)
        state = jnp.zeros((HD, HD), F32)
        if carried:
            state = jnp.where(later, carry[rows, :].astype(F32), state)
        prefixes[0, rows, :] = state.astype(BF16)
        for k in range(group - 1):
            state = decay_row(slots, k, base, j) * state + slots[k, rows, :].astype(F32)
            prefixes[k + 1, rows, :] = state.astype(BF16)
    for s in range(group):
        outs[s][...] = prefixes[rank ^ s]


def intra_kernel(heads, tri_ref, bias_ref, ld_ref, q_ref, ka_ref, va_ref, gate_ref, gain_ref, *outs):
    intra_ref, qa_ref, gain_out, decay_out = outs
    ld = ld_ref[...]
    tri = tri_ref[...]
    bias = bias_ref[...]
    cum = lax.dot_general(tri, ld, NT, precision=HIGH, preferred_element_type=F32)
    cum_t = lax.dot_general(ld, tri, NT, precision=HIGH, preferred_element_type=F32)
    for h in range(heads):
        cols = head_cols(h)
        qa = silu16(q_ref[:, cols])
        qa_ref[:, cols] = qa
        decay_out[:, cols] = jnp.exp(jnp.broadcast_to(cum[:, h : h + 1], qa.shape))
        scores = lax.dot_general(qa, ka_ref[:, cols], NT, preferred_element_type=F32)
        decay = jnp.exp((cum[:, h : h + 1] - cum_t[h : h + 1, :]) + bias)
        weights = (scores * decay).astype(BF16)
        intra_ref[:, cols] = jnp.dot(weights, va_ref[:, cols], preferred_element_type=F32)
        gate = 1.0 / (1.0 + jnp.exp(-gate_ref[:, cols].astype(F32)))
        gain_out[:, cols] = gate * gain_ref[:, cols]


def inter_kernel(group, heads, order, decay_ref, qa_ref, intra_ref, *rest):
    parts, (lin_ref, squares_ref, states) = rest[:group], rest[group:]
    tokens = qa_ref.shape[0]
    per = heads // group
    rank = my_rank(group)
    for s, part in zip(order, parts):
        states[dyn(rank ^ s, per * HD), :] = part[...]
    acc = jnp.zeros((tokens, HD), F32)
    for h in range(heads):
        cols = head_cols(h)
        state = states[h * HD : (h + 1) * HD, :]
        inter = jnp.dot(qa_ref[:, cols], state, preferred_element_type=F32)
        lin = intra_ref[:, cols] + inter * decay_ref[:, cols]
        lin_ref[:, cols] = lin
        acc += lin * lin
    ones = jnp.ones((8, HD), F32)
    squares_ref[...] = lax.dot_general(ones, acc, NT, precision=HIGH, preferred_element_type=F32)


def results_kernel(columns, parts, attended_ref, lin_ref, gain_ref, *rest):
    squares, (mixed_out, attended_out, mixed_ref, sems) = rest[:-4], rest[-4:]
    first = pltpu.make_async_copy(attended_ref, attended_out, sems.at[parts])
    first.start()
    total = squares[0][...]
    for part in squares[1:]:
        total = total + part[...]
    inv = jnp.transpose(lax.rsqrt(total / columns + EPS))[:, 0:1]
    width = lin_ref.shape[1] // parts
    copies = []
    for i in range(parts):
        cols = slice(i * width, (i + 1) * width)
        mixed_ref[:, cols] = (lin_ref[:, cols] * inv * gain_ref[:, cols]).astype(BF16)
        copies.append(
            pltpu.make_async_copy(mixed_ref.at[:, cols], mixed_out.at[:, cols], sems.at[i])
        )
        copies[-1].start()
    for copy in copies:
        copy.wait()
    first.wait()


def softmax_bias(group, sides, order_ref, bias):
    tokens, span = bias.shape[0], bias.shape[1] // len(sides)
    groups = span // tokens
    me = lax.axis_index("ctx")
    rank, mine = lax.rem(me, group), lax.div(me, group)
    qpos = order_ref[0] * tokens + lax.broadcasted_iota(jnp.int32, (tokens, tokens), 0)
    kpos = lax.broadcasted_iota(jnp.int32, (tokens, tokens), 1)
    for i, s in enumerate(sides):
        for d in range(groups):
            place = lax.rem(mine + groups - d, groups) * group + (rank ^ s)
            at = i * span + d * tokens
            bias[:, at : at + tokens] = jnp.where(place * tokens + kpos <= qpos, 0.0, -1e30)


def softmax_values(held, g, kv_heads, values):
    span = held[0].shape[0]
    values[:, HD:] = jnp.ones((span * len(held), HD), BF16)
    for i, ref in enumerate(held):
        values[i * span : (i + 1) * span, :HD] = ref[:, head_cols(kv_heads + g)]


def softmax_scores(query, held, g, bias):
    raw = [
        lax.dot_general(query, ref[:, head_cols(g)], NT, preferred_element_type=F32) for ref in held
    ]
    raw = jnp.concatenate(raw, axis=1)
    raw = raw.reshape(-1, *bias.shape) + bias[...][None]
    return raw.reshape(-1, bias.shape[1])


def stacked(ref, columns):
    return jnp.concatenate([ref[:, cols] for cols in columns], axis=0)


SCORE = math.log2(math.e) / math.sqrt(HD)


def softmax_first_kernel(group, sides, kv_heads, pack, order_ref, q_ref, *rest):
    arrays, rest = rest[: len(sides)], rest[len(sides) :]
    acc_ref, tops, (values, bias) = rest[0], rest[1:-2], rest[-2:]
    tokens = q_ref.shape[0]
    share = q_ref.shape[1] // HD // kv_heads
    softmax_bias(group, sides, order_ref, bias)
    for g in range(kv_heads):
        softmax_values(arrays, g, kv_heads, values)
        for j in range(0, share, pack):
            heads = range(g * share + j, g * share + j + pack)
            raw = softmax_scores(stacked(q_ref, map(head_cols, heads)), arrays, g, bias)
            top = jnp.max(raw, axis=-1, keepdims=True)
            probs = jnp.exp2((raw - top) * SCORE).astype(BF16)
            acc = jnp.dot(probs, values[...], preferred_element_type=F32)
            for i, h in enumerate(heads):
                rows = slice(i * tokens, (i + 1) * tokens)
                acc_ref[:, 2 * h * HD : 2 * (h + 1) * HD] = acc[rows]
                tops[g][:, head_cols(j + i)] = jnp.broadcast_to(top[rows], (tokens, HD))


def softmax_last_kernel(group, sides, kv_heads, pack, order_ref, q_ref, *rest):
    arrays, rest = rest[: len(sides)], rest[len(sides) :]
    acc_ref, tops, (out_ref, values, bias) = rest[0], rest[1:-3], rest[-3:]
    tokens = q_ref.shape[0]
    share = q_ref.shape[1] // HD // kv_heads
    softmax_bias(group, sides, order_ref, bias)
    for g in range(kv_heads):
        softmax_values(arrays, g, kv_heads, values)
        for j in range(0, share, pack):
            heads = range(g * share + j, g * share + j + pack)
            raw = softmax_scores(stacked(q_ref, map(head_cols, heads)), arrays, g, bias)
            old = stacked(tops[g], map(head_cols, range(j, j + pack)))
            top = jnp.maximum(old, jnp.max(raw, axis=-1, keepdims=True))
            spread = jnp.concatenate([top] * (raw.shape[1] // HD), axis=1)
            probs = jnp.exp2((raw - spread) * SCORE).astype(BF16)
            acc = jnp.dot(probs, values[...], preferred_element_type=F32)
            held = stacked(acc_ref, [slice(2 * h * HD, 2 * (h + 1) * HD) for h in heads])
            alpha = jnp.exp2((old - top) * SCORE)
            acc += held * jnp.concatenate([alpha, alpha], axis=1)
            out = (acc[:, :HD] * inverse(acc[:, HD:])).astype(BF16)
            for i, h in enumerate(heads):
                out_ref[:, head_cols(h)] = out[i * tokens : (i + 1) * tokens]


def call(
    kernel, name, outs, args, scratch=(), flops=0, exps=0, limit=16, specs=None, after=(), **more
):
    size = sum(math.prod(x.shape) * x.dtype.itemsize for x in list(args) + list(outs))
    more.setdefault("out_specs", [VMEM for _ in outs])
    specs = list(specs or [VMEM for _ in args]) + [HBM for _ in after]
    count = len(args)

    def run(*refs):
        kernel(*refs[:count], *refs[count + len(after) :])

    return pl.pallas_call(
        run,
        name=name,
        out_shape=list(outs),
        in_specs=specs,
        scratch_shapes=list(scratch),
        cost_estimate=pl.CostEstimate(flops=flops, bytes_accessed=size, transcendentals=exps),
        compiler_params=pltpu.CompilerParams(vmem_limit_bytes=limit * MIB),
        **more,
    )(*args, *after)


def body(q_lin, k_lin, v_lin, log_decay, gate, norm_gain, queries, keys, values, order):
    tokens, width = q_lin.shape
    heads = log_decay.shape[0]
    kv_width = keys.shape[1]
    kv_heads = kv_width // HD
    n, nh = lax.axis_size("ctx"), lax.axis_size("head")
    group = 4
    groups = n // group
    per = heads // group
    rows = per * HD + 16
    cube = tokens * width * HD
    shape = jax.ShapeDtypeStruct

    def swap(x, s):
        return lax.ppermute(x, "ctx", [(c, c ^ s) for c in range(n)])

    to, back = (0, 2, 3, 1), (0, 2, 3, 1)

    def swap_all(xs, order):
        return [swap(xs[s], s) if s else xs[s] for s in order]

    def ahead(x, d):
        return lax.ppermute(x, "ctx", [(c, (c + d * group) % n) for c in range(n)])

    tri, bias = call(
        triangle_kernel, "triangle", [shape((tokens, tokens), F32)] * 2, (), flops=1 << 31
    )
    (kv,) = call(
        beside_kernel,
        "keys_beside_values",
        [shape((tokens, 2 * kv_width), BF16)],
        (keys, values),
        after=(tri,),
    )
    far = [ahead(kv, d) for d in range(1, groups)]

    *pays, ka, va = call(
        functools.partial(state_kernel, group, heads),
        "block_states",
        [shape((rows, HD), BF16)] * group + [shape((tokens, width), BF16)] * 2,
        (tri, log_decay, k_lin, v_lin),
        [pltpu.VMEM((heads * HD, HD), BF16), pltpu.VMEM((group * 16, HD), F32)],
        flops=4 * cube,
        exps=2 * tokens * width,
    )
    pays = swap_all(pays, to)
    intra, qa, gain, decay = call(
        functools.partial(intra_kernel, heads),
        "intra_block",
        [
            shape((tokens, width), F32),
            shape((tokens, width), BF16),
            shape((tokens, width), F32),
            shape((tokens, width), F32),
        ],
        (tri, bias, log_decay, q_lin, ka, va, gate, norm_gain.reshape(1, width)),
        flops=4 * cube,
        exps=4 * tokens * width,
    )

    slots = pltpu.VMEM((group, rows, HD), BF16)
    carry = ()
    if groups > 1:
        (total,) = call(
            functools.partial(total_kernel, group, per, to),
            "group_state",
            [shape((rows, HD), BF16)],
            pays,
            [slots],
            flops=2 * per * HD * HD * group,
            after=(intra,),
        )
        before = ahead(total, 1)
        shift = 1
        while shift < groups - 1:
            mine = lax.div(lax.axis_index("ctx"), group)
            later = jnp.where(mine >= 1, before, 0).astype(F32)
            earlier = ahead(later.astype(BF16), shift)
            earlier = jnp.where(mine >= shift + 1, earlier, 0).astype(F32)
            step = later[per * HD :][:per] + later[per * HD + 8 :][:per]
            prior = earlier[per * HD :][:per] + earlier[per * HD + 8 :][:per]
            state = later[: per * HD] + jnp.repeat(step, HD, axis=0) * earlier[: per * HD]
            both = jnp.where(mine >= shift + 1, step * prior, step)
            high = both.astype(BF16).astype(F32)
            pad = jnp.zeros((8 - per, HD), F32)
            before = jnp.concatenate([state, high, pad, both - high, pad], axis=0).astype(BF16)
            shift *= 2
        carry = (before,)
    prefixes = call(
        functools.partial(prefix_kernel, group, per, to, bool(carry)),
        "prefix_states",
        [shape((per * HD, HD), BF16)] * group,
        (*pays, *carry),
        [slots, pltpu.VMEM((group, per * HD, HD), BF16)],
        flops=1 << 33,
    )
    prefixes = swap_all(prefixes, back)

    (own,) = call(
        stack_kernel,
        "stack_keys_values",
        [shape((groups * tokens, kv.shape[1]), BF16)],
        (kv, *far),
        after=(total,) if groups > 1 else (intra,),
        flops=1 << 32,
    )
    side, near = swap(own, 2), swap(own, 1)
    half = shape((own.shape[0] // 2, own.shape[1]), BF16)
    upper, under = call(halves_kernel, "sent_on", [half] * 2, (side, near))
    across = jnp.concatenate([swap(upper, 1), swap(under, 2)])
    share = width // kv_heads
    pack = 2 if share // HD % 2 == 0 else 1
    span = own.shape[0]
    room = 24 + 48 * span * tokens * 4 // MIB
    smem = pl.BlockSpec(memory_space=pltpu.SMEM)

    def scratch(count):
        keys = count * span
        return [pltpu.VMEM((keys, 2 * HD), BF16), pltpu.VMEM((tokens, keys), F32)]

    acc, *tops = call(
        functools.partial(softmax_first_kernel, group, (0, 2, 1), kv_heads, pack),
        "softmax_first",
        [shape((tokens, 2 * width), F32)] + [shape((tokens, share), F32)] * kv_heads,
        (order, queries, own, side, near),
        scratch(3),
        flops=12 * tokens * width * span,
        exps=3 * tokens * span * width // HD,
        limit=room,
        specs=[smem] + [VMEM] * 4,
    )
    (attended,) = call(
        functools.partial(softmax_last_kernel, group, (3,), kv_heads, pack),
        "softmax_last",
        [shape((tokens, width), BF16)],
        (order, queries, across, acc, *tops),
        scratch(1),
        flops=4 * tokens * width * span,
        exps=tokens * span * width // HD,
        limit=room,
        specs=[smem] + [VMEM] * (3 + kv_heads),
    )

    lin, squares = call(
        functools.partial(inter_kernel, group, heads, back),
        "inter_block",
        [shape((tokens, width), F32), shape((8, tokens), F32)],
        (decay, qa, intra, *prefixes),
        [pltpu.VMEM((heads * HD, HD), BF16)],
        flops=2 * cube,
        after=tops[:1],
    )
    if nh & (nh - 1) == 0:
        turns = [[(i, i ^ d) for i in range(nh)] for d in range(nh - 1, 0, -1)]
    else:
        turns = [[(i, (i + d) % nh) for i in range(nh)] for d in range(1, nh)]
    parts = [squares] + [lax.ppermute(squares, "head", turn) for turn in turns]
    pieces = 4 if width % (4 * HD) == 0 else 1
    return call(
        functools.partial(results_kernel, float(width * nh), pieces),
        "results",
        [shape((tokens, width), BF16)] * 2,
        (attended, lin, gain, *parts),
        [pltpu.VMEM((tokens, width), BF16), pltpu.SemaphoreType.DMA((pieces + 1,))],
        flops=4 * tokens * width,
        out_specs=[HBM] * 2,
    )


def solution(mesh):
    return jax.shard_map(
        body,
        mesh=mesh,
        in_specs=(
            P("ctx", "head"),
            P("ctx", "head"),
            P("ctx", "head"),
            P("head", "ctx"),
            P("ctx", "head"),
            P("head"),
            P("ctx", "head"),
            P("ctx", "head"),
            P("ctx", "head"),
            P("ctx"),
        ),
        out_specs=(P("ctx", "head"), P("ctx", "head")),
        check_vma=False,
    )
```

```python
import functools
import math

import jax
import jax.numpy as jnp
from jax import lax
from jax.experimental import pallas as pl
from jax.experimental.pallas import tpu as pltpu
from jax.sharding import PartitionSpec as P

HD = 128
EPS = 1e-06
HIGH = lax.Precision.HIGHEST
F32 = jnp.float32
BF16 = jnp.bfloat16
NT = (((1,), (1,)), ((), ()))
MIB = 1 << 20
VMEM = pl.BlockSpec(memory_space=pltpu.VMEM)
HBM = pl.BlockSpec(memory_space=pltpu.HBM)


def inverse(x):
    guess = pl.reciprocal(x, approx=True)
    return guess * (2.0 - x * guess)


def silu16(x):
    x = x.astype(F32)
    return (x / (1.0 + jnp.exp(-x))).astype(BF16)


def lower_ones(size):
    rows = lax.broadcasted_iota(jnp.int32, (size, size), 0)
    cols = lax.broadcasted_iota(jnp.int32, (size, size), 1)
    return rows >= cols


def head_cols(h):
    return slice(h * HD, (h + 1) * HD)


def my_rank(group):
    return lax.rem(lax.axis_index("ctx"), group)


def dyn(index, size):
    return pl.ds(pl.multiple_of(index * size, size), size)


def triangle_kernel(ones_ref, bias_ref):
    lower = lower_ones(ones_ref.shape[0])
    ones_ref[...] = lower.astype(F32)
    bias_ref[...] = jnp.where(lower, 0.0, -1e30)


def state_kernel(group, heads, tri_ref, ld_ref, k_ref, v_ref, *rest):
    outs, (ka_ref, va_ref, states, totals) = rest[:group], rest[group:]
    tokens = k_ref.shape[0]
    per = heads // group
    rank = my_rank(group)
    ld = ld_ref[...]
    cum = lax.dot_general(ld, tri_ref[...], NT, precision=HIGH, preferred_element_type=F32)
    weight = jnp.exp(cum[:, tokens - 1 : tokens] - cum)
    total = jnp.broadcast_to(jnp.exp(jnp.sum(ld, axis=1, keepdims=True)), (heads, HD))
    high = total.astype(BF16).astype(F32)
    low = total - high
    totals[...] = jnp.zeros_like(totals)
    for k in range(group):
        totals[k * 16 : k * 16 + per, :] = high[k * per : (k + 1) * per]
        totals[k * 16 + 8 : k * 16 + 8 + per, :] = low[k * per : (k + 1) * per]
    for h in range(heads):
        ka = silu16(k_ref[:, head_cols(h)])
        va = silu16(v_ref[:, head_cols(h)])
        ka_ref[:, head_cols(h)] = ka
        va_ref[:, head_cols(h)] = va
        kdec = jnp.transpose(ka).astype(F32) * weight[h : h + 1, :]
        khigh = kdec.astype(BF16)
        klow = (kdec - khigh.astype(F32)).astype(BF16)
        state = jnp.dot(khigh, va, preferred_element_type=F32)
        state += jnp.dot(klow, va, preferred_element_type=F32)
        states[h * HD : (h + 1) * HD, :] = state.astype(BF16)
    for s in range(group):
        dest = rank ^ s
        outs[s][: per * HD, :] = states[dyn(dest, per * HD), :]
        outs[s][per * HD :, :] = totals[dyn(dest, 16), :].astype(BF16)


def beside_kernel(keys, values, out):
    width = keys.shape[1]
    out[:, :width] = keys[...]
    out[:, width:] = values[...]


def stack_kernel(*refs):
    tokens = refs[0].shape[0]
    for i, part in enumerate(refs[:-1]):
        refs[-1][i * tokens : (i + 1) * tokens, :] = part[...]


def halves_kernel(a_ref, b_ref, a_out, b_out):
    half = a_out.shape[0]
    a_out[...] = a_ref[:half, :]
    b_out[...] = b_ref[half:, :]


def decay_row(slots, k, base, j):
    tail = slots[k, base : base + 16, :].astype(F32)
    return tail[j : j + 1] + tail[8 + j : 9 + j]


def fill_slots(order, rank, pays, slots):
    for s, pay in zip(order, pays):
        slots[rank ^ s] = pay[...]


def total_kernel(group, per, order, *refs):
    pays, out, slots = refs[:group], refs[group], refs[group + 1]
    fill_slots(order, my_rank(group), pays, slots)
    base = per * HD
    tails = []
    for j in range(per):
        state = slots[0, j * HD : (j + 1) * HD, :].astype(F32)
        whole = decay_row(slots, 0, base, j)
        for k in range(1, group):
            decay = decay_row(slots, k, base, j)
            state = decay * state + slots[k, j * HD : (j + 1) * HD, :].astype(F32)
            whole = whole * decay
        out[j * HD : (j + 1) * HD, :] = state.astype(BF16)
        tails.append(whole)
    pad = [jnp.zeros((8 - per, HD), F32)] if per < 8 else []
    total = jnp.concatenate(tails + pad, axis=0)
    high = total.astype(BF16).astype(F32)
    out[base:, :] = jnp.concatenate([high, total - high], axis=0).astype(BF16)


def prefix_kernel(group, per, order, carried, *refs):
    pays, refs = refs[:group], refs[group:]
    carry = None
    if carried:
        carry, refs = refs[0], refs[1:]
    outs, slots, prefixes = refs[:group], refs[group], refs[group + 1]
    rank = my_rank(group)
    later = lax.axis_index("ctx") >= group
    fill_slots(order, rank, pays, slots)
    base = per * HD
    for j in range(per):
        rows = slice(j * HD, (j + 1) * HD)
        state = jnp.zeros((HD, HD), F32)
        if carried:
            state = jnp.where(later, carry[rows, :].astype(F32), state)
        prefixes[0, rows, :] = state.astype(BF16)
        for k in range(group - 1):
            state = decay_row(slots, k, base, j) * state + slots[k, rows, :].astype(F32)
            prefixes[k + 1, rows, :] = state.astype(BF16)
    for s in range(group):
        outs[s][...] = prefixes[rank ^ s]


def intra_kernel(heads, tri_ref, bias_ref, ld_ref, q_ref, ka_ref, va_ref, gate_ref, gain_ref, *outs):
    intra_ref, qa_ref, gain_out, decay_out = outs
    ld = ld_ref[...]
    tri = tri_ref[...]
    bias = bias_ref[...]
    cum = lax.dot_general(tri, ld, NT, precision=HIGH, preferred_element_type=F32)
    cum_t = lax.dot_general(ld, tri, NT, precision=HIGH, preferred_element_type=F32)
    for h in range(heads):
        cols = head_cols(h)
        qa = silu16(q_ref[:, cols])
        qa_ref[:, cols] = qa
        decay_out[:, cols] = jnp.exp(jnp.broadcast_to(cum[:, h : h + 1], qa.shape))
        scores = lax.dot_general(qa, ka_ref[:, cols], NT, preferred_element_type=F32)
        decay = jnp.exp((cum[:, h : h + 1] - cum_t[h : h + 1, :]) + bias)
        weights = (scores * decay).astype(BF16)
        intra_ref[:, cols] = jnp.dot(weights, va_ref[:, cols], preferred_element_type=F32)
        gate = 1.0 / (1.0 + jnp.exp(-gate_ref[:, cols].astype(F32)))
        gain_out[:, cols] = gate * gain_ref[:, cols]


def inter_kernel(group, heads, order, decay_ref, qa_ref, intra_ref, *rest):
    parts, (lin_ref, squares_ref, states) = rest[:group], rest[group:]
    tokens = qa_ref.shape[0]
    per = heads // group
    rank = my_rank(group)
    for s, part in zip(order, parts):
        states[dyn(rank ^ s, per * HD), :] = part[...]
    acc = jnp.zeros((tokens, HD), F32)
    for h in range(heads):
        cols = head_cols(h)
        state = states[h * HD : (h + 1) * HD, :]
        inter = jnp.dot(qa_ref[:, cols], state, preferred_element_type=F32)
        lin = intra_ref[:, cols] + inter * decay_ref[:, cols]
        lin_ref[:, cols] = lin
        acc += lin * lin
    ones = jnp.ones((8, HD), F32)
    squares_ref[...] = lax.dot_general(ones, acc, NT, precision=HIGH, preferred_element_type=F32)


def results_kernel(columns, parts, attended_ref, lin_ref, gain_ref, *rest):
    squares, (mixed_out, attended_out, mixed_ref, sems) = rest[:-4], rest[-4:]
    first = pltpu.make_async_copy(attended_ref, attended_out, sems.at[parts])
    first.start()
    total = squares[0][...]
    for part in squares[1:]:
        total = total + part[...]
    inv = jnp.transpose(lax.rsqrt(total / columns + EPS))[:, 0:1]
    width = lin_ref.shape[1] // parts
    copies = []
    for i in range(parts):
        cols = slice(i * width, (i + 1) * width)
        mixed_ref[:, cols] = (lin_ref[:, cols] * inv * gain_ref[:, cols]).astype(BF16)
        copies.append(
            pltpu.make_async_copy(mixed_ref.at[:, cols], mixed_out.at[:, cols], sems.at[i])
        )
        copies[-1].start()
    for copy in copies:
        copy.wait()
    first.wait()


def softmax_bias(group, sides, order_ref, bias):
    tokens, span = bias.shape[0], bias.shape[1] // len(sides)
    groups = span // tokens
    me = lax.axis_index("ctx")
    rank, mine = lax.rem(me, group), lax.div(me, group)
    qpos = order_ref[0] * tokens + lax.broadcasted_iota(jnp.int32, (tokens, tokens), 0)
    kpos = lax.broadcasted_iota(jnp.int32, (tokens, tokens), 1)
    for i, s in enumerate(sides):
        for d in range(groups):
            place = lax.rem(mine + groups - d, groups) * group + (rank ^ s)
            at = i * span + d * tokens
            bias[:, at : at + tokens] = jnp.where(place * tokens + kpos <= qpos, 0.0, -1e30)


def softmax_values(held, g, kv_heads, values):
    span = held[0].shape[0]
    values[:, HD:] = jnp.ones((span * len(held), HD), BF16)
    for i, ref in enumerate(held):
        values[i * span : (i + 1) * span, :HD] = ref[:, head_cols(kv_heads + g)]


def softmax_scores(query, held, g, bias):
    raw = [
        lax.dot_general(query, ref[:, head_cols(g)], NT, preferred_element_type=F32) for ref in held
    ]
    raw = jnp.concatenate(raw, axis=1)
    raw = raw.reshape(-1, *bias.shape) + bias[...][None]
    return raw.reshape(-1, bias.shape[1])


def stacked(ref, columns):
    return jnp.concatenate([ref[:, cols] for cols in columns], axis=0)


SCORE = math.log2(math.e) / math.sqrt(HD)


def softmax_first_kernel(group, sides, kv_heads, pack, order_ref, q_ref, *rest):
    arrays, rest = rest[: len(sides)], rest[len(sides) :]
    acc_ref, tops, (values, bias) = rest[0], rest[1:-2], rest[-2:]
    tokens = q_ref.shape[0]
    share = q_ref.shape[1] // HD // kv_heads
    softmax_bias(group, sides, order_ref, bias)
    for g in range(kv_heads):
        softmax_values(arrays, g, kv_heads, values)
        for j in range(0, share, pack):
            heads = range(g * share + j, g * share + j + pack)
            raw = softmax_scores(stacked(q_ref, map(head_cols, heads)), arrays, g, bias)
            top = jnp.max(raw, axis=-1, keepdims=True)
            probs = jnp.exp2((raw - top) * SCORE).astype(BF16)
            acc = jnp.dot(probs, values[...], preferred_element_type=F32)
            for i, h in enumerate(heads):
                rows = slice(i * tokens, (i + 1) * tokens)
                acc_ref[:, 2 * h * HD : 2 * (h + 1) * HD] = acc[rows]
                tops[g][:, head_cols(j + i)] = jnp.broadcast_to(top[rows], (tokens, HD))


def softmax_last_kernel(group, sides, kv_heads, pack, order_ref, q_ref, *rest):
    arrays, rest = rest[: len(sides)], rest[len(sides) :]
    acc_ref, tops, (out_ref, values, bias) = rest[0], rest[1:-3], rest[-3:]
    tokens = q_ref.shape[0]
    share = q_ref.shape[1] // HD // kv_heads
    softmax_bias(group, sides, order_ref, bias)
    for g in range(kv_heads):
        softmax_values(arrays, g, kv_heads, values)
        for j in range(0, share, pack):
            heads = range(g * share + j, g * share + j + pack)
            raw = softmax_scores(stacked(q_ref, map(head_cols, heads)), arrays, g, bias)
            old = stacked(tops[g], map(head_cols, range(j, j + pack)))
            top = jnp.maximum(old, jnp.max(raw, axis=-1, keepdims=True))
            spread = jnp.concatenate([top] * (raw.shape[1] // HD), axis=1)
            probs = jnp.exp2((raw - spread) * SCORE).astype(BF16)
            acc = jnp.dot(probs, values[...], preferred_element_type=F32)
            held = stacked(acc_ref, [slice(2 * h * HD, 2 * (h + 1) * HD) for h in heads])
            alpha = jnp.exp2((old - top) * SCORE)
            acc += held * jnp.concatenate([alpha, alpha], axis=1)
            out = (acc[:, :HD] * inverse(acc[:, HD:])).astype(BF16)
            for i, h in enumerate(heads):
                out_ref[:, head_cols(h)] = out[i * tokens : (i + 1) * tokens]


def call(
    kernel, name, outs, args, scratch=(), flops=0, exps=0, limit=16, specs=None, after=(), **more
):
    size = sum(math.prod(x.shape) * x.dtype.itemsize for x in list(args) + list(outs))
    more.setdefault("out_specs", [VMEM for _ in outs])
    specs = list(specs or [VMEM for _ in args]) + [HBM for _ in after]
    count = len(args)

    def run(*refs):
        kernel(*refs[:count], *refs[count + len(after) :])

    return pl.pallas_call(
        run,
        name=name,
        out_shape=list(outs),
        in_specs=specs,
        scratch_shapes=list(scratch),
        cost_estimate=pl.CostEstimate(flops=flops, bytes_accessed=size, transcendentals=exps),
        compiler_params=pltpu.CompilerParams(vmem_limit_bytes=limit * MIB),
        **more,
    )(*args, *after)


def body(q_lin, k_lin, v_lin, log_decay, gate, norm_gain, queries, keys, values, order):
    tokens, width = q_lin.shape
    heads = log_decay.shape[0]
    kv_width = keys.shape[1]
    kv_heads = kv_width // HD
    n, nh = lax.axis_size("ctx"), lax.axis_size("head")
    group = 4
    groups = n // group
    per = heads // group
    rows = per * HD + 16
    cube = tokens * width * HD
    shape = jax.ShapeDtypeStruct

    def swap(x, s):
        return lax.ppermute(x, "ctx", [(c, c ^ s) for c in range(n)])

    to, back = (0, 2, 3, 1), (0, 3, 2, 1)

    def swap_all(xs, order):
        return [swap(xs[s], s) if s else xs[s] for s in order]

    def ahead(x, d):
        return lax.ppermute(x, "ctx", [(c, (c + d * group) % n) for c in range(n)])

    tri, bias = call(
        triangle_kernel, "triangle", [shape((tokens, tokens), F32)] * 2, (), flops=1 << 31
    )
    (kv,) = call(
        beside_kernel,
        "keys_beside_values",
        [shape((tokens, 2 * kv_width), BF16)],
        (keys, values),
        after=(tri,),
    )
    far = [ahead(kv, d) for d in range(1, groups)]

    *pays, ka, va = call(
        functools.partial(state_kernel, group, heads),
        "block_states",
        [shape((rows, HD), BF16)] * group + [shape((tokens, width), BF16)] * 2,
        (tri, log_decay, k_lin, v_lin),
        [pltpu.VMEM((heads * HD, HD), BF16), pltpu.VMEM((group * 16, HD), F32)],
        flops=4 * cube,
        exps=2 * tokens * width,
    )
    pays = swap_all(pays, to)
    intra, qa, gain, decay = call(
        functools.partial(intra_kernel, heads),
        "intra_block",
        [
            shape((tokens, width), F32),
            shape((tokens, width), BF16),
            shape((tokens, width), F32),
            shape((tokens, width), F32),
        ],
        (tri, bias, log_decay, q_lin, ka, va, gate, norm_gain.reshape(1, width)),
        flops=4 * cube,
        exps=4 * tokens * width,
    )

    slots = pltpu.VMEM((group, rows, HD), BF16)
    carry = ()
    if groups > 1:
        (total,) = call(
            functools.partial(total_kernel, group, per, to),
            "group_state",
            [shape((rows, HD), BF16)],
            pays,
            [slots],
            flops=2 * per * HD * HD * group,
            after=(intra,),
        )
        before = ahead(total, 1)
        shift = 1
        while shift < groups - 1:
            mine = lax.div(lax.axis_index("ctx"), group)
            later = jnp.where(mine >= 1, before, 0).astype(F32)
            earlier = ahead(later.astype(BF16), shift)
            earlier = jnp.where(mine >= shift + 1, earlier, 0).astype(F32)
            step = later[per * HD :][:per] + later[per * HD + 8 :][:per]
            prior = earlier[per * HD :][:per] + earlier[per * HD + 8 :][:per]
            state = later[: per * HD] + jnp.repeat(step, HD, axis=0) * earlier[: per * HD]
            both = jnp.where(mine >= shift + 1, step * prior, step)
            high = both.astype(BF16).astype(F32)
            pad = jnp.zeros((8 - per, HD), F32)
            before = jnp.concatenate([state, high, pad, both - high, pad], axis=0).astype(BF16)
            shift *= 2
        carry = (before,)
    prefixes = call(
        functools.partial(prefix_kernel, group, per, to, bool(carry)),
        "prefix_states",
        [shape((per * HD, HD), BF16)] * group,
        (*pays, *carry),
        [slots, pltpu.VMEM((group, per * HD, HD), BF16)],
        flops=1 << 33,
    )
    prefixes = swap_all(prefixes, back)

    (own,) = call(
        stack_kernel,
        "stack_keys_values",
        [shape((groups * tokens, kv.shape[1]), BF16)],
        (kv, *far),
        after=(total,) if groups > 1 else (intra,),
        flops=1 << 32,
    )
    side, near = swap(own, 2), swap(own, 1)
    half = shape((own.shape[0] // 2, own.shape[1]), BF16)
    upper, under = call(halves_kernel, "sent_on", [half] * 2, (side, near))
    across = jnp.concatenate([swap(upper, 1), swap(under, 2)])
    share = width // kv_heads
    pack = 2 if share // HD % 2 == 0 else 1
    span = own.shape[0]
    room = 24 + 48 * span * tokens * 4 // MIB
    smem = pl.BlockSpec(memory_space=pltpu.SMEM)

    def scratch(count):
        keys = count * span
        return [pltpu.VMEM((keys, 2 * HD), BF16), pltpu.VMEM((tokens, keys), F32)]

    acc, *tops = call(
        functools.partial(softmax_first_kernel, group, (0, 1), kv_heads, pack),
        "softmax_first",
        [shape((tokens, 2 * width), F32)] + [shape((tokens, share), F32)] * kv_heads,
        (order, queries, own, near),
        scratch(2),
        flops=12 * tokens * width * span,
        exps=3 * tokens * span * width // HD,
        limit=room,
        specs=[smem] + [VMEM] * 3,
    )
    (attended,) = call(
        functools.partial(softmax_last_kernel, group, (2, 3), kv_heads, pack),
        "softmax_last",
        [shape((tokens, width), BF16)],
        (order, queries, side, across, acc, *tops),
        scratch(2),
        flops=4 * tokens * width * span,
        exps=tokens * span * width // HD,
        limit=room,
        specs=[smem] + [VMEM] * (4 + kv_heads),
    )

    lin, squares = call(
        functools.partial(inter_kernel, group, heads, back),
        "inter_block",
        [shape((tokens, width), F32), shape((8, tokens), F32)],
        (decay, qa, intra, *prefixes),
        [pltpu.VMEM((heads * HD, HD), BF16)],
        flops=2 * cube,
        after=tops[:1],
    )
    if nh & (nh - 1) == 0:
        turns = [[(i, i ^ d) for i in range(nh)] for d in range(nh - 1, 0, -1)]
    else:
        turns = [[(i, (i + d) % nh) for i in range(nh)] for d in range(1, nh)]
    parts = [squares] + [lax.ppermute(squares, "head", turn) for turn in turns]
    pieces = 4 if width % (4 * HD) == 0 else 1
    return call(
        functools.partial(results_kernel, float(width * nh), pieces),
        "results",
        [shape((tokens, width), BF16)] * 2,
        (attended, lin, gain, *parts),
        [pltpu.VMEM((tokens, width), BF16), pltpu.SemaphoreType.DMA((pieces + 1,))],
        flops=4 * tokens * width,
        out_specs=[HBM] * 2,
    )


def solution(mesh):
    return jax.shard_map(
        body,
        mesh=mesh,
        in_specs=(
            P("ctx", "head"),
            P("ctx", "head"),
            P("ctx", "head"),
            P("head", "ctx"),
            P("ctx", "head"),
            P("head"),
            P("ctx", "head"),
            P("ctx", "head"),
            P("ctx", "head"),
            P("ctx"),
        ),
        out_specs=(P("ctx", "head"), P("ctx", "head")),
        check_vma=False,
    )
```
